32 devices in a mesh: fsdp: 8 (over z, x), tp: 4 (over y, core).
Axes of the slice: x: 2, y: 2, z: 4, core: 2. Of those that a mesh axis runs over, the one named last changes fastest.
Arguments:
- inputs: bfloat16 [4096, 2048], P(('fsdp', 'tp')), may hold values from -6 to 6
- out_grad: bfloat16 [4096, 2048], P(('fsdp', 'tp')), may hold values from -6 to 6
- segments: int32 [4096], P('fsdp'), may hold values from 0 to 4095, as said below
- routes: int32 [4096, 8], P(('fsdp', 'tp')), may hold values from 0 to 31, all different within a row; in each aligned block of 128 rows (0 to 127, 128 to 255, ...) at most 48 rows name the same one
- attn_gain: float32 [2048], replicated, may hold values from 0.25 to 1.75
- w_query: bfloat16 [2048, 2048], P('fsdp', 'tp'), may hold values from -0.125 to 0.125
- w_key: bfloat16 [2048, 2048], P('fsdp', 'tp'), may hold values from -0.125 to 0.125
- w_value: bfloat16 [2048, 2048], P('fsdp', 'tp'), may hold values from -0.125 to 0.125
- w_output: bfloat16 [2048, 2048], P('tp', 'fsdp'), may hold values from -0.75 to 0.75
- moe_gain: float32 [2048], replicated, may hold values from 0.25 to 1.75
- router: bfloat16 [2048, 32], replicated, may hold values from -0.0625 to 0.0625
- w_gate: bfloat16 [32, 2048, 1024], P('fsdp', None, 'tp'), may hold values from -0.125 to 0.125
- w_up: bfloat16 [32, 2048, 1024], P('fsdp', None, 'tp'), may hold values from -0.125 to 0.125
- w_down: bfloat16 [32, 1024, 2048], P('fsdp', 'tp'), may hold values from -0.5 to 0.5
Outputs:
- output: bfloat16 [4096, 2048], P(('fsdp', 'tp'))
- input_grad: float32 [4096, 2048], P(('fsdp', 'tp'))
- attn_gain_grad: float32 [2048], P(('fsdp', 'tp'))
- w_query_grad: float32 [2048, 2048], P('fsdp', 'tp')
- w_key_grad: float32 [2048, 2048], P('fsdp', 'tp')
- w_value_grad: float32 [2048, 2048], P('fsdp', 'tp')
- w_output_grad: float32 [2048, 2048], P('tp', 'fsdp')
- moe_gain_grad: float32 [2048], P(('fsdp', 'tp'))
- router_grad: float32 [2048, 32], P(('fsdp', 'tp'))
- w_gate_grad: float32 [32, 2048, 1024], P('fsdp', None, 'tp')
- w_up_grad: float32 [32, 2048, 1024], P('fsdp', None, 'tp')
- w_down_grad: float32 [32, 1024, 2048], P('fsdp', 'tp')
The draws below stay inside these ranges and needn't reach their ends.
Inputs may be any that keep to these rules, and one draw needn't show every extreme that they name: `routes`: each row names 8 different experts; in the rows of one device no expert is named more than 48 times. `segments`: numbers never fall along the tokens; a document's tokens are consecutive and lie within one sequence of 512 tokens; sequence i carries numbers from i * 512 to (i + 1) * 512 - 1, its last token the highest of them.
All inputs are finite; a program needn't handle non-finite values.
Results may differ from the reference program's by a relative error of at most 0.025.
Values may be sent and summed in bfloat16 or wider, within the bound.
A program may use at most 320 MiB of HBM per device.

```python
import math
import jax
import jax.numpy as jnp
import numpy as np
from jax import lax

D = 2048
HEADS = 16
HEAD = 128
FF = 1024
TOP = 8
TOK_DEV = 128
SEQ = 512
TOKENS = 4096
EXPERTS = 32
CAP = 48
N_TP = 4


def draw_segments(key, part):
    key = jax.random.fold_in(key, 7)
    start_key, finish_key, spacing_key, bits_key = jax.random.split(key, 4)
    sequences = TOKENS // SEQ
    starts = jax.random.randint(start_key, (sequences, 1), 0, TOK_DEV)
    finish = jax.random.randint(finish_key, (sequences, 1), SEQ - TOK_DEV + 1, SEQ + 1)
    spacing = jax.random.randint(spacing_key, (sequences, 1), 1, 6)
    random_bits = jax.random.randint(bits_key, (sequences, SEQ), 0, 65536)
    places = jnp.arange(SEQ, dtype=jnp.int32)[None, :]
    boundary = random_bits & jnp.left_shift(1, spacing) - 1 == 0
    inside = (places > starts) & (places < finish)
    boundary = boundary & ~inside | (places == starts) | (places == finish) | (places == 0)
    local_ids = jnp.cumsum(boundary.astype(jnp.int32), axis=1) - 1
    highest = local_ids[:, SEQ - 1:SEQ]
    tops = (jnp.arange(sequences, dtype=jnp.int32)[:, None] + 1) * SEQ - 1
    numbers = local_ids - highest + tops
    return numbers.reshape(TOKENS).astype(jnp.int32)


def strengthened(array, rng, source, target, shards_of, factor):
    owner, partner = [(jnp.arange(array.shape[dim]) // (array.shape[dim] // shards_of)).reshape([-1 if axis == dim else 1 for axis in range(array.ndim)]) for dim in (source, target)]
    chosen = jax.random.permutation(rng, shards_of)[partner]
    strong = (owner == chosen) | (owner == (partner + shards_of // 2) % shards_of)
    return jnp.where(strong, factor * array, array)


def block_levels(rng, dims, cuts, smallest, largest):
    def one(dim, blocks):
        heights = jax.random.uniform(jax.random.fold_in(jax.random.fold_in(rng, 6), dim), (blocks,), jnp.float32, smallest / len(cuts), largest / len(cuts))
        return jnp.repeat(jnp.exp(heights), dims[dim] // blocks).reshape((-1,) + (1,) * (len(dims) - dim - 1))

    level = one(*cuts[0])
    for cut in cuts[1:]:
        level = level * one(*cut)
    return level


def assign_block(rng, own, number, rows, count, top, limit, lean):
    sequence = jax.random.permutation(rng, count)
    heavy_load, ordinary = load_shares(count, rows * top, limit, lean, True), load_shares(count, rows * top, limit, lean, False)
    places = jnp.arange(count)

    def named(tallies, offset_by):
        used = int((tallies > 0).sum())
        fixed = max(1, used // 4)
        moved = fixed + (places - fixed + offset_by * (used - fixed)) % max(1, count - fixed)
        return jnp.zeros((count,), jnp.int32).at[sequence[jnp.where(places < fixed, places, moved)]].set(jnp.asarray(tallies, jnp.int32))

    tallies = jnp.where(number % 4 == 0, named(heavy_load, number // 4), named(ordinary, number - number // 4 - 1))
    mixed = jax.random.permutation(jax.random.fold_in(own, 3), count)
    giver, taker = mixed[0:count // 2 * 2:2], mixed[1:count // 2 * 2:2]
    margin = jnp.minimum(tallies[giver] - 1, limit - tallies[taker]) // 2
    margin = jnp.where((giver == sequence[0]) | (taker == sequence[0]) | (tallies[taker] == 0), 0, jnp.maximum(margin, 0))
    moved = jax.random.randint(jax.random.fold_in(own, 4), (count // 2,), 0, 1 << 20) % (margin + 1)
    tallies = tallies.at[giver].add(-moved).at[taker].add(moved)
    members = jnp.searchsorted(jnp.cumsum(tallies), jnp.arange(rows * top), side="right").astype(jnp.int32)
    grid = members.reshape(top, rows).T
    grid = grid[jax.random.permutation(jax.random.fold_in(own, 1), rows)]
    offset_by = jax.random.randint(jax.random.fold_in(own, 2), (rows, 1), 0, top)
    return jnp.take_along_axis(grid, (jnp.arange(top)[None, :] + offset_by) % top, axis=1)


def load_shares(number_of, total, most, slope, full):
    loads = [(1 << 20) // math.isqrt(standing ** slope) + 1 for standing in range(1, number_of + 1)]
    largest = most if full else min(most, max(-(-total // number_of), total * loads[0] // sum(loads)))
    least = 1 if total - largest >= number_of - 1 else 0
    counts, surplus = [largest] + [least] * (number_of - 1), total - largest - least * (number_of - 1)
    while surplus > 0:
        movable = [i for i in range(1, number_of) if counts[i] < largest] or [i for i in range(1, number_of) if counts[i] < most]
        whole, remaining = sum([loads[i] for i in movable]), surplus
        for i in movable:
            extra = min(most - counts[i], max(1, remaining * loads[i] // whole), surplus)
            counts[i] = counts[i] + extra
            surplus = surplus - extra
    return np.array(counts)


def normal_values(stream_key, shape, width, reach, pieces=(), held_as=jnp.bfloat16):
    loudness = block_levels(stream_key, shape, pieces, -0.22, 0.18) if pieces else 1.0
    drawn = jax.random.normal(stream_key, shape, jnp.float32) * width * loudness
    return jnp.minimum(jnp.maximum(drawn, -reach), reach).astype(held_as)


def bell_draw_with(stream_key, shape, width, most, cuts, heavy, kind=jnp.bfloat16):
    values = width * jax.random.normal(stream_key, shape, jnp.float32)
    if cuts:
        values = values * block_levels(stream_key, shape, cuts, -0.22, 0.18)
    return jnp.clip(strengthened(values, jax.random.fold_in(stream_key, 3), *heavy), -most, most).astype(kind)


def setup_inputs(seed: int = 0) -> dict:
    key_of = jax.random.split(jax.random.key(seed), 15)
    inputs = normal_values(key_of[0], (TOKENS, D), 1.0, 6.0, ((0, 32),))
    out_grad = bell_draw_with(key_of[1], (TOKENS, D), 1.0, 6.0, ((0, 32),), (0, 1, 32, 2.75))
    segments = draw_segments(jax.random.fold_in(key_of[14], 71), 0)
    routes_keys = jax.random.split(jax.random.fold_in(key_of[3], 1), TOKENS // TOK_DEV)
    routes_turns = jax.random.permutation(jax.random.fold_in(key_of[3], 3), TOKENS // TOK_DEV)
    routes = jax.vmap(lambda own, number: assign_block(jax.random.fold_in(key_of[3], 2), own, number, TOK_DEV, EXPERTS, TOP, CAP, 2))(routes_keys, routes_turns).reshape((TOKENS, TOP))
    attn_gain = jnp.clip(1.0 + 0.15 * jax.random.normal(key_of[4], (D,), jnp.float32), 0.25, 1.75)
    w_query = normal_values(key_of[5], (D, HEADS * HEAD), D ** -0.5, 0.125, ((0, 8), (1, 4)))
    w_key = normal_values(key_of[6], (D, HEADS * HEAD), D ** -0.5, 0.125, ((0, 8), (1, 4)))
    w_value = normal_values(key_of[7], (D, HEADS * HEAD), D ** -0.5, 0.125, ((0, 8), (1, 4)))
    w_output = normal_values(key_of[8], (HEADS * HEAD, D), (D // 32) ** -0.5, 0.75, ((0, 4), (1, 8)))
    moe_gain = jnp.clip(1.0 + 0.15 * jax.random.normal(key_of[9], (D,), jnp.float32), 0.25, 1.75)
    router = normal_values(key_of[10], (D, EXPERTS), (4 * D) ** -0.5, 0.0625)
    w_gate = normal_values(key_of[11], (EXPERTS, D, FF), D ** -0.5, 0.125, ((0, 8), (2, 4)))
    w_up = normal_values(key_of[12], (EXPERTS, D, FF), D ** -0.5, 0.125, ((0, 8), (2, 4)))
    w_down = normal_values(key_of[13], (EXPERTS, FF, D), (FF // 8) ** -0.5, 0.5, ((0, 8), (1, 4)))
    return {"inputs": inputs, "out_grad": out_grad, "segments": segments, "routes": routes, "attn_gain": attn_gain, "w_query": w_query, "w_key": w_key, "w_value": w_value, "w_output": w_output, "moe_gain": moe_gain, "router": router, "w_gate": w_gate, "w_up": w_up, "w_down": w_down}


EPSILON = 1e-05
HIGHEST = lax.Precision.HIGHEST

@jax.custom_vjp
def low(v):
    return lax.optimization_barrier(v.astype(jnp.bfloat16)).astype(jnp.float32)

@jax.custom_vjp
def low_back(v):
    return v

def low_keep(v):
    return (low(v), None)

def low_pass(kept, grad):
    return (grad,)

def back_keep(v):
    return (v, None)

def back_low(kept, grad):
    return (low(grad),)
low.defvjp(low_keep, low_pass)
low_back.defvjp(back_keep, back_low)

def rms_norm(values, gain):
    return values * lax.rsqrt(lax.optimization_barrier(jnp.mean(values * values, axis=-1, keepdims=True)) + EPSILON) * gain

def route_tables(routes_seq):
    flat_routes = routes_seq.reshape(-1)
    hits = (flat_routes[:, None] == jnp.arange(EXPERTS, dtype=jnp.int32)[None, :]).astype(jnp.int32)
    ranks = lax.optimization_barrier(jnp.sum((jnp.cumsum(hits, axis=0) - 1) * hits, axis=1))
    slots = (flat_routes * (N_TP * CAP) + ranks).astype(jnp.int32)
    sources = jnp.full((EXPERTS * N_TP * CAP,), SEQ * TOP, jnp.int32)
    sources = sources.at[slots].set(jnp.arange(SEQ * TOP, dtype=jnp.int32))
    return (slots, sources)

def layer_forward(params, tokens_in, segs, routes_seq, slots, sources):
    attn_gain, w_query, w_key, w_value, w_output, moe_gain, router, w_gate, w_up, w_down = params
    act1 = low(rms_norm(tokens_in, attn_gain))

    def project(weight):
        return low(low_back(jnp.dot(act1, weight, precision=HIGHEST))).reshape(SEQ, HEADS, HEAD)
    query = project(w_query)
    key_rows = project(w_key)
    value_rows = project(w_value)
    raw_scores = low_back(jnp.einsum('qhd,khd->hqk', query, key_rows, precision=HIGHEST)) * (1.0 / math.sqrt(HEAD))
    same_doc = segs[:, None] == segs[None, :]
    scores = jnp.where(same_doc[None], raw_scores, -1e+30)
    softmax_rows = low(jax.nn.softmax(scores, axis=-1))
    attended = jnp.einsum('hqk,khd->qhd', softmax_rows, value_rows, precision=HIGHEST).reshape(SEQ, HEADS * HEAD)
    attended = low(low_back(attended))
    resid = tokens_in + low_back(jnp.dot(attended, w_output, precision=HIGHEST))
    act2 = low(rms_norm(resid, moe_gain))
    logits = jnp.dot(act2, router, precision=HIGHEST)
    chosen = jnp.take_along_axis(logits, routes_seq, axis=1)
    gates = jax.nn.softmax(chosen, axis=-1)
    padded_act = jnp.concatenate([act2, jnp.zeros((1, D), jnp.float32)], 0)
    expert_in = low_back(padded_act[sources // TOP]).reshape(EXPERTS, N_TP * CAP, D)
    gate_pre = low_back(jnp.einsum('esd,edf->esf', expert_in, w_gate, precision=HIGHEST))
    up_pre = low_back(jnp.einsum('esd,edf->esf', expert_in, w_up, precision=HIGHEST))
    hidden = low(jax.nn.silu(gate_pre) * up_pre)
    expert_out = jnp.einsum('esf,efd->esd', hidden, w_down, precision=HIGHEST)
    expert_out = low(low_back(expert_out)).reshape(EXPERTS * N_TP * CAP, D)
    routed = expert_out[slots].reshape(SEQ, TOP, D)
    return resid + lax.optimization_barrier(jnp.sum(gates[:, :, None] * routed, axis=1))

def add_pair(first, second):
    return first + second

def reference(inputs, out_grad, segments, routes, attn_gain, w_query, w_key, w_value, w_output, moe_gain, router, w_gate, w_up, w_down):
    params = (attn_gain.astype(jnp.float32), w_query.astype(jnp.float32), w_key.astype(jnp.float32), w_value.astype(jnp.float32), w_output.astype(jnp.float32), moe_gain.astype(jnp.float32), router.astype(jnp.float32), w_gate.astype(jnp.float32), w_up.astype(jnp.float32), w_down.astype(jnp.float32))
    sequences = TOKENS // SEQ
    stacked = (inputs.astype(jnp.float32).reshape(sequences, SEQ, D), out_grad.astype(jnp.float32).reshape(sequences, SEQ, D), segments.reshape(sequences, SEQ), routes.reshape(sequences, SEQ, TOP))

    def one_sequence(totals, item):
        tokens_in, cotangent, segs, routes_seq = item
        slots, sources = route_tables(routes_seq)

        def forward(weights, values):
            return layer_forward(weights, values, segs, routes_seq, slots, sources)
        result, pullback = jax.vjp(forward, params, tokens_in)
        weight_grads, input_grads = pullback(cotangent)
        totals = jax.tree.map(add_pair, totals, weight_grads)
        return (totals, (result.astype(jnp.bfloat16), input_grads))
    zero_grads = jax.tree.map(jnp.zeros_like, params)
    totals, (results, input_grads) = lax.scan(one_sequence, zero_grads, stacked)
    return (results.reshape(TOKENS, D), input_grads.reshape(TOKENS, D), totals[0], totals[1], totals[2], totals[3], totals[4], totals[5], totals[6], totals[7], totals[8], totals[9])
```

```python
import functools
import math

import jax
import jax.numpy as jnp
from jax import lax
from jax.experimental import pallas as pl
from jax.experimental.pallas import tpu as pltpu
from jax.sharding import PartitionSpec as P

HEAD = 128
LANES = 128
EPSILON = 1e-05
HIGHEST = lax.Precision.HIGHEST
MESH = pl.DeviceIdType.MESH
ANY = pl.BlockSpec(memory_space=pl.ANY)
VMEM = pl.BlockSpec(memory_space=pltpu.VMEM)
MIB = 1 << 20
HBM_BUDGET = 300 * MIB
BF16 = jnp.bfloat16
F32 = jnp.float32


class Place:
    def __init__(self, depth):
        self.depth = depth
        f, t = lax.axis_index("fsdp"), lax.axis_index("tp")
        self.f, self.t = f, t
        self.z, self.x = lax.div(f, 2), lax.rem(f, 2)
        self.y, self.c = lax.div(t, 2), lax.rem(t, 2)
        self.to = {
            "x": (self.z * 2 + 1 - self.x, t),
            "y": (f, (1 - self.y) * 2 + self.c),
            "c": (f, self.y * 2 + 1 - self.c),
            "up": (f + 2, t),
            "down": (f - 2, t),
        }
        self.can_up = self.z < depth - 1
        self.can_down = self.z > 0
        offs = [0]
        for step in range(1, depth):
            offs += [-step, step]
        self.offs = offs

    def valid(self, off):
        if off == 0:
            return None
        return self.z + off >= 0 if off < 0 else self.z + off < self.depth


def when(cond, body):
    if cond is None:
        body()
    else:
        pl.when(cond)(body)


def both(first, second):
    if first is None:
        return second
    if second is None:
        return first
    return jnp.logical_and(first, second)


class Net:
    def __init__(self, place, send_sems, recv_sems, local_sems):
        self.place = place
        self.send_sems, self.recv_sems, self.local_sems = send_sems, recv_sems, local_sems
        self.keys, self.sent, self.locals_used = {}, [], 0

    def slot(self, key):
        return self.keys.setdefault(key, len(self.keys))

    def put(self, src, dst, to, key, cond=None, guard=None):
        copy = pltpu.make_async_remote_copy(
            src_ref=src,
            dst_ref=dst,
            send_sem=self.send_sems.at[len(self.sent)],
            recv_sem=self.recv_sems.at[self.slot(key)],
            device_id=self.place.to[to],
            device_id_type=MESH,
        )
        self.sent.append((both(cond, guard), copy))
        when(cond, copy.start)

    def got(self, dst, key):
        pltpu.make_async_remote_copy(
            src_ref=dst,
            dst_ref=dst,
            send_sem=self.send_sems.at[0],
            recv_sem=self.recv_sems.at[self.slot(key)],
            device_id=self.place.to["c"],
            device_id_type=MESH,
        ).wait_recv()

    def local(self, src, dst):
        copy = pltpu.make_async_copy(src, dst, self.local_sems.at[self.locals_used])
        self.locals_used += 1
        copy.start()
        return copy

    def finish(self):
        for cond, copy in self.sent:
            when(cond, copy.wait_send)


def greet(place, links):
    barrier = pltpu.get_barrier_semaphore()
    count = 0
    for link in links:
        if link == "z":
            for name, cond in (("up", place.can_up), ("down", place.can_down)):
                target = place.to[name]
                pl.when(cond)(
                    lambda target=target: pl.semaphore_signal(
                        barrier, inc=1, device_id=target, device_id_type=MESH
                    )
                )
                count = count + cond.astype(jnp.int32)
        else:
            pl.semaphore_signal(barrier, inc=1, device_id=place.to[link], device_id_type=MESH)
            count = count + 1
    pl.semaphore_wait(barrier, count)


SENDS, RECVS, LOCALS = 160, 160, 24


def sems():
    return [
        pltpu.SemaphoreType.DMA((SENDS,)),
        pltpu.SemaphoreType.DMA((RECVS,)),
        pltpu.SemaphoreType.DMA((LOCALS,)),
    ]


def add_rows(dst, src, rows, step=16):
    def body(i, carry):
        at = pl.ds(pl.multiple_of(i * step, step), step)
        dst[at, :] = (dst[at, :].astype(F32) + src[at, :].astype(F32)).astype(dst.dtype)
        return carry

    lax.fori_loop(0, rows // step, body, 0)


def comm_params(ident, mib=None):
    limit = None if mib is None else mib * MIB
    return pltpu.CompilerParams(collective_id=ident, has_side_effects=True, vmem_limit_bytes=limit)


def spread_zx(net, name, block, own):
    p = net.place
    offs = p.offs

    def step(i):
        if i >= len(offs):
            return
        off = offs[i]
        zz = p.z + off
        valid = p.valid(off)
        ref = block(zz, p.x)

        def body():
            if off:
                net.got(ref, (name, "z", off))

        when(valid, body)
        src = ref if off else own
        if off <= 0:
            net.put(src, ref, "up", (name, "z", off - 1), both(valid, p.can_up))
        if off >= 0:
            net.put(src, ref, "down", (name, "z", off + 1), both(valid, p.can_down))
        net.put(src, ref, "x", (name, "x", off), valid)

    def finish():
        for off in offs:
            ref = block(p.z + off, 1 - p.x)
            when(p.valid(off), lambda: net.got(ref, (name, "x", off)))

    return step, finish


def spread_xz(net, name, block, pair, own, placed):
    p = net.place
    offs = p.offs

    def step(i):
        if i >= len(offs):
            return
        off = offs[i]
        if off == 0:
            net.put(own, block(p.z, p.x), "x", (name, "x"))
            placed.wait()
            net.got(block(p.z, 1 - p.x), (name, "x"))
        valid = p.valid(off)
        ref = pair(p.z + off)
        if off:
            when(valid, lambda: net.got(ref, (name, "z", off)))
        if off <= 0:
            net.put(ref, ref, "up", (name, "z", off - 1), both(valid, p.can_up))
        if off >= 0:
            net.put(ref, ref, "down", (name, "z", off + 1), both(valid, p.can_down))

    return step, lambda: None


def spread_all(net, name, block, own, halves):
    p = net.place
    offs = p.offs
    x, y, c = p.x, p.y, p.c

    def step(i):
        if i < len(offs):
            off = offs[i]
            zz, valid = p.z + off, p.valid(off)
            ref = block(zz, x, y, c, None)
            src = own if off == 0 else ref
            if off:
                when(valid, lambda: net.got(ref, (name, "z", off)))
            if off <= 0:
                net.put(src, ref, "up", (name, "z", off - 1), both(valid, p.can_up))
            if off >= 0:
                net.put(src, ref, "down", (name, "z", off + 1), both(valid, p.can_down))
            if halves:
                first, second = block(zz, x, y, c, 0), block(zz, x, y, c, 1)
                src_a, src_b = (first, second) if off else halves
                net.put(src_a, first, "x", (name, "x1", off), valid)
                net.put(src_b, second, "y", (name, "y1", off), valid)
                net.put(src_b, second, "x", (name, "x3", off), valid)
                net.put(src_a, first, "y", (name, "y3", off), valid)
            else:
                net.put(src, ref, "x", (name, "x1", off), valid)
                net.put(src, ref, "y", (name, "y1", off), valid)
            net.put(src, ref, "c", (name, "c0", off), valid)
        if 0 <= i - 1 < len(offs):
            off = offs[i - 1]
            zz, valid = p.z + off, p.valid(off)
            part = 0 if halves else None
            ref = block(zz, 1 - x, y, c, part)
            when(valid, lambda: net.got(ref, (name, "x1", off)))
            net.put(ref, ref, "y", (name, "y2", off), valid)
            net.put(ref, ref, "c", (name, "c1", off), valid)
            part = 1 if halves else None
            ref = block(zz, x, 1 - y, c, part)
            when(valid, lambda: net.got(ref, (name, "y1", off)))
            if halves:
                net.put(ref, ref, "x", (name, "x2", off), valid)
            net.put(ref, ref, "c", (name, "c2", off), valid)
        if 0 <= i - 2 < len(offs):
            off = offs[i - 2]
            zz, valid = p.z + off, p.valid(off)
            part = 0 if halves else None
            ref = block(zz, 1 - x, 1 - y, c, part)
            when(valid, lambda: net.got(ref, (name, "y2", off)))
            net.put(ref, ref, "c", (name, "c3", off), valid)
            if halves:
                for key, xx, yy, part in (("x2", 1 - x, 1 - y, 1), ("x3", 1 - x, y, 1), ("y3", x, 1 - y, 0)):
                    ref = block(zz, xx, yy, c, part)
                    when(valid, lambda ref=ref, key=key: net.got(ref, (name, key, off)))
                    net.put(ref, ref, "c", (name, "c" + key, off), valid)

    def finish():
        for off in offs:
            zz, valid = p.z + off, p.valid(off)

            def body():
                net.got(block(zz, x, y, 1 - c, None), (name, "c0", off))
                part = 0 if halves else None
                net.got(block(zz, 1 - x, y, 1 - c, part), (name, "c1", off))
                net.got(block(zz, 1 - x, 1 - y, 1 - c, part), (name, "c3", off))
                part = 1 if halves else None
                net.got(block(zz, x, 1 - y, 1 - c, part), (name, "c2", off))
                if halves:
                    net.got(block(zz, 1 - x, 1 - y, 1 - c, 1), (name, "cx2", off))
                    net.got(block(zz, 1 - x, y, 1 - c, 1), (name, "cx3", off))
                    net.got(block(zz, x, 1 - y, 1 - c, 0), (name, "cy3", off))

            when(valid, body)

    return step, finish


def run_flows(place, flows, extra=2):
    for i in range(len(place.offs) + extra):
        for step, _ in flows:
            step(i)
    for _, finish in flows:
        finish()


def first_kernel(
    depth, wq, wk, wv, wo, inp, og, qkv, full_o, rows, grads, qkv_own, send, recv, local
):
    p = Place(depth)
    net = Net(p, send, recv, local)
    w_rows, w_cols = wq.shape
    o_cols = wo.shape[1]

    def column(f):
        return full_o.at[:, pl.ds(pl.multiple_of(f * o_cols, LANES), o_cols)]

    def columns(z):
        return full_o.at[:, pl.ds(pl.multiple_of(z * (2 * o_cols), LANES), 2 * o_cols)]

    def token_block(z, x, y, c, part):
        return grads.at[((z * 2 + x) * 2 + y) * 2 + c]

    for i, w in enumerate((wq, wk, wv)):
        qkv_own[:, pl.ds(i * w_cols, w_cols)] = w[...]
    greet(p, ("x", "y", "c", "z"))
    mine = rows.at[p.t]
    copies = [
        net.local(wo, column(p.f)),
        net.local(qkv_own, qkv.at[p.f]),
        net.local(og, token_block(p.z, p.x, p.y, p.c, None)),
        net.local(inp, mine),
    ]
    net.put(inp, mine, "y", ("rows", "y"))
    net.put(inp, mine, "c", ("rows", "c0"))
    flows = [
        spread_xz(net, "o", lambda z, x: column(z * 2 + x), columns, wo, copies[0]),
        spread_zx(net, "qkv", lambda z, x: qkv.at[z * 2 + x], qkv_own),
        spread_all(net, "og", token_block, og, None),
    ]
    for i in range(len(p.offs) + 2):
        for step, _ in flows:
            step(i)
        if i == 1:
            other = rows.at[(1 - p.y) * 2 + p.c]
            net.got(other, ("rows", "y"))
            net.put(other, other, "c", ("rows", "c1"))
    for _, finish in flows:
        finish()
    net.got(rows.at[p.y * 2 + 1 - p.c], ("rows", "c0"))
    net.got(rows.at[(1 - p.y) * 2 + 1 - p.c], ("rows", "c1"))
    for copy in copies[1:]:
        copy.wait()
    net.finish()


def first_gather(depth, w_query, w_key, w_value, w_output, inputs, out_grad, tp):
    fsdp = 2 * depth
    w_rows, w_cols = w_query.shape
    o_rows, o_cols = w_output.shape
    rows, width = inputs.shape
    return pl.pallas_call(
        functools.partial(first_kernel, depth),
        out_shape=[
            jax.ShapeDtypeStruct((fsdp, w_rows, 3 * w_cols), BF16),
            jax.ShapeDtypeStruct((o_rows, fsdp * o_cols), BF16),
            jax.ShapeDtypeStruct((tp, rows, width), BF16),
            jax.ShapeDtypeStruct((fsdp * tp, rows, width), BF16),
        ],
        in_specs=[VMEM] * 6,
        out_specs=[ANY] * 4,
        scratch_shapes=[pltpu.VMEM((w_rows, 3 * w_cols), BF16)] + sems(),
        compiler_params=comm_params(1, 16),
        name="first_gather",
    )(w_query, w_key, w_value, w_output, inputs, out_grad)


def mix_kernel(
    depth, part, inp, gain, router, mask, rank, resid, gates_out, act_all,
    acc, rc, ry, own, send, recv, local,
):
    p = Place(depth)
    net = Net(p, send, recv, local)
    rows, width = inp.shape
    half = rows // 2
    copy = net.local(part.at[:, p.c], acc)
    greet(p, ("x", "y", "c", "z"))
    net.put(part.at[:, 1 - p.c], rc, "c", ("rc",))
    copy.wait()
    net.got(rc, ("rc",))
    far = 1 - p.y
    add_rows(acc.at[far], rc.at[far], rows)
    net.put(acc.at[far], ry, "y", ("ry",))
    add_rows(acc.at[p.y], rc.at[p.y], rows)
    net.got(ry, ("ry",))

    def norm(i, carry):
        at = pl.ds(pl.multiple_of(i * 16, 16), 16)
        branch = acc[p.y, at, :].astype(F32) + ry[at, :].astype(F32)
        values = inp[at, :].astype(F32) + branch
        resid[at, :] = values
        inverse = lax.rsqrt(jnp.mean(values * values, axis=-1, keepdims=True) + EPSILON)
        own[at, pl.ds(0, width)] = (values * inverse * gain[...]).astype(BF16)
        return carry

    lax.fori_loop(0, rows // 16, norm, 0)
    logits = jnp.dot(own[:, pl.ds(0, width)], router[...], preferred_element_type=F32)
    chosen = mask[...] > 0.0
    peak = jnp.max(jnp.where(chosen, logits, -1e30), axis=1, keepdims=True)
    expo = jnp.where(chosen, jnp.exp(jnp.minimum(logits - peak, 0.0)), 0.0)
    experts = router.shape[1] // 4
    lane = lax.broadcasted_iota(jnp.int32, expo.shape, 1)
    total = jnp.sum(jnp.where(lane < experts, expo, 0.0), axis=1, keepdims=True)
    gates = expo / total
    gates_out[...] = gates
    high = gates.astype(BF16).astype(F32)
    tail = jnp.where(lane < experts, high, jnp.where(lane < 2 * experts, gates - high, rank[...]))
    own[:, pl.ds(width, LANES)] = tail.astype(BF16)

    def block(z, x, y, c, part_of):
        ref = act_all.at[((z * 2 + x) * 2 + y) * 2 + c]
        return ref if part_of is None else ref.at[pl.ds(part_of * half, half)]

    keep = net.local(own, block(p.z, p.x, p.y, p.c, None))
    halves = (own.at[pl.ds(0, half)], own.at[pl.ds(half, half)])
    run_flows(p, [spread_all(net, "act", block, own, halves)])
    keep.wait()
    net.finish()


def mix_gather(depth, part, inputs, gain, router, mask, rank):
    tp, rows, width = part.shape
    wide = width + LANES
    return pl.pallas_call(
        functools.partial(mix_kernel, depth),
        out_shape=[
            jax.ShapeDtypeStruct((rows, width), F32),
            jax.ShapeDtypeStruct((rows, LANES), F32),
            jax.ShapeDtypeStruct((2 * depth * tp, rows, wide), BF16),
        ],
        in_specs=[ANY, VMEM, VMEM, VMEM, VMEM, VMEM],
        out_specs=[VMEM, VMEM, ANY],
        scratch_shapes=[
            pltpu.VMEM((2, rows, width), BF16),
            pltpu.VMEM((2, rows, width), BF16),
            pltpu.VMEM((rows, width), BF16),
            pltpu.VMEM((rows, wide), BF16),
        ]
        + sems(),
        compiler_params=comm_params(2, 24),
        name="mix_gather",
    )(part.reshape(tp // 2, 2, rows, width), inputs, gain[None, :], router, mask, rank)


def expert_kernel(
    capacity, experts, blocks, act, grad, w_gate, w_up, w_down,
    out, back, x_out, g_out, hid_out, gate_out, up_out, tails, o_keep, r_keep,
):
    local_experts, width, hidden = w_gate.shape
    rows = act.shape[1]
    slots = local_experts * capacity
    first = lax.axis_index("fsdp") * local_experts
    tp_lane = lax.axis_index("tp") * experts + first
    pick_row = lax.broadcasted_iota(jnp.int32, (8, LANES), 0)
    pick_lane = lax.broadcasted_iota(jnp.int32, (8, LANES), 1)
    pick = (
        (pick_lane == 2 * experts + first + pick_row) & (pick_row < local_experts)
    ).astype(BF16)
    places = lax.broadcasted_iota(jnp.int32, (capacity, rows), 0).astype(F32)

    def one_hot(b):
        tail = act[b, :, pl.ds(width, LANES)]
        ranks = lax.dot_general(
            pick, tail, (((1,), (1,)), ((), ())), preferred_element_type=F32
        )
        return jnp.concatenate(
            [
                (jnp.broadcast_to(ranks[e : e + 1, :], (capacity, rows)) == places).astype(BF16)
                for e in range(local_experts)
            ],
            axis=0,
        )

    def gather(b, carry):
        hot = one_hot(b)
        picked = jnp.dot(hot, act[b], preferred_element_type=F32)
        pulled = jnp.dot(hot, grad[b], preferred_element_type=F32).astype(BF16)
        at = pl.ds(pl.multiple_of(b * capacity, capacity), capacity)
        for e in range(local_experts):
            part = picked[e * capacity : (e + 1) * capacity]
            x_out[e, at, :] = part[:, :width].astype(BF16)
            tails[e, at, :] = part[:, width:]
            g_out[e, at, :] = pulled[e * capacity : (e + 1) * capacity]
        return carry

    lax.fori_loop(0, blocks, gather, 0)
    last = (((1,), (1,)), ((), ()))
    for e in range(local_experts):
        lane = lax.broadcasted_iota(jnp.int32, tails.shape[1:], 1)
        mine = (lane == first + e) | (lane == experts + first + e)
        gates = jnp.sum(jnp.where(mine, tails[e], 0.0), axis=1, keepdims=True)
        x_rows, g_rows = x_out[e], g_out[e]
        pre = jnp.dot(x_rows, w_gate[e], preferred_element_type=F32)
        up = jnp.dot(x_rows, w_up[e], preferred_element_type=F32)
        raw = lax.dot_general(g_rows, w_down[e], last, preferred_element_type=F32)
        sig = jax.nn.sigmoid(pre)
        silu = pre * sig
        hid = silu * up
        gate_grad = jnp.sum(hid * raw, axis=1, keepdims=True)
        scaled = raw * gates
        hid_low = (hid * gates).astype(BF16)
        gate_low = (scaled * up * sig * (1.0 + pre * (1.0 - sig))).astype(BF16)
        up_low = (scaled * silu).astype(BF16)
        hid_out[e] = hid_low
        gate_out[e] = gate_low
        up_out[e] = up_low
        o_rows = jnp.dot(hid_low, w_down[e], preferred_element_type=F32).astype(BF16)
        r_rows = (
            lax.dot_general(gate_low, w_gate[e], last, preferred_element_type=F32)
            + lax.dot_general(up_low, w_up[e], last, preferred_element_type=F32)
        ).astype(BF16)
        r_tail = jnp.where(lane == tp_lane + e, gate_grad, 0.0).astype(BF16)
        for b in range(blocks):
            at = slice(b * capacity, (b + 1) * capacity)
            o_keep[b, e * capacity : (e + 1) * capacity, :] = o_rows[at]
            r_keep[b, e * capacity : (e + 1) * capacity, pl.ds(0, width)] = r_rows[at]
            r_keep[b, e * capacity : (e + 1) * capacity, pl.ds(width, LANES)] = r_tail[at]

    def combine(b, carry):
        hot = one_hot(b)
        firsts = (((0,), (0,)), ((), ()))
        out[b] = lax.dot_general(hot, o_keep[b], firsts, preferred_element_type=F32).astype(BF16)
        back[b] = lax.dot_general(hot, r_keep[b], firsts, preferred_element_type=F32).astype(BF16)
        return carry

    lax.fori_loop(0, blocks, combine, 0)


def run_experts(act_all, grad_all, w_gate, w_up, w_down, capacity, experts, blocks):
    count, rows, wide = act_all.shape
    width = wide - LANES
    local_experts, _, hidden = w_gate.shape
    steps = count // blocks
    slots = blocks * capacity

    def whole(array):
        return pl.BlockSpec(array.shape, lambda i: (0, 0, 0), pipeline_mode=pl.Buffered(1))

    def token_spec(columns):
        return pl.BlockSpec((blocks, rows, columns), lambda i: (i, 0, 0))

    def slot_spec(columns):
        return pl.BlockSpec((local_experts, slots, columns), lambda i: (0, i, 0))

    total = count * capacity
    shape = jax.ShapeDtypeStruct
    return pl.pallas_call(
        functools.partial(expert_kernel, capacity, experts, blocks),
        grid=(steps,),
        out_shape=[
            shape((count, rows, width), BF16),
            shape((count, rows, wide), BF16),
            shape((local_experts, total, width), BF16),
            shape((local_experts, total, width), BF16),
            shape((local_experts, total, hidden), BF16),
            shape((local_experts, total, hidden), BF16),
            shape((local_experts, total, hidden), BF16),
        ],
        in_specs=[token_spec(wide), token_spec(width), whole(w_gate), whole(w_up), whole(w_down)],
        out_specs=[
            token_spec(width),
            token_spec(wide),
            slot_spec(width),
            slot_spec(width),
            slot_spec(hidden),
            slot_spec(hidden),
            slot_spec(hidden),
        ],
        scratch_shapes=[
            pltpu.VMEM((local_experts, slots, LANES), F32),
            pltpu.VMEM((blocks, local_experts * capacity, width), BF16),
            pltpu.VMEM((blocks, local_experts * capacity, wide), BF16),
        ],
        compiler_params=pltpu.CompilerParams(vmem_limit_bytes=60 * MIB),
        name="experts",
    )(act_all, grad_all, w_gate, w_up, w_down)


def chain_z(net, name, off, acc, up, down, rows):
    p = net.place
    zz, valid = p.z + off, p.valid(off)

    def take(buffer, key):
        net.got(buffer.at[zz], key)
        add_rows(acc(zz), buffer.at[zz], rows)

    if off >= 0:
        when(both(valid, p.can_down), lambda: take(up, (name, "up", off)))
    if off <= 0:
        when(both(valid, p.can_up), lambda: take(down, (name, "down", off)))
    if off > 0:
        net.put(acc(zz), up.at[zz], "up", (name, "up", off - 1), valid)
    if off < 0:
        net.put(acc(zz), down.at[zz], "down", (name, "down", off + 1), valid)


def back_kernel(depth, part, total, acc, rc, ya, xa, xb, yb, up, down, send, recv, local):
    p = Place(depth)
    net = Net(p, send, recv, local)
    x, y, c = p.x, p.y, p.c
    rows, width = total.shape
    half = rows // 2
    a, b = pl.ds(0, half), pl.ds(half, half)
    offs = p.offs[::-1]
    copies = {}
    for off in offs:
        zz, valid = p.z + off, p.valid(off)
        copy = pltpu.make_async_copy(part.at[zz, :, :, c], acc.at[zz], net.local_sems.at[len(copies)])
        when(valid, copy.start)
        copies[off] = copy
    greet(p, ("x", "y", "c", "z"))
    for off in offs:
        zz = p.z + off
        net.put(part.at[zz, :, :, 1 - c], rc.at[zz], "c", ("c", off), p.valid(off))

    def step(i):
        if i < len(offs):
            off = offs[i]
            zz, valid = p.z + off, p.valid(off)

            def body():
                copies[off].wait()
                net.got(rc.at[zz], ("c", off))
                for xx in range(2):
                    for yy in range(2):
                        add_rows(acc.at[zz, xx, yy], rc.at[zz, xx, yy], rows)

            when(valid, body)
            net.put(acc.at[zz, :, 1 - y, a], ya.at[zz], "y", ("ya", off), valid)
            net.put(acc.at[zz, 1 - x, :, b], xb.at[zz], "x", ("xb", off), valid)
        if 0 <= i - 1 < len(offs):
            off = offs[i - 1]
            zz, valid = p.z + off, p.valid(off)

            def body():
                net.got(ya.at[zz], ("ya", off))
                for xx in range(2):
                    add_rows(acc.at[zz, xx, y, a], ya.at[zz, xx], half)

            when(valid, body)
            net.put(acc.at[zz, 1 - x, y, a], xa.at[zz], "x", ("xa", off), valid)

            def body():
                net.got(xb.at[zz], ("xb", off))
                for yy in range(2):
                    add_rows(acc.at[zz, x, yy, b], xb.at[zz, yy], half)

            when(valid, body)
            net.put(acc.at[zz, x, 1 - y, b], yb.at[zz], "y", ("yb", off), valid)
        if 0 <= i - 2 < len(offs):
            off = offs[i - 2]
            zz, valid = p.z + off, p.valid(off)

            def body():
                net.got(xa.at[zz], ("xa", off))
                add_rows(acc.at[zz, x, y, a], xa.at[zz], half)
                net.got(yb.at[zz], ("yb", off))
                add_rows(acc.at[zz, x, y, b], yb.at[zz], half)

            when(valid, body)
            chain_z(net, "z", off, lambda zz: acc.at[zz, x, y], up, down, rows)

    for i in range(len(offs) + 2):
        step(i)

    def last(i, carry):
        at = pl.ds(pl.multiple_of(i * 16, 16), 16)
        total[at, :] = acc[p.z, x, y, at, :].astype(F32)
        return carry

    lax.fori_loop(0, rows // 16, last, 0)
    net.finish()


def reduce_back(depth, part):
    count, rows, wide = part.shape
    half = rows // 2
    return pl.pallas_call(
        functools.partial(back_kernel, depth),
        out_shape=jax.ShapeDtypeStruct((rows, wide), F32),
        in_specs=[ANY],
        out_specs=VMEM,
        scratch_shapes=[
            pltpu.VMEM((depth, 2, 2, rows, wide), BF16),
            pltpu.VMEM((depth, 2, 2, rows, wide), BF16),
            pltpu.VMEM((depth, 2, half, wide), BF16),
            pltpu.VMEM((depth, half, wide), BF16),
            pltpu.VMEM((depth, 2, half, wide), BF16),
            pltpu.VMEM((depth, half, wide), BF16),
            pltpu.VMEM((depth, rows, wide), BF16),
            pltpu.VMEM((depth, rows, wide), BF16),
        ]
        + sems(),
        compiler_params=comm_params(3, 48),
        name="reduce_back",
    )(part.reshape(depth, 2, 2, 2, rows, wide))


def rows_kernel(depth, mine, whole, send, recv, local):
    p = Place(depth)
    net = Net(p, send, recv, local)
    keep = net.local(mine, whole.at[p.t])
    greet(p, ("y", "c"))
    net.put(mine, whole.at[p.t], "y", ("y",))
    net.put(mine, whole.at[p.t], "c", ("c0",))
    other = whole.at[(1 - p.y) * 2 + p.c]
    net.got(other, ("y",))
    net.put(other, other, "c", ("c1",))
    net.got(whole.at[p.y * 2 + 1 - p.c], ("c0",))
    net.got(whole.at[(1 - p.y) * 2 + 1 - p.c], ("c1",))
    keep.wait()
    net.finish()


def gather_rows(depth, mine, tp):
    rows, width = mine.shape
    return pl.pallas_call(
        functools.partial(rows_kernel, depth),
        out_shape=jax.ShapeDtypeStruct((tp, rows, width), mine.dtype),
        in_specs=[ANY],
        out_specs=ANY,
        scratch_shapes=sems(),
        compiler_params=comm_params(4),
        name="gather_rows",
    )(mine)


def last_kernel(
    depth, out_part, tail, qkv_part, o_part, row_part,
    out_sum, q_sum, k_sum, v_sum, o_sum, row_sum,
    acc, rc, ry, rx, up, down, q_acc, q_rx, q_up, q_down, o_acc, o_up, o_down, o_rx,
    t_acc, t_rc, t_ry, send, recv, local,
):
    p = Place(depth)
    net = Net(p, send, recv, local)
    x, y, c = p.x, p.y, p.c
    rows, width = row_sum.shape
    w_rows, w_cols = q_sum.shape
    o_cols = o_sum.shape[1]
    offs = p.offs[::-1]
    main, side = pl.ds(0, width), pl.ds(width, LANES)
    copies, waits = {}, []
    used = 0

    def load(off, src, dst):
        nonlocal used
        copy = pltpu.make_async_copy(src, dst, net.local_sems.at[used])
        used += 1
        when(p.valid(off), copy.start)
        copies.setdefault(off, []).append(copy)

    def pair(ref, z):
        return ref.at[:, pl.ds(pl.multiple_of(z * (2 * o_cols), LANES), 2 * o_cols)]

    o_load = pltpu.make_async_copy(o_part, o_acc, net.local_sems.at[LOCALS - 1])
    o_load.start()
    t_load = pltpu.make_async_copy(row_part.at[:, c], t_acc, net.local_sems.at[LOCALS - 2])
    t_load.start()
    for off in offs:
        zz = p.z + off
        load(off, out_part.at[zz, :, :, c], acc.at[zz, :, :, :, main])
        load(off, tail.at[zz, :, :, c], acc.at[zz, :, :, :, side])
        load(off, qkv_part.at[zz, x], q_acc.at[zz])
    greet(p, ("x", "y", "c", "z"))
    net.put(row_part.at[:, 1 - c], t_rc, "c", ("tc",))
    for off in offs:
        zz, valid = p.z + off, p.valid(off)
        net.put(qkv_part.at[zz, 1 - x], q_rx.at[zz], "x", ("qx", off), valid)
        net.put(out_part.at[zz, :, :, 1 - c], rc.at[zz, :, :, :, main], "c", ("c", off), valid)
        net.put(tail.at[zz, :, :, 1 - c], rc.at[zz, :, :, :, side], "c", ("ct", off), valid)
    o_load.wait()
    t_load.wait()
    net.got(t_rc, ("tc",))
    add_rows(t_acc.at[1 - y], t_rc.at[1 - y], rows)
    net.put(t_acc.at[1 - y], t_ry, "y", ("ty",))

    def step(i):
        if i < len(offs):
            off = offs[i]
            zz, valid = p.z + off, p.valid(off)

            def take(buffer, key):
                net.got(buffer.at[zz], key)
                add_rows(pair(o_acc, zz), buffer.at[zz], o_acc.shape[0])

            if off >= 0:
                when(both(valid, p.can_down), lambda: take(o_up, ("oup", off)))
            if off <= 0:
                when(both(valid, p.can_up), lambda: take(o_down, ("odown", off)))
            if off > 0:
                net.put(pair(o_acc, zz), o_up.at[zz], "up", ("oup", off - 1), valid)
            if off < 0:
                net.put(pair(o_acc, zz), o_down.at[zz], "down", ("odown", off + 1), valid)

            def body():
                for copy in copies[off]:
                    copy.wait()
                net.got(rc.at[zz, :, :, :, main], ("c", off))
                net.got(rc.at[zz, :, :, :, side], ("ct", off))
                for xx in range(2):
                    for yy in range(2):
                        add_rows(acc.at[zz, xx, yy], rc.at[zz, xx, yy], rows)

            when(valid, body)
            net.put(acc.at[zz, :, 1 - y], ry.at[zz], "y", ("y", off), valid)

            def body():
                net.got(q_rx.at[zz], ("qx", off))
                add_rows(q_acc.at[zz], q_rx.at[zz], w_rows)

            when(valid, body)
            chain_z(net, "q", off, lambda zz: q_acc.at[zz], q_up, q_down, w_rows)
        if 0 <= i - 1 < len(offs):
            off = offs[i - 1]
            zz, valid = p.z + off, p.valid(off)

            def body():
                net.got(ry.at[zz], ("y", off))
                for xx in range(2):
                    add_rows(acc.at[zz, xx, y], ry.at[zz, xx], rows)

            when(valid, body)
            net.put(acc.at[zz, 1 - x, y], rx.at[zz], "x", ("x", off), valid)
        if 0 <= i - 2 < len(offs):
            off = offs[i - 2]
            zz, valid = p.z + off, p.valid(off)

            def body():
                net.got(rx.at[zz], ("x", off))
                add_rows(acc.at[zz, x, y], rx.at[zz], rows)

            when(valid, body)
            chain_z(net, "z", off, lambda zz: acc.at[zz, x, y], up, down, rows)
        if i == len(offs) - 1:
            net.put(
                o_acc.at[:, pl.ds(pl.multiple_of((p.z * 2 + 1 - x) * o_cols, LANES), o_cols)],
                o_rx, "x", ("ox",),
            )

    for i in range(len(offs) + 2):
        step(i)
    at_o = pl.ds(pl.multiple_of((p.z * 2 + x) * o_cols, LANES), o_cols)
    net.got(o_rx, ("ox",))

    def o_last(i, carry):
        at = pl.ds(pl.multiple_of(i * 16, 16), 16)
        o_sum[at, :] = o_acc[at, at_o].astype(F32) + o_rx[at, :].astype(F32)
        return carry

    lax.fori_loop(0, o_sum.shape[0] // 16, o_last, 0)

    def q_last(i, carry):
        at = pl.ds(pl.multiple_of(i * 16, 16), 16)
        for j, ref in enumerate((q_sum, k_sum, v_sum)):
            ref[at, :] = q_acc[p.z, at, pl.ds(j * w_cols, w_cols)].astype(F32)
        return carry

    lax.fori_loop(0, w_rows // 16, q_last, 0)
    net.got(t_ry, ("ty",))

    def rows_last(i, carry):
        at = pl.ds(pl.multiple_of(i * 16, 16), 16)
        out_sum[at, :] = acc[p.z, x, y, at, :].astype(F32)
        row_sum[at, :] = (
            t_acc[y, at, :].astype(F32) + t_rc[y, at, :].astype(F32) + t_ry[at, :].astype(F32)
        )
        return carry

    lax.fori_loop(0, rows // 16, rows_last, 0)
    net.finish()


def last_reduce(depth, out_part, tail, qkv_part, o_part, row_part, w_rows, o_cols):
    count, rows, width = out_part.shape
    wide = width + LANES
    w_cols = qkv_part.shape[1] // 3
    o_rows = o_part.shape[0]
    shape = jax.ShapeDtypeStruct
    return pl.pallas_call(
        functools.partial(last_kernel, depth),
        out_shape=[shape((rows, wide), F32)]
        + [shape((w_rows, w_cols), F32)] * 3
        + [shape((o_rows, o_cols), F32), shape((rows, width), F32)],
        in_specs=[ANY] * 5,
        out_specs=[VMEM] * 6,
        scratch_shapes=[
            pltpu.VMEM((depth, 2, 2, rows, wide), BF16),
            pltpu.VMEM((depth, 2, 2, rows, wide), BF16),
            pltpu.VMEM((depth, 2, rows, wide), BF16),
            pltpu.VMEM((depth, rows, wide), BF16),
            pltpu.VMEM((depth, rows, wide), BF16),
            pltpu.VMEM((depth, rows, wide), BF16),
            pltpu.VMEM((depth, w_rows, 3 * w_cols), BF16),
            pltpu.VMEM((depth, w_rows, 3 * w_cols), BF16),
            pltpu.VMEM((depth, w_rows, 3 * w_cols), BF16),
            pltpu.VMEM((depth, w_rows, 3 * w_cols), BF16),
            pltpu.VMEM((o_rows, depth * 2 * o_cols), BF16),
            pltpu.VMEM((depth, o_rows, 2 * o_cols), BF16),
            pltpu.VMEM((depth, o_rows, 2 * o_cols), BF16),
            pltpu.VMEM((o_rows, o_cols), BF16),
            pltpu.VMEM((2, rows, width), BF16),
            pltpu.VMEM((2, rows, width), BF16),
            pltpu.VMEM((rows, width), BF16),
        ]
        + sems(),
        compiler_params=comm_params(5, 62),
        name="last_reduce",
    )(
        out_part.reshape(depth, 2, 2, 2, rows, width),
        tail.reshape(depth, 2, 2, 2, rows, LANES),
        qkv_part.reshape(depth, 2, w_rows, 3 * w_cols),
        o_part,
        row_part.reshape(2, 2, rows, width),
    )


def norm_rows(values, gain):
    inverse = lax.rsqrt(jnp.mean(values * values, axis=-1, keepdims=True) + EPSILON)
    return (values * inverse * gain, inverse)


def norm_back(values, inverse, gain, grad):
    scaled = gain * grad
    gain_grad = jnp.sum(grad * values * inverse, axis=0)
    cubed = inverse * inverse * inverse
    values_grad = inverse * scaled - values * cubed * jnp.mean(
        values * scaled, axis=-1, keepdims=True
    )
    return (values_grad, gain_grad)


def contract_last(left, right):
    return lax.dot_general(
        left, right, (((1,), (1,)), ((), ())), preferred_element_type=jnp.float32
    )


def contract_first(left, right):
    return lax.dot_general(
        left, right, (((0,), (0,)), ((), ())), preferred_element_type=jnp.float32
    )


def dense_layer(
    inputs, out_grad, segments, routes, attn_gain, w_query, w_key, w_value, w_output,
    moe_gain, router, w_gate, w_up, w_down,
):
    tp, fsdp = lax.axis_size("tp"), lax.axis_size("fsdp")
    depth = fsdp // 2
    rows, width = inputs.shape
    local_experts = w_gate.shape[0]
    experts = local_experts * fsdp
    top_k = routes.shape[1]
    capacity = 3 * rows * top_k // (2 * experts)
    w_rows, w_cols = w_query.shape
    heads = w_cols // HEAD
    seq = tp * rows

    named = jnp.any(
        routes[:, :, None] == jnp.arange(experts, dtype=jnp.int32)[None, None, :], axis=1
    )
    hits = named.astype(F32)
    before = (jnp.arange(rows)[:, None] > jnp.arange(rows)[None, :]).astype(F32)
    ranks = jnp.where(named, jnp.dot(before, hits, preferred_element_type=F32), -1.0)
    fill = jnp.zeros((rows, LANES - 3 * experts), F32)
    blank = jnp.zeros((rows, experts), F32)
    mask = jnp.concatenate([hits, hits, blank, fill], axis=1)
    rank = jnp.concatenate([blank, blank, ranks, fill], axis=1)
    router_pad = jnp.concatenate(
        [router, router, jnp.zeros((width, LANES - 2 * experts), BF16)], axis=1
    )

    qkv_full, full_output, whole, grad_all = first_gather(
        depth, w_query, w_key, w_value, w_output, inputs, out_grad, tp
    )
    whole_float = whole.reshape(seq, width).astype(F32)
    normed_one, inverse_one = norm_rows(whole_float, attn_gain)
    act_one = normed_one.astype(BF16)
    qkv_full = qkv_full.reshape(width, 3 * w_cols)
    qkv = jnp.dot(act_one, qkv_full, preferred_element_type=F32).astype(BF16)
    query, key_rows, value_rows = [
        qkv[:, i * w_cols : (i + 1) * w_cols].reshape(seq, heads, HEAD) for i in range(3)
    ]
    score_scale = 1.0 / math.sqrt(HEAD)
    scores = jnp.einsum("qhd,khd->hqk", query, key_rows, preferred_element_type=F32) * score_scale
    scores = jnp.where((segments[:, None] == segments[None, :])[None], scores, -1e30)
    probs = jax.nn.softmax(scores, axis=-1)
    attended = (
        jnp.einsum("hqk,khd->qhd", probs.astype(BF16), value_rows, preferred_element_type=F32)
        .reshape(seq, -1)
        .astype(BF16)
    )
    partial = jnp.dot(attended, full_output, preferred_element_type=F32).astype(BF16)
    resid, gates_wide, act_all = mix_gather(
        depth, partial.reshape(tp, rows, width), inputs, moe_gain, router_pad, mask, rank
    )
    out_part, back_part, x_rows, g_rows, hid_low, gate_low, up_low = run_experts(
        act_all, grad_all, w_gate, w_up, w_down, capacity, experts, min(4, fsdp * tp)
    )
    back = reduce_back(depth, back_part)

    def slots(left, right):
        return jnp.einsum("esd,esf->edf", left, right, preferred_element_type=F32)

    w_gate_grad = slots(x_rows, gate_low)
    w_up_grad = slots(x_rows, up_low)
    w_down_grad = slots(hid_low, g_rows)

    gates = gates_wide[:, :experts]
    act_two = (
        resid
        * (inverse_two := lax.rsqrt(jnp.mean(resid * resid, axis=-1, keepdims=True) + EPSILON))
        * moe_gain
    ).astype(BF16)
    gate_grad = jnp.sum(back[:, width : width + tp * experts].reshape(rows, tp, experts), axis=1)
    logit_grad = gates * (gate_grad - jnp.sum(gates * gate_grad, axis=1, keepdims=True))
    act_two_grad = back[:, :width] + lax.dot_general(
        logit_grad, router.astype(F32), (((1,), (1,)), ((), ())), precision=HIGHEST
    )
    router_part = lax.dot_general(
        act_two.astype(F32), logit_grad, (((0,), (0,)), ((), ())), precision=HIGHEST
    )
    resid_part, gain_two_part = norm_back(resid, inverse_two, moe_gain, act_two_grad)
    resid_grad = out_grad.astype(F32) + resid_part
    branch_grad = gather_rows(depth, resid_grad.astype(BF16), tp).reshape(seq, width)

    attended_grad = (
        contract_last(branch_grad, full_output).astype(BF16).reshape(seq, heads, HEAD)
    )
    o_part = contract_first(attended, branch_grad).astype(BF16)
    prob_grad = jnp.einsum("qhd,khd->hqk", attended_grad, value_rows, preferred_element_type=F32)
    inner = jnp.sum(probs * prob_grad, axis=-1, keepdims=True)
    score_grad = (probs * (prob_grad - inner) * score_scale).astype(BF16)
    query_grad = jnp.einsum("hqk,khd->qhd", score_grad, key_rows, preferred_element_type=F32)
    key_grad = jnp.einsum("hqk,qhd->khd", score_grad, query, preferred_element_type=F32)
    value_grad = jnp.einsum(
        "hqk,qhd->khd", probs.astype(BF16), attended_grad, preferred_element_type=F32
    )
    low = jnp.concatenate(
        [g.reshape(seq, -1).astype(BF16) for g in (query_grad, key_grad, value_grad)], axis=1
    )
    qkv_part = contract_first(act_one, low).astype(BF16)
    act_one_grad = contract_last(low, qkv_full)
    whole_part, gain_one_part = norm_back(whole_float, inverse_one, attn_gain, act_one_grad)

    count = fsdp * tp
    small = jnp.concatenate([router_part, gain_one_part[:, None], gain_two_part[:, None]], axis=1)
    small = small.astype(BF16).reshape(count, width // count, experts + 2)
    tail = jnp.pad(
        small, ((0, 0), (0, rows - width // count), (0, LANES - experts - 2))
    )
    out_sum, q_sum, k_sum, v_sum, o_sum, row_sum = last_reduce(
        depth, out_part, tail, qkv_part, o_part, whole_part.astype(BF16), w_rows, w_output.shape[1]
    )
    output = (resid + out_sum[:, :width]).astype(BF16)
    input_grad = resid_grad + row_sum
    side = out_sum[: width // count, width:]
    return (
        output,
        input_grad,
        side[:, experts],
        q_sum,
        k_sum,
        v_sum,
        o_sum,
        side[:, experts + 1],
        side[:, :experts],
        w_gate_grad,
        w_up_grad,
        w_down_grad,
    )


def send_rows(buffer):
    return lax.all_to_all(buffer, "fsdp", split_axis=1, concat_axis=1, tiled=True)


def per_device(
    inputs,
    out_grad,
    segments,
    routes,
    attn_gain,
    w_query,
    w_key,
    w_value,
    w_output,
    moe_gain,
    router,
    w_gate,
    w_up,
    w_down,
):
    tp_count = lax.axis_size("tp")
    fsdp_count = lax.axis_size("fsdp")
    rows_piece, width = inputs.shape
    head_size = HEAD
    full_query, full_key, full_value, full_output = (
        lax.all_gather(w_query, "fsdp", axis=0, tiled=True),
        lax.all_gather(w_key, "fsdp", axis=0, tiled=True),
        lax.all_gather(w_value, "fsdp", axis=0, tiled=True),
        lax.all_gather(w_output, "fsdp", axis=1, tiled=True),
    )
    whole_rows = lax.all_gather(inputs, "tp", axis=0, tiled=True)
    seq_len = whole_rows.shape[0]
    whole_float = whole_rows.astype(jnp.float32)
    normed_one, inverse_one = norm_rows(whole_float, attn_gain)
    act_one = normed_one.astype(jnp.bfloat16)
    local_heads = full_query.shape[1] // head_size
    query = (
        jnp.dot(act_one, full_query, preferred_element_type=jnp.float32)
        .astype(jnp.bfloat16)
        .reshape(seq_len, local_heads, head_size)
    )
    key_rows = (
        jnp.dot(act_one, full_key, preferred_element_type=jnp.float32)
        .astype(jnp.bfloat16)
        .reshape(seq_len, local_heads, head_size)
    )
    value_rows = (
        jnp.dot(act_one, full_value, preferred_element_type=jnp.float32)
        .astype(jnp.bfloat16)
        .reshape(seq_len, local_heads, head_size)
    )
    block_rows = min(512, seq_len)
    score_scale = 1.0 / math.sqrt(head_size)

    def block_scores(query_block):
        scores = (
            jnp.einsum("qhd,khd->hqk", query_block, key_rows, preferred_element_type=jnp.float32)
            * score_scale
        )
        same_doc = segments[:, None] == segments[None, :]
        return jnp.where(same_doc[None], scores, -1e30)

    scores = block_scores(query)
    peak = jnp.max(scores, axis=-1, keepdims=True)
    expo = jnp.exp(scores - peak)
    total = jnp.sum(expo, axis=-1, keepdims=True)
    softmax_rows = (expo / total).astype(jnp.bfloat16)
    block_outputs = jnp.einsum(
        "hqk,khd->qhd", softmax_rows, value_rows, preferred_element_type=jnp.float32
    )
    log_totals = [peak + jnp.log(total)]
    attended = block_outputs.reshape(seq_len, -1).astype(jnp.bfloat16)
    branch = lax.psum_scatter(
        jnp.dot(attended, full_output, preferred_element_type=jnp.float32).astype(jnp.bfloat16),
        "tp",
        scatter_dimension=0,
        tiled=True,
    ).astype(jnp.float32)
    resid = inputs.astype(jnp.float32) + branch
    normed_two, inverse_two = norm_rows(resid, moe_gain)
    act_two = normed_two.astype(jnp.bfloat16)
    local_experts = w_gate.shape[0]
    experts = local_experts * fsdp_count
    top_k = routes.shape[1]
    capacity = 3 * rows_piece * top_k // (2 * experts)
    logits = jnp.dot(act_two, router, preferred_element_type=jnp.float32)
    picks = (routes[:, :, None] == jnp.arange(experts, dtype=jnp.int32)[None, None, :]).astype(
        jnp.float32
    )
    chosen = jnp.einsum("tke,te->tk", picks, logits, precision=HIGHEST)
    gates = jax.nn.softmax(chosen, axis=-1)
    flat_routes = routes.reshape(-1)
    route_count = flat_routes.shape[0]
    hits = (flat_routes[:, None] == jnp.arange(experts, dtype=jnp.int32)[None, :]).astype(jnp.int32)
    ranks = jnp.sum((jnp.cumsum(hits, axis=0) - 1) * hits, axis=1)
    slots = flat_routes * capacity + ranks
    sources = (
        jnp.full((experts * capacity,), route_count, jnp.int32)
        .at[slots]
        .set(jnp.arange(route_count, dtype=jnp.int32))
    )
    padded_act = jnp.concatenate([act_two, jnp.zeros((1, width), jnp.bfloat16)], 0)
    send_buffer = padded_act[sources // top_k].reshape(
        1, fsdp_count, local_experts * capacity, width
    )
    gate_full, up_full, down_full = (
        lax.all_gather(w_gate, "tp", axis=2, tiled=True),
        lax.all_gather(w_up, "tp", axis=2, tiled=True),
        lax.all_gather(w_down, "tp", axis=1, tiled=True),
    )
    own_in = send_rows(send_buffer)
    own_rows = own_in.reshape(fsdp_count, local_experts, capacity, width)
    own_gate = jnp.einsum("secd,edf->secf", own_rows, gate_full, preferred_element_type=jnp.float32)
    own_up = jnp.einsum("secd,edf->secf", own_rows, up_full, preferred_element_type=jnp.float32)
    own_sigmoid = jax.nn.sigmoid(own_gate)
    own_silu = own_gate * own_sigmoid
    own_hidden = (own_silu * own_up).astype(jnp.bfloat16)
    own_out = jnp.einsum(
        "secf,efd->secd", own_hidden, down_full, preferred_element_type=jnp.float32
    )
    expert_out = own_out.reshape(1, fsdp_count, local_experts * capacity, width).astype(
        jnp.bfloat16
    )
    returned = lax.all_to_all(expert_out, "fsdp", split_axis=1, concat_axis=1, tiled=True).reshape(
        experts * capacity, width
    )
    routed = returned[slots].reshape(rows_piece, top_k, width).astype(jnp.float32)
    mixture = jnp.sum(gates[:, :, None] * routed, axis=1)
    output = (resid + mixture).astype(jnp.bfloat16)
    grad_float = out_grad.astype(jnp.float32)
    gate_grad = jnp.sum(routed * grad_float[:, None, :], axis=2)
    route_grad = (
        (gates[:, :, None] * grad_float[:, None, :])
        .astype(jnp.bfloat16)
        .reshape(route_count, width)
    )
    padded_grad = jnp.concatenate([route_grad, jnp.zeros((1, width), jnp.bfloat16)], 0)
    grad_buffer = padded_grad[sources].reshape(1, fsdp_count, local_experts * capacity, width)
    own_grads = send_rows(grad_buffer).reshape(fsdp_count, local_experts, capacity, width)
    own_hidden_grad = jnp.einsum(
        "secd,efd->secf", own_grads, down_full, preferred_element_type=jnp.float32
    )
    own_gate_low = (
        own_hidden_grad * own_up * own_sigmoid * (1.0 + own_gate * (1.0 - own_sigmoid))
    ).astype(jnp.bfloat16)
    own_up_low = (own_hidden_grad * own_silu).astype(jnp.bfloat16)
    down_term = jnp.einsum(
        "secf,secd->efd", own_hidden, own_grads, preferred_element_type=jnp.float32
    )
    gate_term = jnp.einsum(
        "secd,secf->edf", own_rows, own_gate_low, preferred_element_type=jnp.float32
    )
    up_term = jnp.einsum("secd,secf->edf", own_rows, own_up_low, preferred_element_type=jnp.float32)
    w_gate_grad, w_up_grad, w_down_grad = (
        lax.psum_scatter(
            gate_term.astype(jnp.bfloat16), "tp", scatter_dimension=2, tiled=True
        ).astype(jnp.float32),
        lax.psum_scatter(
            up_term.astype(jnp.bfloat16), "tp", scatter_dimension=2, tiled=True
        ).astype(jnp.float32),
        lax.psum_scatter(
            down_term.astype(jnp.bfloat16), "tp", scatter_dimension=1, tiled=True
        ).astype(jnp.float32),
    )
    own_back = jnp.einsum(
        "secf,edf->secd", own_gate_low, gate_full, preferred_element_type=jnp.float32
    )
    own_back = own_back + jnp.einsum(
        "secf,edf->secd", own_up_low, up_full, preferred_element_type=jnp.float32
    )
    expert_grad = own_back.reshape(1, fsdp_count, local_experts * capacity, width).astype(
        jnp.bfloat16
    )
    back_rows = lax.all_to_all(
        expert_grad, "fsdp", split_axis=1, concat_axis=1, tiled=True
    ).reshape(experts * capacity, width)
    act_two_grad = jnp.sum(
        back_rows[slots].reshape(rows_piece, top_k, width).astype(jnp.float32), axis=1
    )
    centered = gate_grad - jnp.sum(gates * gate_grad, axis=1, keepdims=True)
    chosen_grad = gates * centered
    logit_grad = jnp.einsum("tke,tk->te", picks, chosen_grad, precision=HIGHEST)
    router_float = router.astype(jnp.float32)
    act_two_grad = act_two_grad + lax.dot_general(
        logit_grad, router_float, (((1,), (1,)), ((), ())), precision=HIGHEST
    )
    router_part = lax.dot_general(
        act_two.astype(jnp.float32), logit_grad, (((0,), (0,)), ((), ())), precision=HIGHEST
    )
    resid_part, gain_two_part = norm_back(resid, inverse_two, moe_gain, act_two_grad)
    resid_grad = grad_float + resid_part
    branch_grad = lax.all_gather(resid_grad.astype(jnp.bfloat16), "tp", axis=0, tiled=True)
    attended_grad = (
        contract_last(branch_grad, full_output)
        .astype(jnp.bfloat16)
        .reshape(seq_len, local_heads, head_size)
    )
    w_output_part = contract_first(attended, branch_grad)
    query_parts = []
    key_grad = jnp.zeros((seq_len, local_heads, head_size), jnp.float32)
    value_grad = jnp.zeros((seq_len, local_heads, head_size), jnp.float32)
    for block_index, first_row in enumerate(range(0, seq_len, block_rows)):
        query_block = query
        scores = block_scores(query_block)
        softmax_rows = jnp.exp(scores - log_totals[block_index])
        prob_grad = jnp.einsum(
            "qhd,khd->hqk", attended_grad, value_rows, preferred_element_type=jnp.float32
        )
        inner = jnp.sum(softmax_rows * prob_grad, axis=-1, keepdims=True)
        score_grad = (softmax_rows * (prob_grad - inner) * score_scale).astype(jnp.bfloat16)
        query_parts.append(
            jnp.einsum("hqk,khd->qhd", score_grad, key_rows, preferred_element_type=jnp.float32)
        )
        key_grad = jnp.einsum(
            "hqk,qhd->khd", score_grad, query_block, preferred_element_type=jnp.float32
        )
        value_grad = jnp.einsum(
            "hqk,qhd->khd",
            softmax_rows.astype(jnp.bfloat16),
            attended_grad,
            preferred_element_type=jnp.float32,
        )
    query_low = query_parts[0].reshape(seq_len, -1).astype(jnp.bfloat16)
    key_low = key_grad.reshape(seq_len, -1).astype(jnp.bfloat16)
    value_low = value_grad.reshape(seq_len, -1).astype(jnp.bfloat16)
    w_query_part = contract_first(act_one, query_low)
    w_key_part = contract_first(act_one, key_low)
    w_value_part = contract_first(act_one, value_low)
    act_one_grad = (
        contract_last(query_low, full_query)
        + contract_last(key_low, full_key)
        + contract_last(value_low, full_value)
    )
    whole_part, gain_one_part = norm_back(whole_float, inverse_one, attn_gain, act_one_grad)

    def arrange(values):
        shaped = values.reshape((fsdp_count, tp_count, -1) + values.shape[1:])
        return jnp.swapaxes(shaped, 0, 1)

    input_part, gain_one_tp, gain_two_tp, router_tp = (
        lax.psum_scatter(
            whole_part.astype(jnp.bfloat16), "tp", scatter_dimension=0, tiled=True
        ).astype(jnp.float32),
        lax.psum_scatter(
            arrange(gain_one_part).astype(jnp.bfloat16), "tp", scatter_dimension=0, tiled=True
        ).astype(jnp.float32),
        lax.psum_scatter(
            arrange(gain_two_part).astype(jnp.bfloat16), "tp", scatter_dimension=0, tiled=True
        ).astype(jnp.float32),
        lax.psum_scatter(
            arrange(router_part).astype(jnp.bfloat16), "tp", scatter_dimension=0, tiled=True
        ).astype(jnp.float32),
    )
    input_grad = resid_grad + input_part
    query_sum, key_sum, value_sum, output_sum, gain_one_sum, gain_two_sum, router_sum = (
        lax.psum_scatter(
            w_query_part.astype(jnp.bfloat16), "fsdp", scatter_dimension=0, tiled=True
        ).astype(jnp.float32),
        lax.psum_scatter(
            w_key_part.astype(jnp.bfloat16), "fsdp", scatter_dimension=0, tiled=True
        ).astype(jnp.float32),
        lax.psum_scatter(
            w_value_part.astype(jnp.bfloat16), "fsdp", scatter_dimension=0, tiled=True
        ).astype(jnp.float32),
        lax.psum_scatter(
            w_output_part.astype(jnp.bfloat16), "fsdp", scatter_dimension=1, tiled=True
        ).astype(jnp.float32),
        lax.psum_scatter(
            gain_one_tp.astype(jnp.bfloat16), "fsdp", scatter_dimension=1, tiled=True
        ).astype(jnp.float32),
        lax.psum_scatter(
            gain_two_tp.astype(jnp.bfloat16), "fsdp", scatter_dimension=1, tiled=True
        ).astype(jnp.float32),
        lax.psum_scatter(
            router_tp.astype(jnp.bfloat16), "fsdp", scatter_dimension=1, tiled=True
        ).astype(jnp.float32),
    )
    return (
        output,
        input_grad,
        gain_one_sum.reshape(-1),
        query_sum,
        key_sum,
        value_sum,
        output_sum,
        gain_two_sum.reshape(-1),
        router_sum.reshape(-1, experts),
        w_gate_grad,
        w_up_grad,
        w_down_grad,
    )


def layer(*args):
    tokens = args[0].shape[0] * lax.axis_size("fsdp") * lax.axis_size("tp")
    held = 6 * tokens * (args[0].shape[1] + LANES) * 2
    even = lax.axis_size("tp") == 4 and lax.axis_size("fsdp") % 2 == 0
    experts = args[11].shape[0] * lax.axis_size("fsdp")
    narrow = lax.axis_size("tp") * experts <= LANES and args[1].shape[1] // (lax.axis_size("tp") * lax.axis_size("fsdp")) <= args[0].shape[0]
    if held <= HBM_BUDGET and even and narrow:
        return dense_layer(*args)
    return per_device(*args)


def solution(mesh):
    return jax.shard_map(
        layer,
        mesh=mesh,
        in_specs=(
            P(("fsdp", "tp"), None),
            P(("fsdp", "tp"), None),
            P("fsdp"),
            P(("fsdp", "tp"), None),
            P(),
            P("fsdp", "tp"),
            P("fsdp", "tp"),
            P("fsdp", "tp"),
            P("tp", "fsdp"),
            P(),
            P(),
            P("fsdp", None, "tp"),
            P("fsdp", None, "tp"),
            P("fsdp", "tp", None),
        ),
        out_specs=(
            P(("fsdp", "tp"), None),
            P(("fsdp", "tp"), None),
            P(("fsdp", "tp")),
            P("fsdp", "tp"),
            P("fsdp", "tp"),
            P("fsdp", "tp"),
            P("tp", "fsdp"),
            P(("fsdp", "tp")),
            P(("fsdp", "tp"), None),
            P("fsdp", None, "tp"),
            P("fsdp", None, "tp"),
            P("fsdp", "tp", None),
        ),
        check_vma=False,
    )
```

```python
import functools
import math

import jax
import jax.numpy as jnp
from jax import lax
from jax.experimental import pallas as pl
from jax.experimental.pallas import tpu as pltpu
from jax.sharding import PartitionSpec as P

HEAD = 128
LANES = 128
EPSILON = 1e-05
HIGHEST = lax.Precision.HIGHEST
MESH = pl.DeviceIdType.MESH
ANY = pl.BlockSpec(memory_space=pl.ANY)
VMEM = pl.BlockSpec(memory_space=pltpu.VMEM)
MIB = 1 << 20
HBM_BUDGET = 300 * MIB
BF16 = jnp.bfloat16
F32 = jnp.float32
CONTRACT_FIRST = (((0,), (0,)), ((), ()))
CONTRACT_LAST = (((1,), (1,)), ((), ()))


class Place:
    def __init__(self, depth):
        self.depth = depth
        f, t = lax.axis_index("fsdp"), lax.axis_index("tp")
        self.f, self.t = f, t
        self.z, self.x = lax.div(f, 2), lax.rem(f, 2)
        self.y, self.c = lax.div(t, 2), lax.rem(t, 2)
        self.to = {
            "x": (self.z * 2 + 1 - self.x, t),
            "y": (f, (1 - self.y) * 2 + self.c),
            "c": (f, self.y * 2 + 1 - self.c),
            "up": (f + 2, t),
            "down": (f - 2, t),
        }
        self.can_up = self.z < depth - 1
        self.can_down = self.z > 0
        offs = [0]
        for step in range(1, depth):
            offs += [-step, step]
        self.offs = offs
        tables = [sorted(range(depth), key=lambda zz: (abs(zz - z), zz)) for z in range(depth)]
        self.near = [
            sum(jnp.where(self.z == z, tables[z][i], 0) for z in range(depth)) for i in range(depth)
        ]
        self.far = self.near[::-1]
        self.tables = tables

    def nearest(self, i):
        pairs = [(z, k) for z in range(self.depth) for k in range(self.depth)]
        return sum(
            jnp.where((self.z == z) & (i == k), self.tables[z][k], 0) for z, k in pairs
        )

    def valid(self, off):
        if off == 0:
            return None
        return self.z + off >= 0 if off < 0 else self.z + off < self.depth


def when(cond, body):
    if cond is None:
        body()
    else:
        pl.when(cond)(body)


def both(first, second):
    if first is None:
        return second
    if second is None:
        return first
    return jnp.logical_and(first, second)


class Net:
    def __init__(self, place, send_sems, recv_sems, local_sems):
        self.place = place
        self.send_sems, self.recv_sems, self.local_sems = send_sems, recv_sems, local_sems
        self.keys, self.used, self.sent, self.locals_used = {}, 0, [], 0

    def slot(self, key):
        if len(key) == 4 and key[1] == "at":
            base = self.keys.setdefault(key[0], self.used)
            if base == self.used:
                self.used += key[2]
            return base + key[3]
        base = self.keys.setdefault(key, self.used)
        if base == self.used:
            self.used += 1
        return base

    def put(self, src, dst, to, key, cond=None, guard=None):
        copy = pltpu.make_async_remote_copy(
            src_ref=src,
            dst_ref=dst,
            send_sem=self.send_sems.at[len(self.sent)],
            recv_sem=self.recv_sems.at[self.slot(key)],
            device_id=self.place.to[to],
            device_id_type=MESH,
        )
        self.sent.append((both(cond, guard), copy))
        when(cond, copy.start)

    def got(self, dst, key):
        pltpu.make_async_remote_copy(
            src_ref=dst,
            dst_ref=dst,
            send_sem=self.send_sems.at[0],
            recv_sem=self.recv_sems.at[self.slot(key)],
            device_id=self.place.to["c"],
            device_id_type=MESH,
        ).wait_recv()

    def local(self, src, dst):
        copy = pltpu.make_async_copy(src, dst, self.local_sems.at[self.locals_used])
        self.locals_used += 1
        copy.start()
        return copy

    def finish(self):
        for cond, copy in self.sent:
            when(cond, copy.wait_send)


def greet(place, links):
    barrier = pltpu.get_barrier_semaphore()
    count = 0
    for link in links:
        if link == "z":
            for name, cond in (("up", place.can_up), ("down", place.can_down)):
                target = place.to[name]
                pl.when(cond)(
                    lambda target=target: pl.semaphore_signal(
                        barrier, inc=1, device_id=target, device_id_type=MESH
                    )
                )
                count = count + cond.astype(jnp.int32)
        else:
            pl.semaphore_signal(barrier, inc=1, device_id=place.to[link], device_id_type=MESH)
            count = count + 1
    pl.semaphore_wait(barrier, count)


SENDS, RECVS, LOCALS = 160, 160, 24


def sems():
    return [
        pltpu.SemaphoreType.DMA((SENDS,)),
        pltpu.SemaphoreType.DMA((RECVS,)),
        pltpu.SemaphoreType.DMA((LOCALS,)),
    ]


def add_rows(dst, src, rows, step=16):
    def body(i, carry):
        at = pl.ds(pl.multiple_of(i * step, step), step)
        dst[at, :] = (dst[at, :].astype(F32) + src[at, :].astype(F32)).astype(dst.dtype)
        return carry

    lax.fori_loop(0, rows // step, body, 0)


def comm_params(ident, mib=None):
    limit = None if mib is None else mib * MIB
    return pltpu.CompilerParams(collective_id=ident, has_side_effects=True, vmem_limit_bytes=limit)


def spread_zx(net, name, block, own):
    p = net.place
    offs = p.offs

    def step(i):
        if i >= len(offs):
            return
        off = offs[i]
        zz = p.z + off
        valid = p.valid(off)
        ref = block(zz, p.x)

        def body():
            if off:
                net.got(ref, (name, "z", off))

        when(valid, body)
        src = ref if off else own
        if off <= 0:
            net.put(src, ref, "up", (name, "z", off - 1), both(valid, p.can_up))
        if off >= 0:
            net.put(src, ref, "down", (name, "z", off + 1), both(valid, p.can_down))
        net.put(src, ref, "x", (name, "x", off), valid)

    def finish():
        for off in offs:
            ref = block(p.z + off, 1 - p.x)
            when(p.valid(off), lambda: net.got(ref, (name, "x", off)))

    return step, finish


def spread_xz(net, name, block, pair, own, placed):
    p = net.place
    offs = p.offs

    def step(i):
        if i >= len(offs):
            return
        off = offs[i]
        if off == 0:
            net.put(own, block(p.z, p.x), "x", (name, "x"))
            placed.wait()
            net.got(block(p.z, 1 - p.x), (name, "x"))
        valid = p.valid(off)
        ref = pair(p.z + off)
        if off:
            when(valid, lambda: net.got(ref, (name, "z", off)))
        if off <= 0:
            net.put(ref, ref, "up", (name, "z", off - 1), both(valid, p.can_up))
        if off >= 0:
            net.put(ref, ref, "down", (name, "z", off + 1), both(valid, p.can_down))

    return step, lambda: None


def first_kernel(
    depth, wq, wk, wv, wo, inp, qkv, full_o, rows, send, recv, local
):
    p = Place(depth)
    net = Net(p, send, recv, local)
    w_rows, w_cols = wq.shape
    o_cols = wo.shape[1]

    def column(f):
        return full_o.at[:, pl.ds(pl.multiple_of(f * o_cols, LANES), o_cols)]

    def columns(z):
        return full_o.at[:, pl.ds(pl.multiple_of(z * (2 * o_cols), LANES), 2 * o_cols)]

    greet(p, ("x", "y", "c", "z"))
    mine = rows.at[p.t]
    copies = [net.local(wo, column(p.f)), net.local(inp, mine)] + [
        net.local(w, qkv.at[p.f, :, pl.ds(i * w_cols, w_cols)])
        for i, w in enumerate((wq, wk, wv))
    ]
    net.put(inp, mine, "y", ("rows", "y"))
    net.put(inp, mine, "c", ("rows", "c0"))
    def slab(i):
        at = pl.ds(i * w_cols, w_cols)
        return lambda z, x: qkv.at[z * 2 + x, :, at]

    flows = [
        spread_zx(net, f"w{i}", slab(i), w) for i, w in enumerate((wq, wk, wv))
    ] + [spread_xz(net, "o", lambda z, x: column(z * 2 + x), columns, wo, copies[0])]
    for i in range(len(p.offs) + 2):
        for step, _ in flows:
            step(i)
        if i == 1:
            other = rows.at[(1 - p.y) * 2 + p.c]
            net.got(other, ("rows", "y"))
            net.put(other, other, "c", ("rows", "c1"))
    for _, finish in flows:
        finish()
    net.got(rows.at[p.y * 2 + 1 - p.c], ("rows", "c0"))
    net.got(rows.at[(1 - p.y) * 2 + 1 - p.c], ("rows", "c1"))
    for copy in copies[1:]:
        copy.wait()
    net.finish()


def first_gather(depth, w_query, w_key, w_value, w_output, inputs, tp):
    fsdp = 2 * depth
    w_rows, w_cols = w_query.shape
    o_rows, o_cols = w_output.shape
    rows, width = inputs.shape
    return pl.pallas_call(
        functools.partial(first_kernel, depth),
        out_shape=[
            jax.ShapeDtypeStruct((fsdp, w_rows, 3 * w_cols), BF16),
            jax.ShapeDtypeStruct((o_rows, fsdp * o_cols), BF16),
            jax.ShapeDtypeStruct((tp, rows, width), BF16),
        ],
        in_specs=[VMEM] * 5,
        out_specs=[ANY] * 3,
        scratch_shapes=sems(),
        compiler_params=comm_params(1, 60),
        name="first_gather",
    )(w_query, w_key, w_value, w_output, inputs)


SITES = {
    "x1": ("x", 0, 0, 0),
    "y1": ("y", 0, 0, 1),
    "x3": ("x", 0, 0, 1),
    "y3": ("y", 0, 0, 0),
    "y2": ("y", 1, 0, 0),
    "x2": ("x", 0, 1, 1),
    "c0": ("c", 0, 0, None),
    "cx": ("c", 1, 0, None),
    "cy": ("c", 0, 1, None),
    "cxy": ("c", 1, 1, None),
}
NAMES = list(SITES)


class Plane:
    def __init__(self, place, everyone, own, sends, recvs):
        self.place, self.everyone, self.own = place, everyone, own
        self.sends, self.recvs = sends, recvs
        self.half = own.shape[0] // 2

    def ref(self, zz, dx, dy, dc, part):
        p = self.place
        x, y, c = p.x + dx - 2 * p.x * dx, p.y + dy - 2 * p.y * dy, p.c + dc - 2 * p.c * dc
        ref = self.everyone.at[((zz * 2 + x) * 2 + y) * 2 + c]
        return ref if part is None else ref.at[pl.ds(part * self.half, self.half)]

    def copy(self, site, zz, src=None):
        link, dx, dy, part = SITES[site]
        dst = self.ref(zz, dx, dy, 0, part)
        at = NAMES.index(site) * self.place.depth + zz
        return pltpu.make_async_remote_copy(
            src_ref=dst if src is None else src,
            dst_ref=dst,
            send_sem=self.sends.at[at],
            recv_sem=self.recvs.at[at],
            device_id=self.place.to[link],
            device_id_type=MESH,
        )

    def take(self, site, zz):
        link, dx, dy, part = SITES[site]
        dx, dy = dx ^ (link == "x"), dy ^ (link == "y")
        ref = self.ref(zz, dx, dy, int(link == "c"), part)
        at = NAMES.index(site) * self.place.depth + zz
        pltpu.make_async_remote_copy(
            src_ref=ref,
            dst_ref=ref,
            send_sem=self.sends.at[at],
            recv_sem=self.recvs.at[at],
            device_id=self.place.to[link],
            device_id_type=MESH,
        ).wait_recv()

    def z_copy(self, zz):
        p = self.place
        base = len(NAMES) * p.depth
        return pltpu.make_async_remote_copy(
            src_ref=self.own,
            dst_ref=self.ref(p.z, 0, 0, 0, None),
            send_sem=self.sends.at[base + zz],
            recv_sem=self.recvs.at[base + p.z],
            device_id=(zz * 2 + p.x, p.t),
            device_id_type=MESH,
        )

    def send_z(self):
        for zz in self.place.near[1:]:
            self.z_copy(zz).start()

    def first(self, zz, mine=False):
        p = self.place
        whole, part_a, part_b = None, None, None
        if mine:
            whole = self.own
            part_a, part_b = whole.at[pl.ds(0, self.half)], whole.at[pl.ds(self.half, self.half)]
        else:
            ref = self.ref(zz, 0, 0, 0, None)
            at = len(NAMES) * p.depth + zz
            pltpu.make_async_remote_copy(
                src_ref=ref,
                dst_ref=ref,
                send_sem=self.sends.at[at],
                recv_sem=self.recvs.at[at],
                device_id=(zz * 2 + p.x, p.t),
                device_id_type=MESH,
            ).wait_recv()
        self.copy("x1", zz, part_a).start()
        self.copy("y1", zz, part_b).start()
        self.copy("x3", zz, part_b).start()
        self.copy("y3", zz, part_a).start()
        self.copy("c0", zz, whole).start()

    def second(self, zz):
        self.take("x1", zz)
        self.copy("y2", zz).start()
        self.take("y1", zz)
        self.copy("x2", zz).start()

    def third(self, zz):
        self.take("x3", zz)
        self.copy("cx", zz).start()
        self.take("y3", zz)
        self.copy("cy", zz).start()
        self.take("x2", zz)
        self.take("y2", zz)
        self.copy("cxy", zz).start()

    def arrived(self, zz):
        for site in ("c0", "cx", "cy", "cxy"):
            self.take(site, zz)

    def finish(self):
        for zz in range(self.place.depth):
            for site in NAMES:
                self.copy(site, zz).wait_send()
            pl.when(self.place.z != zz)(self.z_copy(zz).wait_send)


def plane_sems(depth):
    return [pltpu.SemaphoreType.DMA(((len(NAMES) + 1) * depth,))] * 2


def moe_kernel(
    depth, capacity, experts, blocks,
    part, inp, og, gain, router, mask, rank, gate_hbm, up_hbm, down_hbm,
    resid, gates_out, act_all, grad_all, out_hbm, back_hbm, x_hbm, g_hbm, hid_hbm, gl_hbm, ul_hbm,
    acc, rc, ry, own, w_gate, w_up, w_down, act_in, grad_in, x_rows, g_rows, tails, hid, gl, ul,
    o_keep, r_keep, out, back,
    act_send, act_recv, og_send, og_recv, send, recv, local, load_sems, save_sems,
):
    p = Place(depth)
    net = Net(p, send, recv, local)
    rows, width = inp.shape
    local_experts = w_gate.shape[0]
    weights = [
        net.local(src, dst)
        for src, dst in ((gate_hbm, w_gate), (up_hbm, w_up), (down_hbm, w_down))
    ]
    part_in = net.local(part.at[:, p.c], acc)
    acts = Plane(p, act_all, own, act_send, act_recv)
    grads = Plane(p, grad_all, og, og_send, og_recv)
    barrier = pltpu.get_barrier_semaphore()
    peers = [p.to["x"], p.to["y"], p.to["c"]] + [(zz * 2 + p.x, p.t) for zz in p.near[1:]]
    for peer in peers:
        pl.semaphore_signal(barrier, inc=1, device_id=peer, device_id_type=MESH)
    pl.semaphore_wait(barrier, len(peers))

    net.put(part.at[:, 1 - p.c], rc, "c", ("rc",))
    og_kept = net.local(og, grads.ref(p.z, 0, 0, 0, None))
    grads.send_z()
    part_in.wait()
    net.got(rc, ("rc",))
    far = 1 - p.y
    add_rows(acc.at[far], rc.at[far], rows)
    net.put(acc.at[far], ry, "y", ("ry",))
    grads.first(p.z, True)
    add_rows(acc.at[p.y], rc.at[p.y], rows)
    net.got(ry, ("ry",))

    def norm(i, carry):
        at = pl.ds(pl.multiple_of(i * 16, 16), 16)
        branch = acc[p.y, at, :].astype(F32) + ry[at, :].astype(F32)
        values = inp[at, :].astype(F32) + branch
        resid[at, :] = values
        inverse = lax.rsqrt(jnp.mean(values * values, axis=-1, keepdims=True) + EPSILON)
        own[at, pl.ds(0, width)] = (values * inverse * gain[...]).astype(BF16)
        return carry

    lax.fori_loop(0, rows // 16, norm, 0)
    logits = jnp.dot(own[:, pl.ds(0, width)], router[...], preferred_element_type=F32)
    chosen = mask[...] > 0.0
    peak = jnp.max(jnp.where(chosen, logits, -1e30), axis=1, keepdims=True)
    expo = jnp.where(chosen, jnp.exp(jnp.minimum(logits - peak, 0.0)), 0.0)
    lane = lax.broadcasted_iota(jnp.int32, expo.shape, 1)
    total = jnp.sum(jnp.where(lane < experts, expo, 0.0), axis=1, keepdims=True)
    gates = expo / total
    gates_out[...] = gates
    high = gates.astype(BF16).astype(F32)
    tail = jnp.where(lane < experts, high, jnp.where(lane < 2 * experts, gates - high, rank[...]))
    own[:, pl.ds(width, LANES)] = tail.astype(BF16)
    acts.send_z()
    acts.first(p.z, True)
    act_kept = net.local(own, acts.ref(p.z, 0, 0, 0, None))
    grads.second(p.z)
    acts.second(p.z)
    grads.first(p.near[1])
    grads.third(p.z)
    acts.third(p.z)
    acts.first(p.near[1])
    grads.arrived(p.z)
    acts.arrived(p.z)
    og_kept.wait()
    act_kept.wait()
    for copy in weights:
        copy.wait()

    first_expert = p.f * local_experts
    tp_lane = p.t * experts + first_expert
    pick_row = lax.broadcasted_iota(jnp.int32, (8, LANES), 0)
    pick_lane = lax.broadcasted_iota(jnp.int32, (8, LANES), 1)
    pick = (
        (pick_lane == 2 * experts + first_expert + pick_row) & (pick_row < local_experts)
    ).astype(BF16)
    places = lax.broadcasted_iota(jnp.int32, (capacity, rows), 0).astype(F32)
    slots = blocks * capacity

    def loads(zz, j):
        at = pl.ds((zz * 2 + j) * blocks, blocks)
        return [
            pltpu.make_async_copy(act_all.at[at], act_in.at[j], load_sems.at[j, 0]),
            pltpu.make_async_copy(grad_all.at[at], grad_in.at[j], load_sems.at[j, 1]),
        ]

    def save(zz, j, k):
        if k < 5:
            where = pl.ds(pl.multiple_of((zz * 2 + j) * slots, 16), slots)
            src = (x_rows, g_rows, hid, gl, ul)[k]
            dst = (x_hbm, g_hbm, hid_hbm, gl_hbm, ul_hbm)[k].at[:, where]
        else:
            src = (out, back)[k - 5]
            dst = (out_hbm, back_hbm)[k - 5].at[pl.ds((zz * 2 + j) * blocks, blocks)]
        return pltpu.make_async_copy(src, dst, save_sems.at[k])

    def one_hot(j, b):
        tail = act_in[j, b, :, pl.ds(width, LANES)]
        ranks = lax.dot_general(pick, tail, CONTRACT_LAST, preferred_element_type=F32)
        return jnp.concatenate(
            [
                (jnp.broadcast_to(ranks[e : e + 1, :], (capacity, rows)) == places).astype(BF16)
                for e in range(local_experts)
            ],
            axis=0,
        )

    def work(zz, j, started, serve):
        for copy in loads(zz, j):
            copy.wait()

        def settle(ks):
            def body():
                for k in ks:
                    save(zz, j, k).wait()

            when(started, body)

        settle((0, 1))

        def gather(b, carry):
            hot = one_hot(j, b)
            picked = jnp.dot(hot, act_in[j, b], preferred_element_type=F32)
            pulled = jnp.dot(hot, grad_in[j, b], preferred_element_type=F32).astype(BF16)
            at = pl.ds(pl.multiple_of(b * capacity, 16), capacity)
            for e in range(local_experts):
                piece = picked[e * capacity : (e + 1) * capacity]
                x_rows[e, at, :] = piece[:, :width].astype(BF16)
                tails[e, at, :] = piece[:, width:]
                g_rows[e, at, :] = pulled[e * capacity : (e + 1) * capacity]
            return carry

        lax.fori_loop(0, blocks, gather, 0)
        for k in (0, 1):
            save(zz, j, k).start()
        serve(0)
        settle((2, 3, 4))
        for e in range(local_experts):
            tail_lane = lax.broadcasted_iota(jnp.int32, (slots, LANES), 1)
            mine = (tail_lane == first_expert + e) | (tail_lane == experts + first_expert + e)
            gates_of = jnp.sum(jnp.where(mine, tails[e], 0.0), axis=1, keepdims=True)
            pre = jnp.dot(x_rows[e], w_gate[e], preferred_element_type=F32)
            up = jnp.dot(x_rows[e], w_up[e], preferred_element_type=F32)
            raw = lax.dot_general(g_rows[e], w_down[e], CONTRACT_LAST, preferred_element_type=F32)
            sig = jax.nn.sigmoid(pre)
            silu = pre * sig
            hidden = silu * up
            gate_grad = jnp.sum(hidden * raw, axis=1, keepdims=True)
            scaled = raw * gates_of
            hid_low = (hidden * gates_of).astype(BF16)
            gate_low = (scaled * up * sig * (1.0 + pre * (1.0 - sig))).astype(BF16)
            up_low = (scaled * silu).astype(BF16)
            hid[e] = hid_low
            gl[e] = gate_low
            ul[e] = up_low
            o_rows = jnp.dot(hid_low, w_down[e], preferred_element_type=F32).astype(BF16)
            r_rows = (
                lax.dot_general(gate_low, w_gate[e], CONTRACT_LAST, preferred_element_type=F32)
                + lax.dot_general(up_low, w_up[e], CONTRACT_LAST, preferred_element_type=F32)
            ).astype(BF16)
            r_tail = jnp.where(tail_lane == tp_lane + e, gate_grad, 0.0).astype(BF16)
            for b in range(blocks):
                at = slice(b * capacity, (b + 1) * capacity)
                to = slice(e * capacity, (e + 1) * capacity)
                o_keep[b, to, :] = o_rows[at]
                r_keep[b, to, pl.ds(0, width)] = r_rows[at]
                r_keep[b, to, pl.ds(width, LANES)] = r_tail[at]
            serve(1 + e)
        for k in (2, 3, 4):
            save(zz, j, k).start()
        settle((5, 6))

        def combine(b, carry):
            hot = one_hot(j, b)
            out[b] = lax.dot_general(
                hot, o_keep[b], CONTRACT_FIRST, preferred_element_type=F32
            ).astype(BF16)
            back[b] = lax.dot_general(
                hot, r_keep[b], CONTRACT_FIRST, preferred_element_type=F32
            ).astype(BF16)
            return carry

        lax.fori_loop(0, blocks, combine, 0)
        for k in (5, 6):
            save(zz, j, k).start()

    for copy in loads(p.z, 0):
        copy.start()

    def group(g, carry):
        zz, later, last = p.nearest(g), p.nearest(g + 1), p.nearest(g + 2)
        more, still = g + 1 < depth, g + 2 < depth
        for copy in loads(zz, 1):
            copy.start()

        def serve_one(k):
            if k == 0:
                pl.when(more)(lambda: grads.second(later))
            if k == 1:
                pl.when(more)(lambda: acts.second(later))
            if k == 2:
                pl.when(still)(lambda: grads.first(last))
            if k == 4:
                pl.when(more)(lambda: grads.third(later))

        work(zz, 0, g > 0, serve_one)

        def serve_two(k):
            if k == 0:
                pl.when(more)(lambda: acts.third(later))
            if k == 1:
                pl.when(still)(lambda: acts.first(last))
            if k == 4:

                def ready():
                    grads.arrived(later)
                    acts.arrived(later)
                    for copy in loads(later, 0):
                        copy.start()

                pl.when(more)(ready)

        work(zz, 1, None, serve_two)
        return carry

    lax.fori_loop(0, depth, group, 0)
    for k in range(7):
        save(0, 1, k).wait()
    acts.finish()
    grads.finish()
    net.finish()


def run_moe(
    depth, capacity, experts, part, inputs, out_grad, gain, router, mask, rank, w_gate, w_up, w_down
):
    tp, rows, width = part.shape
    wide = width + LANES
    count = 2 * depth * tp
    local_experts, _, hidden = w_gate.shape
    blocks = tp
    slots = blocks * capacity
    total = count * capacity
    shape = jax.ShapeDtypeStruct
    kept = [shape((local_experts, total, width), BF16)] * 2
    kept += [shape((local_experts, total, hidden), BF16)] * 3
    return pl.pallas_call(
        functools.partial(moe_kernel, depth, capacity, experts, blocks),
        out_shape=[
            shape((rows, width), F32),
            shape((rows, LANES), F32),
            shape((count, rows, wide), BF16),
            shape((count, rows, width), BF16),
            shape((count, rows, width), BF16),
            shape((count, rows, wide), BF16),
        ]
        + kept,
        in_specs=[ANY] + [VMEM] * 6 + [ANY] * 3,
        out_specs=[VMEM] * 2 + [ANY] * 9,
        scratch_shapes=[
            pltpu.VMEM((2, rows, width), BF16),
            pltpu.VMEM((2, rows, width), BF16),
            pltpu.VMEM((rows, width), BF16),
            pltpu.VMEM((rows, wide), BF16),
            pltpu.VMEM(w_gate.shape, BF16),
            pltpu.VMEM(w_up.shape, BF16),
            pltpu.VMEM(w_down.shape, BF16),
            pltpu.VMEM((2, blocks, rows, wide), BF16),
            pltpu.VMEM((2, blocks, rows, width), BF16),
            pltpu.VMEM((local_experts, slots, width), BF16),
            pltpu.VMEM((local_experts, slots, width), BF16),
            pltpu.VMEM((local_experts, slots, LANES), F32),
            pltpu.VMEM((local_experts, slots, hidden), BF16),
            pltpu.VMEM((local_experts, slots, hidden), BF16),
            pltpu.VMEM((local_experts, slots, hidden), BF16),
            pltpu.VMEM((blocks, local_experts * capacity, width), BF16),
            pltpu.VMEM((blocks, local_experts * capacity, wide), BF16),
            pltpu.VMEM((blocks, rows, width), BF16),
            pltpu.VMEM((blocks, rows, wide), BF16),
        ]
        + plane_sems(depth) * 2
        + sems()
        + [pltpu.SemaphoreType.DMA((2, 2)), pltpu.SemaphoreType.DMA((7,))],
        compiler_params=comm_params(2, 60),
        name="moe",
    )(
        part.reshape(tp // 2, 2, rows, width), inputs, out_grad, gain[None, :], router, mask, rank,
        w_gate, w_up, w_down,
    )


def chain_z(net, name, zz, acc, inbox, rows):
    p = net.place
    extra = p.depth

    def take(slot):
        net.got(inbox.at[slot], (name, "at", extra + 1, slot))
        add_rows(acc, inbox.at[slot], rows)

    pl.when((zz >= p.z) & p.can_down)(lambda: take(jnp.where(zz == p.z, extra, zz)))
    pl.when((zz <= p.z) & p.can_up)(lambda: take(zz))
    slot = jnp.where(zz == p.z + 1, extra, zz)
    net.put(acc, inbox.at[slot], "up", (name, "at", extra + 1, slot), zz > p.z)
    net.put(acc, inbox.at[zz], "down", (name, "at", extra + 1, zz), zz < p.z)


def reduce_xy(net, name, fill, acc, ya, xa, xb, yb, inbox):
    p = net.place
    x, y, depth = p.x, p.y, p.depth
    rows = acc.shape[3]
    half = rows // 2
    a, b = pl.ds(0, half), pl.ds(half, half)

    def key(what, zz):
        return (name + what, "at", depth, zz)

    def step(i):
        if i < depth:
            zz = p.far[i]
            fill(i, zz)
            net.put(acc.at[zz, :, 1 - y, a], ya.at[zz], "y", key("ya", zz))
            net.put(acc.at[zz, 1 - x, :, b], xb.at[zz], "x", key("xb", zz))
        if 0 <= i - 1 < depth:
            zz = p.far[i - 1]
            net.got(ya.at[zz], key("ya", zz))
            add_rows(acc.at[zz, 1 - x, y, a], ya.at[zz, 1 - x], half)
            net.put(acc.at[zz, 1 - x, y, a], xa.at[zz], "x", key("xa", zz))
            net.got(xb.at[zz], key("xb", zz))
            add_rows(acc.at[zz, x, 1 - y, b], xb.at[zz, 1 - y], half)
            net.put(acc.at[zz, x, 1 - y, b], yb.at[zz], "y", key("yb", zz))
            add_rows(acc.at[zz, x, y, a], ya.at[zz, x], half)
            add_rows(acc.at[zz, x, y, b], xb.at[zz, y], half)
        if 0 <= i - 2 < depth:
            zz = p.far[i - 2]
            net.got(xa.at[zz], key("xa", zz))
            add_rows(acc.at[zz, x, y, a], xa.at[zz], half)
            net.got(yb.at[zz], key("yb", zz))
            add_rows(acc.at[zz, x, y, b], yb.at[zz], half)
            chain_z(net, name + "z", zz, acc.at[zz, x, y], inbox, rows)

    return step


def reduce_scratch(depth, rows, wide):
    half = rows // 2
    return [
        pltpu.VMEM((depth, 2, 2, rows, wide), BF16),
        pltpu.VMEM((depth, 2, half, wide), BF16),
        pltpu.VMEM((depth, half, wide), BF16),
        pltpu.VMEM((depth, 2, half, wide), BF16),
        pltpu.VMEM((depth, half, wide), BF16),
        pltpu.VMEM((depth + 1, rows, wide), BF16),
    ]


def widen(dst, src, rows):
    def body(i, carry):
        at = pl.ds(pl.multiple_of(i * 16, 16), 16)
        dst[at, :] = src[at, :].astype(F32)
        return carry

    lax.fori_loop(0, rows // 16, body, 0)


def back_kernel(
    depth, part, out_part, x_rows, g_rows, hid, gate_low, up_low,
    total, out_other, w_gate_grad, w_up_grad, w_down_grad,
    acc, ya, xa, xb, yb, inbox, rc, big, left, right, found, found_down,
    send, recv, local, load_sems, save_sems,
):
    p = Place(depth)
    net = Net(p, send, recv, local)
    c = p.c
    rows, width = total.shape
    local_experts = x_rows.shape[0]

    def loads(u):
        e, slot = u // 2, u % 2
        if u % 2 == 0:
            pairs = ((x_rows, big.at[slot]), (gate_low, left.at[slot]), (up_low, right.at[slot]))
        else:
            pairs = ((g_rows, big.at[slot]), (hid, left.at[slot]))
        return [
            pltpu.make_async_copy(src.at[e], dst, load_sems.at[slot, j])
            for j, (src, dst) in enumerate(pairs)
        ]

    def saves(u):
        e = u // 2
        if u % 2 == 0:
            targets = (w_gate_grad, w_up_grad)
            return [
                pltpu.make_async_copy(found.at[j], ref.at[e], save_sems.at[j])
                for j, ref in enumerate(targets)
            ]
        return [pltpu.make_async_copy(found_down, w_down_grad.at[e], save_sems.at[2])]

    units = 2 * local_experts

    def unit(u):
        slot = u % 2
        for copy in loads(u):
            copy.wait()
        if u >= 2:
            for copy in saves(u - 2):
                copy.wait()
        if u % 2 == 0:
            wide = 256

            def body(i, carry):
                at = pl.ds(pl.multiple_of(i * wide, wide), wide)
                tile = big[slot, :, at]
                for j, ref in enumerate((left, right)):
                    found[j, at, :] = lax.dot_general(
                        tile, ref[slot], CONTRACT_FIRST, preferred_element_type=F32
                    )
                return carry

            lax.fori_loop(0, width // wide, body, 0)
        else:
            wide = 512

            def body(i, carry):
                at = pl.ds(pl.multiple_of(i * wide, wide), wide)
                found_down[:, at] = lax.dot_general(
                    left[slot], big[slot, :, at], CONTRACT_FIRST, preferred_element_type=F32
                )
                return carry

            lax.fori_loop(0, width // wide, body, 0)
        for copy in saves(u):
            copy.start()
        if u + 2 < units:
            for copy in loads(u + 2):
                copy.start()

    fills = []
    for i in range(depth):
        zz = p.far[i]
        fills.append(net.local(part.at[zz, :, :, c], acc.at[zz]))
    for u in range(2):
        for copy in loads(u):
            copy.start()
    greet(p, ("x", "y", "c", "z"))
    for i in range(depth):
        zz = p.far[i]
        net.put(part.at[zz, :, :, 1 - c], rc.at[zz], "c", ("c", "at", depth, zz))
    for zz in range(depth):
        net.put(out_part.at[zz, :, :, 1 - c], out_other.at[zz], "c", ("oc", "at", depth, zz))

    def fill(i, zz):
        fills[i].wait()
        net.got(rc.at[zz], ("c", "at", depth, zz))
        for xx in range(2):
            for yy in range(2):
                add_rows(acc.at[zz, xx, yy], rc.at[zz, xx, yy], rows)

    step = reduce_xy(net, "b", fill, acc, ya, xa, xb, yb, inbox)
    u = 0
    for i in range(depth + 2):
        step(i)
        for _ in range(2 if i < depth - 1 else 1):
            if u < units:
                unit(u)
                u += 1
    while u < units:
        unit(u)
        u += 1
    for k in (units - 2, units - 1):
        for copy in saves(k):
            copy.wait()

    def last(i, carry):
        at = pl.ds(pl.multiple_of(i * 16, 16), 16)
        total[at, :] = acc[p.z, p.x, p.y, at, :].astype(F32)
        return carry

    lax.fori_loop(0, rows // 16, last, 0)
    for zz in range(depth):
        net.got(out_other.at[zz], ("oc", "at", depth, zz))
    net.finish()


def reduce_back(depth, part, out_part, x_rows, g_rows, hid, gate_low, up_low):
    count, rows, wide = part.shape
    width = out_part.shape[2]
    local_experts, slots, hidden = hid.shape
    shape = jax.ShapeDtypeStruct
    return pl.pallas_call(
        functools.partial(back_kernel, depth),
        out_shape=[
            shape((rows, wide), F32),
            shape((depth, 2, 2, rows, width), BF16),
            shape((local_experts, width, hidden), F32),
            shape((local_experts, width, hidden), F32),
            shape((local_experts, hidden, width), F32),
        ],
        in_specs=[ANY] * 7,
        out_specs=[VMEM] + [ANY] * 4,
        scratch_shapes=reduce_scratch(depth, rows, wide)
        + [
            pltpu.VMEM((depth, 2, 2, rows, wide), BF16),
            pltpu.VMEM((2, slots, width), BF16),
            pltpu.VMEM((2, slots, hidden), BF16),
            pltpu.VMEM((2, slots, hidden), BF16),
            pltpu.VMEM((2, width, hidden), F32),
            pltpu.VMEM((hidden, width), F32),
        ]
        + sems()
        + [pltpu.SemaphoreType.DMA((2, 3)), pltpu.SemaphoreType.DMA((3,))],
        compiler_params=comm_params(3, 60),
        name="reduce_back",
    )(
        part.reshape(depth, 2, 2, 2, rows, wide),
        out_part.reshape(depth, 2, 2, 2, rows, width),
        x_rows, g_rows, hid, gate_low, up_low,
    )


def attend_back_kernel(
    depth, mine, act_hbm, wqkv_hbm, wo_hbm, qkv_hbm, att_hbm, seg_col, seg_row, out_part, out_other,
    qkv_part, act_grad, o_sum, out_sum,
    acc, ya, xa, xb, yb, inbox, other, bg, act, wqkv, wo, qkv, att, ag, low, o_acc, o_inbox, o_rx,
    send, recv, local, other_sems,
):
    p = Place(depth)
    net = Net(p, send, recv, local)
    x, y, c = p.x, p.y, p.c
    rows, width = out_sum.shape
    seq = act.shape[0]
    cols = wo.shape[0]
    heads = cols // HEAD
    o_cols = o_sum.shape[1]

    def block(t):
        return bg.at[pl.ds(pl.multiple_of(t * rows, rows), rows)]

    own = net.local(mine, block(p.t))
    load_wo = net.local(wo_hbm, wo)
    load_att = net.local(att_hbm, att)
    load_qkv = net.local(qkv_hbm, qkv)
    load_act = net.local(act_hbm, act)
    load_w = net.local(wqkv_hbm, wqkv)
    greet(p, ("x", "y", "c", "z"))
    own.wait()
    net.put(block(p.t), block(p.t), "y", ("bg", "y"))
    net.put(block(p.t), block(p.t), "c", ("bg", "c0"))

    def load_other(i):
        zz = p.far[i]
        return [
            pltpu.make_async_copy(out_part.at[zz, :, :, c], acc.at[zz], other_sems.at[0, i % 2]),
            pltpu.make_async_copy(out_other.at[zz], other.at[i % 2], other_sems.at[1, i % 2]),
        ]

    for i in range(2):
        for copy in load_other(i):
            copy.start()

    def fill(i, zz):
        for copy in load_other(i):
            copy.wait()
        for xx in range(2):
            for yy in range(2):
                add_rows(acc.at[zz, xx, yy], other.at[i % 2, xx, yy], rows)
        if i + 2 < depth:
            for copy in load_other(i + 2):
                copy.start()

    out_step = reduce_xy(net, "out", fill, acc, ya, xa, xb, yb, inbox)

    def o_pair(z):
        return o_acc.at[:, pl.ds(pl.multiple_of(z * (2 * o_cols), LANES), 2 * o_cols)]

    def o_step(i):
        if i < depth:
            chain_z(net, "oz", p.far[i], o_pair(p.far[i]), o_inbox, cols)
        if i == depth - 1:
            theirs = pl.ds(pl.multiple_of((p.z * 2 + 1 - x) * o_cols, LANES), o_cols)
            net.put(o_acc.at[:, theirs], o_rx, "x", ("ox",))

    out_step(0)
    far = block((1 - y) * 2 + c)
    net.got(far, ("bg", "y"))
    net.put(far, far, "c", ("bg", "c1"))
    net.got(block(y * 2 + 1 - c), ("bg", "c0"))
    net.got(block((1 - y) * 2 + 1 - c), ("bg", "c1"))
    load_wo.wait()
    ag[...] = lax.dot_general(
        bg[...], wo[...], CONTRACT_LAST, preferred_element_type=F32
    ).astype(BF16)
    out_step(1)
    load_att.wait()
    wide = 512

    def o_body(i, carry):
        at = pl.ds(pl.multiple_of(i * wide, wide), wide)
        o_acc[:, at] = lax.dot_general(
            att[...], bg[:, at], CONTRACT_FIRST, preferred_element_type=F32
        ).astype(BF16)
        return carry

    lax.fori_loop(0, width // wide, o_body, 0)
    load_qkv.wait()
    scale = 1.0 / math.sqrt(HEAD)
    same = seg_col[...] == seg_row[...]
    for h in range(heads):
        o_step(h)
        out_step(2 + h)
        at = slice(h * HEAD, (h + 1) * HEAD)
        query = qkv[:, h * HEAD : (h + 1) * HEAD]
        keys = qkv[:, cols + h * HEAD : cols + (h + 1) * HEAD]
        values = qkv[:, 2 * cols + h * HEAD : 2 * cols + (h + 1) * HEAD]
        grad = ag[:, at]
        scores = lax.dot_general(query, keys, CONTRACT_LAST, preferred_element_type=F32) * scale
        scores = jnp.where(same, scores, -1e30)
        expo = jnp.exp(scores - jnp.max(scores, axis=-1, keepdims=True))
        probs = expo / jnp.sum(expo, axis=-1, keepdims=True)
        prob_grad = lax.dot_general(grad, values, CONTRACT_LAST, preferred_element_type=F32)
        inner = jnp.sum(probs * prob_grad, axis=-1, keepdims=True)
        score_grad = (probs * (prob_grad - inner) * scale).astype(BF16)
        low[:, at] = jnp.dot(score_grad, keys, preferred_element_type=F32).astype(BF16)
        low[:, cols + h * HEAD : cols + (h + 1) * HEAD] = lax.dot_general(
            score_grad, query, CONTRACT_FIRST, preferred_element_type=F32
        ).astype(BF16)
        low[:, 2 * cols + h * HEAD : 2 * cols + (h + 1) * HEAD] = lax.dot_general(
            probs.astype(BF16), grad, CONTRACT_FIRST, preferred_element_type=F32
        ).astype(BF16)
    for i in range(heads, max(depth, heads)):
        o_step(i)
        out_step(2 + i)
    load_act.wait()
    load_w.wait()
    w_rows = wqkv.shape[1]

    def w_body(f, carry):
        at = pl.ds(pl.multiple_of(f * w_rows, w_rows), w_rows)
        qkv_part[f] = lax.dot_general(
            act[:, at], low[...], CONTRACT_FIRST, preferred_element_type=F32
        ).astype(BF16)
        act_grad[:, at] = lax.dot_general(
            low[...], wqkv[f], CONTRACT_LAST, preferred_element_type=F32
        )
        return carry

    lax.fori_loop(0, wqkv.shape[0], w_body, 0)
    widen(out_sum, acc.at[p.z, x, y], rows)
    net.got(o_rx, ("ox",))
    at_o = pl.ds(pl.multiple_of((p.z * 2 + x) * o_cols, LANES), o_cols)

    def o_last(i, carry):
        at = pl.ds(pl.multiple_of(i * 16, 16), 16)
        o_sum[at, :] = o_acc[at, at_o].astype(F32) + o_rx[at, :].astype(F32)
        return carry

    lax.fori_loop(0, cols // 16, o_last, 0)
    net.finish()


def attend_back(depth, mine, act, wqkv, wo, qkv, att, segments, out_part, out_other, o_cols):
    rows, width = mine.shape
    seq, cols = att.shape
    fsdp, w_rows, w_wide = wqkv.shape
    shape = jax.ShapeDtypeStruct
    return pl.pallas_call(
        functools.partial(attend_back_kernel, depth),
        out_shape=[
            shape((fsdp, w_rows, w_wide), BF16),
            shape((seq, width), F32),
            shape((cols, o_cols), F32),
            shape((rows, width), F32),
        ],
        in_specs=[ANY] * 6 + [VMEM] * 2 + [ANY] * 2,
        out_specs=[VMEM] * 4,
        scratch_shapes=reduce_scratch(depth, rows, width)
        + [
            pltpu.VMEM((2, 2, 2, rows, width), BF16),
            pltpu.VMEM((seq, width), BF16),
            pltpu.VMEM((seq, width), BF16),
            pltpu.VMEM((fsdp, w_rows, w_wide), BF16),
            pltpu.VMEM((cols, width), BF16),
            pltpu.VMEM((seq, w_wide), BF16),
            pltpu.VMEM((seq, cols), BF16),
            pltpu.VMEM((seq, cols), BF16),
            pltpu.VMEM((seq, w_wide), BF16),
            pltpu.VMEM((cols, width), BF16),
            pltpu.VMEM((depth + 1, cols, 2 * o_cols), BF16),
            pltpu.VMEM((cols, o_cols), BF16),
        ]
        + sems()
        + [pltpu.SemaphoreType.DMA((2, 2))],
        compiler_params=comm_params(4, 63),
        name="attend_back",
    )(
        mine, act, wqkv, wo, qkv, att, segments[:, None], segments[None, :],
        out_part.reshape(depth, 2, 2, 2, rows, width), out_other,
    )


def last_kernel(
    depth, tail, qkv_part, row_part, q_sum, k_sum, v_sum, row_sum, tail_sum,
    q_acc, q_rx, q_inbox, t_acc, t_rc, t_ry, s_acc, s_rc, s_ry, s_rx, s_inbox, send, recv, local,
):
    p = Place(depth)
    net = Net(p, send, recv, local)
    x, y, c = p.x, p.y, p.c
    rows, width = row_sum.shape
    w_rows, w_cols = q_sum.shape
    small = s_acc.shape[3]
    loads = [net.local(qkv_part.at[p.far[i], x], q_acc.at[p.far[i]]) for i in range(depth)]
    t_load = net.local(row_part.at[:, c], t_acc)
    s_load = net.local(tail.at[:, :, :, c], s_acc)
    greet(p, ("x", "y", "c", "z"))
    for i in range(depth):
        zz = p.far[i]
        net.put(qkv_part.at[zz, 1 - x], q_rx.at[zz], "x", ("qx", "at", depth, zz))
    net.put(tail.at[:, :, :, 1 - c], s_rc, "c", ("sc",))
    net.put(row_part.at[:, 1 - c], t_rc, "c", ("tc",))
    t_load.wait()
    net.got(t_rc, ("tc",))
    add_rows(t_acc.at[1 - y], t_rc.at[1 - y], rows)
    net.put(t_acc.at[1 - y], t_ry, "y", ("ty",))
    s_load.wait()
    net.got(s_rc, ("sc",))
    for zz in range(depth):
        for xx in range(2):
            add_rows(s_acc.at[zz, xx, 1 - y], s_rc.at[zz, xx, 1 - y], small)
    net.put(s_acc.at[:, :, 1 - y], s_ry, "y", ("sy",))
    for zz in range(depth):
        for xx in range(2):
            add_rows(s_acc.at[zz, xx, y], s_rc.at[zz, xx, y], small)
    for i in range(depth):
        zz = p.far[i]
        loads[i].wait()
        net.got(q_rx.at[zz], ("qx", "at", depth, zz))
        add_rows(q_acc.at[zz], q_rx.at[zz], w_rows)
        chain_z(net, "qz", zz, q_acc.at[zz], q_inbox, w_rows)
        if i == 0:
            net.got(s_ry, ("sy",))
            for z in range(depth):
                for xx in range(2):
                    add_rows(s_acc.at[z, xx, y], s_ry.at[z, xx], small)
            net.put(s_acc.at[:, 1 - x, y], s_rx, "x", ("sx",))
    net.got(s_rx, ("sx",))
    for z in range(depth):
        add_rows(s_acc.at[z, x, y], s_rx.at[z], small)
    for i in range(depth):
        chain_z(net, "sz", p.far[i], s_acc.at[p.far[i], x, y], s_inbox, small)

    def q_last(i, carry):
        at = pl.ds(pl.multiple_of(i * 16, 16), 16)
        for j, ref in enumerate((q_sum, k_sum, v_sum)):
            ref[at, :] = q_acc[p.z, at, pl.ds(j * w_cols, w_cols)].astype(F32)
        return carry

    lax.fori_loop(0, w_rows // 16, q_last, 0)
    net.got(t_ry, ("ty",))

    def rows_last(i, carry):
        at = pl.ds(pl.multiple_of(i * 16, 16), 16)
        row_sum[at, :] = (
            t_acc[y, at, :].astype(F32) + t_rc[y, at, :].astype(F32) + t_ry[at, :].astype(F32)
        )
        return carry

    lax.fori_loop(0, rows // 16, rows_last, 0)
    widen(tail_sum, s_acc.at[p.z, x, y], small)
    net.finish()


def last_reduce(depth, tail, qkv_part, row_part):
    count, small, lanes = tail.shape
    fsdp, w_rows, w_wide = qkv_part.shape
    tp, rows, width = row_part.shape
    w_cols = w_wide // 3
    shape = jax.ShapeDtypeStruct
    return pl.pallas_call(
        functools.partial(last_kernel, depth),
        out_shape=[shape((w_rows, w_cols), F32)] * 3
        + [shape((rows, width), F32), shape((small, lanes), F32)],
        in_specs=[ANY] * 3,
        out_specs=[VMEM] * 5,
        scratch_shapes=[
            pltpu.VMEM((depth, w_rows, w_wide), BF16),
            pltpu.VMEM((depth, w_rows, w_wide), BF16),
            pltpu.VMEM((depth + 1, w_rows, w_wide), BF16),
            pltpu.VMEM((2, rows, width), BF16),
            pltpu.VMEM((2, rows, width), BF16),
            pltpu.VMEM((rows, width), BF16),
            pltpu.VMEM((depth, 2, 2, small, lanes), BF16),
            pltpu.VMEM((depth, 2, 2, small, lanes), BF16),
            pltpu.VMEM((depth, 2, small, lanes), BF16),
            pltpu.VMEM((depth, small, lanes), BF16),
            pltpu.VMEM((depth + 1, small, lanes), BF16),
        ]
        + sems(),
        compiler_params=comm_params(5, 40),
        name="last_reduce",
    )(
        tail.reshape(depth, 2, 2, 2, small, lanes),
        qkv_part.reshape(depth, 2, w_rows, w_wide),
        row_part.reshape(2, 2, rows, width),
    )


def norm_rows(values, gain):
    inverse = lax.rsqrt(jnp.mean(values * values, axis=-1, keepdims=True) + EPSILON)
    return (values * inverse * gain, inverse)


def norm_back(values, inverse, gain, grad):
    scaled = gain * grad
    gain_grad = jnp.sum(grad * values * inverse, axis=0)
    cubed = inverse * inverse * inverse
    values_grad = inverse * scaled - values * cubed * jnp.mean(
        values * scaled, axis=-1, keepdims=True
    )
    return (values_grad, gain_grad)


def contract_last(left, right):
    return lax.dot_general(
        left, right, (((1,), (1,)), ((), ())), preferred_element_type=jnp.float32
    )


def contract_first(left, right):
    return lax.dot_general(
        left, right, (((0,), (0,)), ((), ())), preferred_element_type=jnp.float32
    )


def dense_layer(
    inputs, out_grad, segments, routes, attn_gain, w_query, w_key, w_value, w_output,
    moe_gain, router, w_gate, w_up, w_down,
):
    tp, fsdp = lax.axis_size("tp"), lax.axis_size("fsdp")
    depth = fsdp // 2
    rows, width = inputs.shape
    local_experts = w_gate.shape[0]
    experts = local_experts * fsdp
    top_k = routes.shape[1]
    capacity = 3 * rows * top_k // (2 * experts)
    w_rows, w_cols = w_query.shape
    heads = w_cols // HEAD
    seq = tp * rows

    named = jnp.any(
        routes[:, :, None] == jnp.arange(experts, dtype=jnp.int32)[None, None, :], axis=1
    )
    hits = named.astype(F32)
    before = (jnp.arange(rows)[:, None] > jnp.arange(rows)[None, :]).astype(F32)
    ranks = jnp.where(named, jnp.dot(before, hits, preferred_element_type=F32), -1.0)
    fill = jnp.zeros((rows, LANES - 3 * experts), F32)
    blank = jnp.zeros((rows, experts), F32)
    mask = jnp.concatenate([hits, hits, blank, fill], axis=1)
    rank = jnp.concatenate([blank, blank, ranks, fill], axis=1)
    router_pad = jnp.concatenate(
        [router, router, jnp.zeros((width, LANES - 2 * experts), BF16)], axis=1
    )

    qkv_full, full_output, whole = first_gather(
        depth, w_query, w_key, w_value, w_output, inputs, tp
    )
    whole_float = whole.reshape(seq, width).astype(F32)
    normed_one, inverse_one = norm_rows(whole_float, attn_gain)
    act_one = normed_one.astype(BF16)
    qkv = jnp.dot(act_one, qkv_full.reshape(width, 3 * w_cols), preferred_element_type=F32).astype(BF16)
    query, key_rows, value_rows = [
        qkv[:, i * w_cols : (i + 1) * w_cols].reshape(seq, heads, HEAD) for i in range(3)
    ]
    score_scale = 1.0 / math.sqrt(HEAD)
    scores = jnp.einsum("qhd,khd->hqk", query, key_rows, preferred_element_type=F32) * score_scale
    scores = jnp.where((segments[:, None] == segments[None, :])[None], scores, -1e30)
    probs = jax.nn.softmax(scores, axis=-1)
    attended = (
        jnp.einsum("hqk,khd->qhd", probs.astype(BF16), value_rows, preferred_element_type=F32)
        .reshape(seq, -1)
        .astype(BF16)
    )
    partial = jnp.dot(attended, full_output, preferred_element_type=F32).astype(BF16)
    resid, gates_wide, _, _, out_part, back_part, x_rows, g_rows, hid_low, gate_low, up_low = run_moe(
        depth, capacity, experts, partial.reshape(tp, rows, width), inputs, out_grad, moe_gain,
        router_pad, mask, rank, w_gate, w_up, w_down,
    )
    back, out_other, w_gate_grad, w_up_grad, w_down_grad = reduce_back(
        depth, back_part, out_part, x_rows, g_rows, hid_low, gate_low, up_low
    )
    gates = gates_wide[:, :experts]
    act_two = (
        resid
        * (inverse_two := lax.rsqrt(jnp.mean(resid * resid, axis=-1, keepdims=True) + EPSILON))
        * moe_gain
    ).astype(BF16)
    gate_grad = jnp.sum(back[:, width : width + tp * experts].reshape(rows, tp, experts), axis=1)
    logit_grad = gates * (gate_grad - jnp.sum(gates * gate_grad, axis=1, keepdims=True))
    act_two_grad = back[:, :width] + lax.dot_general(
        logit_grad, router.astype(F32), (((1,), (1,)), ((), ())), precision=HIGHEST
    )
    router_part = lax.dot_general(
        act_two.astype(F32), logit_grad, (((0,), (0,)), ((), ())), precision=HIGHEST
    )
    resid_part, gain_two_part = norm_back(resid, inverse_two, moe_gain, act_two_grad)
    resid_grad = out_grad.astype(F32) + resid_part
    qkv_part, act_one_grad, o_sum, out_sum = attend_back(
        depth, resid_grad.astype(BF16), act_one, qkv_full, full_output, qkv, attended, segments,
        out_part, out_other, w_output.shape[1],
    )
    whole_part, gain_one_part = norm_back(whole_float, inverse_one, attn_gain, act_one_grad)

    count = fsdp * tp
    piece = width // count
    small = jnp.concatenate([router_part, gain_one_part[:, None], gain_two_part[:, None]], axis=1)
    small = small.astype(BF16).reshape(count, piece, experts + 2)
    tail = jnp.pad(small, ((0, 0), (0, -piece % 16), (0, LANES - experts - 2)))
    q_sum, k_sum, v_sum, row_sum, side = last_reduce(
        depth, tail, qkv_part, whole_part.astype(BF16).reshape(tp, rows, width)
    )
    output = (resid + out_sum).astype(BF16)
    input_grad = resid_grad + row_sum
    side = side[:piece]
    return (
        output,
        input_grad,
        side[:, experts],
        q_sum,
        k_sum,
        v_sum,
        o_sum,
        side[:, experts + 1],
        side[:, :experts],
        w_gate_grad,
        w_up_grad,
        w_down_grad,
    )


def send_rows(buffer):
    return lax.all_to_all(buffer, "fsdp", split_axis=1, concat_axis=1, tiled=True)


def per_device(
    inputs,
    out_grad,
    segments,
    routes,
    attn_gain,
    w_query,
    w_key,
    w_value,
    w_output,
    moe_gain,
    router,
    w_gate,
    w_up,
    w_down,
):
    tp_count = lax.axis_size("tp")
    fsdp_count = lax.axis_size("fsdp")
    rows_piece, width = inputs.shape
    head_size = HEAD
    full_query, full_key, full_value, full_output = (
        lax.all_gather(w_query, "fsdp", axis=0, tiled=True),
        lax.all_gather(w_key, "fsdp", axis=0, tiled=True),
        lax.all_gather(w_value, "fsdp", axis=0, tiled=True),
        lax.all_gather(w_output, "fsdp", axis=1, tiled=True),
    )
    whole_rows = lax.all_gather(inputs, "tp", axis=0, tiled=True)
    seq_len = whole_rows.shape[0]
    whole_float = whole_rows.astype(jnp.float32)
    normed_one, inverse_one = norm_rows(whole_float, attn_gain)
    act_one = normed_one.astype(jnp.bfloat16)
    local_heads = full_query.shape[1] // head_size
    query = (
        jnp.dot(act_one, full_query, preferred_element_type=jnp.float32)
        .astype(jnp.bfloat16)
        .reshape(seq_len, local_heads, head_size)
    )
    key_rows = (
        jnp.dot(act_one, full_key, preferred_element_type=jnp.float32)
        .astype(jnp.bfloat16)
        .reshape(seq_len, local_heads, head_size)
    )
    value_rows = (
        jnp.dot(act_one, full_value, preferred_element_type=jnp.float32)
        .astype(jnp.bfloat16)
        .reshape(seq_len, local_heads, head_size)
    )
    block_rows = min(512, seq_len)
    score_scale = 1.0 / math.sqrt(head_size)

    def block_scores(query_block):
        scores = (
            jnp.einsum("qhd,khd->hqk", query_block, key_rows, preferred_element_type=jnp.float32)
            * score_scale
        )
        same_doc = segments[:, None] == segments[None, :]
        return jnp.where(same_doc[None], scores, -1e30)

    scores = block_scores(query)
    peak = jnp.max(scores, axis=-1, keepdims=True)
    expo = jnp.exp(scores - peak)
    total = jnp.sum(expo, axis=-1, keepdims=True)
    softmax_rows = (expo / total).astype(jnp.bfloat16)
    block_outputs = jnp.einsum(
        "hqk,khd->qhd", softmax_rows, value_rows, preferred_element_type=jnp.float32
    )
    log_totals = [peak + jnp.log(total)]
    attended = block_outputs.reshape(seq_len, -1).astype(jnp.bfloat16)
    branch = lax.psum_scatter(
        jnp.dot(attended, full_output, preferred_element_type=jnp.float32).astype(jnp.bfloat16),
        "tp",
        scatter_dimension=0,
        tiled=True,
    ).astype(jnp.float32)
    resid = inputs.astype(jnp.float32) + branch
    normed_two, inverse_two = norm_rows(resid, moe_gain)
    act_two = normed_two.astype(jnp.bfloat16)
    local_experts = w_gate.shape[0]
    experts = local_experts * fsdp_count
    top_k = routes.shape[1]
    capacity = 3 * rows_piece * top_k // (2 * experts)
    logits = jnp.dot(act_two, router, preferred_element_type=jnp.float32)
    picks = (routes[:, :, None] == jnp.arange(experts, dtype=jnp.int32)[None, None, :]).astype(
        jnp.float32
    )
    chosen = jnp.einsum("tke,te->tk", picks, logits, precision=HIGHEST)
    gates = jax.nn.softmax(chosen, axis=-1)
    flat_routes = routes.reshape(-1)
    route_count = flat_routes.shape[0]
    hits = (flat_routes[:, None] == jnp.arange(experts, dtype=jnp.int32)[None, :]).astype(jnp.int32)
    ranks = jnp.sum((jnp.cumsum(hits, axis=0) - 1) * hits, axis=1)
    slots = flat_routes * capacity + ranks
    sources = (
        jnp.full((experts * capacity,), route_count, jnp.int32)
        .at[slots]
        .set(jnp.arange(route_count, dtype=jnp.int32))
    )
    padded_act = jnp.concatenate([act_two, jnp.zeros((1, width), jnp.bfloat16)], 0)
    send_buffer = padded_act[sources // top_k].reshape(
        1, fsdp_count, local_experts * capacity, width
    )
    gate_full, up_full, down_full = (
        lax.all_gather(w_gate, "tp", axis=2, tiled=True),
        lax.all_gather(w_up, "tp", axis=2, tiled=True),
        lax.all_gather(w_down, "tp", axis=1, tiled=True),
    )
    own_in = send_rows(send_buffer)
    own_rows = own_in.reshape(fsdp_count, local_experts, capacity, width)
    own_gate = jnp.einsum("secd,edf->secf", own_rows, gate_full, preferred_element_type=jnp.float32)
    own_up = jnp.einsum("secd,edf->secf", own_rows, up_full, preferred_element_type=jnp.float32)
    own_sigmoid = jax.nn.sigmoid(own_gate)
    own_silu = own_gate * own_sigmoid
    own_hidden = (own_silu * own_up).astype(jnp.bfloat16)
    own_out = jnp.einsum(
        "secf,efd->secd", own_hidden, down_full, preferred_element_type=jnp.float32
    )
    expert_out = own_out.reshape(1, fsdp_count, local_experts * capacity, width).astype(
        jnp.bfloat16
    )
    returned = lax.all_to_all(expert_out, "fsdp", split_axis=1, concat_axis=1, tiled=True).reshape(
        experts * capacity, width
    )
    routed = returned[slots].reshape(rows_piece, top_k, width).astype(jnp.float32)
    mixture = jnp.sum(gates[:, :, None] * routed, axis=1)
    output = (resid + mixture).astype(jnp.bfloat16)
    grad_float = out_grad.astype(jnp.float32)
    gate_grad = jnp.sum(routed * grad_float[:, None, :], axis=2)
    route_grad = (
        (gates[:, :, None] * grad_float[:, None, :])
        .astype(jnp.bfloat16)
        .reshape(route_count, width)
    )
    padded_grad = jnp.concatenate([route_grad, jnp.zeros((1, width), jnp.bfloat16)], 0)
    grad_buffer = padded_grad[sources].reshape(1, fsdp_count, local_experts * capacity, width)
    own_grads = send_rows(grad_buffer).reshape(fsdp_count, local_experts, capacity, width)
    own_hidden_grad = jnp.einsum(
        "secd,efd->secf", own_grads, down_full, preferred_element_type=jnp.float32
    )
    own_gate_low = (
        own_hidden_grad * own_up * own_sigmoid * (1.0 + own_gate * (1.0 - own_sigmoid))
    ).astype(jnp.bfloat16)
    own_up_low = (own_hidden_grad * own_silu).astype(jnp.bfloat16)
    down_term = jnp.einsum(
        "secf,secd->efd", own_hidden, own_grads, preferred_element_type=jnp.float32
    )
    gate_term = jnp.einsum(
        "secd,secf->edf", own_rows, own_gate_low, preferred_element_type=jnp.float32
    )
    up_term = jnp.einsum("secd,secf->edf", own_rows, own_up_low, preferred_element_type=jnp.float32)
    w_gate_grad, w_up_grad, w_down_grad = (
        lax.psum_scatter(
            gate_term.astype(jnp.bfloat16), "tp", scatter_dimension=2, tiled=True
        ).astype(jnp.float32),
        lax.psum_scatter(
            up_term.astype(jnp.bfloat16), "tp", scatter_dimension=2, tiled=True
        ).astype(jnp.float32),
        lax.psum_scatter(
            down_term.astype(jnp.bfloat16), "tp", scatter_dimension=1, tiled=True
        ).astype(jnp.float32),
    )
    own_back = jnp.einsum(
        "secf,edf->secd", own_gate_low, gate_full, preferred_element_type=jnp.float32
    )
    own_back = own_back + jnp.einsum(
        "secf,edf->secd", own_up_low, up_full, preferred_element_type=jnp.float32
    )
    expert_grad = own_back.reshape(1, fsdp_count, local_experts * capacity, width).astype(
        jnp.bfloat16
    )
    back_rows = lax.all_to_all(
        expert_grad, "fsdp", split_axis=1, concat_axis=1, tiled=True
    ).reshape(experts * capacity, width)
    act_two_grad = jnp.sum(
        back_rows[slots].reshape(rows_piece, top_k, width).astype(jnp.float32), axis=1
    )
    centered = gate_grad - jnp.sum(gates * gate_grad, axis=1, keepdims=True)
    chosen_grad = gates * centered
    logit_grad = jnp.einsum("tke,tk->te", picks, chosen_grad, precision=HIGHEST)
    router_float = router.astype(jnp.float32)
    act_two_grad = act_two_grad + lax.dot_general(
        logit_grad, router_float, (((1,), (1,)), ((), ())), precision=HIGHEST
    )
    router_part = lax.dot_general(
        act_two.astype(jnp.float32), logit_grad, (((0,), (0,)), ((), ())), precision=HIGHEST
    )
    resid_part, gain_two_part = norm_back(resid, inverse_two, moe_gain, act_two_grad)
    resid_grad = grad_float + resid_part
    branch_grad = lax.all_gather(resid_grad.astype(jnp.bfloat16), "tp", axis=0, tiled=True)
    attended_grad = (
        contract_last(branch_grad, full_output)
        .astype(jnp.bfloat16)
        .reshape(seq_len, local_heads, head_size)
    )
    w_output_part = contract_first(attended, branch_grad)
    query_parts = []
    key_grad = jnp.zeros((seq_len, local_heads, head_size), jnp.float32)
    value_grad = jnp.zeros((seq_len, local_heads, head_size), jnp.float32)
    for block_index, first_row in enumerate(range(0, seq_len, block_rows)):
        query_block = query
        scores = block_scores(query_block)
        softmax_rows = jnp.exp(scores - log_totals[block_index])
        prob_grad = jnp.einsum(
            "qhd,khd->hqk", attended_grad, value_rows, preferred_element_type=jnp.float32
        )
        inner = jnp.sum(softmax_rows * prob_grad, axis=-1, keepdims=True)
        score_grad = (softmax_rows * (prob_grad - inner) * score_scale).astype(jnp.bfloat16)
        query_parts.append(
            jnp.einsum("hqk,khd->qhd", score_grad, key_rows, preferred_element_type=jnp.float32)
        )
        key_grad = jnp.einsum(
            "hqk,qhd->khd", score_grad, query_block, preferred_element_type=jnp.float32
        )
        value_grad = jnp.einsum(
            "hqk,qhd->khd",
            softmax_rows.astype(jnp.bfloat16),
            attended_grad,
            preferred_element_type=jnp.float32,
        )
    query_low = query_parts[0].reshape(seq_len, -1).astype(jnp.bfloat16)
    key_low = key_grad.reshape(seq_len, -1).astype(jnp.bfloat16)
    value_low = value_grad.reshape(seq_len, -1).astype(jnp.bfloat16)
    w_query_part = contract_first(act_one, query_low)
    w_key_part = contract_first(act_one, key_low)
    w_value_part = contract_first(act_one, value_low)
    act_one_grad = (
        contract_last(query_low, full_query)
        + contract_last(key_low, full_key)
        + contract_last(value_low, full_value)
    )
    whole_part, gain_one_part = norm_back(whole_float, inverse_one, attn_gain, act_one_grad)

    def arrange(values):
        shaped = values.reshape((fsdp_count, tp_count, -1) + values.shape[1:])
        return jnp.swapaxes(shaped, 0, 1)

    input_part, gain_one_tp, gain_two_tp, router_tp = (
        lax.psum_scatter(
            whole_part.astype(jnp.bfloat16), "tp", scatter_dimension=0, tiled=True
        ).astype(jnp.float32),
        lax.psum_scatter(
            arrange(gain_one_part).astype(jnp.bfloat16), "tp", scatter_dimension=0, tiled=True
        ).astype(jnp.float32),
        lax.psum_scatter(
            arrange(gain_two_part).astype(jnp.bfloat16), "tp", scatter_dimension=0, tiled=True
        ).astype(jnp.float32),
        lax.psum_scatter(
            arrange(router_part).astype(jnp.bfloat16), "tp", scatter_dimension=0, tiled=True
        ).astype(jnp.float32),
    )
    input_grad = resid_grad + input_part
    query_sum, key_sum, value_sum, output_sum, gain_one_sum, gain_two_sum, router_sum = (
        lax.psum_scatter(
            w_query_part.astype(jnp.bfloat16), "fsdp", scatter_dimension=0, tiled=True
        ).astype(jnp.float32),
        lax.psum_scatter(
            w_key_part.astype(jnp.bfloat16), "fsdp", scatter_dimension=0, tiled=True
        ).astype(jnp.float32),
        lax.psum_scatter(
            w_value_part.astype(jnp.bfloat16), "fsdp", scatter_dimension=0, tiled=True
        ).astype(jnp.float32),
        lax.psum_scatter(
            w_output_part.astype(jnp.bfloat16), "fsdp", scatter_dimension=1, tiled=True
        ).astype(jnp.float32),
        lax.psum_scatter(
            gain_one_tp.astype(jnp.bfloat16), "fsdp", scatter_dimension=1, tiled=True
        ).astype(jnp.float32),
        lax.psum_scatter(
            gain_two_tp.astype(jnp.bfloat16), "fsdp", scatter_dimension=1, tiled=True
        ).astype(jnp.float32),
        lax.psum_scatter(
            router_tp.astype(jnp.bfloat16), "fsdp", scatter_dimension=1, tiled=True
        ).astype(jnp.float32),
    )
    return (
        output,
        input_grad,
        gain_one_sum.reshape(-1),
        query_sum,
        key_sum,
        value_sum,
        output_sum,
        gain_two_sum.reshape(-1),
        router_sum.reshape(-1, experts),
        w_gate_grad,
        w_up_grad,
        w_down_grad,
    )


def layer(*args):
    tokens = args[0].shape[0] * lax.axis_size("fsdp") * lax.axis_size("tp")
    held = 6 * tokens * (args[0].shape[1] + LANES) * 2
    even = lax.axis_size("tp") == 4 and lax.axis_size("fsdp") % 2 == 0
    experts = args[11].shape[0] * lax.axis_size("fsdp")
    narrow = lax.axis_size("tp") * experts <= LANES and args[1].shape[1] // (lax.axis_size("tp") * lax.axis_size("fsdp")) <= args[0].shape[0]
    if held <= HBM_BUDGET and even and narrow:
        return dense_layer(*args)
    return per_device(*args)


def solution(mesh):
    return jax.shard_map(
        layer,
        mesh=mesh,
        in_specs=(
            P(("fsdp", "tp"), None),
            P(("fsdp", "tp"), None),
            P("fsdp"),
            P(("fsdp", "tp"), None),
            P(),
            P("fsdp", "tp"),
            P("fsdp", "tp"),
            P("fsdp", "tp"),
            P("tp", "fsdp"),
            P(),
            P(),
            P("fsdp", None, "tp"),
            P("fsdp", None, "tp"),
            P("fsdp", "tp", None),
        ),
        out_specs=(
            P(("fsdp", "tp"), None),
            P(("fsdp", "tp"), None),
            P(("fsdp", "tp")),
            P("fsdp", "tp"),
            P("fsdp", "tp"),
            P("fsdp", "tp"),
            P("tp", "fsdp"),
            P(("fsdp", "tp")),
            P(("fsdp", "tp"), None),
            P("fsdp", None, "tp"),
            P("fsdp", None, "tp"),
            P("fsdp", "tp", None),
        ),
        check_vma=False,
    )
```

```python
import functools
import math

import jax
import jax.numpy as jnp
from jax import lax
from jax.experimental import pallas as pl
from jax.experimental.pallas import tpu as pltpu
from jax.sharding import PartitionSpec as P

HEAD = 128
LANES = 128
EPSILON = 1e-05
HIGHEST = lax.Precision.HIGHEST
MESH = pl.DeviceIdType.MESH
ANY = pl.BlockSpec(memory_space=pl.ANY)
VMEM = pl.BlockSpec(memory_space=pltpu.VMEM)
MIB = 1 << 20
HBM_BUDGET = 300 * MIB
BF16 = jnp.bfloat16
F32 = jnp.float32
CONTRACT_FIRST = (((0,), (0,)), ((), ()))
CONTRACT_LAST = (((1,), (1,)), ((), ()))


class Place:
    def __init__(self, depth):
        self.depth = depth
        f, t = lax.axis_index("fsdp"), lax.axis_index("tp")
        self.f, self.t = f, t
        self.z, self.x = lax.div(f, 2), lax.rem(f, 2)
        self.y, self.c = lax.div(t, 2), lax.rem(t, 2)
        self.to = {
            "x": (self.z * 2 + 1 - self.x, t),
            "y": (f, (1 - self.y) * 2 + self.c),
            "c": (f, self.y * 2 + 1 - self.c),
            "up": (f + 2, t),
            "down": (f - 2, t),
        }
        self.can_up = self.z < depth - 1
        self.can_down = self.z > 0
        offs = [0]
        for step in range(1, depth):
            offs += [-step, step]
        self.offs = offs
        tables = [sorted(range(depth), key=lambda zz: (abs(zz - z), zz)) for z in range(depth)]
        self.near = [
            sum(jnp.where(self.z == z, tables[z][i], 0) for z in range(depth)) for i in range(depth)
        ]
        self.far = self.near[::-1]
        self.tables = tables

    def nearest(self, i):
        pairs = [(z, k) for z in range(self.depth) for k in range(self.depth)]
        return sum(
            jnp.where((self.z == z) & (i == k), self.tables[z][k], 0) for z, k in pairs
        )

    def valid(self, off):
        if off == 0:
            return None
        return self.z + off >= 0 if off < 0 else self.z + off < self.depth


def when(cond, body):
    if cond is None:
        body()
    else:
        pl.when(cond)(body)


def both(first, second):
    if first is None:
        return second
    if second is None:
        return first
    return jnp.logical_and(first, second)


class Net:
    def __init__(self, place, send_sems, recv_sems, local_sems):
        self.place = place
        self.send_sems, self.recv_sems, self.local_sems = send_sems, recv_sems, local_sems
        self.keys, self.used, self.sent, self.locals_used = {}, 0, [], 0

    def slot(self, key):
        if len(key) == 4 and key[1] == "at":
            base = self.keys.setdefault(key[0], self.used)
            if base == self.used:
                self.used += key[2]
            return base + key[3]
        base = self.keys.setdefault(key, self.used)
        if base == self.used:
            self.used += 1
        return base

    def put(self, src, dst, to, key, cond=None, guard=None):
        copy = pltpu.make_async_remote_copy(
            src_ref=src,
            dst_ref=dst,
            send_sem=self.send_sems.at[len(self.sent)],
            recv_sem=self.recv_sems.at[self.slot(key)],
            device_id=self.place.to[to],
            device_id_type=MESH,
        )
        self.sent.append((both(cond, guard), copy))
        when(cond, copy.start)

    def got(self, dst, key):
        pltpu.make_async_remote_copy(
            src_ref=dst,
            dst_ref=dst,
            send_sem=self.send_sems.at[0],
            recv_sem=self.recv_sems.at[self.slot(key)],
            device_id=self.place.to["c"],
            device_id_type=MESH,
        ).wait_recv()

    def local(self, src, dst):
        copy = pltpu.make_async_copy(src, dst, self.local_sems.at[self.locals_used])
        self.locals_used += 1
        copy.start()
        return copy

    def finish(self):
        for cond, copy in self.sent:
            when(cond, copy.wait_send)


def greet(place, links):
    barrier = pltpu.get_barrier_semaphore()
    count = 0
    for link in links:
        if link == "z":
            for name, cond in (("up", place.can_up), ("down", place.can_down)):
                target = place.to[name]
                pl.when(cond)(
                    lambda target=target: pl.semaphore_signal(
                        barrier, inc=1, device_id=target, device_id_type=MESH
                    )
                )
                count = count + cond.astype(jnp.int32)
        else:
            pl.semaphore_signal(barrier, inc=1, device_id=place.to[link], device_id_type=MESH)
            count = count + 1
    pl.semaphore_wait(barrier, count)


SENDS, RECVS, LOCALS = 160, 160, 24


def sems():
    return [
        pltpu.SemaphoreType.DMA((SENDS,)),
        pltpu.SemaphoreType.DMA((RECVS,)),
        pltpu.SemaphoreType.DMA((LOCALS,)),
    ]


def add_rows(dst, src, rows, step=16):
    def body(i, carry):
        at = pl.ds(pl.multiple_of(i * step, step), step)
        dst[at, :] = (dst[at, :].astype(F32) + src[at, :].astype(F32)).astype(dst.dtype)
        return carry

    lax.fori_loop(0, rows // step, body, 0)


def comm_params(ident, mib=None):
    limit = None if mib is None else mib * MIB
    return pltpu.CompilerParams(collective_id=ident, has_side_effects=True, vmem_limit_bytes=limit)


def spread_zx(net, name, block, own):
    p = net.place
    offs = p.offs

    def step(i):
        if i >= len(offs):
            return
        off = offs[i]
        zz = p.z + off
        valid = p.valid(off)
        ref = block(zz, p.x)

        def body():
            if off:
                net.got(ref, (name, "z", off))

        when(valid, body)
        src = ref if off else own
        if off <= 0:
            net.put(src, ref, "up", (name, "z", off - 1), both(valid, p.can_up))
        if off >= 0:
            net.put(src, ref, "down", (name, "z", off + 1), both(valid, p.can_down))
        net.put(src, ref, "x", (name, "x", off), valid)

    def finish():
        for off in offs:
            ref = block(p.z + off, 1 - p.x)
            when(p.valid(off), lambda: net.got(ref, (name, "x", off)))

    return step, finish


def spread_xz(net, name, block, pair, own, placed):
    p = net.place
    offs = p.offs

    def begin():
        net.put(own, block(p.z, p.x), "x", (name, "x"))

    def step(i):
        off = offs[i]
        if off == 0:
            placed.wait()
            net.got(block(p.z, 1 - p.x), (name, "x"))
        valid = p.valid(off)
        ref = pair(p.z + off)
        if off:
            when(valid, lambda: net.got(ref, (name, "z", off)))
        if off <= 0:
            net.put(ref, ref, "up", (name, "z", off - 1), both(valid, p.can_up))
        if off >= 0:
            net.put(ref, ref, "down", (name, "z", off + 1), both(valid, p.can_down))

    return begin, step


SITES = {
    "x1": ("x", 0, 0, 0),
    "y1": ("y", 0, 0, 1),
    "x3": ("x", 0, 0, 1),
    "y3": ("y", 0, 0, 0),
    "y2": ("y", 1, 0, 0),
    "x2": ("x", 0, 1, 1),
    "c0": ("c", 0, 0, None),
    "cx": ("c", 1, 0, None),
    "cy": ("c", 0, 1, None),
    "cxy": ("c", 1, 1, None),
}
NAMES = list(SITES)


class Plane:
    def __init__(self, place, everyone, own, sends, recvs):
        self.place, self.everyone, self.own = place, everyone, own
        self.sends, self.recvs = sends, recvs
        self.half = own.shape[0] // 2

    def ref(self, zz, dx, dy, dc, part):
        p = self.place
        x, y, c = p.x + dx - 2 * p.x * dx, p.y + dy - 2 * p.y * dy, p.c + dc - 2 * p.c * dc
        ref = self.everyone.at[((zz * 2 + x) * 2 + y) * 2 + c]
        return ref if part is None else ref.at[pl.ds(part * self.half, self.half)]

    def copy(self, site, zz, src=None):
        link, dx, dy, part = SITES[site]
        dst = self.ref(zz, dx, dy, 0, part)
        at = NAMES.index(site) * self.place.depth + zz
        return pltpu.make_async_remote_copy(
            src_ref=dst if src is None else src,
            dst_ref=dst,
            send_sem=self.sends.at[at],
            recv_sem=self.recvs.at[at],
            device_id=self.place.to[link],
            device_id_type=MESH,
        )

    def take(self, site, zz):
        link, dx, dy, part = SITES[site]
        dx, dy = dx ^ (link == "x"), dy ^ (link == "y")
        ref = self.ref(zz, dx, dy, int(link == "c"), part)
        at = NAMES.index(site) * self.place.depth + zz
        pltpu.make_async_remote_copy(
            src_ref=ref,
            dst_ref=ref,
            send_sem=self.sends.at[at],
            recv_sem=self.recvs.at[at],
            device_id=self.place.to[link],
            device_id_type=MESH,
        ).wait_recv()

    def z_copy(self, zz, up):
        p = self.place
        ref = self.ref(zz, 0, 0, 0, None)
        base = len(NAMES) * p.depth
        return pltpu.make_async_remote_copy(
            src_ref=ref,
            dst_ref=ref,
            send_sem=self.sends.at[base + (0 if up else p.depth) + zz],
            recv_sem=self.recvs.at[base + zz],
            device_id=p.to["up" if up else "down"],
            device_id_type=MESH,
        )

    def each_z(self, zz, act):
        p = self.place
        pl.when((zz <= p.z) & p.can_up)(lambda: act(True))
        pl.when((zz >= p.z) & p.can_down)(lambda: act(False))

    def own_along_z(self):
        p = self.place
        base = len(NAMES) * p.depth

        def start(up):
            pltpu.make_async_remote_copy(
                src_ref=self.own,
                dst_ref=self.ref(p.z, 0, 0, 0, None),
                send_sem=self.sends.at[base + (0 if up else p.depth) + p.z],
                recv_sem=self.recvs.at[base + p.z],
                device_id=p.to["up" if up else "down"],
                device_id_type=MESH,
            ).start()

        self.each_z(p.z, start)

    def take_z(self, zz):
        self.z_copy(zz, True).wait_recv()

    def along_z(self, zz, near_too=True):
        p = self.place
        if near_too:
            self.take_z(zz)
        else:
            pl.when((zz != p.z + 1) & (zz != p.z - 1))(lambda: self.take_z(zz))
        self.each_z(zz, lambda up: self.z_copy(zz, up).start())

    def first(self, zz, mine=False):
        whole, part_a, part_b = None, None, None
        if mine:
            whole = self.own
            part_a, part_b = whole.at[pl.ds(0, self.half)], whole.at[pl.ds(self.half, self.half)]
        self.copy("x1", zz, part_a).start()
        self.copy("y1", zz, part_b).start()
        self.copy("x3", zz, part_b).start()
        self.copy("y3", zz, part_a).start()
        self.copy("c0", zz, whole).start()

    def second(self, zz):
        self.take("x1", zz)
        self.copy("y2", zz).start()
        self.take("y1", zz)
        self.copy("x2", zz).start()

    def third(self, zz):
        self.take("x3", zz)
        self.copy("cx", zz).start()
        self.take("y3", zz)
        self.copy("cy", zz).start()
        self.take("x2", zz)
        self.take("y2", zz)
        self.copy("cxy", zz).start()

    def arrived(self, zz):
        for site in ("c0", "cx", "cy", "cxy"):
            self.take(site, zz)

    def finish(self, zs, z_zs):
        for zz in zs:
            for site in NAMES:
                self.copy(site, zz).wait_send()
        for zz in z_zs:
            self.each_z(zz, lambda up, zz=zz: self.z_copy(zz, up).wait_send())


def plane_sems(depth):
    return [pltpu.SemaphoreType.DMA(((len(NAMES) + 2) * depth,))] * 2


def same_document(seg_row):
    row = seg_row[...]
    column = jnp.transpose(jnp.broadcast_to(row, (LANES, row.shape[1])))[:, 0:1]
    return column == row


def first_kernel(
    depth, wq, wk, wv, wo, inp, og, gain, seg_row,
    qkv_hbm, o_hbm, rows_hbm, act_hbm, proj_hbm, att_hbm, part_hbm, grad_all,
    weights, full_o, rows, act, proj, att, part, og_send, og_recv, send, recv, local,
):
    p = Place(depth)
    net = Net(p, send, recv, local)
    grads = Plane(p, grad_all, og, og_send, og_recv)
    w_rows, w_cols = wq.shape
    o_cols = wo.shape[1]
    count, width = inp.shape
    fsdp, heads = 2 * depth, w_cols // HEAD

    def column(f):
        return full_o.at[:, pl.ds(pl.multiple_of(f * o_cols, LANES), o_cols)]

    def columns(z):
        return full_o.at[:, pl.ds(pl.multiple_of(z * (2 * o_cols), LANES), 2 * o_cols)]

    def slab(i):
        return lambda z, x: weights.at[i, z * 2 + x]

    greet(p, ("x", "y", "c", "z"))
    mine = rows.at[p.t]
    net.put(inp, mine, "y", ("rows", "y"))
    net.put(inp, mine, "c", ("rows", "c0"))
    placed = net.local(wo, column(p.f))
    owns = [net.local(inp, mine)]
    owns += [net.local(w, weights.at[i, p.f]) for i, w in enumerate((wq, wk, wv))]
    kept = net.local(og, grads.ref(p.z, 0, 0, 0, None))
    flows = [spread_zx(net, f"w{i}", slab(i), w) for i, w in enumerate((wq, wk, wv))]
    o_begin, o_step = spread_xz(net, "o", lambda z, x: column(z * 2 + x), columns, wo, placed)
    steps = len(p.offs)

    def norm():
        other = rows.at[(1 - p.y) * 2 + p.c]
        net.got(other, ("rows", "y"))
        net.put(other, other, "c", ("rows", "c1"))
        net.got(rows.at[p.y * 2 + 1 - p.c], ("rows", "c0"))
        net.got(rows.at[(1 - p.y) * 2 + 1 - p.c], ("rows", "c1"))
        owns[0].wait()
        for t in range(rows.shape[0]):

            def body(i, carry):
                at = pl.ds(pl.multiple_of(i * 16, 16), 16)
                values = rows[t, at, :].astype(F32)
                inverse = lax.rsqrt(jnp.mean(values * values, axis=-1, keepdims=True) + EPSILON)
                to = pl.ds(pl.multiple_of(t * count + i * 16, 16), 16)
                act[to, :] = (values * inverse * gain[...]).astype(BF16)
                return carry

            lax.fori_loop(0, count // 16, body, 0)

    saves = []

    def rows_in():
        norm()
        saves.append(net.local(rows, rows_hbm))
        saves.append(net.local(act, act_hbm))

    def project_with(i):
        owns[1 + i].wait()
        flows[i][1]()
        saves.append(net.local(weights.at[i], qkv_hbm.at[i]))
        wide = 256

        def project(k, carry):
            at = pl.ds(pl.multiple_of(k * wide, wide), wide)
            to = pl.ds(pl.multiple_of(i * w_cols + k * wide, wide), wide)
            matrix = weights[i, :, :, at].reshape(width, wide)
            proj[:, to] = jnp.dot(act[...], matrix, preferred_element_type=F32).astype(BF16)
            return carry

        lax.fori_loop(0, w_cols // wide, project, 0)

    scale = 1.0 / math.sqrt(HEAD)

    def head(h):
        if h == 0:
            saves.append(net.local(proj, proj_hbm))
        same = same_document(seg_row)
        query, keys, values = [
            proj[:, i * w_cols + h * HEAD : i * w_cols + (h + 1) * HEAD] for i in range(3)
        ]
        scores = lax.dot_general(query, keys, CONTRACT_LAST, preferred_element_type=F32) * scale
        scores = jnp.where(same, scores, -1e30)
        expo = jnp.exp(scores - jnp.max(scores, axis=-1, keepdims=True))
        probs = (expo / jnp.sum(expo, axis=-1, keepdims=True)).astype(BF16)
        att[:, h * HEAD : (h + 1) * HEAD] = jnp.dot(
            probs, values, preferred_element_type=F32
        ).astype(BF16)

    def out_rows(k, carry):
        at = pl.ds(pl.multiple_of(k * 256, 256), 256)
        part[:, at] = jnp.dot(att[...], full_o[:, at], preferred_element_type=F32).astype(BF16)
        return carry

    def branch():
        saves.append(net.local(full_o, o_hbm))
        saves.append(net.local(att, att_hbm))
        lax.fori_loop(0, width // 256, out_rows, 0)
        saves.append(net.local(part, part_hbm))

    (q_step, _), (k_step, _), (v_step, _) = flows

    def g_first():
        grads.first(p.z, True)

    if depth == 4 and heads == 4:
        perform(
            (v_step, 0), (o_begin,), (k_step, 0), (q_step, 0), (o_step, 0), (q_step, 1),
            (q_step, 2), (v_step, 1), (v_step, 2), (q_step, 3), (k_step, 1), (k_step, 2),
            (v_step, 3), (k_step, 3), (q_step, 4), (o_step, 1), (v_step, 4), (q_step, 5),
            (k_step, 4), (o_step, 2), (q_step, 6), (rows_in,), (k_step, 5), (v_step, 5),
            (v_step, 6), (project_with, 0), (k_step, 6), (g_first,), (o_step, 3), (o_step, 4),
            (project_with, 1), (grads.own_along_z,), (project_with, 2), (head, 0), (grads.second, p.z),
            (head, 1), (head, 2), (grads.third, p.z), (o_step, 5), (head, 3), (o_step, 6), (branch,),
            (grads.arrived, p.z),
        )
    else:
        perform((o_begin,), (g_first,), *every(steps, q_step, k_step, v_step, o_step), (rows_in,))
        perform((grads.second, p.z), (grads.third, p.z), *every(3, project_with))
        perform(*every(heads, head), (branch,), (grads.own_along_z,), (grads.arrived, p.z))
    pl.when(p.can_down)(lambda: grads.take_z(p.z - 1))
    pl.when(p.can_up)(lambda: grads.take_z(p.z + 1))
    kept.wait()
    for copy in saves:
        copy.wait()
    grads.finish([p.z], [p.z])
    net.finish()


def first_gather(depth, w_query, w_key, w_value, w_output, inputs, out_grad, gain, segments, tp):
    fsdp = 2 * depth
    w_rows, w_cols = w_query.shape
    o_rows, o_cols = w_output.shape
    rows, width = inputs.shape
    seq = tp * rows
    shape = jax.ShapeDtypeStruct
    return pl.pallas_call(
        functools.partial(first_kernel, depth),
        out_shape=[
            shape((3, fsdp, w_rows, w_cols), BF16),
            shape((o_rows, fsdp * o_cols), BF16),
            shape((tp, rows, width), BF16),
            shape((seq, width), BF16),
            shape((seq, 3 * w_cols), BF16),
            shape((seq, w_cols), BF16),
            shape((seq, width), BF16),
            shape((fsdp * tp, rows, width), BF16),
        ],
        in_specs=[VMEM] * 8,
        out_specs=[ANY] * 8,
        scratch_shapes=[
            pltpu.VMEM((3, fsdp, w_rows, w_cols), BF16),
            pltpu.VMEM((o_rows, fsdp * o_cols), BF16),
            pltpu.VMEM((tp, rows, width), BF16),
            pltpu.VMEM((seq, width), BF16),
            pltpu.VMEM((seq, 3 * w_cols), BF16),
            pltpu.VMEM((seq, w_cols), BF16),
            pltpu.VMEM((seq, width), BF16),
        ]
        + plane_sems(depth)
        + sems(),
        compiler_params=comm_params(1, 60),
        name="first_gather",
    )(
        w_query, w_key, w_value, w_output, inputs, out_grad, gain[None, :], segments[None, :],
    )


def moe_kernel(
    depth, capacity, experts, blocks,
    part, inp, og, gain, router, mask, rank, gate_hbm, up_hbm, down_hbm, grad_in_hbm,
    resid, gates_out, act_all, grad_all, out_hbm, back_hbm, x_hbm, g_hbm, hid_hbm, gl_hbm, ul_hbm,
    acc, rc, ry, own, w_gate, w_up, w_down, act_in, grad_in, x_rows, g_rows, tails, hid, gl, ul,
    o_keep, r_keep, out, back,
    act_send, act_recv, og_send, og_recv, send, recv, local, load_sems, save_sems,
):
    p = Place(depth)
    net = Net(p, send, recv, local)
    rows, width = inp.shape
    local_experts = w_gate.shape[0]
    weights = [
        net.local(src, dst)
        for src, dst in ((gate_hbm, w_gate), (up_hbm, w_up), (down_hbm, w_down))
    ]
    part_in = net.local(part.at[:, p.c], acc)
    acts = Plane(p, act_all, own, act_send, act_recv)
    grads = Plane(p, grad_all, og, og_send, og_recv)
    greet(p, ("x", "y", "c", "z"))

    net.put(part.at[:, 1 - p.c], rc, "c", ("rc",))
    far = 1 - p.y

    def along_y():
        part_in.wait()
        net.got(rc, ("rc",))
        add_rows(acc.at[far], rc.at[far], rows)
        net.put(acc.at[far], ry, "y", ("ry",))
        add_rows(acc.at[p.y], rc.at[p.y], rows)

    kept = []

    def norm():
        net.got(ry, ("ry",))

        def body(i, carry):
            at = pl.ds(pl.multiple_of(i * 16, 16), 16)
            branch = acc[p.y, at, :].astype(F32) + ry[at, :].astype(F32)
            values = inp[at, :].astype(F32) + branch
            resid[at, :] = values
            inverse = lax.rsqrt(jnp.mean(values * values, axis=-1, keepdims=True) + EPSILON)
            own[at, pl.ds(0, width)] = (values * inverse * gain[...]).astype(BF16)
            return carry

        lax.fori_loop(0, rows // 16, body, 0)
        twice = jnp.concatenate(
            [router[...]] * 2 + [jnp.zeros((LANES - 2 * experts, width), BF16)], axis=0
        )
        logits = lax.dot_general(
            own[:, pl.ds(0, width)], twice, CONTRACT_LAST, preferred_element_type=F32
        )
        chosen = mask[...] > 0.0
        peak = jnp.max(jnp.where(chosen, logits, -1e30), axis=1, keepdims=True)
        expo = jnp.where(chosen, jnp.exp(jnp.minimum(logits - peak, 0.0)), 0.0)
        lane = lax.broadcasted_iota(jnp.int32, expo.shape, 1)
        total = jnp.sum(jnp.where(lane < experts, expo, 0.0), axis=1, keepdims=True)
        gates = expo / total
        gates_out[...] = gates
        high = gates.astype(BF16).astype(F32)
        tail = jnp.where(
            lane < experts, high, jnp.where(lane < 2 * experts, gates - high, rank[...])
        )
        own[:, pl.ds(width, LANES)] = tail.astype(BF16)
        kept.append(net.local(own, acts.ref(p.z, 0, 0, 0, None)))

    first_expert = p.f * local_experts
    tp_lane = p.t * experts + first_expert
    pick_row = lax.broadcasted_iota(jnp.int32, (8, LANES), 0)
    pick_lane = lax.broadcasted_iota(jnp.int32, (8, LANES), 1)
    pick = (
        (pick_lane == 2 * experts + first_expert + pick_row) & (pick_row < local_experts)
    ).astype(BF16)
    places = lax.broadcasted_iota(jnp.int32, (capacity, rows), 0).astype(F32)
    slots = blocks * capacity

    def loads(zz, j):
        at = pl.ds((zz * 2 + j) * blocks, blocks)
        return [
            pltpu.make_async_copy(act_all.at[at], act_in.at[j], load_sems.at[j, 0]),
            pltpu.make_async_copy(grad_all.at[at], grad_in.at[j], load_sems.at[j, 1]),
        ]

    def save(zz, j, k):
        if k < 5:
            where = pl.ds(pl.multiple_of((zz * 2 + j) * slots, 16), slots)
            src = (x_rows, g_rows, hid, gl, ul)[k]
            dst = (x_hbm, g_hbm, hid_hbm, gl_hbm, ul_hbm)[k].at[:, where]
        else:
            src = (out, back)[k - 5]
            dst = (out_hbm, back_hbm)[k - 5].at[pl.ds((zz * 2 + j) * blocks, blocks)]
        return pltpu.make_async_copy(src, dst, save_sems.at[k])

    def one_hot(j, b):
        tail = act_in[j, b, :, pl.ds(width, LANES)]
        ranks = lax.dot_general(pick, tail, CONTRACT_LAST, preferred_element_type=F32)
        return jnp.concatenate(
            [
                (jnp.broadcast_to(ranks[e : e + 1, :], (capacity, rows)) == places).astype(BF16)
                for e in range(local_experts)
            ],
            axis=0,
        )

    def work(zz, j, started, serve):
        for copy in loads(zz, j):
            copy.wait()

        def settle(ks):
            def body():
                for k in ks:
                    save(zz, j, k).wait()

            when(started, body)

        settle((0, 1))

        def gather(b, carry):
            hot = one_hot(j, b)
            picked = jnp.dot(hot, act_in[j, b], preferred_element_type=F32)
            pulled = jnp.dot(hot, grad_in[j, b], preferred_element_type=F32).astype(BF16)
            at = pl.ds(pl.multiple_of(b * capacity, 16), capacity)
            for e in range(local_experts):
                piece = picked[e * capacity : (e + 1) * capacity]
                x_rows[e, at, :] = piece[:, :width].astype(BF16)
                tails[e, at, :] = piece[:, width:]
                g_rows[e, at, :] = pulled[e * capacity : (e + 1) * capacity]
            return carry

        lax.fori_loop(0, blocks, gather, 0)
        for k in (0, 1):
            save(zz, j, k).start()
        serve(0)
        settle((2, 3, 4))
        for e in range(local_experts):
            tail_lane = lax.broadcasted_iota(jnp.int32, (slots, LANES), 1)
            mine = (tail_lane == first_expert + e) | (tail_lane == experts + first_expert + e)
            gates_of = jnp.sum(jnp.where(mine, tails[e], 0.0), axis=1, keepdims=True)
            pre = jnp.dot(x_rows[e], w_gate[e], preferred_element_type=F32)
            up = jnp.dot(x_rows[e], w_up[e], preferred_element_type=F32)
            raw = lax.dot_general(g_rows[e], w_down[e], CONTRACT_LAST, preferred_element_type=F32)
            sig = jax.nn.sigmoid(pre)
            silu = pre * sig
            hidden = silu * up
            gate_grad = jnp.sum(hidden * raw, axis=1, keepdims=True)
            scaled = raw * gates_of
            hid_low = (hidden * gates_of).astype(BF16)
            gate_low = (scaled * up * sig * (1.0 + pre * (1.0 - sig))).astype(BF16)
            up_low = (scaled * silu).astype(BF16)
            hid[e] = hid_low
            gl[e] = gate_low
            ul[e] = up_low
            o_rows = jnp.dot(hid_low, w_down[e], preferred_element_type=F32).astype(BF16)
            r_rows = (
                lax.dot_general(gate_low, w_gate[e], CONTRACT_LAST, preferred_element_type=F32)
                + lax.dot_general(up_low, w_up[e], CONTRACT_LAST, preferred_element_type=F32)
            ).astype(BF16)
            r_tail = jnp.where(tail_lane == tp_lane + e, gate_grad, 0.0).astype(BF16)
            for b in range(blocks):
                at = slice(b * capacity, (b + 1) * capacity)
                to = slice(e * capacity, (e + 1) * capacity)
                o_keep[b, to, :] = o_rows[at]
                r_keep[b, to, pl.ds(0, width)] = r_rows[at]
                r_keep[b, to, pl.ds(width, LANES)] = r_tail[at]
            serve(1 + e)
        for k in (2, 3, 4):
            save(zz, j, k).start()
        settle((5, 6))

        def combine(b, carry):
            hot = one_hot(j, b)
            out[b] = lax.dot_general(
                hot, o_keep[b], CONTRACT_FIRST, preferred_element_type=F32
            ).astype(BF16)
            back[b] = lax.dot_general(
                hot, r_keep[b], CONTRACT_FIRST, preferred_element_type=F32
            ).astype(BF16)
            return carry

        lax.fori_loop(0, blocks, combine, 0)
        for k in (5, 6):
            save(zz, j, k).start()
        serve(5)

    def load(i):
        if i == 0:
            kept[0].wait()
            for copy in weights:
                copy.wait()
        for copy in loads(p.near[i], 0):
            copy.start()

    near = p.near
    g1, g2, g3 = grads.first, grads.second, grads.third
    a1, a2, a3 = acts.first, acts.second, acts.third
    if depth == 4:
        perform(
            (grads.along_z, near[1], False), (along_y,), (g1, near[1]),
            (grads.along_z, near[2], False), (norm,), (acts.own_along_z,), (a1, p.z, True),
            (acts.along_z, near[1]), (a2, p.z), (g2, near[1]), (a1, near[1]),
            (acts.along_z, near[2]), (a3, p.z), (a1, near[2]), (acts.arrived, p.z), (load, 0),
        )
        service = {
            (0, 0, 0): [(g3, near[1])],
            (0, 0, 1): [(acts.along_z, near[3])],
            (0, 0, 3): [(a2, near[1]), (g1, near[2])],
            (0, 1, 1): [(grads.along_z, near[3], False)],
            (0, 1, 2): [(a3, near[1]), (a2, near[2])],
            (0, 1, 4): [(acts.arrived, near[1])],
            (0, 1, 5): [(g2, near[2]), (grads.arrived, near[1]), (load, 1)],
            (1, 0, 4): [(a1, near[3])],
            (1, 0, 5): [(g3, near[2])],
            (1, 1, 1): [(grads.arrived, near[2])],
            (1, 1, 2): [(a3, near[2]), (a2, near[3])],
            (1, 1, 4): [(acts.arrived, near[2]), (load, 2)],
            (2, 0, 0): [(g1, near[3])],
            (2, 0, 1): [(a3, near[3])],
            (2, 0, 5): [(g2, near[3])],
            (2, 1, 3): [(g3, near[3])],
            (2, 1, 5): [(acts.arrived, near[3]), (grads.arrived, near[3]), (load, 3)],
        }
    else:
        perform((along_y,), (norm,), (acts.own_along_z,))
        for i, zz in enumerate(near):
            if i:
                perform((acts.along_z, zz), (grads.along_z, zz, False))
                perform((g1, zz), (g2, zz), (g3, zz), (grads.arrived, zz))
            perform((a1, zz, i == 0), (a2, zz), (a3, zz), (acts.arrived, zz))
        load(0)
        service = {(g, 1, 4): [(load, g + 1)] for g in range(depth - 1)}

    def group(g, carry):
        zz = p.nearest(g)
        for copy in loads(zz, 1):
            copy.start()

        def serve(j, k):
            for (at, half, place), steps in service.items():
                if (half, place) == (j, k):
                    pl.when(g == at)(functools.partial(perform, *steps))

        work(zz, 0, g > 0, functools.partial(serve, 0))
        work(zz, 1, None, functools.partial(serve, 1))
        return carry

    lax.fori_loop(0, depth, group, 0)
    for k in range(7):
        save(0, 1, k).wait()
    acts.finish(range(depth), range(depth))
    grads.finish(near[1:], near[1:])
    net.finish()


def run_moe(
    depth, capacity, experts, part, inputs, out_grad, gain, router, mask, rank, w_gate, w_up, w_down,
    grad_all,
):
    tp, rows, width = part.shape
    wide = width + LANES
    count = 2 * depth * tp
    local_experts, _, hidden = w_gate.shape
    blocks = tp
    slots = blocks * capacity
    total = count * capacity
    shape = jax.ShapeDtypeStruct
    kept = [shape((local_experts, total, width), BF16)] * 2
    kept += [shape((local_experts, total, hidden), BF16)] * 3
    return pl.pallas_call(
        functools.partial(moe_kernel, depth, capacity, experts, blocks),
        out_shape=[
            shape((rows, width), F32),
            shape((rows, LANES), F32),
            shape((count, rows, wide), BF16),
            shape((count, rows, width), BF16),
            shape((count, rows, width), BF16),
            shape((count, rows, wide), BF16),
        ]
        + kept,
        in_specs=[ANY] + [VMEM] * 6 + [ANY] * 4,
        out_specs=[VMEM] * 2 + [ANY] * 9,
        input_output_aliases={10: 3},
        scratch_shapes=[
            pltpu.VMEM((2, rows, width), BF16),
            pltpu.VMEM((2, rows, width), BF16),
            pltpu.VMEM((rows, width), BF16),
            pltpu.VMEM((rows, wide), BF16),
            pltpu.VMEM(w_gate.shape, BF16),
            pltpu.VMEM(w_up.shape, BF16),
            pltpu.VMEM(w_down.shape, BF16),
            pltpu.VMEM((2, blocks, rows, wide), BF16),
            pltpu.VMEM((2, blocks, rows, width), BF16),
            pltpu.VMEM((local_experts, slots, width), BF16),
            pltpu.VMEM((local_experts, slots, width), BF16),
            pltpu.VMEM((local_experts, slots, LANES), F32),
            pltpu.VMEM((local_experts, slots, hidden), BF16),
            pltpu.VMEM((local_experts, slots, hidden), BF16),
            pltpu.VMEM((local_experts, slots, hidden), BF16),
            pltpu.VMEM((blocks, local_experts * capacity, width), BF16),
            pltpu.VMEM((blocks, local_experts * capacity, wide), BF16),
            pltpu.VMEM((blocks, rows, width), BF16),
            pltpu.VMEM((blocks, rows, wide), BF16),
        ]
        + plane_sems(depth) * 2
        + sems()
        + [pltpu.SemaphoreType.DMA((2, 2)), pltpu.SemaphoreType.DMA((7,))],
        compiler_params=comm_params(2, 60),
        name="moe",
    )(
        part.reshape(tp // 2, 2, rows, width), inputs, out_grad, gain[None, :], router, mask, rank,
        w_gate, w_up, w_down, grad_all,
    )


def chain_z(net, name, zz, acc, inbox, rows, add=None):
    p = net.place
    extra = p.depth

    def take(slot):
        net.got(inbox.at[slot], (name, "at", extra + 1, slot))
        (add or add_rows)(acc, inbox.at[slot], rows)

    pl.when((zz >= p.z) & p.can_down)(lambda: take(jnp.where(zz == p.z, extra, zz)))
    pl.when((zz <= p.z) & p.can_up)(lambda: take(zz))
    slot = jnp.where(zz == p.z + 1, extra, zz)
    net.put(acc, inbox.at[slot], "up", (name, "at", extra + 1, slot), zz > p.z)
    net.put(acc, inbox.at[zz], "down", (name, "at", extra + 1, zz), zz < p.z)


class Reduce:
    def __init__(self, net, name, fill, acc, ya, xa, xb, yb, inbox, z_inbox, xc, yc):
        self.net, self.name, self.fill, self.acc = net, name, fill, acc
        self.ya, self.xa, self.xb, self.yb = ya, xa, xb, yb
        self.inbox, self.z_inbox, self.xc, self.yc = inbox, z_inbox, xc, yc
        self.rows_a, self.rows_b, self.rows_c = ya.shape[2], xb.shape[2], yc.shape[0]
        self.rows_ab = self.rows_a + self.rows_b
        self.a, self.b = pl.ds(0, self.rows_a), pl.ds(self.rows_a, self.rows_b)
        self.ab, self.c = pl.ds(0, self.rows_ab), pl.ds(self.rows_ab, self.rows_c)

    def key(self, what, zz):
        return (self.name + what, "at", self.net.place.depth, zz)

    def one(self, i):
        p, net, acc = self.net.place, self.net, self.acc
        zz = p.far[i]
        self.fill(i, zz)
        net.put(acc.at[zz, :, 1 - p.y, self.a], self.ya.at[zz], "y", self.key("ya", zz))
        net.put(acc.at[zz, 1 - p.x, :, self.b], self.xb.at[zz], "x", self.key("xb", zz))

    def two(self, i):
        p, net, acc = self.net.place, self.net, self.acc
        x, y, zz = p.x, p.y, p.far[i]
        net.got(self.xb.at[zz], self.key("xb", zz))
        add_rows(acc.at[zz, x, 1 - y, self.b], self.xb.at[zz, 1 - y], self.rows_b)
        net.put(acc.at[zz, x, 1 - y, self.b], self.yb.at[zz], "y", self.key("yb", zz))
        net.got(self.ya.at[zz], self.key("ya", zz))
        add_rows(acc.at[zz, 1 - x, y, self.a], self.ya.at[zz, 1 - x], self.rows_a)
        net.put(acc.at[zz, 1 - x, y, self.a], self.xa.at[zz], "x", self.key("xa", zz))
        add_rows(acc.at[zz, x, y, self.a], self.ya.at[zz, x], self.rows_a)
        add_rows(acc.at[zz, x, y, self.b], self.xb.at[zz, y], self.rows_b)

    def three(self, i):
        p, net, acc = self.net.place, self.net, self.acc
        x, y, zz = p.x, p.y, p.far[i]
        net.got(self.xa.at[zz], self.key("xa", zz))
        add_rows(acc.at[zz, x, y, self.a], self.xa.at[zz], self.rows_a)
        net.got(self.yb.at[zz], self.key("yb", zz))
        add_rows(acc.at[zz, x, y, self.b], self.yb.at[zz], self.rows_b)
        chain_z(net, self.name + "z", zz, acc.at[zz, x, y, self.ab], self.inbox, self.rows_ab)

    def along_z(self, i):
        p = self.net.place
        zz = p.far[i]

        def add(dst, src, rows):
            for xx in range(2):
                for yy in range(2):
                    add_rows(dst.at[xx, yy], src.at[xx, yy], rows)

        chain_z(
            self.net, self.name + "c", zz, self.acc.at[zz, :, :, self.c], self.z_inbox, self.rows_c, add
        )

    def then_x(self):
        p, net = self.net.place, self.net
        net.put(self.acc.at[p.z, 1 - p.x, :, self.c], self.xc, "x", (self.name + "xc",))

    def then_y(self):
        p, net, x, y = self.net.place, self.net, self.net.place.x, self.net.place.y
        net.got(self.xc, (self.name + "xc",))
        add_rows(self.acc.at[p.z, x, 1 - y, self.c], self.xc.at[1 - y], self.rows_c)
        net.put(self.acc.at[p.z, x, 1 - y, self.c], self.yc, "y", (self.name + "yc",))
        add_rows(self.acc.at[p.z, x, y, self.c], self.xc.at[y], self.rows_c)

    def end(self):
        p, net = self.net.place, self.net
        net.got(self.yc, (self.name + "yc",))
        add_rows(self.acc.at[p.z, p.x, p.y, self.c], self.yc, self.rows_c)


def reduce_scratch(depth, rows, wide, parts):
    a, b = parts
    c = rows - a - b
    return [
        pltpu.VMEM((depth, 2, 2, rows, wide), BF16),
        pltpu.VMEM((depth, 2, a, wide), BF16),
        pltpu.VMEM((depth, a, wide), BF16),
        pltpu.VMEM((depth, 2, b, wide), BF16),
        pltpu.VMEM((depth, b, wide), BF16),
        pltpu.VMEM((depth + 1, a + b, wide), BF16),
        pltpu.VMEM((depth + 1, 2, 2, c, wide), BF16),
        pltpu.VMEM((2, c, wide), BF16),
        pltpu.VMEM((c, wide), BF16),
    ]


def tile_rows(rows, share):
    return max(16, int(rows * share) // 16 * 16)


def perform(*steps):
    for function, *args in steps:
        function(*args)


def every(depth, *functions):
    return [(function, i) for function in functions for i in range(depth)]


def widen(dst, src, rows):
    def body(i, carry):
        at = pl.ds(pl.multiple_of(i * 16, 16), 16)
        dst[at, :] = src[at, :].astype(F32)
        return carry

    lax.fori_loop(0, rows // 16, body, 0)


def back_kernel(
    depth, part, out_part, x_rows, g_rows, hid, gate_low, up_low,
    total, out_other, w_gate_grad, w_up_grad, w_down_grad,
    acc, ya, xa, xb, yb, inbox, z_inbox, xc, yc, rc, big, left, right, found, found_down,
    send, recv, local, load_sems, save_sems,
):
    p = Place(depth)
    net = Net(p, send, recv, local)
    c = p.c
    rows, width = total.shape
    local_experts = x_rows.shape[0]

    def loads(u):
        e, slot = u // 2, u % 2
        if u % 2 == 0:
            pairs = ((x_rows, big.at[slot]), (gate_low, left.at[slot]), (up_low, right.at[slot]))
        else:
            pairs = ((g_rows, big.at[slot]), (hid, left.at[slot]))
        return [
            pltpu.make_async_copy(src.at[e], dst, load_sems.at[slot, j])
            for j, (src, dst) in enumerate(pairs)
        ]

    def saves(u):
        e = u // 2
        if u % 2 == 0:
            targets = (w_gate_grad, w_up_grad)
            return [
                pltpu.make_async_copy(found.at[j], ref.at[e], save_sems.at[j])
                for j, ref in enumerate(targets)
            ]
        return [pltpu.make_async_copy(found_down, w_down_grad.at[e], save_sems.at[2])]

    units = 2 * local_experts

    def unit(u):
        slot = u % 2
        for copy in loads(u):
            copy.wait()
        if u >= 2:
            for copy in saves(u - 2):
                copy.wait()
        if u % 2 == 0:
            wide = 256

            def body(i, carry):
                at = pl.ds(pl.multiple_of(i * wide, wide), wide)
                tile = big[slot, :, at]
                for j, ref in enumerate((left, right)):
                    found[j, at, :] = lax.dot_general(
                        tile, ref[slot], CONTRACT_FIRST, preferred_element_type=F32
                    ).astype(BF16)
                return carry

            lax.fori_loop(0, width // wide, body, 0)
        else:
            wide = 512

            def body(i, carry):
                at = pl.ds(pl.multiple_of(i * wide, wide), wide)
                found_down[:, at] = lax.dot_general(
                    left[slot], big[slot, :, at], CONTRACT_FIRST, preferred_element_type=F32
                ).astype(BF16)
                return carry

            lax.fori_loop(0, width // wide, body, 0)
        for copy in saves(u):
            copy.start()
        if u + 2 < units:
            for copy in loads(u + 2):
                copy.start()

    fills = []
    for i in range(depth):
        zz = p.far[i]
        fills.append(net.local(part.at[zz, :, :, c], acc.at[zz]))
    greet(p, ("x", "y", "c", "z"))
    for i in range(depth):
        zz = p.far[i]
        net.put(part.at[zz, :, :, 1 - c], rc.at[zz], "c", ("c", "at", depth, zz))

    def fill(i, zz):
        fills[i].wait()
        net.got(rc.at[zz], ("c", "at", depth, zz))
        for xx in range(2):
            for yy in range(2):
                add_rows(acc.at[zz, xx, yy], rc.at[zz, xx, yy], rows)

    flow = Reduce(net, "b", fill, acc, ya, xa, xb, yb, inbox, z_inbox, xc, yc)
    def begin():
        for v in range(2):
            for copy in loads(v):
                copy.start()
        for zz in range(depth):
            net.put(out_part.at[zz, :, :, 1 - c], out_other.at[zz], "c", ("oc", "at", depth, zz))

    one, two, three, along_z = flow.one, flow.two, flow.three, flow.along_z
    if depth == 4 and units == 8:
        perform(
            (one, 0), (along_z, 0), (one, 1), (begin,), (one, 2), (unit, 0), (along_z, 1),
            (along_z, 2), (two, 0), (one, 3), (unit, 1), (unit, 2), (two, 1), (unit, 3), (two, 2),
            (three, 0), (unit, 4), (along_z, 3), (flow.then_x,), (unit, 5), (three, 1),
            (three, 2), (two, 3), (unit, 6), (flow.then_y,), (unit, 7), (flow.end,), (three, 3),
        )
    else:
        perform(*every(depth, one), (begin,), *every(depth, two, three, along_z))
        perform((flow.then_x,), (flow.then_y,), (flow.end,), *every(units, unit))
    for k in (units - 2, units - 1):
        for copy in saves(k):
            copy.wait()

    def last(i, carry):
        at = pl.ds(pl.multiple_of(i * 16, 16), 16)
        total[at, :] = acc[p.z, p.x, p.y, at, :].astype(F32)
        return carry

    lax.fori_loop(0, rows // 16, last, 0)
    for zz in range(depth):
        net.got(out_other.at[zz], ("oc", "at", depth, zz))
    net.finish()


def reduce_back(depth, part, out_part, x_rows, g_rows, hid, gate_low, up_low):
    count, rows, wide = part.shape
    width = out_part.shape[2]
    local_experts, slots, hidden = hid.shape
    shape = jax.ShapeDtypeStruct
    return pl.pallas_call(
        functools.partial(back_kernel, depth),
        out_shape=[
            shape((rows, wide), F32),
            shape((depth, 2, 2, rows, width), BF16),
            shape((local_experts, width, hidden), BF16),
            shape((local_experts, width, hidden), BF16),
            shape((local_experts, hidden, width), BF16),
        ],
        in_specs=[ANY] * 7,
        out_specs=[VMEM] + [ANY] * 4,
        scratch_shapes=reduce_scratch(depth, rows, wide, [tile_rows(rows, 0.375)] * 2)
        + [
            pltpu.VMEM((depth, 2, 2, rows, wide), BF16),
            pltpu.VMEM((2, slots, width), BF16),
            pltpu.VMEM((2, slots, hidden), BF16),
            pltpu.VMEM((2, slots, hidden), BF16),
            pltpu.VMEM((2, width, hidden), BF16),
            pltpu.VMEM((hidden, width), BF16),
        ]
        + sems()
        + [pltpu.SemaphoreType.DMA((2, 3)), pltpu.SemaphoreType.DMA((3,))],
        compiler_params=comm_params(3, 60),
        name="reduce_back",
    )(
        part.reshape(depth, 2, 2, 2, rows, wide),
        out_part.reshape(depth, 2, 2, 2, rows, width),
        x_rows, g_rows, hid, gate_low, up_low,
    )


def attend_back_kernel(
    depth, mine, act_hbm, wqkv_hbm, wo_hbm, qkv_hbm, att_hbm, whole_hbm, seg_row, gain, out_part, out_other,
    qkv_part, whole_part, gain_part, o_sum, o_rest, out_sum,
    acc, ya, xa, xb, yb, inbox, z_inbox, xc, yc, other, bg, act, wqkv, wo, qkv, att, ag, low, o_acc, o_inbox, o_rx,
    whole, act_grad, send, recv, local, other_sems,
):
    p = Place(depth)
    net = Net(p, send, recv, local)
    x, y, c = p.x, p.y, p.c
    rows, width = out_sum.shape
    seq = act.shape[0]
    cols = wo.shape[0]
    heads = cols // HEAD
    o_rows, o_cols = o_sum.shape

    def block(t):
        return bg.at[pl.ds(pl.multiple_of(t * rows, rows), rows)]

    own = net.local(mine, block(p.t))
    load_wo = net.local(wo_hbm, wo)
    load_att = net.local(att_hbm, att)
    load_qkv = net.local(qkv_hbm, qkv)
    load_act = net.local(act_hbm, act)
    load_w = net.local(wqkv_hbm, wqkv)
    load_whole = net.local(whole_hbm, whole)
    greet(p, ("x", "y", "c", "z"))
    own.wait()
    net.put(block(p.t), block(p.t), "y", ("bg", "y"))
    net.put(block(p.t), block(p.t), "c", ("bg", "c0"))

    def load_other(i):
        zz = p.far[i]
        return [
            pltpu.make_async_copy(out_part.at[zz, :, :, c], acc.at[zz], other_sems.at[0, i % 2]),
            pltpu.make_async_copy(out_other.at[zz], other.at[i % 2], other_sems.at[1, i % 2]),
        ]

    for i in range(2):
        for copy in load_other(i):
            copy.start()

    def fill(i, zz):
        for copy in load_other(i):
            copy.wait()
        for xx in range(2):
            for yy in range(2):
                add_rows(acc.at[zz, xx, yy], other.at[i % 2, xx, yy], rows)
        if i + 2 < depth:
            for copy in load_other(i + 2):
                copy.start()

    flow = Reduce(net, "out", fill, acc, ya, xa, xb, yb, inbox, z_inbox, xc, yc)

    def o_pair(z):
        return o_acc.at[:, pl.ds(pl.multiple_of(z * (2 * o_cols), LANES), 2 * o_cols)]

    def o_step(i):
        if i < depth:
            chain_z(net, "oz", p.far[i], o_pair(p.far[i]), o_inbox, o_rows)

    def o_along_x():
        theirs = pl.ds(pl.multiple_of((p.z * 2 + 1 - x) * o_cols, LANES), o_cols)
        net.put(o_acc.at[:, theirs], o_rx, "x", ("ox",))

    def rows_in():
        far = block((1 - y) * 2 + c)
        net.got(far, ("bg", "y"))
        net.put(far, far, "c", ("bg", "c1"))
        net.got(block(y * 2 + 1 - c), ("bg", "c0"))
        net.got(block((1 - y) * 2 + 1 - c), ("bg", "c1"))

    def attended_grad():
        load_wo.wait()
        ag[...] = lax.dot_general(
            bg[...], wo[...], CONTRACT_LAST, preferred_element_type=F32
        ).astype(BF16)

    wide = 512

    def o_body(i, carry):
        at = pl.ds(pl.multiple_of(i * wide, wide), wide)
        found = lax.dot_general(
            att[...], bg[:, at], CONTRACT_FIRST, preferred_element_type=F32
        ).astype(BF16)
        o_acc[:, at] = found[:o_rows]
        o_rest[:, at] = found[o_rows:]
        return carry

    def o_terms():
        load_att.wait()
        load_qkv.wait()
        lax.fori_loop(0, width // wide, o_body, 0)

    scale = 1.0 / math.sqrt(HEAD)
    same = same_document(seg_row)

    def head(h):
        at = slice(h * HEAD, (h + 1) * HEAD)
        query = qkv[:, h * HEAD : (h + 1) * HEAD]
        keys = qkv[:, cols + h * HEAD : cols + (h + 1) * HEAD]
        values = qkv[:, 2 * cols + h * HEAD : 2 * cols + (h + 1) * HEAD]
        grad = ag[:, at]
        scores = lax.dot_general(query, keys, CONTRACT_LAST, preferred_element_type=F32) * scale
        scores = jnp.where(same, scores, -1e30)
        expo = jnp.exp(scores - jnp.max(scores, axis=-1, keepdims=True))
        probs = expo / jnp.sum(expo, axis=-1, keepdims=True)
        prob_grad = lax.dot_general(grad, values, CONTRACT_LAST, preferred_element_type=F32)
        inner = jnp.sum(probs * prob_grad, axis=-1, keepdims=True)
        score_grad = (probs * (prob_grad - inner) * scale).astype(BF16)
        low[:, at] = jnp.dot(score_grad, keys, preferred_element_type=F32).astype(BF16)
        low[:, cols + h * HEAD : cols + (h + 1) * HEAD] = lax.dot_general(
            score_grad, query, CONTRACT_FIRST, preferred_element_type=F32
        ).astype(BF16)
        low[:, 2 * cols + h * HEAD : 2 * cols + (h + 1) * HEAD] = lax.dot_general(
            probs.astype(BF16), grad, CONTRACT_FIRST, preferred_element_type=F32
        ).astype(BF16)

    w_rows, w_cols = wqkv.shape[2:]

    def w_body(f, carry):
        at = pl.ds(pl.multiple_of(f * w_rows, w_rows), w_rows)
        qkv_part[f] = lax.dot_general(
            act[:, at], low[...], CONTRACT_FIRST, preferred_element_type=F32
        ).astype(BF16)
        act_grad[:, at] = sum(
            lax.dot_general(
                low[:, i * w_cols : (i + 1) * w_cols], wqkv[i, f], CONTRACT_LAST,
                preferred_element_type=F32,
            )
            for i in range(3)
        )
        return carry

    count = wqkv.shape[1]
    pieces = 4

    def w_piece(i):
        if i == 0:
            load_act.wait()
            load_w.wait()
        lax.fori_loop(i * count // pieces, (i + 1) * count // pieces, w_body, 0)

    def norm_piece(i):
        if i == 0:
            load_whole.wait()
            gain_part[...] = jnp.zeros_like(gain_part)
        span = seq // pieces // 16

        def body(k, total):
            at = pl.ds(pl.multiple_of((i * span + k) * 16, 16), 16)
            values, grad = whole[at, :].astype(F32), act_grad[at, :]
            inverse = lax.rsqrt(jnp.mean(values * values, axis=-1, keepdims=True) + EPSILON)
            scaled = gain[...] * grad
            pull = jnp.mean(values * scaled, axis=-1, keepdims=True)
            whole_part[at, :] = (
                inverse * scaled - values * (inverse * inverse * inverse) * pull
            ).astype(BF16)
            return total + jnp.sum(grad * values * inverse, axis=0, keepdims=True)

        total = lax.fori_loop(0, span, body, jnp.zeros(gain_part.shape, F32))
        gain_part[...] += total

    one, two, three, along_z = flow.one, flow.two, flow.three, flow.along_z
    if depth == 4 and heads == 4:
        perform(
            (one, 0), (one, 1), (one, 2), (along_z, 0), (along_z, 1), (rows_in,),
            (attended_grad,), (o_terms,), (o_step, 0), (along_z, 2), (two, 0), (head, 0),
            (two, 1), (one, 3), (o_step, 1), (o_step, 2), (head, 1), (head, 2), (head, 3),
            (two, 2), (three, 0), (w_piece, 0), (o_step, 3), (w_piece, 1), (along_z, 3),
            (flow.then_x,), (o_along_x,), (w_piece, 2), (three, 1), (three, 2), (flow.then_y,),
            (w_piece, 3), (norm_piece, 0), (norm_piece, 1), (two, 3), (norm_piece, 2), (flow.end,), (norm_piece, 3), (three, 3),
        )
    else:
        perform(*every(depth, one), (rows_in,), (attended_grad,), (o_terms,))
        perform(*every(heads, head), *every(pieces, w_piece, norm_piece))
        perform(*every(depth, two, three, along_z, o_step), (o_along_x,))
        perform((flow.then_x,), (flow.then_y,), (flow.end,))
    widen(out_sum, acc.at[p.z, x, y], rows)
    net.got(o_rx, ("ox",))
    at_o = pl.ds(pl.multiple_of((p.z * 2 + x) * o_cols, LANES), o_cols)

    def o_last(i, carry):
        at = pl.ds(pl.multiple_of(i * 16, 16), 16)
        o_sum[at, :] = o_acc[at, at_o].astype(F32) + o_rx[at, :].astype(F32)
        return carry

    lax.fori_loop(0, o_rows // 16, o_last, 0)
    net.finish()


def attend_back(
    depth, mine, act, wqkv, wo, qkv, att, whole, segments, gain, out_part, out_other, o_cols
):
    rows, width = mine.shape
    seq, cols = att.shape
    _, fsdp, w_rows, w_cols = wqkv.shape
    w_wide = 3 * w_cols
    shape = jax.ShapeDtypeStruct
    return pl.pallas_call(
        functools.partial(attend_back_kernel, depth),
        out_shape=[
            shape((fsdp, w_rows, w_wide), BF16),
            shape((seq, width), BF16),
            shape((1, width), F32),
            shape((cols // 2, o_cols), F32),
            shape((cols // 2, width), BF16),
            shape((rows, width), F32),
        ],
        in_specs=[ANY] * 7 + [VMEM] * 2 + [ANY] * 2,
        out_specs=[VMEM] * 6,
        scratch_shapes=reduce_scratch(
            depth, rows, width, [tile_rows(rows, 0.375), tile_rows(rows, 0.5)]
        )
        + [
            pltpu.VMEM((2, 2, 2, rows, width), BF16),
            pltpu.VMEM((seq, width), BF16),
            pltpu.VMEM((seq, width), BF16),
            pltpu.VMEM(wqkv.shape, BF16),
            pltpu.VMEM((cols, width), BF16),
            pltpu.VMEM((seq, w_wide), BF16),
            pltpu.VMEM((seq, cols), BF16),
            pltpu.VMEM((seq, cols), BF16),
            pltpu.VMEM((seq, w_wide), BF16),
            pltpu.VMEM((cols // 2, width), BF16),
            pltpu.VMEM((depth + 1, cols // 2, 2 * o_cols), BF16),
            pltpu.VMEM((cols // 2, o_cols), BF16),
            pltpu.VMEM((seq, width), BF16),
            pltpu.VMEM((seq, width), F32),
        ]
        + sems()
        + [pltpu.SemaphoreType.DMA((2, 2))],
        compiler_params=comm_params(4, 63),
        name="attend_back",
    )(
        mine, act, wqkv, wo, qkv, att, whole, segments[None, :], gain[None, :],
        out_part.reshape(depth, 2, 2, 2, rows, width), out_other,
    )


def last_kernel(
    depth, tail, qkv_part, row_part, o_part, q_sum, k_sum, v_sum, row_sum, tail_sum, o_sum,
    q_acc, q_rx, q_inbox, t_acc, t_rc, t_ry, s_acc, s_rc, s_ry, s_rx, s_inbox,
    o_acc, o_inbox, o_rx, send, recv, local,
):
    p = Place(depth)
    net = Net(p, send, recv, local)
    x, y, c = p.x, p.y, p.c
    rows, width = row_sum.shape
    w_rows, w_cols = q_sum.shape
    o_rows, o_cols = o_sum.shape
    small = s_acc.shape[3]
    o_load = net.local(o_part, o_acc)
    t_load = net.local(row_part.at[:, c], t_acc)
    s_load = net.local(tail.at[:, :, :, c], s_acc)
    loads = [net.local(qkv_part.at[p.far[i], x], q_acc.at[p.far[i]]) for i in range(depth)]
    greet(p, ("x", "y", "c", "z"))

    def q_along_x(i):
        zz = p.far[i]
        net.put(qkv_part.at[zz, 1 - x], q_rx.at[zz], "x", ("qx", "at", depth, zz))

    def q_along_z(i):
        zz = p.far[i]
        loads[i].wait()
        net.got(q_rx.at[zz], ("qx", "at", depth, zz))
        add_rows(q_acc.at[zz], q_rx.at[zz], w_rows)
        chain_z(net, "qz", zz, q_acc.at[zz], q_inbox, w_rows)

    def o_along_z(i):
        if i == 0:
            o_load.wait()
        zz = p.far[i]
        pair = o_acc.at[:, pl.ds(pl.multiple_of(zz * (2 * o_cols), LANES), 2 * o_cols)]
        chain_z(net, "oz", zz, pair, o_inbox, o_rows)

    def o_along_x():
        theirs = pl.ds(pl.multiple_of((p.z * 2 + 1 - x) * o_cols, LANES), o_cols)
        net.put(o_acc.at[:, theirs], o_rx, "x", ("ox",))

    def cores():
        net.put(row_part.at[:, 1 - c], t_rc, "c", ("tc",))
        net.put(tail.at[:, :, :, 1 - c], s_rc, "c", ("sc",))

    def along_y():
        t_load.wait()
        net.got(t_rc, ("tc",))
        add_rows(t_acc.at[1 - y], t_rc.at[1 - y], rows)
        net.put(t_acc.at[1 - y], t_ry, "y", ("ty",))
        s_load.wait()
        net.got(s_rc, ("sc",))
        for zz in range(depth):
            for xx in range(2):
                add_rows(s_acc.at[zz, xx, 1 - y], s_rc.at[zz, xx, 1 - y], small)
        net.put(s_acc.at[:, :, 1 - y], s_ry, "y", ("sy",))
        for zz in range(depth):
            for xx in range(2):
                add_rows(s_acc.at[zz, xx, y], s_rc.at[zz, xx, y], small)

    def s_along_x():
        net.got(s_ry, ("sy",))
        for z in range(depth):
            for xx in range(2):
                add_rows(s_acc.at[z, xx, y], s_ry.at[z, xx], small)
        net.put(s_acc.at[:, 1 - x, y], s_rx, "x", ("sx",))

    def s_in():
        net.got(s_rx, ("sx",))
        for z in range(depth):
            add_rows(s_acc.at[z, x, y], s_rx.at[z], small)

    def s_along_z(i):
        chain_z(net, "sz", p.far[i], s_acc.at[p.far[i], x, y], s_inbox, small)

    def rows_in():
        net.got(t_ry, ("ty",))

        def body(i, carry):
            at = pl.ds(pl.multiple_of(i * 16, 16), 16)
            row_sum[at, :] = (
                t_acc[y, at, :].astype(F32) + t_rc[y, at, :].astype(F32) + t_ry[at, :].astype(F32)
            )
            return carry

        lax.fori_loop(0, rows // 16, body, 0)

    def o_in():
        net.got(o_rx, ("ox",))
        at_o = pl.ds(pl.multiple_of((p.z * 2 + x) * o_cols, LANES), o_cols)

        def body(i, carry):
            at = pl.ds(pl.multiple_of(i * 16, 16), 16)
            o_sum[at, :] = o_acc[at, at_o].astype(F32) + o_rx[at, :].astype(F32)
            return carry

        lax.fori_loop(0, o_rows // 16, body, 0)

    if depth == 4:
        perform(
            (q_along_x, 0), (cores,), (o_along_z, 0), (q_along_x, 1), (o_along_z, 1), (along_y,),
            (o_along_z, 2), (s_along_x,), (q_along_x, 2), (q_along_z, 0), (q_along_x, 3),
            (o_along_z, 3), (rows_in,), (s_in,), (o_along_x,), (s_along_z, 0), (q_along_z, 1),
            (q_along_z, 2), (s_along_z, 1), (o_in,), (s_along_z, 2), (q_along_z, 3),
            (s_along_z, 3),
        )
    else:
        perform(*every(depth, q_along_x), (cores,), (along_y,), (s_along_x,))
        perform(*every(depth, q_along_z, o_along_z), (s_in,), (o_along_x,))
        perform(*every(depth, s_along_z), (rows_in,), (o_in,))

    def q_last(i, carry):
        at = pl.ds(pl.multiple_of(i * 16, 16), 16)
        for j, ref in enumerate((q_sum, k_sum, v_sum)):
            ref[at, :] = q_acc[p.z, at, pl.ds(j * w_cols, w_cols)].astype(F32)
        return carry

    lax.fori_loop(0, w_rows // 16, q_last, 0)
    widen(tail_sum, s_acc.at[p.z, x, y], small)
    net.finish()


def last_reduce(depth, tail, qkv_part, row_part, o_part):
    count, small, lanes = tail.shape
    fsdp, w_rows, w_wide = qkv_part.shape
    tp, rows, width = row_part.shape
    w_cols = w_wide // 3
    o_rows, o_cols = o_part.shape[0], width // fsdp
    shape = jax.ShapeDtypeStruct
    return pl.pallas_call(
        functools.partial(last_kernel, depth),
        out_shape=[shape((w_rows, w_cols), F32)] * 3
        + [shape((rows, width), F32), shape((small, lanes), F32), shape((o_rows, o_cols), F32)],
        in_specs=[ANY] * 4,
        out_specs=[VMEM] * 6,
        scratch_shapes=[
            pltpu.VMEM((depth, w_rows, w_wide), BF16),
            pltpu.VMEM((depth, w_rows, w_wide), BF16),
            pltpu.VMEM((depth + 1, w_rows, w_wide), BF16),
            pltpu.VMEM((2, rows, width), BF16),
            pltpu.VMEM((2, rows, width), BF16),
            pltpu.VMEM((rows, width), BF16),
            pltpu.VMEM((depth, 2, 2, small, lanes), BF16),
            pltpu.VMEM((depth, 2, 2, small, lanes), BF16),
            pltpu.VMEM((depth, 2, small, lanes), BF16),
            pltpu.VMEM((depth, small, lanes), BF16),
            pltpu.VMEM((depth + 1, small, lanes), BF16),
            pltpu.VMEM((o_rows, width), BF16),
            pltpu.VMEM((depth + 1, o_rows, 2 * o_cols), BF16),
            pltpu.VMEM((o_rows, o_cols), BF16),
        ]
        + sems(),
        compiler_params=comm_params(5, 48),
        name="last_reduce",
    )(
        tail.reshape(depth, 2, 2, 2, small, lanes),
        qkv_part.reshape(depth, 2, w_rows, w_wide),
        row_part.reshape(2, 2, rows, width),
        o_part,
    )


def norm_rows(values, gain):
    inverse = lax.rsqrt(jnp.mean(values * values, axis=-1, keepdims=True) + EPSILON)
    return (values * inverse * gain, inverse)


def norm_back(values, inverse, gain, grad):
    scaled = gain * grad
    gain_grad = jnp.sum(grad * values * inverse, axis=0)
    cubed = inverse * inverse * inverse
    values_grad = inverse * scaled - values * cubed * jnp.mean(
        values * scaled, axis=-1, keepdims=True
    )
    return (values_grad, gain_grad)


def contract_last(left, right):
    return lax.dot_general(
        left, right, (((1,), (1,)), ((), ())), preferred_element_type=jnp.float32
    )


def contract_first(left, right):
    return lax.dot_general(
        left, right, (((0,), (0,)), ((), ())), preferred_element_type=jnp.float32
    )


def dense_layer(
    inputs, out_grad, segments, routes, attn_gain, w_query, w_key, w_value, w_output,
    moe_gain, router, w_gate, w_up, w_down,
):
    tp, fsdp = lax.axis_size("tp"), lax.axis_size("fsdp")
    depth = fsdp // 2
    rows, width = inputs.shape
    local_experts = w_gate.shape[0]
    experts = local_experts * fsdp
    top_k = routes.shape[1]
    capacity = 3 * rows * top_k // (2 * experts)
    w_rows, w_cols = w_query.shape
    heads = w_cols // HEAD
    seq = tp * rows

    named = jnp.any(
        routes[:, :, None] == jnp.arange(experts, dtype=jnp.int32)[None, None, :], axis=1
    )
    hits = named.astype(F32)
    before = (jnp.arange(rows)[:, None] > jnp.arange(rows)[None, :]).astype(F32)
    ranks = jnp.where(named, jnp.dot(before, hits, preferred_element_type=F32), -1.0)
    fill = jnp.zeros((rows, LANES - 3 * experts), F32)
    blank = jnp.zeros((rows, experts), F32)
    mask = jnp.concatenate([hits, hits, blank, fill], axis=1)
    rank = jnp.concatenate([blank, blank, ranks, fill], axis=1)
    qkv_full, full_output, whole, act_one, qkv, attended, partial, grad_all = first_gather(
        depth, w_query, w_key, w_value, w_output, inputs, out_grad, attn_gain, segments, tp
    )
    resid, gates_wide, _, _, out_part, back_part, x_rows, g_rows, hid_low, gate_low, up_low = run_moe(
        depth, capacity, experts, partial.reshape(tp, rows, width), inputs, out_grad, moe_gain,
        router.T, mask, rank, w_gate, w_up, w_down, grad_all,
    )
    back, out_other, w_gate_grad, w_up_grad, w_down_grad = reduce_back(
        depth, back_part, out_part, x_rows, g_rows, hid_low, gate_low, up_low
    )
    gates = gates_wide[:, :experts]
    act_two = (
        resid
        * (inverse_two := lax.rsqrt(jnp.mean(resid * resid, axis=-1, keepdims=True) + EPSILON))
        * moe_gain
    ).astype(BF16)
    gate_grad = jnp.sum(back[:, width : width + tp * experts].reshape(rows, tp, experts), axis=1)
    logit_grad = gates * (gate_grad - jnp.sum(gates * gate_grad, axis=1, keepdims=True))
    act_two_grad = back[:, :width] + lax.dot_general(
        logit_grad, router.astype(F32), (((1,), (1,)), ((), ())), precision=HIGHEST
    )
    router_part = lax.dot_general(
        act_two.astype(F32), logit_grad, (((0,), (0,)), ((), ())), precision=HIGHEST
    )
    resid_part, gain_two_part = norm_back(resid, inverse_two, moe_gain, act_two_grad)
    resid_grad = out_grad.astype(F32) + resid_part
    qkv_part, whole_part, gain_one_part, o_first, o_rest, out_sum = attend_back(
        depth, resid_grad.astype(BF16), act_one, qkv_full, full_output, qkv, attended,
        whole.reshape(seq, width), segments, attn_gain, out_part, out_other, w_output.shape[1],
    )
    count = fsdp * tp
    piece = width // count
    small = jnp.concatenate([router_part, gain_one_part.reshape(-1, 1), gain_two_part[:, None]], axis=1)
    small = small.astype(BF16).reshape(count, piece, experts + 2)
    tail = jnp.pad(small, ((0, 0), (0, -piece % 16), (0, LANES - experts - 2)))
    q_sum, k_sum, v_sum, row_sum, side, o_second = last_reduce(
        depth, tail, qkv_part, whole_part.reshape(tp, rows, width), o_rest
    )
    o_sum = jnp.concatenate([o_first, o_second], axis=0)
    output = (resid + out_sum).astype(BF16)
    input_grad = resid_grad + row_sum
    side = side[:piece]
    return (
        output,
        input_grad,
        side[:, experts],
        q_sum,
        k_sum,
        v_sum,
        o_sum,
        side[:, experts + 1],
        side[:, :experts],
        w_gate_grad.astype(F32),
        w_up_grad.astype(F32),
        w_down_grad.astype(F32),
    )


def send_rows(buffer):
    return lax.all_to_all(buffer, "fsdp", split_axis=1, concat_axis=1, tiled=True)


def per_device(
    inputs,
    out_grad,
    segments,
    routes,
    attn_gain,
    w_query,
    w_key,
    w_value,
    w_output,
    moe_gain,
    router,
    w_gate,
    w_up,
    w_down,
):
    tp_count = lax.axis_size("tp")
    fsdp_count = lax.axis_size("fsdp")
    rows_piece, width = inputs.shape
    head_size = HEAD
    full_query, full_key, full_value, full_output = (
        lax.all_gather(w_query, "fsdp", axis=0, tiled=True),
        lax.all_gather(w_key, "fsdp", axis=0, tiled=True),
        lax.all_gather(w_value, "fsdp", axis=0, tiled=True),
        lax.all_gather(w_output, "fsdp", axis=1, tiled=True),
    )
    whole_rows = lax.all_gather(inputs, "tp", axis=0, tiled=True)
    seq_len = whole_rows.shape[0]
    whole_float = whole_rows.astype(jnp.float32)
    normed_one, inverse_one = norm_rows(whole_float, attn_gain)
    act_one = normed_one.astype(jnp.bfloat16)
    local_heads = full_query.shape[1] // head_size
    query = (
        jnp.dot(act_one, full_query, preferred_element_type=jnp.float32)
        .astype(jnp.bfloat16)
        .reshape(seq_len, local_heads, head_size)
    )
    key_rows = (
        jnp.dot(act_one, full_key, preferred_element_type=jnp.float32)
        .astype(jnp.bfloat16)
        .reshape(seq_len, local_heads, head_size)
    )
    value_rows = (
        jnp.dot(act_one, full_value, preferred_element_type=jnp.float32)
        .astype(jnp.bfloat16)
        .reshape(seq_len, local_heads, head_size)
    )
    block_rows = min(512, seq_len)
    score_scale = 1.0 / math.sqrt(head_size)

    def block_scores(query_block):
        scores = (
            jnp.einsum("qhd,khd->hqk", query_block, key_rows, preferred_element_type=jnp.float32)
            * score_scale
        )
        same_doc = segments[:, None] == segments[None, :]
        return jnp.where(same_doc[None], scores, -1e30)

    scores = block_scores(query)
    peak = jnp.max(scores, axis=-1, keepdims=True)
    expo = jnp.exp(scores - peak)
    total = jnp.sum(expo, axis=-1, keepdims=True)
    softmax_rows = (expo / total).astype(jnp.bfloat16)
    block_outputs = jnp.einsum(
        "hqk,khd->qhd", softmax_rows, value_rows, preferred_element_type=jnp.float32
    )
    log_totals = [peak + jnp.log(total)]
    attended = block_outputs.reshape(seq_len, -1).astype(jnp.bfloat16)
    branch = lax.psum_scatter(
        jnp.dot(attended, full_output, preferred_element_type=jnp.float32).astype(jnp.bfloat16),
        "tp",
        scatter_dimension=0,
        tiled=True,
    ).astype(jnp.float32)
    resid = inputs.astype(jnp.float32) + branch
    normed_two, inverse_two = norm_rows(resid, moe_gain)
    act_two = normed_two.astype(jnp.bfloat16)
    local_experts = w_gate.shape[0]
    experts = local_experts * fsdp_count
    top_k = routes.shape[1]
    capacity = 3 * rows_piece * top_k // (2 * experts)
    logits = jnp.dot(act_two, router, preferred_element_type=jnp.float32)
    picks = (routes[:, :, None] == jnp.arange(experts, dtype=jnp.int32)[None, None, :]).astype(
        jnp.float32
    )
    chosen = jnp.einsum("tke,te->tk", picks, logits, precision=HIGHEST)
    gates = jax.nn.softmax(chosen, axis=-1)
    flat_routes = routes.reshape(-1)
    route_count = flat_routes.shape[0]
    hits = (flat_routes[:, None] == jnp.arange(experts, dtype=jnp.int32)[None, :]).astype(jnp.int32)
    ranks = jnp.sum((jnp.cumsum(hits, axis=0) - 1) * hits, axis=1)
    slots = flat_routes * capacity + ranks
    sources = (
        jnp.full((experts * capacity,), route_count, jnp.int32)
        .at[slots]
        .set(jnp.arange(route_count, dtype=jnp.int32))
    )
    padded_act = jnp.concatenate([act_two, jnp.zeros((1, width), jnp.bfloat16)], 0)
    send_buffer = padded_act[sources // top_k].reshape(
        1, fsdp_count, local_experts * capacity, width
    )
    gate_full, up_full, down_full = (
        lax.all_gather(w_gate, "tp", axis=2, tiled=True),
        lax.all_gather(w_up, "tp", axis=2, tiled=True),
        lax.all_gather(w_down, "tp", axis=1, tiled=True),
    )
    own_in = send_rows(send_buffer)
    own_rows = own_in.reshape(fsdp_count, local_experts, capacity, width)
    own_gate = jnp.einsum("secd,edf->secf", own_rows, gate_full, preferred_element_type=jnp.float32)
    own_up = jnp.einsum("secd,edf->secf", own_rows, up_full, preferred_element_type=jnp.float32)
    own_sigmoid = jax.nn.sigmoid(own_gate)
    own_silu = own_gate * own_sigmoid
    own_hidden = (own_silu * own_up).astype(jnp.bfloat16)
    own_out = jnp.einsum(
        "secf,efd->secd", own_hidden, down_full, preferred_element_type=jnp.float32
    )
    expert_out = own_out.reshape(1, fsdp_count, local_experts * capacity, width).astype(
        jnp.bfloat16
    )
    returned = lax.all_to_all(expert_out, "fsdp", split_axis=1, concat_axis=1, tiled=True).reshape(
        experts * capacity, width
    )
    routed = returned[slots].reshape(rows_piece, top_k, width).astype(jnp.float32)
    mixture = jnp.sum(gates[:, :, None] * routed, axis=1)
    output = (resid + mixture).astype(jnp.bfloat16)
    grad_float = out_grad.astype(jnp.float32)
    gate_grad = jnp.sum(routed * grad_float[:, None, :], axis=2)
    route_grad = (
        (gates[:, :, None] * grad_float[:, None, :])
        .astype(jnp.bfloat16)
        .reshape(route_count, width)
    )
    padded_grad = jnp.concatenate([route_grad, jnp.zeros((1, width), jnp.bfloat16)], 0)
    grad_buffer = padded_grad[sources].reshape(1, fsdp_count, local_experts * capacity, width)
    own_grads = send_rows(grad_buffer).reshape(fsdp_count, local_experts, capacity, width)
    own_hidden_grad = jnp.einsum(
        "secd,efd->secf", own_grads, down_full, preferred_element_type=jnp.float32
    )
    own_gate_low = (
        own_hidden_grad * own_up * own_sigmoid * (1.0 + own_gate * (1.0 - own_sigmoid))
    ).astype(jnp.bfloat16)
    own_up_low = (own_hidden_grad * own_silu).astype(jnp.bfloat16)
    down_term = jnp.einsum(
        "secf,secd->efd", own_hidden, own_grads, preferred_element_type=jnp.float32
    )
    gate_term = jnp.einsum(
        "secd,secf->edf", own_rows, own_gate_low, preferred_element_type=jnp.float32
    )
    up_term = jnp.einsum("secd,secf->edf", own_rows, own_up_low, preferred_element_type=jnp.float32)
    w_gate_grad, w_up_grad, w_down_grad = (
        lax.psum_scatter(
            gate_term.astype(jnp.bfloat16), "tp", scatter_dimension=2, tiled=True
        ).astype(jnp.float32),
        lax.psum_scatter(
            up_term.astype(jnp.bfloat16), "tp", scatter_dimension=2, tiled=True
        ).astype(jnp.float32),
        lax.psum_scatter(
            down_term.astype(jnp.bfloat16), "tp", scatter_dimension=1, tiled=True
        ).astype(jnp.float32),
    )
    own_back = jnp.einsum(
        "secf,edf->secd", own_gate_low, gate_full, preferred_element_type=jnp.float32
    )
    own_back = own_back + jnp.einsum(
        "secf,edf->secd", own_up_low, up_full, preferred_element_type=jnp.float32
    )
    expert_grad = own_back.reshape(1, fsdp_count, local_experts * capacity, width).astype(
        jnp.bfloat16
    )
    back_rows = lax.all_to_all(
        expert_grad, "fsdp", split_axis=1, concat_axis=1, tiled=True
    ).reshape(experts * capacity, width)
    act_two_grad = jnp.sum(
        back_rows[slots].reshape(rows_piece, top_k, width).astype(jnp.float32), axis=1
    )
    centered = gate_grad - jnp.sum(gates * gate_grad, axis=1, keepdims=True)
    chosen_grad = gates * centered
    logit_grad = jnp.einsum("tke,tk->te", picks, chosen_grad, precision=HIGHEST)
    router_float = router.astype(jnp.float32)
    act_two_grad = act_two_grad + lax.dot_general(
        logit_grad, router_float, (((1,), (1,)), ((), ())), precision=HIGHEST
    )
    router_part = lax.dot_general(
        act_two.astype(jnp.float32), logit_grad, (((0,), (0,)), ((), ())), precision=HIGHEST
    )
    resid_part, gain_two_part = norm_back(resid, inverse_two, moe_gain, act_two_grad)
    resid_grad = grad_float + resid_part
    branch_grad = lax.all_gather(resid_grad.astype(jnp.bfloat16), "tp", axis=0, tiled=True)
    attended_grad = (
        contract_last(branch_grad, full_output)
        .astype(jnp.bfloat16)
        .reshape(seq_len, local_heads, head_size)
    )
    w_output_part = contract_first(attended, branch_grad)
    query_parts = []
    key_grad = jnp.zeros((seq_len, local_heads, head_size), jnp.float32)
    value_grad = jnp.zeros((seq_len, local_heads, head_size), jnp.float32)
    for block_index, first_row in enumerate(range(0, seq_len, block_rows)):
        query_block = query
        scores = block_scores(query_block)
        softmax_rows = jnp.exp(scores - log_totals[block_index])
        prob_grad = jnp.einsum(
            "qhd,khd->hqk", attended_grad, value_rows, preferred_element_type=jnp.float32
        )
        inner = jnp.sum(softmax_rows * prob_grad, axis=-1, keepdims=True)
        score_grad = (softmax_rows * (prob_grad - inner) * score_scale).astype(jnp.bfloat16)
        query_parts.append(
            jnp.einsum("hqk,khd->qhd", score_grad, key_rows, preferred_element_type=jnp.float32)
        )
        key_grad = jnp.einsum(
            "hqk,qhd->khd", score_grad, query_block, preferred_element_type=jnp.float32
        )
        value_grad = jnp.einsum(
            "hqk,qhd->khd",
            softmax_rows.astype(jnp.bfloat16),
            attended_grad,
            preferred_element_type=jnp.float32,
        )
    query_low = query_parts[0].reshape(seq_len, -1).astype(jnp.bfloat16)
    key_low = key_grad.reshape(seq_len, -1).astype(jnp.bfloat16)
    value_low = value_grad.reshape(seq_len, -1).astype(jnp.bfloat16)
    w_query_part = contract_first(act_one, query_low)
    w_key_part = contract_first(act_one, key_low)
    w_value_part = contract_first(act_one, value_low)
    act_one_grad = (
        contract_last(query_low, full_query)
        + contract_last(key_low, full_key)
        + contract_last(value_low, full_value)
    )
    whole_part, gain_one_part = norm_back(whole_float, inverse_one, attn_gain, act_one_grad)

    def arrange(values):
        shaped = values.reshape((fsdp_count, tp_count, -1) + values.shape[1:])
        return jnp.swapaxes(shaped, 0, 1)

    input_part, gain_one_tp, gain_two_tp, router_tp = (
        lax.psum_scatter(
            whole_part.astype(jnp.bfloat16), "tp", scatter_dimension=0, tiled=True
        ).astype(jnp.float32),
        lax.psum_scatter(
            arrange(gain_one_part).astype(jnp.bfloat16), "tp", scatter_dimension=0, tiled=True
        ).astype(jnp.float32),
        lax.psum_scatter(
            arrange(gain_two_part).astype(jnp.bfloat16), "tp", scatter_dimension=0, tiled=True
        ).astype(jnp.float32),
        lax.psum_scatter(
            arrange(router_part).astype(jnp.bfloat16), "tp", scatter_dimension=0, tiled=True
        ).astype(jnp.float32),
    )
    input_grad = resid_grad + input_part
    query_sum, key_sum, value_sum, output_sum, gain_one_sum, gain_two_sum, router_sum = (
        lax.psum_scatter(
            w_query_part.astype(jnp.bfloat16), "fsdp", scatter_dimension=0, tiled=True
        ).astype(jnp.float32),
        lax.psum_scatter(
            w_key_part.astype(jnp.bfloat16), "fsdp", scatter_dimension=0, tiled=True
        ).astype(jnp.float32),
        lax.psum_scatter(
            w_value_part.astype(jnp.bfloat16), "fsdp", scatter_dimension=0, tiled=True
        ).astype(jnp.float32),
        lax.psum_scatter(
            w_output_part.astype(jnp.bfloat16), "fsdp", scatter_dimension=1, tiled=True
        ).astype(jnp.float32),
        lax.psum_scatter(
            gain_one_tp.astype(jnp.bfloat16), "fsdp", scatter_dimension=1, tiled=True
        ).astype(jnp.float32),
        lax.psum_scatter(
            gain_two_tp.astype(jnp.bfloat16), "fsdp", scatter_dimension=1, tiled=True
        ).astype(jnp.float32),
        lax.psum_scatter(
            router_tp.astype(jnp.bfloat16), "fsdp", scatter_dimension=1, tiled=True
        ).astype(jnp.float32),
    )
    return (
        output,
        input_grad,
        gain_one_sum.reshape(-1),
        query_sum,
        key_sum,
        value_sum,
        output_sum,
        gain_two_sum.reshape(-1),
        router_sum.reshape(-1, experts),
        w_gate_grad,
        w_up_grad,
        w_down_grad,
    )


def layer(*args):
    tokens = args[0].shape[0] * lax.axis_size("fsdp") * lax.axis_size("tp")
    held = 6 * tokens * (args[0].shape[1] + LANES) * 2
    even = lax.axis_size("tp") == 4 and lax.axis_size("fsdp") % 2 == 0
    experts = args[11].shape[0] * lax.axis_size("fsdp")
    narrow = lax.axis_size("tp") * experts <= LANES and args[1].shape[1] // (lax.axis_size("tp") * lax.axis_size("fsdp")) <= args[0].shape[0]
    if held <= HBM_BUDGET and even and narrow:
        return dense_layer(*args)
    return per_device(*args)


def solution(mesh):
    return jax.shard_map(
        layer,
        mesh=mesh,
        in_specs=(
            P(("fsdp", "tp"), None),
            P(("fsdp", "tp"), None),
            P("fsdp"),
            P(("fsdp", "tp"), None),
            P(),
            P("fsdp", "tp"),
            P("fsdp", "tp"),
            P("fsdp", "tp"),
            P("tp", "fsdp"),
            P(),
            P(),
            P("fsdp", None, "tp"),
            P("fsdp", None, "tp"),
            P("fsdp", "tp", None),
        ),
        out_specs=(
            P(("fsdp", "tp"), None),
            P(("fsdp", "tp"), None),
            P(("fsdp", "tp")),
            P("fsdp", "tp"),
            P("fsdp", "tp"),
            P("fsdp", "tp"),
            P("tp", "fsdp"),
            P(("fsdp", "tp")),
            P(("fsdp", "tp"), None),
            P("fsdp", None, "tp"),
            P("fsdp", None, "tp"),
            P("fsdp", "tp", None),
        ),
        check_vma=False,
    )
```

```python
import functools
import math

import jax
import jax.numpy as jnp
from jax import lax
from jax.experimental import pallas as pl
from jax.experimental.pallas import tpu as pltpu
from jax.sharding import PartitionSpec as P

HEAD = 128
LANES = 128
EPSILON = 1e-05
HIGHEST = lax.Precision.HIGHEST
MESH = pl.DeviceIdType.MESH
ANY = pl.BlockSpec(memory_space=pl.ANY)
VMEM = pl.BlockSpec(memory_space=pltpu.VMEM)
MIB = 1 << 20
HBM_BUDGET = 300 * MIB
BF16 = jnp.bfloat16
F32 = jnp.float32
CONTRACT_FIRST = (((0,), (0,)), ((), ()))
CONTRACT_LAST = (((1,), (1,)), ((), ()))


class Place:
    def __init__(self, depth):
        self.depth = depth
        f, t = lax.axis_index("fsdp"), lax.axis_index("tp")
        self.f, self.t = f, t
        self.z, self.x = lax.div(f, 2), lax.rem(f, 2)
        self.y, self.c = lax.div(t, 2), lax.rem(t, 2)
        self.to = {
            "x": (self.z * 2 + 1 - self.x, t),
            "y": (f, (1 - self.y) * 2 + self.c),
            "c": (f, self.y * 2 + 1 - self.c),
            "up": (f + 2, t),
            "down": (f - 2, t),
        }
        self.can_up = self.z < depth - 1
        self.can_down = self.z > 0
        offs = [0]
        for step in range(1, depth):
            offs += [-step, step]
        self.offs = offs
        tables = [sorted(range(depth), key=lambda zz: (abs(zz - z), zz)) for z in range(depth)]
        self.near = [
            sum(jnp.where(self.z == z, tables[z][i], 0) for z in range(depth)) for i in range(depth)
        ]
        self.far = self.near[::-1]
        self.tables = tables

    def nearest(self, i):
        pairs = [(z, k) for z in range(self.depth) for k in range(self.depth)]
        return sum(
            jnp.where((self.z == z) & (i == k), self.tables[z][k], 0) for z, k in pairs
        )

    def valid(self, off):
        if off == 0:
            return None
        return self.z + off >= 0 if off < 0 else self.z + off < self.depth


def when(cond, body):
    if cond is None:
        body()
    else:
        pl.when(cond)(body)


def both(first, second):
    if first is None:
        return second
    if second is None:
        return first
    return jnp.logical_and(first, second)


class Net:
    def __init__(self, place, send_sems, recv_sems, local_sems):
        self.place = place
        self.send_sems, self.recv_sems, self.local_sems = send_sems, recv_sems, local_sems
        self.keys, self.used, self.sent, self.locals_used = {}, 0, [], 0

    def slot(self, key):
        if len(key) == 4 and key[1] == "at":
            base = self.keys.setdefault(key[0], self.used)
            if base == self.used:
                self.used += key[2]
            return base + key[3]
        base = self.keys.setdefault(key, self.used)
        if base == self.used:
            self.used += 1
        return base

    def put(self, src, dst, to, key, cond=None, guard=None):
        copy = pltpu.make_async_remote_copy(
            src_ref=src,
            dst_ref=dst,
            send_sem=self.send_sems.at[len(self.sent)],
            recv_sem=self.recv_sems.at[self.slot(key)],
            device_id=self.place.to[to],
            device_id_type=MESH,
        )
        self.sent.append((both(cond, guard), copy))
        when(cond, copy.start)

    def got(self, dst, key):
        pltpu.make_async_remote_copy(
            src_ref=dst,
            dst_ref=dst,
            send_sem=self.send_sems.at[0],
            recv_sem=self.recv_sems.at[self.slot(key)],
            device_id=self.place.to["c"],
            device_id_type=MESH,
        ).wait_recv()

    def local(self, src, dst):
        copy = pltpu.make_async_copy(src, dst, self.local_sems.at[self.locals_used])
        self.locals_used += 1
        copy.start()
        return copy

    def finish(self):
        for cond, copy in self.sent:
            when(cond, copy.wait_send)


def greet(place, links):
    barrier = pltpu.get_barrier_semaphore()
    count = 0
    for link in links:
        if link == "z":
            for name, cond in (("up", place.can_up), ("down", place.can_down)):
                target = place.to[name]
                pl.when(cond)(
                    lambda target=target: pl.semaphore_signal(
                        barrier, inc=1, device_id=target, device_id_type=MESH
                    )
                )
                count = count + cond.astype(jnp.int32)
        else:
            pl.semaphore_signal(barrier, inc=1, device_id=place.to[link], device_id_type=MESH)
            count = count + 1
    pl.semaphore_wait(barrier, count)


SENDS, RECVS, LOCALS = 160, 160, 24


def sems():
    return [
        pltpu.SemaphoreType.DMA((SENDS,)),
        pltpu.SemaphoreType.DMA((RECVS,)),
        pltpu.SemaphoreType.DMA((LOCALS,)),
    ]


def add_rows(dst, src, rows, step=16):
    def body(i, carry):
        at = pl.ds(pl.multiple_of(i * step, step), step)
        dst[at, :] = (dst[at, :].astype(F32) + src[at, :].astype(F32)).astype(dst.dtype)
        return carry

    lax.fori_loop(0, rows // step, body, 0)


def comm_params(ident, mib=None):
    limit = None if mib is None else mib * MIB
    return pltpu.CompilerParams(collective_id=ident, has_side_effects=True, vmem_limit_bytes=limit)


def spread_zx(net, name, block, own):
    p = net.place
    offs = p.offs

    def step(i):
        if i >= len(offs):
            return
        off = offs[i]
        zz = p.z + off
        valid = p.valid(off)
        ref = block(zz, p.x)

        def body():
            if off:
                net.got(ref, (name, "z", off))

        when(valid, body)
        src = ref if off else own
        if off <= 0:
            net.put(src, ref, "up", (name, "z", off - 1), both(valid, p.can_up))
        if off >= 0:
            net.put(src, ref, "down", (name, "z", off + 1), both(valid, p.can_down))
        net.put(src, ref, "x", (name, "x", off), valid)

    def finish():
        for off in offs:
            ref = block(p.z + off, 1 - p.x)
            when(p.valid(off), lambda: net.got(ref, (name, "x", off)))

    return step, finish


def spread_xz(net, name, block, pair, own, placed):
    p = net.place
    offs = p.offs

    def begin():
        net.put(own, block(p.z, p.x), "x", (name, "x"))

    def step(i):
        off = offs[i]
        if off == 0:
            placed.wait()
            net.got(block(p.z, 1 - p.x), (name, "x"))
        valid = p.valid(off)
        ref = pair(p.z + off)
        if off:
            when(valid, lambda: net.got(ref, (name, "z", off)))
        if off <= 0:
            net.put(ref, ref, "up", (name, "z", off - 1), both(valid, p.can_up))
        if off >= 0:
            net.put(ref, ref, "down", (name, "z", off + 1), both(valid, p.can_down))

    return begin, step


SITES = {
    "x1": ("x", 0, 0, 0),
    "y1": ("y", 0, 0, 1),
    "x3": ("x", 0, 0, 1),
    "y3": ("y", 0, 0, 0),
    "y2": ("y", 1, 0, 0),
    "x2": ("x", 0, 1, 1),
    "c0": ("c", 0, 0, None),
    "cx": ("c", 1, 0, None),
    "cy": ("c", 0, 1, None),
    "cxy": ("c", 1, 1, None),
}
NAMES = list(SITES)


class Plane:
    def __init__(self, place, everyone, own, sends, recvs):
        self.place, self.everyone, self.own = place, everyone, own
        self.sends, self.recvs = sends, recvs
        self.half = own.shape[0] // 2

    def ref(self, zz, dx, dy, dc, part):
        p = self.place
        x, y, c = p.x + dx - 2 * p.x * dx, p.y + dy - 2 * p.y * dy, p.c + dc - 2 * p.c * dc
        ref = self.everyone.at[((zz * 2 + x) * 2 + y) * 2 + c]
        return ref if part is None else ref.at[pl.ds(part * self.half, self.half)]

    def copy(self, site, zz, src=None):
        link, dx, dy, part = SITES[site]
        dst = self.ref(zz, dx, dy, 0, part)
        at = NAMES.index(site) * self.place.depth + zz
        return pltpu.make_async_remote_copy(
            src_ref=dst if src is None else src,
            dst_ref=dst,
            send_sem=self.sends.at[at],
            recv_sem=self.recvs.at[at],
            device_id=self.place.to[link],
            device_id_type=MESH,
        )

    def take(self, site, zz):
        link, dx, dy, part = SITES[site]
        dx, dy = dx ^ (link == "x"), dy ^ (link == "y")
        ref = self.ref(zz, dx, dy, int(link == "c"), part)
        at = NAMES.index(site) * self.place.depth + zz
        pltpu.make_async_remote_copy(
            src_ref=ref,
            dst_ref=ref,
            send_sem=self.sends.at[at],
            recv_sem=self.recvs.at[at],
            device_id=self.place.to[link],
            device_id_type=MESH,
        ).wait_recv()

    def z_copy(self, zz, up):
        p = self.place
        ref = self.ref(zz, 0, 0, 0, None)
        base = len(NAMES) * p.depth
        return pltpu.make_async_remote_copy(
            src_ref=ref,
            dst_ref=ref,
            send_sem=self.sends.at[base + (0 if up else p.depth) + zz],
            recv_sem=self.recvs.at[base + zz],
            device_id=p.to["up" if up else "down"],
            device_id_type=MESH,
        )

    def each_z(self, zz, act):
        p = self.place
        pl.when((zz <= p.z) & p.can_up)(lambda: act(True))
        pl.when((zz >= p.z) & p.can_down)(lambda: act(False))

    def own_along_z(self):
        p = self.place
        base = len(NAMES) * p.depth

        def start(up):
            pltpu.make_async_remote_copy(
                src_ref=self.own,
                dst_ref=self.ref(p.z, 0, 0, 0, None),
                send_sem=self.sends.at[base + (0 if up else p.depth) + p.z],
                recv_sem=self.recvs.at[base + p.z],
                device_id=p.to["up" if up else "down"],
                device_id_type=MESH,
            ).start()

        self.each_z(p.z, start)

    def take_z(self, zz):
        self.z_copy(zz, True).wait_recv()

    def along_z(self, zz):
        self.take_z(zz)
        self.each_z(zz, lambda up: self.z_copy(zz, up).start())

    def first(self, zz, mine=False):
        whole, part_a, part_b = None, None, None
        if mine:
            whole = self.own
            part_a, part_b = whole.at[pl.ds(0, self.half)], whole.at[pl.ds(self.half, self.half)]
        self.copy("x1", zz, part_a).start()
        self.copy("y1", zz, part_b).start()
        self.copy("x3", zz, part_b).start()
        self.copy("y3", zz, part_a).start()
        self.copy("c0", zz, whole).start()

    def second(self, zz):
        self.take("x1", zz)
        self.copy("y2", zz).start()
        self.take("y1", zz)
        self.copy("x2", zz).start()

    def third_y(self, zz):
        self.take("y3", zz)
        self.copy("cy", zz).start()

    def third_x(self, zz):
        self.take("x3", zz)
        self.copy("cx", zz).start()
        self.take("x2", zz)
        self.take("y2", zz)
        self.copy("cxy", zz).start()

    def arrived_y(self, zz):
        self.take("c0", zz)
        self.take("cy", zz)

    def arrived_x(self, zz):
        self.take("cx", zz)
        self.take("cxy", zz)

    def finish(self, zs, z_zs):
        for zz in zs:
            for site in NAMES:
                self.copy(site, zz).wait_send()
        for zz in z_zs:
            self.each_z(zz, lambda up, zz=zz: self.z_copy(zz, up).wait_send())


def plane_sems(depth):
    return [pltpu.SemaphoreType.DMA(((len(NAMES) + 2) * depth,))] * 2


def same_document(seg_row):
    row = seg_row[...]
    column = jnp.transpose(jnp.broadcast_to(row, (LANES, row.shape[1])))[:, 0:1]
    return column == row


def first_kernel(
    depth, wq, wk, wv, wo, inp, og, gain, seg_row,
    qkv_hbm, o_hbm, rows_hbm, act_hbm, proj_hbm, att_hbm, part_hbm, grad_all,
    weights, full_o, rows, act, proj, att, part, og_send, og_recv, send, recv, local,
):
    p = Place(depth)
    net = Net(p, send, recv, local)
    grads = Plane(p, grad_all, og, og_send, og_recv)
    w_rows, w_cols = wq.shape
    o_cols = wo.shape[1]
    count, width = inp.shape
    fsdp, heads = 2 * depth, w_cols // HEAD

    def column(f):
        return full_o.at[:, pl.ds(pl.multiple_of(f * o_cols, LANES), o_cols)]

    def columns(z):
        return full_o.at[:, pl.ds(pl.multiple_of(z * (2 * o_cols), LANES), 2 * o_cols)]

    def slab(i):
        return lambda z, x: weights.at[i, z * 2 + x]

    greet(p, ("x", "y", "c", "z"))
    mine = rows.at[p.t]
    net.put(inp, mine, "y", ("rows", "y"))
    net.put(inp, mine, "c", ("rows", "c0"))
    placed = net.local(wo, column(p.f))
    owns = [net.local(inp, mine)]
    owns += [net.local(w, weights.at[i, p.f]) for i, w in enumerate((wq, wk, wv))]
    kept = net.local(og, grads.ref(p.z, 0, 0, 0, None))
    flows = [spread_zx(net, f"w{i}", slab(i), w) for i, w in enumerate((wq, wk, wv))]
    o_begin, o_step = spread_xz(net, "o", lambda z, x: column(z * 2 + x), columns, wo, placed)
    steps = len(p.offs)

    def norm():
        other = rows.at[(1 - p.y) * 2 + p.c]
        net.got(other, ("rows", "y"))
        net.put(other, other, "c", ("rows", "c1"))
        net.got(rows.at[p.y * 2 + 1 - p.c], ("rows", "c0"))
        net.got(rows.at[(1 - p.y) * 2 + 1 - p.c], ("rows", "c1"))
        owns[0].wait()
        for t in range(rows.shape[0]):

            def body(i, carry):
                at = pl.ds(pl.multiple_of(i * 16, 16), 16)
                values = rows[t, at, :].astype(F32)
                inverse = lax.rsqrt(jnp.mean(values * values, axis=-1, keepdims=True) + EPSILON)
                to = pl.ds(pl.multiple_of(t * count + i * 16, 16), 16)
                act[to, :] = (values * inverse * gain[...]).astype(BF16)
                return carry

            lax.fori_loop(0, count // 16, body, 0)

    saves = []

    def rows_in():
        norm()
        saves.append(net.local(rows, rows_hbm))
        saves.append(net.local(act, act_hbm))

    def project_with(i):
        owns[1 + i].wait()
        flows[i][1]()
        saves.append(net.local(weights.at[i], qkv_hbm.at[i]))
        wide = 256

        def project(k, carry):
            at = pl.ds(pl.multiple_of(k * wide, wide), wide)
            to = pl.ds(pl.multiple_of(i * w_cols + k * wide, wide), wide)
            matrix = weights[i, :, :, at].reshape(width, wide)
            proj[:, to] = jnp.dot(act[...], matrix, preferred_element_type=F32).astype(BF16)
            return carry

        lax.fori_loop(0, w_cols // wide, project, 0)

    scale = 1.0 / math.sqrt(HEAD)

    def head(h):
        if h == 0:
            saves.append(net.local(proj, proj_hbm))
        same = same_document(seg_row)
        query, keys, values = [
            proj[:, i * w_cols + h * HEAD : i * w_cols + (h + 1) * HEAD] for i in range(3)
        ]
        scores = lax.dot_general(query, keys, CONTRACT_LAST, preferred_element_type=F32) * scale
        scores = jnp.where(same, scores, -1e30)
        expo = jnp.exp(scores - jnp.max(scores, axis=-1, keepdims=True))
        probs = (expo / jnp.sum(expo, axis=-1, keepdims=True)).astype(BF16)
        att[:, h * HEAD : (h + 1) * HEAD] = jnp.dot(
            probs, values, preferred_element_type=F32
        ).astype(BF16)

    def out_rows(k, carry):
        at = pl.ds(pl.multiple_of(k * 256, 256), 256)
        part[:, at] = jnp.dot(att[...], full_o[:, at], preferred_element_type=F32).astype(BF16)
        return carry

    def branch():
        saves.append(net.local(full_o, o_hbm))
        saves.append(net.local(att, att_hbm))
        lax.fori_loop(0, width // 256, out_rows, 0)
        saves.append(net.local(part, part_hbm))

    (q_step, _), (k_step, _), (v_step, _) = flows

    def g_first():
        grads.first(p.z, True)

    if depth == 4 and heads == 4:
        perform(
            (o_begin,), (v_step, 0), (q_step, 0), (k_step, 0), (q_step, 1), (q_step, 2),
            (q_step, 3), (v_step, 1), (k_step, 1), (k_step, 2), (q_step, 4), (k_step, 3),
            (v_step, 2), (q_step, 5), (rows_in,), (v_step, 3), (q_step, 6), (k_step, 4),
            (o_step, 0), (v_step, 4), (k_step, 5), (o_step, 1), (v_step, 5), (o_step, 2),
            (k_step, 6), (project_with, 0), (v_step, 6), (project_with, 1), (g_first,),
            (o_step, 3), (o_step, 4), (project_with, 2), (head, 0), (grads.second, p.z),
            (head, 1), (head, 2), (head, 3), (o_step, 5), (o_step, 6), (branch,),
            (grads.third_y, p.z), (grads.third_x, p.z),
            (grads.arrived_y, p.z), (grads.arrived_x, p.z),
        )
    else:
        perform((o_begin,), (g_first,), *every(steps, q_step, k_step, v_step, o_step), (rows_in,))
        perform((grads.second, p.z), (grads.third_y, p.z), (grads.third_x, p.z))
        perform(*every(3, project_with))
        perform(*every(heads, head), (branch,))
        perform((grads.arrived_y, p.z), (grads.arrived_x, p.z))
    kept.wait()
    for copy in saves:
        copy.wait()
    grads.finish([p.z], [])
    net.finish()


def first_gather(depth, w_query, w_key, w_value, w_output, inputs, out_grad, gain, segments, tp):
    fsdp = 2 * depth
    w_rows, w_cols = w_query.shape
    o_rows, o_cols = w_output.shape
    rows, width = inputs.shape
    seq = tp * rows
    shape = jax.ShapeDtypeStruct
    return pl.pallas_call(
        functools.partial(first_kernel, depth),
        out_shape=[
            shape((3, fsdp, w_rows, w_cols), BF16),
            shape((o_rows, fsdp * o_cols), BF16),
            shape((tp, rows, width), BF16),
            shape((seq, width), BF16),
            shape((seq, 3 * w_cols), BF16),
            shape((seq, w_cols), BF16),
            shape((seq, width), BF16),
            shape((fsdp * tp, rows, width), BF16),
        ],
        in_specs=[VMEM] * 8,
        out_specs=[ANY] * 8,
        scratch_shapes=[
            pltpu.VMEM((3, fsdp, w_rows, w_cols), BF16),
            pltpu.VMEM((o_rows, fsdp * o_cols), BF16),
            pltpu.VMEM((tp, rows, width), BF16),
            pltpu.VMEM((seq, width), BF16),
            pltpu.VMEM((seq, 3 * w_cols), BF16),
            pltpu.VMEM((seq, w_cols), BF16),
            pltpu.VMEM((seq, width), BF16),
        ]
        + plane_sems(depth)
        + sems(),
        compiler_params=comm_params(1, 60),
        name="first_gather",
    )(
        w_query, w_key, w_value, w_output, inputs, out_grad, gain[None, :], segments[None, :],
    )


def moe_kernel(
    depth, capacity, experts, blocks,
    part, inp, og, gain, router, mask, rank, gate_hbm, up_hbm, down_hbm, grad_in_hbm,
    resid, gates_out, act_all, grad_all, out_hbm, back_hbm, x_hbm, g_hbm, hid_hbm, gl_hbm, ul_hbm,
    acc, rc, ry, own, w_gate, w_up, w_down, act_in, grad_in, x_rows, g_rows, tails, hid, gl, ul,
    o_keep, r_keep, out, back,
    act_send, act_recv, og_send, og_recv, send, recv, local, load_sems, save_sems,
):
    p = Place(depth)
    net = Net(p, send, recv, local)
    rows, width = inp.shape
    local_experts = w_gate.shape[0]
    weights = [
        net.local(src, dst)
        for src, dst in ((gate_hbm, w_gate), (up_hbm, w_up), (down_hbm, w_down))
    ]
    part_in = net.local(part.at[:, p.c], acc)
    acts = Plane(p, act_all, own, act_send, act_recv)
    grads = Plane(p, grad_all, og, og_send, og_recv)
    greet(p, ("x", "y", "c", "z"))

    net.put(part.at[:, 1 - p.c], rc, "c", ("rc",))
    far = 1 - p.y

    def along_y():
        part_in.wait()
        net.got(rc, ("rc",))
        add_rows(acc.at[far], rc.at[far], rows)
        net.put(acc.at[far], ry, "y", ("ry",))
        add_rows(acc.at[p.y], rc.at[p.y], rows)

    kept = []

    def norm():
        net.got(ry, ("ry",))

        def body(i, carry):
            at = pl.ds(pl.multiple_of(i * 16, 16), 16)
            branch = acc[p.y, at, :].astype(F32) + ry[at, :].astype(F32)
            values = inp[at, :].astype(F32) + branch
            resid[at, :] = values
            inverse = lax.rsqrt(jnp.mean(values * values, axis=-1, keepdims=True) + EPSILON)
            own[at, pl.ds(0, width)] = (values * inverse * gain[...]).astype(BF16)
            return carry

        lax.fori_loop(0, rows // 16, body, 0)
        twice = jnp.concatenate(
            [router[...]] * 2 + [jnp.zeros((LANES - 2 * experts, width), BF16)], axis=0
        )
        logits = lax.dot_general(
            own[:, pl.ds(0, width)], twice, CONTRACT_LAST, preferred_element_type=F32
        )
        chosen = mask[...] > 0.0
        peak = jnp.max(jnp.where(chosen, logits, -1e30), axis=1, keepdims=True)
        expo = jnp.where(chosen, jnp.exp(jnp.minimum(logits - peak, 0.0)), 0.0)
        lane = lax.broadcasted_iota(jnp.int32, expo.shape, 1)
        total = jnp.sum(jnp.where(lane < experts, expo, 0.0), axis=1, keepdims=True)
        gates = expo / total
        gates_out[...] = gates
        high = gates.astype(BF16).astype(F32)
        tail = jnp.where(
            lane < experts, high, jnp.where(lane < 2 * experts, gates - high, rank[...])
        )
        own[:, pl.ds(width, LANES)] = tail.astype(BF16)
        kept.append(net.local(own, acts.ref(p.z, 0, 0, 0, None)))

    first_expert = p.f * local_experts
    tp_lane = p.t * experts + first_expert
    pick_row = lax.broadcasted_iota(jnp.int32, (8, LANES), 0)
    pick_lane = lax.broadcasted_iota(jnp.int32, (8, LANES), 1)
    pick = (
        (pick_lane == 2 * experts + first_expert + pick_row) & (pick_row < local_experts)
    ).astype(BF16)
    places = lax.broadcasted_iota(jnp.int32, (capacity, rows), 0).astype(F32)
    slots = blocks * capacity

    def blocks_of(zz, j):
        return (zz * 2 + (1 - p.x if j else p.x)) * blocks

    def loads(zz, j):
        at = pl.ds(blocks_of(zz, j), blocks)
        return [
            pltpu.make_async_copy(act_all.at[at], act_in.at[j], load_sems.at[j, 0]),
            pltpu.make_async_copy(grad_all.at[at], grad_in.at[j], load_sems.at[j, 1]),
        ]

    def save(zz, j, k):
        if k < 5:
            where = pl.ds(pl.multiple_of(blocks_of(zz, j) * capacity, 16), slots)
            src = (x_rows, g_rows, hid, gl, ul)[k]
            dst = (x_hbm, g_hbm, hid_hbm, gl_hbm, ul_hbm)[k].at[:, where]
        else:
            src = (out, back)[k - 5]
            dst = (out_hbm, back_hbm)[k - 5].at[pl.ds(blocks_of(zz, j), blocks)]
        return pltpu.make_async_copy(src, dst, save_sems.at[k])

    def one_hot(j, b):
        tail = act_in[j, b, :, pl.ds(width, LANES)]
        ranks = lax.dot_general(pick, tail, CONTRACT_LAST, preferred_element_type=F32)
        return jnp.concatenate(
            [
                (jnp.broadcast_to(ranks[e : e + 1, :], (capacity, rows)) == places).astype(BF16)
                for e in range(local_experts)
            ],
            axis=0,
        )

    def work(zz, j, started, serve):
        for copy in loads(zz, j):
            copy.wait()

        def settle(ks):
            def body():
                for k in ks:
                    save(zz, j, k).wait()

            when(started, body)

        settle((0, 1))

        def gather(b, carry):
            hot = one_hot(j, b)
            picked = jnp.dot(hot, act_in[j, b], preferred_element_type=F32)
            pulled = jnp.dot(hot, grad_in[j, b], preferred_element_type=F32).astype(BF16)
            at = pl.ds(pl.multiple_of(b * capacity, 16), capacity)
            for e in range(local_experts):
                piece = picked[e * capacity : (e + 1) * capacity]
                x_rows[e, at, :] = piece[:, :width].astype(BF16)
                tails[e, at, :] = piece[:, width:]
                g_rows[e, at, :] = pulled[e * capacity : (e + 1) * capacity]
            return carry

        lax.fori_loop(0, blocks, gather, 0)
        for k in (0, 1):
            save(zz, j, k).start()
        serve(0)
        settle((2, 3, 4))
        for e in range(local_experts):
            tail_lane = lax.broadcasted_iota(jnp.int32, (slots, LANES), 1)
            mine = (tail_lane == first_expert + e) | (tail_lane == experts + first_expert + e)
            gates_of = jnp.sum(jnp.where(mine, tails[e], 0.0), axis=1, keepdims=True)
            pre = jnp.dot(x_rows[e], w_gate[e], preferred_element_type=F32)
            up = jnp.dot(x_rows[e], w_up[e], preferred_element_type=F32)
            raw = lax.dot_general(g_rows[e], w_down[e], CONTRACT_LAST, preferred_element_type=F32)
            sig = jax.nn.sigmoid(pre)
            silu = pre * sig
            hidden = silu * up
            gate_grad = jnp.sum(hidden * raw, axis=1, keepdims=True)
            scaled = raw * gates_of
            hid_low = (hidden * gates_of).astype(BF16)
            gate_low = (scaled * up * sig * (1.0 + pre * (1.0 - sig))).astype(BF16)
            up_low = (scaled * silu).astype(BF16)
            hid[e] = hid_low
            gl[e] = gate_low
            ul[e] = up_low
            o_rows = jnp.dot(hid_low, w_down[e], preferred_element_type=F32).astype(BF16)
            r_rows = (
                lax.dot_general(gate_low, w_gate[e], CONTRACT_LAST, preferred_element_type=F32)
                + lax.dot_general(up_low, w_up[e], CONTRACT_LAST, preferred_element_type=F32)
            ).astype(BF16)
            r_tail = jnp.where(tail_lane == tp_lane + e, gate_grad, 0.0).astype(BF16)
            for b in range(blocks):
                at = slice(b * capacity, (b + 1) * capacity)
                to = slice(e * capacity, (e + 1) * capacity)
                o_keep[b, to, :] = o_rows[at]
                r_keep[b, to, pl.ds(0, width)] = r_rows[at]
                r_keep[b, to, pl.ds(width, LANES)] = r_tail[at]
            serve(1 + e)
        for k in (2, 3, 4):
            save(zz, j, k).start()
        settle((5, 6))

        def combine(b, carry):
            hot = one_hot(j, b)
            out[b] = lax.dot_general(
                hot, o_keep[b], CONTRACT_FIRST, preferred_element_type=F32
            ).astype(BF16)
            back[b] = lax.dot_general(
                hot, r_keep[b], CONTRACT_FIRST, preferred_element_type=F32
            ).astype(BF16)
            return carry

        lax.fori_loop(0, blocks, combine, 0)
        for k in (5, 6):
            save(zz, j, k).start()
        serve(5)

    def load(i, j):
        if i == j == 0:
            kept[0].wait()
            for copy in weights:
                copy.wait()
        for copy in loads(p.near[i], j):
            copy.start()

    near = p.near
    g1, g2, g3y, g3x = grads.first, grads.second, grads.third_y, grads.third_x
    a1, a2, a3y, a3x = acts.first, acts.second, acts.third_y, acts.third_x
    if depth == 4:
        perform(
            (grads.own_along_z,), (along_y,), (grads.along_z, near[1]), (g1, near[1]), (norm,),
            (acts.own_along_z,), (a1, p.z, True), (a2, p.z), (acts.along_z, near[1]), (a3y, p.z),
            (a1, near[1]), (acts.arrived_y, p.z), (load, 0, 0), (g2, near[1]),
            (grads.along_z, near[2]), (g1, near[2]),
        )
        service = {
            (0, 0, 1): [(a3x, p.z)],
            (0, 0, 3): [(acts.arrived_x, p.z), (load, 0, 1)],
            (0, 0, 4): [(acts.along_z, near[2])],
            (0, 0, 5): [(a2, near[1])],
            (0, 1, 0): [(a1, near[2]), (g3y, near[1])],
            (0, 1, 2): [(a3y, near[1])],
            (0, 1, 3): [
                (acts.arrived_y, near[1]), (grads.along_z, near[3]), (grads.arrived_y, near[1]),
                (load, 1, 0),
            ],
            (1, 0, 0): [(g2, near[2])],
            (1, 0, 1): [(g3x, near[1]), (g3y, near[2])],
            (1, 0, 2): [(g1, near[3])],
            (1, 0, 3): [(a3x, near[1])],
            (1, 0, 4): [
                (acts.along_z, near[3]), (a2, near[2]), (a3y, near[2]), (acts.arrived_x, near[1]),
                (grads.arrived_x, near[1]), (load, 1, 1),
            ],
            (1, 0, 5): [(g3x, near[2])],
            (1, 1, 3): [(grads.arrived_y, near[2]), (acts.arrived_y, near[2]), (load, 2, 0)],
            (1, 1, 4): [(a1, near[3])],
            (2, 0, 0): [(a3x, near[2])],
            (2, 0, 3): [(g2, near[3]), (grads.arrived_x, near[2])],
            (2, 0, 4): [(g3y, near[3]), (a2, near[3]), (acts.arrived_x, near[2]), (load, 2, 1)],
            (2, 0, 5): [(a3y, near[3])],
            (2, 1, 1): [(acts.arrived_y, near[3]), (grads.arrived_y, near[3]), (load, 3, 0)],
            (3, 0, 0): [(a3x, near[3])],
            (3, 0, 1): [(g3x, near[3])],
            (3, 0, 4): [(grads.arrived_x, near[3]), (acts.arrived_x, near[3]), (load, 3, 1)],
        }
    else:
        perform((along_y,), (norm,), (acts.own_along_z,), (grads.own_along_z,))
        for i, zz in enumerate(near):
            if i:
                perform((acts.along_z, zz), (grads.along_z, zz), (g1, zz), (g2, zz))
                perform((g3y, zz), (g3x, zz), (grads.arrived_y, zz), (grads.arrived_x, zz))
            perform((a1, zz, i == 0), (a2, zz), (a3y, zz), (a3x, zz))
            perform((acts.arrived_y, zz), (acts.arrived_x, zz))
        load(0, 0)
        service = {(g, 0, 0): [(load, g, 1)] for g in range(depth)}
        service.update({(g, 1, 4): [(load, g + 1, 0)] for g in range(depth - 1)})

    def group(g, carry):
        zz = p.nearest(g)

        def serve(j, k):
            for (at, half, place), steps in service.items():
                if (half, place) == (j, k):
                    pl.when(g == at)(functools.partial(perform, *steps))

        work(zz, 0, g > 0, functools.partial(serve, 0))
        work(zz, 1, None, functools.partial(serve, 1))
        return carry

    lax.fori_loop(0, depth, group, 0)
    for k in range(7):
        save(0, 1, k).wait()
    acts.finish(range(depth), range(depth))
    grads.finish(near[1:], near)
    net.finish()


def run_moe(
    depth, capacity, experts, part, inputs, out_grad, gain, router, mask, rank, w_gate, w_up, w_down,
    grad_all,
):
    tp, rows, width = part.shape
    wide = width + LANES
    count = 2 * depth * tp
    local_experts, _, hidden = w_gate.shape
    blocks = tp
    slots = blocks * capacity
    total = count * capacity
    shape = jax.ShapeDtypeStruct
    kept = [shape((local_experts, total, width), BF16)] * 2
    kept += [shape((local_experts, total, hidden), BF16)] * 3
    return pl.pallas_call(
        functools.partial(moe_kernel, depth, capacity, experts, blocks),
        out_shape=[
            shape((rows, width), F32),
            shape((rows, LANES), F32),
            shape((count, rows, wide), BF16),
            shape((count, rows, width), BF16),
            shape((count, rows, width), BF16),
            shape((count, rows, wide), BF16),
        ]
        + kept,
        in_specs=[ANY] + [VMEM] * 6 + [ANY] * 4,
        out_specs=[VMEM] * 2 + [ANY] * 9,
        input_output_aliases={10: 3},
        scratch_shapes=[
            pltpu.VMEM((2, rows, width), BF16),
            pltpu.VMEM((2, rows, width), BF16),
            pltpu.VMEM((rows, width), BF16),
            pltpu.VMEM((rows, wide), BF16),
            pltpu.VMEM(w_gate.shape, BF16),
            pltpu.VMEM(w_up.shape, BF16),
            pltpu.VMEM(w_down.shape, BF16),
            pltpu.VMEM((2, blocks, rows, wide), BF16),
            pltpu.VMEM((2, blocks, rows, width), BF16),
            pltpu.VMEM((local_experts, slots, width), BF16),
            pltpu.VMEM((local_experts, slots, width), BF16),
            pltpu.VMEM((local_experts, slots, LANES), F32),
            pltpu.VMEM((local_experts, slots, hidden), BF16),
            pltpu.VMEM((local_experts, slots, hidden), BF16),
            pltpu.VMEM((local_experts, slots, hidden), BF16),
            pltpu.VMEM((blocks, local_experts * capacity, width), BF16),
            pltpu.VMEM((blocks, local_experts * capacity, wide), BF16),
            pltpu.VMEM((blocks, rows, width), BF16),
            pltpu.VMEM((blocks, rows, wide), BF16),
        ]
        + plane_sems(depth) * 2
        + sems()
        + [pltpu.SemaphoreType.DMA((2, 2)), pltpu.SemaphoreType.DMA((7,))],
        compiler_params=comm_params(2, 60),
        name="moe",
    )(
        part.reshape(tp // 2, 2, rows, width), inputs, out_grad, gain[None, :], router, mask, rank,
        w_gate, w_up, w_down, grad_all,
    )


def chain_z(net, name, zz, acc, inbox, rows, add=None):
    p = net.place
    extra = p.depth

    def take(slot):
        net.got(inbox.at[slot], (name, "at", extra + 1, slot))
        (add or add_rows)(acc, inbox.at[slot], rows)

    pl.when((zz >= p.z) & p.can_down)(lambda: take(jnp.where(zz == p.z, extra, zz)))
    pl.when((zz <= p.z) & p.can_up)(lambda: take(zz))
    slot = jnp.where(zz == p.z + 1, extra, zz)
    net.put(acc, inbox.at[slot], "up", (name, "at", extra + 1, slot), zz > p.z)
    net.put(acc, inbox.at[zz], "down", (name, "at", extra + 1, zz), zz < p.z)


class Reduce:
    def __init__(self, net, name, fill, acc, ya, xa, xb, yb, inbox, z_inbox, xc, yc):
        self.net, self.name, self.fill, self.acc = net, name, fill, acc
        self.ya, self.xa, self.xb, self.yb = ya, xa, xb, yb
        self.inbox, self.z_inbox, self.xc, self.yc = inbox, z_inbox, xc, yc
        self.rows_a, self.rows_b, self.rows_c = ya.shape[2], xb.shape[2], yc.shape[0]
        self.rows_ab = self.rows_a + self.rows_b
        self.a, self.b = pl.ds(0, self.rows_a), pl.ds(self.rows_a, self.rows_b)
        self.ab, self.c = pl.ds(0, self.rows_ab), pl.ds(self.rows_ab, self.rows_c)

    def key(self, what, zz):
        return (self.name + what, "at", self.net.place.depth, zz)

    def one(self, i):
        p, net, acc = self.net.place, self.net, self.acc
        zz = p.far[i]
        self.fill(i, zz)
        net.put(acc.at[zz, :, 1 - p.y, self.a], self.ya.at[zz], "y", self.key("ya", zz))
        net.put(acc.at[zz, 1 - p.x, :, self.b], self.xb.at[zz], "x", self.key("xb", zz))

    def two(self, i):
        p, net, acc = self.net.place, self.net, self.acc
        x, y, zz = p.x, p.y, p.far[i]
        net.got(self.xb.at[zz], self.key("xb", zz))
        add_rows(acc.at[zz, x, 1 - y, self.b], self.xb.at[zz, 1 - y], self.rows_b)
        net.put(acc.at[zz, x, 1 - y, self.b], self.yb.at[zz], "y", self.key("yb", zz))
        net.got(self.ya.at[zz], self.key("ya", zz))
        add_rows(acc.at[zz, 1 - x, y, self.a], self.ya.at[zz, 1 - x], self.rows_a)
        net.put(acc.at[zz, 1 - x, y, self.a], self.xa.at[zz], "x", self.key("xa", zz))
        add_rows(acc.at[zz, x, y, self.a], self.ya.at[zz, x], self.rows_a)
        add_rows(acc.at[zz, x, y, self.b], self.xb.at[zz, y], self.rows_b)

    def three(self, i):
        p, net, acc = self.net.place, self.net, self.acc
        x, y, zz = p.x, p.y, p.far[i]
        net.got(self.xa.at[zz], self.key("xa", zz))
        add_rows(acc.at[zz, x, y, self.a], self.xa.at[zz], self.rows_a)
        net.got(self.yb.at[zz], self.key("yb", zz))
        add_rows(acc.at[zz, x, y, self.b], self.yb.at[zz], self.rows_b)
        chain_z(net, self.name + "z", zz, acc.at[zz, x, y, self.ab], self.inbox, self.rows_ab)

    def along_z(self, i):
        p = self.net.place
        zz = p.far[i]

        def add(dst, src, rows):
            for xx in range(2):
                for yy in range(2):
                    add_rows(dst.at[xx, yy], src.at[xx, yy], rows)

        chain_z(
            self.net, self.name + "c", zz, self.acc.at[zz, :, :, self.c], self.z_inbox, self.rows_c, add
        )

    def then_x(self):
        p, net = self.net.place, self.net
        net.put(self.acc.at[p.z, 1 - p.x, :, self.c], self.xc, "x", (self.name + "xc",))

    def then_y(self):
        p, net, x, y = self.net.place, self.net, self.net.place.x, self.net.place.y
        net.got(self.xc, (self.name + "xc",))
        add_rows(self.acc.at[p.z, x, 1 - y, self.c], self.xc.at[1 - y], self.rows_c)
        net.put(self.acc.at[p.z, x, 1 - y, self.c], self.yc, "y", (self.name + "yc",))
        add_rows(self.acc.at[p.z, x, y, self.c], self.xc.at[y], self.rows_c)

    def end(self):
        p, net = self.net.place, self.net
        net.got(self.yc, (self.name + "yc",))
        add_rows(self.acc.at[p.z, p.x, p.y, self.c], self.yc, self.rows_c)


def reduce_scratch(depth, rows, wide, parts):
    a, b = parts
    c = rows - a - b
    return [
        pltpu.VMEM((depth, 2, 2, rows, wide), BF16),
        pltpu.VMEM((depth, 2, a, wide), BF16),
        pltpu.VMEM((depth, a, wide), BF16),
        pltpu.VMEM((depth, 2, b, wide), BF16),
        pltpu.VMEM((depth, b, wide), BF16),
        pltpu.VMEM((depth + 1, a + b, wide), BF16),
        pltpu.VMEM((depth + 1, 2, 2, c, wide), BF16),
        pltpu.VMEM((2, c, wide), BF16),
        pltpu.VMEM((c, wide), BF16),
    ]


def tile_rows(rows, share):
    return max(16, int(rows * share) // 16 * 16)


def perform(*steps):
    for function, *args in steps:
        function(*args)


def every(depth, *functions):
    return [(function, i) for function in functions for i in range(depth)]


def widen(dst, src, rows):
    def body(i, carry):
        at = pl.ds(pl.multiple_of(i * 16, 16), 16)
        dst[at, :] = src[at, :].astype(F32)
        return carry

    lax.fori_loop(0, rows // 16, body, 0)


def back_kernel(
    depth, part, out_part, x_rows, g_rows, hid, gate_low, up_low,
    total, out_other, w_gate_grad, w_up_grad, w_down_grad,
    acc, ya, xa, xb, yb, inbox, z_inbox, xc, yc, rc, big, left, right, found, found_down,
    send, recv, local, load_sems, save_sems,
):
    p = Place(depth)
    net = Net(p, send, recv, local)
    c = p.c
    rows, width = total.shape
    local_experts = x_rows.shape[0]

    def loads(u):
        e, slot = u // 2, u % 2
        if u % 2 == 0:
            pairs = ((x_rows, big.at[slot]), (gate_low, left.at[slot]), (up_low, right.at[slot]))
        else:
            pairs = ((g_rows, big.at[slot]), (hid, left.at[slot]))
        return [
            pltpu.make_async_copy(src.at[e], dst, load_sems.at[slot, j])
            for j, (src, dst) in enumerate(pairs)
        ]

    def saves(u):
        e = u // 2
        if u % 2 == 0:
            targets = (w_gate_grad, w_up_grad)
            return [
                pltpu.make_async_copy(found.at[j], ref.at[e], save_sems.at[j])
                for j, ref in enumerate(targets)
            ]
        return [pltpu.make_async_copy(found_down, w_down_grad.at[e], save_sems.at[2])]

    units = 2 * local_experts

    def unit(u):
        slot = u % 2
        for copy in loads(u):
            copy.wait()
        if u >= 2:
            for copy in saves(u - 2):
                copy.wait()
        if u % 2 == 0:
            wide = 256

            def body(i, carry):
                at = pl.ds(pl.multiple_of(i * wide, wide), wide)
                tile = big[slot, :, at]
                for j, ref in enumerate((left, right)):
                    found[j, at, :] = lax.dot_general(
                        tile, ref[slot], CONTRACT_FIRST, preferred_element_type=F32
                    ).astype(BF16)
                return carry

            lax.fori_loop(0, width // wide, body, 0)
        else:
            wide = 512

            def body(i, carry):
                at = pl.ds(pl.multiple_of(i * wide, wide), wide)
                found_down[:, at] = lax.dot_general(
                    left[slot], big[slot, :, at], CONTRACT_FIRST, preferred_element_type=F32
                ).astype(BF16)
                return carry

            lax.fori_loop(0, width // wide, body, 0)
        for copy in saves(u):
            copy.start()
        if u + 2 < units:
            for copy in loads(u + 2):
                copy.start()

    fills = []
    for i in range(depth):
        zz = p.far[i]
        fills.append(net.local(part.at[zz, :, :, c], acc.at[zz]))
    greet(p, ("x", "y", "c", "z"))
    for i in range(depth):
        zz = p.far[i]
        net.put(part.at[zz, :, :, 1 - c], rc.at[zz], "c", ("c", "at", depth, zz))

    def fill(i, zz):
        fills[i].wait()
        net.got(rc.at[zz], ("c", "at", depth, zz))
        for xx in range(2):
            for yy in range(2):
                add_rows(acc.at[zz, xx, yy], rc.at[zz, xx, yy], rows)

    flow = Reduce(net, "b", fill, acc, ya, xa, xb, yb, inbox, z_inbox, xc, yc)
    def begin():
        for v in range(2):
            for copy in loads(v):
                copy.start()
        for zz in range(depth):
            net.put(out_part.at[zz, :, :, 1 - c], out_other.at[zz], "c", ("oc", "at", depth, zz))

    one, two, three, along_z = flow.one, flow.two, flow.three, flow.along_z
    if depth == 4 and units == 8:
        perform(
            (one, 0), (along_z, 0), (one, 1), (begin,), (one, 2), (unit, 0), (along_z, 1),
            (along_z, 2), (two, 0), (one, 3), (unit, 1), (unit, 2), (two, 1), (unit, 3), (two, 2),
            (three, 0), (unit, 4), (along_z, 3), (flow.then_x,), (unit, 5), (three, 1),
            (three, 2), (two, 3), (unit, 6), (flow.then_y,), (unit, 7), (flow.end,), (three, 3),
        )
    else:
        perform(*every(depth, one), (begin,), *every(depth, two, three, along_z))
        perform((flow.then_x,), (flow.then_y,), (flow.end,), *every(units, unit))
    for k in (units - 2, units - 1):
        for copy in saves(k):
            copy.wait()

    def last(i, carry):
        at = pl.ds(pl.multiple_of(i * 16, 16), 16)
        total[at, :] = acc[p.z, p.x, p.y, at, :].astype(F32)
        return carry

    lax.fori_loop(0, rows // 16, last, 0)
    for zz in range(depth):
        net.got(out_other.at[zz], ("oc", "at", depth, zz))
    net.finish()


def reduce_back(depth, part, out_part, x_rows, g_rows, hid, gate_low, up_low):
    count, rows, wide = part.shape
    width = out_part.shape[2]
    local_experts, slots, hidden = hid.shape
    shape = jax.ShapeDtypeStruct
    return pl.pallas_call(
        functools.partial(back_kernel, depth),
        out_shape=[
            shape((rows, wide), F32),
            shape((depth, 2, 2, rows, width), BF16),
            shape((local_experts, width, hidden), BF16),
            shape((local_experts, width, hidden), BF16),
            shape((local_experts, hidden, width), BF16),
        ],
        in_specs=[ANY] * 7,
        out_specs=[VMEM] + [ANY] * 4,
        scratch_shapes=reduce_scratch(depth, rows, wide, [tile_rows(rows, 0.375)] * 2)
        + [
            pltpu.VMEM((depth, 2, 2, rows, wide), BF16),
            pltpu.VMEM((2, slots, width), BF16),
            pltpu.VMEM((2, slots, hidden), BF16),
            pltpu.VMEM((2, slots, hidden), BF16),
            pltpu.VMEM((2, width, hidden), BF16),
            pltpu.VMEM((hidden, width), BF16),
        ]
        + sems()
        + [pltpu.SemaphoreType.DMA((2, 3)), pltpu.SemaphoreType.DMA((3,))],
        compiler_params=comm_params(3, 60),
        name="reduce_back",
    )(
        part.reshape(depth, 2, 2, 2, rows, wide),
        out_part.reshape(depth, 2, 2, 2, rows, width),
        x_rows, g_rows, hid, gate_low, up_low,
    )


def attend_back_kernel(
    depth, mine, act_hbm, wqkv_hbm, wo_hbm, qkv_hbm, att_hbm, whole_hbm, seg_row, gain, out_part, out_other,
    qkv_part, whole_part, gain_part, o_sum, o_rest, out_sum,
    acc, ya, xa, xb, yb, inbox, z_inbox, xc, yc, other, bg, act, wqkv, wo, qkv, att, ag, low, o_acc, o_inbox, o_rx,
    whole, act_grad, send, recv, local, other_sems,
):
    p = Place(depth)
    net = Net(p, send, recv, local)
    x, y, c = p.x, p.y, p.c
    rows, width = out_sum.shape
    seq = act.shape[0]
    cols = wo.shape[0]
    heads = cols // HEAD
    o_rows, o_cols = o_sum.shape

    def block(t):
        return bg.at[pl.ds(pl.multiple_of(t * rows, rows), rows)]

    own = net.local(mine, block(p.t))
    load_wo = net.local(wo_hbm, wo)
    load_att = net.local(att_hbm, att)
    load_qkv = net.local(qkv_hbm, qkv)
    load_act = net.local(act_hbm, act)
    load_w = net.local(wqkv_hbm, wqkv)
    load_whole = net.local(whole_hbm, whole)
    greet(p, ("x", "y", "c", "z"))
    own.wait()
    net.put(block(p.t), block(p.t), "y", ("bg", "y"))
    net.put(block(p.t), block(p.t), "c", ("bg", "c0"))

    def load_other(i):
        zz = p.far[i]
        return [
            pltpu.make_async_copy(out_part.at[zz, :, :, c], acc.at[zz], other_sems.at[0, i % 2]),
            pltpu.make_async_copy(out_other.at[zz], other.at[i % 2], other_sems.at[1, i % 2]),
        ]

    for i in range(2):
        for copy in load_other(i):
            copy.start()

    def fill(i, zz):
        for copy in load_other(i):
            copy.wait()
        for xx in range(2):
            for yy in range(2):
                add_rows(acc.at[zz, xx, yy], other.at[i % 2, xx, yy], rows)
        if i + 2 < depth:
            for copy in load_other(i + 2):
                copy.start()

    flow = Reduce(net, "out", fill, acc, ya, xa, xb, yb, inbox, z_inbox, xc, yc)

    def o_pair(z):
        return o_acc.at[:, pl.ds(pl.multiple_of(z * (2 * o_cols), LANES), 2 * o_cols)]

    def o_step(i):
        if i < depth:
            chain_z(net, "oz", p.far[i], o_pair(p.far[i]), o_inbox, o_rows)

    def o_along_x():
        theirs = pl.ds(pl.multiple_of((p.z * 2 + 1 - x) * o_cols, LANES), o_cols)
        net.put(o_acc.at[:, theirs], o_rx, "x", ("ox",))

    def rows_in():
        far = block((1 - y) * 2 + c)
        net.got(far, ("bg", "y"))
        net.put(far, far, "c", ("bg", "c1"))
        net.got(block(y * 2 + 1 - c), ("bg", "c0"))
        net.got(block((1 - y) * 2 + 1 - c), ("bg", "c1"))

    def attended_grad():
        load_wo.wait()
        ag[...] = lax.dot_general(
            bg[...], wo[...], CONTRACT_LAST, preferred_element_type=F32
        ).astype(BF16)

    wide = 512

    def o_body(i, carry):
        at = pl.ds(pl.multiple_of(i * wide, wide), wide)
        found = lax.dot_general(
            att[...], bg[:, at], CONTRACT_FIRST, preferred_element_type=F32
        ).astype(BF16)
        o_acc[:, at] = found[:o_rows]
        o_rest[:, at] = found[o_rows:]
        return carry

    def o_terms():
        load_att.wait()
        load_qkv.wait()
        lax.fori_loop(0, width // wide, o_body, 0)

    scale = 1.0 / math.sqrt(HEAD)
    same = same_document(seg_row)

    def head(h):
        at = slice(h * HEAD, (h + 1) * HEAD)
        query = qkv[:, h * HEAD : (h + 1) * HEAD]
        keys = qkv[:, cols + h * HEAD : cols + (h + 1) * HEAD]
        values = qkv[:, 2 * cols + h * HEAD : 2 * cols + (h + 1) * HEAD]
        grad = ag[:, at]
        scores = lax.dot_general(query, keys, CONTRACT_LAST, preferred_element_type=F32) * scale
        scores = jnp.where(same, scores, -1e30)
        expo = jnp.exp(scores - jnp.max(scores, axis=-1, keepdims=True))
        probs = expo / jnp.sum(expo, axis=-1, keepdims=True)
        prob_grad = lax.dot_general(grad, values, CONTRACT_LAST, preferred_element_type=F32)
        inner = jnp.sum(probs * prob_grad, axis=-1, keepdims=True)
        score_grad = (probs * (prob_grad - inner) * scale).astype(BF16)
        low[:, at] = jnp.dot(score_grad, keys, preferred_element_type=F32).astype(BF16)
        low[:, cols + h * HEAD : cols + (h + 1) * HEAD] = lax.dot_general(
            score_grad, query, CONTRACT_FIRST, preferred_element_type=F32
        ).astype(BF16)
        low[:, 2 * cols + h * HEAD : 2 * cols + (h + 1) * HEAD] = lax.dot_general(
            probs.astype(BF16), grad, CONTRACT_FIRST, preferred_element_type=F32
        ).astype(BF16)

    w_rows, w_cols = wqkv.shape[2:]

    def w_body(f, carry):
        at = pl.ds(pl.multiple_of(f * w_rows, w_rows), w_rows)
        qkv_part[f] = lax.dot_general(
            act[:, at], low[...], CONTRACT_FIRST, preferred_element_type=F32
        ).astype(BF16)
        act_grad[:, at] = sum(
            lax.dot_general(
                low[:, i * w_cols : (i + 1) * w_cols], wqkv[i, f], CONTRACT_LAST,
                preferred_element_type=F32,
            )
            for i in range(3)
        )
        return carry

    count = wqkv.shape[1]
    pieces = 4

    def w_piece(i):
        if i == 0:
            load_act.wait()
            load_w.wait()
        lax.fori_loop(i * count // pieces, (i + 1) * count // pieces, w_body, 0)

    def norm_piece(i):
        if i == 0:
            load_whole.wait()
            gain_part[...] = jnp.zeros_like(gain_part)
        span = seq // pieces // 16

        def body(k, total):
            at = pl.ds(pl.multiple_of((i * span + k) * 16, 16), 16)
            values, grad = whole[at, :].astype(F32), act_grad[at, :]
            inverse = lax.rsqrt(jnp.mean(values * values, axis=-1, keepdims=True) + EPSILON)
            scaled = gain[...] * grad
            pull = jnp.mean(values * scaled, axis=-1, keepdims=True)
            whole_part[at, :] = (
                inverse * scaled - values * (inverse * inverse * inverse) * pull
            ).astype(BF16)
            return total + jnp.sum(grad * values * inverse, axis=0, keepdims=True)

        total = lax.fori_loop(0, span, body, jnp.zeros(gain_part.shape, F32))
        gain_part[...] += total

    one, two, three, along_z = flow.one, flow.two, flow.three, flow.along_z
    if depth == 4 and heads == 4:
        perform(
            (one, 0), (one, 1), (one, 2), (along_z, 0), (along_z, 1), (rows_in,),
            (attended_grad,), (o_terms,), (o_step, 0), (along_z, 2), (two, 0), (head, 0),
            (two, 1), (one, 3), (o_step, 1), (o_step, 2), (head, 1), (head, 2), (head, 3),
            (two, 2), (three, 0), (w_piece, 0), (o_step, 3), (w_piece, 1), (along_z, 3),
            (flow.then_x,), (o_along_x,), (w_piece, 2), (three, 1), (three, 2), (flow.then_y,),
            (w_piece, 3), (norm_piece, 0), (norm_piece, 1), (two, 3), (norm_piece, 2), (flow.end,), (norm_piece, 3), (three, 3),
        )
    else:
        perform(*every(depth, one), (rows_in,), (attended_grad,), (o_terms,))
        perform(*every(heads, head), *every(pieces, w_piece, norm_piece))
        perform(*every(depth, two, three, along_z, o_step), (o_along_x,))
        perform((flow.then_x,), (flow.then_y,), (flow.end,))
    widen(out_sum, acc.at[p.z, x, y], rows)
    net.got(o_rx, ("ox",))
    at_o = pl.ds(pl.multiple_of((p.z * 2 + x) * o_cols, LANES), o_cols)

    def o_last(i, carry):
        at = pl.ds(pl.multiple_of(i * 16, 16), 16)
        o_sum[at, :] = o_acc[at, at_o].astype(F32) + o_rx[at, :].astype(F32)
        return carry

    lax.fori_loop(0, o_rows // 16, o_last, 0)
    net.finish()


def attend_back(
    depth, mine, act, wqkv, wo, qkv, att, whole, segments, gain, out_part, out_other, o_cols
):
    rows, width = mine.shape
    seq, cols = att.shape
    _, fsdp, w_rows, w_cols = wqkv.shape
    w_wide = 3 * w_cols
    shape = jax.ShapeDtypeStruct
    return pl.pallas_call(
        functools.partial(attend_back_kernel, depth),
        out_shape=[
            shape((fsdp, w_rows, w_wide), BF16),
            shape((seq, width), BF16),
            shape((1, width), F32),
            shape((cols // 2, o_cols), F32),
            shape((cols // 2, width), BF16),
            shape((rows, width), F32),
        ],
        in_specs=[ANY] * 7 + [VMEM] * 2 + [ANY] * 2,
        out_specs=[VMEM] * 6,
        scratch_shapes=reduce_scratch(
            depth, rows, width, [tile_rows(rows, 0.375), tile_rows(rows, 0.5)]
        )
        + [
            pltpu.VMEM((2, 2, 2, rows, width), BF16),
            pltpu.VMEM((seq, width), BF16),
            pltpu.VMEM((seq, width), BF16),
            pltpu.VMEM(wqkv.shape, BF16),
            pltpu.VMEM((cols, width), BF16),
            pltpu.VMEM((seq, w_wide), BF16),
            pltpu.VMEM((seq, cols), BF16),
            pltpu.VMEM((seq, cols), BF16),
            pltpu.VMEM((seq, w_wide), BF16),
            pltpu.VMEM((cols // 2, width), BF16),
            pltpu.VMEM((depth + 1, cols // 2, 2 * o_cols), BF16),
            pltpu.VMEM((cols // 2, o_cols), BF16),
            pltpu.VMEM((seq, width), BF16),
            pltpu.VMEM((seq, width), F32),
        ]
        + sems()
        + [pltpu.SemaphoreType.DMA((2, 2))],
        compiler_params=comm_params(4, 63),
        name="attend_back",
    )(
        mine, act, wqkv, wo, qkv, att, whole, segments[None, :], gain[None, :],
        out_part.reshape(depth, 2, 2, 2, rows, width), out_other,
    )


def last_kernel(
    depth, tail, qkv_part, row_part, o_part, q_sum, k_sum, v_sum, row_sum, tail_sum, o_sum,
    q_acc, q_rx, q_inbox, t_acc, t_rc, t_ry, s_acc, s_rc, s_ry, s_rx, s_inbox,
    o_acc, o_inbox, o_rx, send, recv, local,
):
    p = Place(depth)
    net = Net(p, send, recv, local)
    x, y, c = p.x, p.y, p.c
    rows, width = row_sum.shape
    w_rows, w_cols = q_sum.shape
    o_rows, o_cols = o_sum.shape
    small = s_acc.shape[3]
    o_load = net.local(o_part, o_acc)
    t_load = net.local(row_part.at[:, c], t_acc)
    s_load = net.local(tail.at[:, :, :, c], s_acc)
    loads = [net.local(qkv_part.at[p.far[i], x], q_acc.at[p.far[i]]) for i in range(depth)]
    greet(p, ("x", "y", "c", "z"))

    def q_along_x(i):
        zz = p.far[i]
        net.put(qkv_part.at[zz, 1 - x], q_rx.at[zz], "x", ("qx", "at", depth, zz))

    def q_along_z(i):
        zz = p.far[i]
        loads[i].wait()
        net.got(q_rx.at[zz], ("qx", "at", depth, zz))
        add_rows(q_acc.at[zz], q_rx.at[zz], w_rows)
        chain_z(net, "qz", zz, q_acc.at[zz], q_inbox, w_rows)

    def o_along_z(i):
        if i == 0:
            o_load.wait()
        zz = p.far[i]
        pair = o_acc.at[:, pl.ds(pl.multiple_of(zz * (2 * o_cols), LANES), 2 * o_cols)]
        chain_z(net, "oz", zz, pair, o_inbox, o_rows)

    def o_along_x():
        theirs = pl.ds(pl.multiple_of((p.z * 2 + 1 - x) * o_cols, LANES), o_cols)
        net.put(o_acc.at[:, theirs], o_rx, "x", ("ox",))

    def cores():
        net.put(row_part.at[:, 1 - c], t_rc, "c", ("tc",))
        net.put(tail.at[:, :, :, 1 - c], s_rc, "c", ("sc",))

    def along_y():
        t_load.wait()
        net.got(t_rc, ("tc",))
        add_rows(t_acc.at[1 - y], t_rc.at[1 - y], rows)
        net.put(t_acc.at[1 - y], t_ry, "y", ("ty",))
        s_load.wait()
        net.got(s_rc, ("sc",))
        for zz in range(depth):
            for xx in range(2):
                add_rows(s_acc.at[zz, xx, 1 - y], s_rc.at[zz, xx, 1 - y], small)
        net.put(s_acc.at[:, :, 1 - y], s_ry, "y", ("sy",))
        for zz in range(depth):
            for xx in range(2):
                add_rows(s_acc.at[zz, xx, y], s_rc.at[zz, xx, y], small)

    def s_along_x():
        net.got(s_ry, ("sy",))
        for z in range(depth):
            for xx in range(2):
                add_rows(s_acc.at[z, xx, y], s_ry.at[z, xx], small)
        net.put(s_acc.at[:, 1 - x, y], s_rx, "x", ("sx",))

    def s_in():
        net.got(s_rx, ("sx",))
        for z in range(depth):
            add_rows(s_acc.at[z, x, y], s_rx.at[z], small)

    def s_along_z(i):
        chain_z(net, "sz", p.far[i], s_acc.at[p.far[i], x, y], s_inbox, small)

    def rows_in():
        net.got(t_ry, ("ty",))

        def body(i, carry):
            at = pl.ds(pl.multiple_of(i * 16, 16), 16)
            row_sum[at, :] = (
                t_acc[y, at, :].astype(F32) + t_rc[y, at, :].astype(F32) + t_ry[at, :].astype(F32)
            )
            return carry

        lax.fori_loop(0, rows // 16, body, 0)

    def o_in():
        net.got(o_rx, ("ox",))
        at_o = pl.ds(pl.multiple_of((p.z * 2 + x) * o_cols, LANES), o_cols)

        def body(i, carry):
            at = pl.ds(pl.multiple_of(i * 16, 16), 16)
            o_sum[at, :] = o_acc[at, at_o].astype(F32) + o_rx[at, :].astype(F32)
            return carry

        lax.fori_loop(0, o_rows // 16, body, 0)

    if depth == 4:
        perform(
            (q_along_x, 0), (cores,), (o_along_z, 0), (q_along_x, 1), (o_along_z, 1), (along_y,),
            (o_along_z, 2), (s_along_x,), (q_along_x, 2), (q_along_z, 0), (q_along_x, 3),
            (o_along_z, 3), (rows_in,), (s_in,), (o_along_x,), (s_along_z, 0), (q_along_z, 1),
            (q_along_z, 2), (s_along_z, 1), (o_in,), (s_along_z, 2), (q_along_z, 3),
            (s_along_z, 3),
        )
    else:
        perform(*every(depth, q_along_x), (cores,), (along_y,), (s_along_x,))
        perform(*every(depth, q_along_z, o_along_z), (s_in,), (o_along_x,))
        perform(*every(depth, s_along_z), (rows_in,), (o_in,))

    def q_last(i, carry):
        at = pl.ds(pl.multiple_of(i * 16, 16), 16)
        for j, ref in enumerate((q_sum, k_sum, v_sum)):
            ref[at, :] = q_acc[p.z, at, pl.ds(j * w_cols, w_cols)].astype(F32)
        return carry

    lax.fori_loop(0, w_rows // 16, q_last, 0)
    widen(tail_sum, s_acc.at[p.z, x, y], small)
    net.finish()


def last_reduce(depth, tail, qkv_part, row_part, o_part):
    count, small, lanes = tail.shape
    fsdp, w_rows, w_wide = qkv_part.shape
    tp, rows, width = row_part.shape
    w_cols = w_wide // 3
    o_rows, o_cols = o_part.shape[0], width // fsdp
    shape = jax.ShapeDtypeStruct
    return pl.pallas_call(
        functools.partial(last_kernel, depth),
        out_shape=[shape((w_rows, w_cols), F32)] * 3
        + [shape((rows, width), F32), shape((small, lanes), F32), shape((o_rows, o_cols), F32)],
        in_specs=[ANY] * 4,
        out_specs=[VMEM] * 6,
        scratch_shapes=[
            pltpu.VMEM((depth, w_rows, w_wide), BF16),
            pltpu.VMEM((depth, w_rows, w_wide), BF16),
            pltpu.VMEM((depth + 1, w_rows, w_wide), BF16),
            pltpu.VMEM((2, rows, width), BF16),
            pltpu.VMEM((2, rows, width), BF16),
            pltpu.VMEM((rows, width), BF16),
            pltpu.VMEM((depth, 2, 2, small, lanes), BF16),
            pltpu.VMEM((depth, 2, 2, small, lanes), BF16),
            pltpu.VMEM((depth, 2, small, lanes), BF16),
            pltpu.VMEM((depth, small, lanes), BF16),
            pltpu.VMEM((depth + 1, small, lanes), BF16),
            pltpu.VMEM((o_rows, width), BF16),
            pltpu.VMEM((depth + 1, o_rows, 2 * o_cols), BF16),
            pltpu.VMEM((o_rows, o_cols), BF16),
        ]
        + sems(),
        compiler_params=comm_params(5, 48),
        name="last_reduce",
    )(
        tail.reshape(depth, 2, 2, 2, small, lanes),
        qkv_part.reshape(depth, 2, w_rows, w_wide),
        row_part.reshape(2, 2, rows, width),
        o_part,
    )


def norm_rows(values, gain):
    inverse = lax.rsqrt(jnp.mean(values * values, axis=-1, keepdims=True) + EPSILON)
    return (values * inverse * gain, inverse)


def norm_back(values, inverse, gain, grad):
    scaled = gain * grad
    gain_grad = jnp.sum(grad * values * inverse, axis=0)
    cubed = inverse * inverse * inverse
    values_grad = inverse * scaled - values * cubed * jnp.mean(
        values * scaled, axis=-1, keepdims=True
    )
    return (values_grad, gain_grad)


def contract_last(left, right):
    return lax.dot_general(
        left, right, (((1,), (1,)), ((), ())), preferred_element_type=jnp.float32
    )


def contract_first(left, right):
    return lax.dot_general(
        left, right, (((0,), (0,)), ((), ())), preferred_element_type=jnp.float32
    )


def dense_layer(
    inputs, out_grad, segments, routes, attn_gain, w_query, w_key, w_value, w_output,
    moe_gain, router, w_gate, w_up, w_down,
):
    tp, fsdp = lax.axis_size("tp"), lax.axis_size("fsdp")
    depth = fsdp // 2
    rows, width = inputs.shape
    local_experts = w_gate.shape[0]
    experts = local_experts * fsdp
    top_k = routes.shape[1]
    capacity = 3 * rows * top_k // (2 * experts)
    w_rows, w_cols = w_query.shape
    heads = w_cols // HEAD
    seq = tp * rows

    named = jnp.any(
        routes[:, :, None] == jnp.arange(experts, dtype=jnp.int32)[None, None, :], axis=1
    )
    hits = named.astype(F32)
    before = (jnp.arange(rows)[:, None] > jnp.arange(rows)[None, :]).astype(F32)
    ranks = jnp.where(named, jnp.dot(before, hits, preferred_element_type=F32), -1.0)
    fill = jnp.zeros((rows, LANES - 3 * experts), F32)
    blank = jnp.zeros((rows, experts), F32)
    mask = jnp.concatenate([hits, hits, blank, fill], axis=1)
    rank = jnp.concatenate([blank, blank, ranks, fill], axis=1)
    qkv_full, full_output, whole, act_one, qkv, attended, partial, grad_all = first_gather(
        depth, w_query, w_key, w_value, w_output, inputs, out_grad, attn_gain, segments, tp
    )
    resid, gates_wide, _, _, out_part, back_part, x_rows, g_rows, hid_low, gate_low, up_low = run_moe(
        depth, capacity, experts, partial.reshape(tp, rows, width), inputs, out_grad, moe_gain,
        router.T, mask, rank, w_gate, w_up, w_down, grad_all,
    )
    back, out_other, w_gate_grad, w_up_grad, w_down_grad = reduce_back(
        depth, back_part, out_part, x_rows, g_rows, hid_low, gate_low, up_low
    )
    gates = gates_wide[:, :experts]
    act_two = (
        resid
        * (inverse_two := lax.rsqrt(jnp.mean(resid * resid, axis=-1, keepdims=True) + EPSILON))
        * moe_gain
    ).astype(BF16)
    gate_grad = jnp.sum(back[:, width : width + tp * experts].reshape(rows, tp, experts), axis=1)
    logit_grad = gates * (gate_grad - jnp.sum(gates * gate_grad, axis=1, keepdims=True))
    act_two_grad = back[:, :width] + lax.dot_general(
        logit_grad, router.astype(F32), (((1,), (1,)), ((), ())), precision=HIGHEST
    )
    router_part = lax.dot_general(
        act_two.astype(F32), logit_grad, (((0,), (0,)), ((), ())), precision=HIGHEST
    )
    resid_part, gain_two_part = norm_back(resid, inverse_two, moe_gain, act_two_grad)
    resid_grad = out_grad.astype(F32) + resid_part
    qkv_part, whole_part, gain_one_part, o_first, o_rest, out_sum = attend_back(
        depth, resid_grad.astype(BF16), act_one, qkv_full, full_output, qkv, attended,
        whole.reshape(seq, width), segments, attn_gain, out_part, out_other, w_output.shape[1],
    )
    count = fsdp * tp
    piece = width // count
    small = jnp.concatenate([router_part, gain_one_part.reshape(-1, 1), gain_two_part[:, None]], axis=1)
    small = small.astype(BF16).reshape(count, piece, experts + 2)
    tail = jnp.pad(small, ((0, 0), (0, -piece % 16), (0, LANES - experts - 2)))
    q_sum, k_sum, v_sum, row_sum, side, o_second = last_reduce(
        depth, tail, qkv_part, whole_part.reshape(tp, rows, width), o_rest
    )
    o_sum = jnp.concatenate([o_first, o_second], axis=0)
    output = (resid + out_sum).astype(BF16)
    input_grad = resid_grad + row_sum
    side = side[:piece]
    return (
        output,
        input_grad,
        side[:, experts],
        q_sum,
        k_sum,
        v_sum,
        o_sum,
        side[:, experts + 1],
        side[:, :experts],
        w_gate_grad.astype(F32),
        w_up_grad.astype(F32),
        w_down_grad.astype(F32),
    )


def send_rows(buffer):
    return lax.all_to_all(buffer, "fsdp", split_axis=1, concat_axis=1, tiled=True)


def per_device(
    inputs,
    out_grad,
    segments,
    routes,
    attn_gain,
    w_query,
    w_key,
    w_value,
    w_output,
    moe_gain,
    router,
    w_gate,
    w_up,
    w_down,
):
    tp_count = lax.axis_size("tp")
    fsdp_count = lax.axis_size("fsdp")
    rows_piece, width = inputs.shape
    head_size = HEAD
    full_query, full_key, full_value, full_output = (
        lax.all_gather(w_query, "fsdp", axis=0, tiled=True),
        lax.all_gather(w_key, "fsdp", axis=0, tiled=True),
        lax.all_gather(w_value, "fsdp", axis=0, tiled=True),
        lax.all_gather(w_output, "fsdp", axis=1, tiled=True),
    )
    whole_rows = lax.all_gather(inputs, "tp", axis=0, tiled=True)
    seq_len = whole_rows.shape[0]
    whole_float = whole_rows.astype(jnp.float32)
    normed_one, inverse_one = norm_rows(whole_float, attn_gain)
    act_one = normed_one.astype(jnp.bfloat16)
    local_heads = full_query.shape[1] // head_size
    query = (
        jnp.dot(act_one, full_query, preferred_element_type=jnp.float32)
        .astype(jnp.bfloat16)
        .reshape(seq_len, local_heads, head_size)
    )
    key_rows = (
        jnp.dot(act_one, full_key, preferred_element_type=jnp.float32)
        .astype(jnp.bfloat16)
        .reshape(seq_len, local_heads, head_size)
    )
    value_rows = (
        jnp.dot(act_one, full_value, preferred_element_type=jnp.float32)
        .astype(jnp.bfloat16)
        .reshape(seq_len, local_heads, head_size)
    )
    block_rows = min(512, seq_len)
    score_scale = 1.0 / math.sqrt(head_size)

    def block_scores(query_block):
        scores = (
            jnp.einsum("qhd,khd->hqk", query_block, key_rows, preferred_element_type=jnp.float32)
            * score_scale
        )
        same_doc = segments[:, None] == segments[None, :]
        return jnp.where(same_doc[None], scores, -1e30)

    scores = block_scores(query)
    peak = jnp.max(scores, axis=-1, keepdims=True)
    expo = jnp.exp(scores - peak)
    total = jnp.sum(expo, axis=-1, keepdims=True)
    softmax_rows = (expo / total).astype(jnp.bfloat16)
    block_outputs = jnp.einsum(
        "hqk,khd->qhd", softmax_rows, value_rows, preferred_element_type=jnp.float32
    )
    log_totals = [peak + jnp.log(total)]
    attended = block_outputs.reshape(seq_len, -1).astype(jnp.bfloat16)
    branch = lax.psum_scatter(
        jnp.dot(attended, full_output, preferred_element_type=jnp.float32).astype(jnp.bfloat16),
        "tp",
        scatter_dimension=0,
        tiled=True,
    ).astype(jnp.float32)
    resid = inputs.astype(jnp.float32) + branch
    normed_two, inverse_two = norm_rows(resid, moe_gain)
    act_two = normed_two.astype(jnp.bfloat16)
    local_experts = w_gate.shape[0]
    experts = local_experts * fsdp_count
    top_k = routes.shape[1]
    capacity = 3 * rows_piece * top_k // (2 * experts)
    logits = jnp.dot(act_two, router, preferred_element_type=jnp.float32)
    picks = (routes[:, :, None] == jnp.arange(experts, dtype=jnp.int32)[None, None, :]).astype(
        jnp.float32
    )
    chosen = jnp.einsum("tke,te->tk", picks, logits, precision=HIGHEST)
    gates = jax.nn.softmax(chosen, axis=-1)
    flat_routes = routes.reshape(-1)
    route_count = flat_routes.shape[0]
    hits = (flat_routes[:, None] == jnp.arange(experts, dtype=jnp.int32)[None, :]).astype(jnp.int32)
    ranks = jnp.sum((jnp.cumsum(hits, axis=0) - 1) * hits, axis=1)
    slots = flat_routes * capacity + ranks
    sources = (
        jnp.full((experts * capacity,), route_count, jnp.int32)
        .at[slots]
        .set(jnp.arange(route_count, dtype=jnp.int32))
    )
    padded_act = jnp.concatenate([act_two, jnp.zeros((1, width), jnp.bfloat16)], 0)
    send_buffer = padded_act[sources // top_k].reshape(
        1, fsdp_count, local_experts * capacity, width
    )
    gate_full, up_full, down_full = (
        lax.all_gather(w_gate, "tp", axis=2, tiled=True),
        lax.all_gather(w_up, "tp", axis=2, tiled=True),
        lax.all_gather(w_down, "tp", axis=1, tiled=True),
    )
    own_in = send_rows(send_buffer)
    own_rows = own_in.reshape(fsdp_count, local_experts, capacity, width)
    own_gate = jnp.einsum("secd,edf->secf", own_rows, gate_full, preferred_element_type=jnp.float32)
    own_up = jnp.einsum("secd,edf->secf", own_rows, up_full, preferred_element_type=jnp.float32)
    own_sigmoid = jax.nn.sigmoid(own_gate)
    own_silu = own_gate * own_sigmoid
    own_hidden = (own_silu * own_up).astype(jnp.bfloat16)
    own_out = jnp.einsum(
        "secf,efd->secd", own_hidden, down_full, preferred_element_type=jnp.float32
    )
    expert_out = own_out.reshape(1, fsdp_count, local_experts * capacity, width).astype(
        jnp.bfloat16
    )
    returned = lax.all_to_all(expert_out, "fsdp", split_axis=1, concat_axis=1, tiled=True).reshape(
        experts * capacity, width
    )
    routed = returned[slots].reshape(rows_piece, top_k, width).astype(jnp.float32)
    mixture = jnp.sum(gates[:, :, None] * routed, axis=1)
    output = (resid + mixture).astype(jnp.bfloat16)
    grad_float = out_grad.astype(jnp.float32)
    gate_grad = jnp.sum(routed * grad_float[:, None, :], axis=2)
    route_grad = (
        (gates[:, :, None] * grad_float[:, None, :])
        .astype(jnp.bfloat16)
        .reshape(route_count, width)
    )
    padded_grad = jnp.concatenate([route_grad, jnp.zeros((1, width), jnp.bfloat16)], 0)
    grad_buffer = padded_grad[sources].reshape(1, fsdp_count, local_experts * capacity, width)
    own_grads = send_rows(grad_buffer).reshape(fsdp_count, local_experts, capacity, width)
    own_hidden_grad = jnp.einsum(
        "secd,efd->secf", own_grads, down_full, preferred_element_type=jnp.float32
    )
    own_gate_low = (
        own_hidden_grad * own_up * own_sigmoid * (1.0 + own_gate * (1.0 - own_sigmoid))
    ).astype(jnp.bfloat16)
    own_up_low = (own_hidden_grad * own_silu).astype(jnp.bfloat16)
    down_term = jnp.einsum(
        "secf,secd->efd", own_hidden, own_grads, preferred_element_type=jnp.float32
    )
    gate_term = jnp.einsum(
        "secd,secf->edf", own_rows, own_gate_low, preferred_element_type=jnp.float32
    )
    up_term = jnp.einsum("secd,secf->edf", own_rows, own_up_low, preferred_element_type=jnp.float32)
    w_gate_grad, w_up_grad, w_down_grad = (
        lax.psum_scatter(
            gate_term.astype(jnp.bfloat16), "tp", scatter_dimension=2, tiled=True
        ).astype(jnp.float32),
        lax.psum_scatter(
            up_term.astype(jnp.bfloat16), "tp", scatter_dimension=2, tiled=True
        ).astype(jnp.float32),
        lax.psum_scatter(
            down_term.astype(jnp.bfloat16), "tp", scatter_dimension=1, tiled=True
        ).astype(jnp.float32),
    )
    own_back = jnp.einsum(
        "secf,edf->secd", own_gate_low, gate_full, preferred_element_type=jnp.float32
    )
    own_back = own_back + jnp.einsum(
        "secf,edf->secd", own_up_low, up_full, preferred_element_type=jnp.float32
    )
    expert_grad = own_back.reshape(1, fsdp_count, local_experts * capacity, width).astype(
        jnp.bfloat16
    )
    back_rows = lax.all_to_all(
        expert_grad, "fsdp", split_axis=1, concat_axis=1, tiled=True
    ).reshape(experts * capacity, width)
    act_two_grad = jnp.sum(
        back_rows[slots].reshape(rows_piece, top_k, width).astype(jnp.float32), axis=1
    )
    centered = gate_grad - jnp.sum(gates * gate_grad, axis=1, keepdims=True)
    chosen_grad = gates * centered
    logit_grad = jnp.einsum("tke,tk->te", picks, chosen_grad, precision=HIGHEST)
    router_float = router.astype(jnp.float32)
    act_two_grad = act_two_grad + lax.dot_general(
        logit_grad, router_float, (((1,), (1,)), ((), ())), precision=HIGHEST
    )
    router_part = lax.dot_general(
        act_two.astype(jnp.float32), logit_grad, (((0,), (0,)), ((), ())), precision=HIGHEST
    )
    resid_part, gain_two_part = norm_back(resid, inverse_two, moe_gain, act_two_grad)
    resid_grad = grad_float + resid_part
    branch_grad = lax.all_gather(resid_grad.astype(jnp.bfloat16), "tp", axis=0, tiled=True)
    attended_grad = (
        contract_last(branch_grad, full_output)
        .astype(jnp.bfloat16)
        .reshape(seq_len, local_heads, head_size)
    )
    w_output_part = contract_first(attended, branch_grad)
    query_parts = []
    key_grad = jnp.zeros((seq_len, local_heads, head_size), jnp.float32)
    value_grad = jnp.zeros((seq_len, local_heads, head_size), jnp.float32)
    for block_index, first_row in enumerate(range(0, seq_len, block_rows)):
        query_block = query
        scores = block_scores(query_block)
        softmax_rows = jnp.exp(scores - log_totals[block_index])
        prob_grad = jnp.einsum(
            "qhd,khd->hqk", attended_grad, value_rows, preferred_element_type=jnp.float32
        )
        inner = jnp.sum(softmax_rows * prob_grad, axis=-1, keepdims=True)
        score_grad = (softmax_rows * (prob_grad - inner) * score_scale).astype(jnp.bfloat16)
        query_parts.append(
            jnp.einsum("hqk,khd->qhd", score_grad, key_rows, preferred_element_type=jnp.float32)
        )
        key_grad = jnp.einsum(
            "hqk,qhd->khd", score_grad, query_block, preferred_element_type=jnp.float32
        )
        value_grad = jnp.einsum(
            "hqk,qhd->khd",
            softmax_rows.astype(jnp.bfloat16),
            attended_grad,
            preferred_element_type=jnp.float32,
        )
    query_low = query_parts[0].reshape(seq_len, -1).astype(jnp.bfloat16)
    key_low = key_grad.reshape(seq_len, -1).astype(jnp.bfloat16)
    value_low = value_grad.reshape(seq_len, -1).astype(jnp.bfloat16)
    w_query_part = contract_first(act_one, query_low)
    w_key_part = contract_first(act_one, key_low)
    w_value_part = contract_first(act_one, value_low)
    act_one_grad = (
        contract_last(query_low, full_query)
        + contract_last(key_low, full_key)
        + contract_last(value_low, full_value)
    )
    whole_part, gain_one_part = norm_back(whole_float, inverse_one, attn_gain, act_one_grad)

    def arrange(values):
        shaped = values.reshape((fsdp_count, tp_count, -1) + values.shape[1:])
        return jnp.swapaxes(shaped, 0, 1)

    input_part, gain_one_tp, gain_two_tp, router_tp = (
        lax.psum_scatter(
            whole_part.astype(jnp.bfloat16), "tp", scatter_dimension=0, tiled=True
        ).astype(jnp.float32),
        lax.psum_scatter(
            arrange(gain_one_part).astype(jnp.bfloat16), "tp", scatter_dimension=0, tiled=True
        ).astype(jnp.float32),
        lax.psum_scatter(
            arrange(gain_two_part).astype(jnp.bfloat16), "tp", scatter_dimension=0, tiled=True
        ).astype(jnp.float32),
        lax.psum_scatter(
            arrange(router_part).astype(jnp.bfloat16), "tp", scatter_dimension=0, tiled=True
        ).astype(jnp.float32),
    )
    input_grad = resid_grad + input_part
    query_sum, key_sum, value_sum, output_sum, gain_one_sum, gain_two_sum, router_sum = (
        lax.psum_scatter(
            w_query_part.astype(jnp.bfloat16), "fsdp", scatter_dimension=0, tiled=True
        ).astype(jnp.float32),
        lax.psum_scatter(
            w_key_part.astype(jnp.bfloat16), "fsdp", scatter_dimension=0, tiled=True
        ).astype(jnp.float32),
        lax.psum_scatter(
            w_value_part.astype(jnp.bfloat16), "fsdp", scatter_dimension=0, tiled=True
        ).astype(jnp.float32),
        lax.psum_scatter(
            w_output_part.astype(jnp.bfloat16), "fsdp", scatter_dimension=1, tiled=True
        ).astype(jnp.float32),
        lax.psum_scatter(
            gain_one_tp.astype(jnp.bfloat16), "fsdp", scatter_dimension=1, tiled=True
        ).astype(jnp.float32),
        lax.psum_scatter(
            gain_two_tp.astype(jnp.bfloat16), "fsdp", scatter_dimension=1, tiled=True
        ).astype(jnp.float32),
        lax.psum_scatter(
            router_tp.astype(jnp.bfloat16), "fsdp", scatter_dimension=1, tiled=True
        ).astype(jnp.float32),
    )
    return (
        output,
        input_grad,
        gain_one_sum.reshape(-1),
        query_sum,
        key_sum,
        value_sum,
        output_sum,
        gain_two_sum.reshape(-1),
        router_sum.reshape(-1, experts),
        w_gate_grad,
        w_up_grad,
        w_down_grad,
    )


def layer(*args):
    tokens = args[0].shape[0] * lax.axis_size("fsdp") * lax.axis_size("tp")
    held = 6 * tokens * (args[0].shape[1] + LANES) * 2
    even = lax.axis_size("tp") == 4 and lax.axis_size("fsdp") % 2 == 0
    experts = args[11].shape[0] * lax.axis_size("fsdp")
    narrow = lax.axis_size("tp") * experts <= LANES and args[1].shape[1] // (lax.axis_size("tp") * lax.axis_size("fsdp")) <= args[0].shape[0]
    if held <= HBM_BUDGET and even and narrow:
        return dense_layer(*args)
    return per_device(*args)


def solution(mesh):
    return jax.shard_map(
        layer,
        mesh=mesh,
        in_specs=(
            P(("fsdp", "tp"), None),
            P(("fsdp", "tp"), None),
            P("fsdp"),
            P(("fsdp", "tp"), None),
            P(),
            P("fsdp", "tp"),
            P("fsdp", "tp"),
            P("fsdp", "tp"),
            P("tp", "fsdp"),
            P(),
            P(),
            P("fsdp", None, "tp"),
            P("fsdp", None, "tp"),
            P("fsdp", "tp", None),
        ),
        out_specs=(
            P(("fsdp", "tp"), None),
            P(("fsdp", "tp"), None),
            P(("fsdp", "tp")),
            P("fsdp", "tp"),
            P("fsdp", "tp"),
            P("fsdp", "tp"),
            P("tp", "fsdp"),
            P(("fsdp", "tp")),
            P(("fsdp", "tp"), None),
            P("fsdp", None, "tp"),
            P("fsdp", None, "tp"),
            P("fsdp", "tp", None),
        ),
        check_vma=False,
    )
```

```python
import functools
import math

import jax
import jax.numpy as jnp
from jax import lax
from jax.experimental import pallas as pl
from jax.experimental.pallas import tpu as pltpu
from jax.sharding import PartitionSpec as P

HEAD = 128
LANES = 128
EPSILON = 1e-05
HIGHEST = lax.Precision.HIGHEST
MESH = pl.DeviceIdType.MESH
ANY = pl.BlockSpec(memory_space=pl.ANY)
VMEM = pl.BlockSpec(memory_space=pltpu.VMEM)
MIB = 1 << 20
HBM_BUDGET = 300 * MIB
BF16 = jnp.bfloat16
F32 = jnp.float32
CONTRACT_FIRST = (((0,), (0,)), ((), ()))
CONTRACT_LAST = (((1,), (1,)), ((), ()))


class Place:
    def __init__(self, depth):
        self.depth = depth
        f, t = lax.axis_index("fsdp"), lax.axis_index("tp")
        self.f, self.t = f, t
        self.z, self.x = lax.div(f, 2), lax.rem(f, 2)
        self.y, self.c = lax.div(t, 2), lax.rem(t, 2)
        self.to = {
            "x": (self.z * 2 + 1 - self.x, t),
            "y": (f, (1 - self.y) * 2 + self.c),
            "c": (f, self.y * 2 + 1 - self.c),
            "up": (f + 2, t),
            "down": (f - 2, t),
        }
        self.can_up = self.z < depth - 1
        self.can_down = self.z > 0
        offs = [0]
        for step in range(1, depth):
            offs += [-step, step]
        self.offs = offs
        tables = [sorted(range(depth), key=lambda zz: (abs(zz - z), zz)) for z in range(depth)]
        self.near = [
            sum(jnp.where(self.z == z, tables[z][i], 0) for z in range(depth)) for i in range(depth)
        ]
        self.far = self.near[::-1]
        self.tables = tables

    def nearest(self, i):
        pairs = [(z, k) for z in range(self.depth) for k in range(self.depth)]
        return sum(
            jnp.where((self.z == z) & (i == k), self.tables[z][k], 0) for z, k in pairs
        )

    def valid(self, off):
        if off == 0:
            return None
        return self.z + off >= 0 if off < 0 else self.z + off < self.depth


def when(cond, body):
    if cond is None:
        body()
    else:
        pl.when(cond)(body)


def both(first, second):
    if first is None:
        return second
    if second is None:
        return first
    return jnp.logical_and(first, second)


class Net:
    def __init__(self, place, send_sems, recv_sems, local_sems):
        self.place = place
        self.send_sems, self.recv_sems, self.local_sems = send_sems, recv_sems, local_sems
        self.keys, self.used, self.sent, self.locals_used = {}, 0, [], 0

    def slot(self, key):
        if len(key) == 4 and key[1] == "at":
            base = self.keys.setdefault(key[0], self.used)
            if base == self.used:
                self.used += key[2]
            return base + key[3]
        base = self.keys.setdefault(key, self.used)
        if base == self.used:
            self.used += 1
        return base

    def put(self, src, dst, to, key, cond=None, guard=None):
        copy = pltpu.make_async_remote_copy(
            src_ref=src,
            dst_ref=dst,
            send_sem=self.send_sems.at[len(self.sent)],
            recv_sem=self.recv_sems.at[self.slot(key)],
            device_id=self.place.to[to],
            device_id_type=MESH,
        )
        self.sent.append((both(cond, guard), copy))
        when(cond, copy.start)

    def got(self, dst, key):
        pltpu.make_async_remote_copy(
            src_ref=dst,
            dst_ref=dst,
            send_sem=self.send_sems.at[0],
            recv_sem=self.recv_sems.at[self.slot(key)],
            device_id=self.place.to["c"],
            device_id_type=MESH,
        ).wait_recv()

    def local(self, src, dst):
        copy = pltpu.make_async_copy(src, dst, self.local_sems.at[self.locals_used])
        self.locals_used += 1
        copy.start()
        return copy

    def finish(self):
        for cond, copy in self.sent:
            when(cond, copy.wait_send)


def greet(place, links):
    barrier = pltpu.get_barrier_semaphore()
    count = 0
    for link in links:
        if link == "z":
            for name, cond in (("up", place.can_up), ("down", place.can_down)):
                target = place.to[name]
                pl.when(cond)(
                    lambda target=target: pl.semaphore_signal(
                        barrier, inc=1, device_id=target, device_id_type=MESH
                    )
                )
                count = count + cond.astype(jnp.int32)
        else:
            pl.semaphore_signal(barrier, inc=1, device_id=place.to[link], device_id_type=MESH)
            count = count + 1
    pl.semaphore_wait(barrier, count)


SENDS, RECVS, LOCALS = 160, 160, 24


def sems():
    return [
        pltpu.SemaphoreType.DMA((SENDS,)),
        pltpu.SemaphoreType.DMA((RECVS,)),
        pltpu.SemaphoreType.DMA((LOCALS,)),
    ]


def add_rows(dst, src, rows, step=16):
    def body(i, carry):
        at = pl.ds(pl.multiple_of(i * step, step), step)
        dst[at, :] = (dst[at, :].astype(F32) + src[at, :].astype(F32)).astype(dst.dtype)
        return carry

    lax.fori_loop(0, rows // step, body, 0)


def comm_params(ident, mib=None):
    limit = None if mib is None else mib * MIB
    return pltpu.CompilerParams(collective_id=ident, has_side_effects=True, vmem_limit_bytes=limit)


def spread_zx(net, name, block, own):
    p = net.place
    offs = p.offs

    def step(i):
        if i >= len(offs):
            return
        off = offs[i]
        zz = p.z + off
        valid = p.valid(off)
        ref = block(zz, p.x)

        def body():
            if off:
                net.got(ref, (name, "z", off))

        when(valid, body)
        src = ref if off else own
        if off <= 0:
            net.put(src, ref, "up", (name, "z", off - 1), both(valid, p.can_up))
        if off >= 0:
            net.put(src, ref, "down", (name, "z", off + 1), both(valid, p.can_down))
        net.put(src, ref, "x", (name, "x", off), valid)

    def finish():
        for off in offs:
            ref = block(p.z + off, 1 - p.x)
            when(p.valid(off), lambda: net.got(ref, (name, "x", off)))

    return step, finish


def spread_xz(net, name, block, pair, own, placed):
    p = net.place
    offs = p.offs

    def begin():
        net.put(own, block(p.z, p.x), "x", (name, "x"))

    def step(i):
        off = offs[i]
        if off == 0:
            placed.wait()
            net.got(block(p.z, 1 - p.x), (name, "x"))
        valid = p.valid(off)
        ref = pair(p.z + off)
        if off:
            when(valid, lambda: net.got(ref, (name, "z", off)))
        if off <= 0:
            net.put(ref, ref, "up", (name, "z", off - 1), both(valid, p.can_up))
        if off >= 0:
            net.put(ref, ref, "down", (name, "z", off + 1), both(valid, p.can_down))

    return begin, step


SITES = {
    "x1": ("x", 0, 0, 0),
    "y1": ("y", 0, 0, 1),
    "x3": ("x", 0, 0, 1),
    "y3": ("y", 0, 0, 0),
    "y2": ("y", 1, 0, 0),
    "x2": ("x", 0, 1, 1),
    "c0": ("c", 0, 0, None),
    "cx": ("c", 1, 0, None),
    "cy": ("c", 0, 1, None),
    "cxy": ("c", 1, 1, None),
}
NAMES = list(SITES)


class Plane:
    def __init__(self, place, everyone, own, sends, recvs):
        self.place, self.everyone, self.own = place, everyone, own
        self.sends, self.recvs = sends, recvs
        self.half = own.shape[0] // 2

    def ref(self, zz, dx, dy, dc, part):
        p = self.place
        x, y, c = p.x + dx - 2 * p.x * dx, p.y + dy - 2 * p.y * dy, p.c + dc - 2 * p.c * dc
        ref = self.everyone.at[((zz * 2 + x) * 2 + y) * 2 + c]
        return ref if part is None else ref.at[pl.ds(part * self.half, self.half)]

    def copy(self, site, zz, src=None):
        link, dx, dy, part = SITES[site]
        dst = self.ref(zz, dx, dy, 0, part)
        at = NAMES.index(site) * self.place.depth + zz
        return pltpu.make_async_remote_copy(
            src_ref=dst if src is None else src,
            dst_ref=dst,
            send_sem=self.sends.at[at],
            recv_sem=self.recvs.at[at],
            device_id=self.place.to[link],
            device_id_type=MESH,
        )

    def take(self, site, zz):
        link, dx, dy, part = SITES[site]
        dx, dy = dx ^ (link == "x"), dy ^ (link == "y")
        ref = self.ref(zz, dx, dy, int(link == "c"), part)
        at = NAMES.index(site) * self.place.depth + zz
        pltpu.make_async_remote_copy(
            src_ref=ref,
            dst_ref=ref,
            send_sem=self.sends.at[at],
            recv_sem=self.recvs.at[at],
            device_id=self.place.to[link],
            device_id_type=MESH,
        ).wait_recv()

    def z_copy(self, zz, up):
        p = self.place
        ref = self.ref(zz, 0, 0, 0, None)
        base = len(NAMES) * p.depth
        return pltpu.make_async_remote_copy(
            src_ref=ref,
            dst_ref=ref,
            send_sem=self.sends.at[base + (0 if up else p.depth) + zz],
            recv_sem=self.recvs.at[base + zz],
            device_id=p.to["up" if up else "down"],
            device_id_type=MESH,
        )

    def each_z(self, zz, act):
        p = self.place
        pl.when((zz <= p.z) & p.can_up)(lambda: act(True))
        pl.when((zz >= p.z) & p.can_down)(lambda: act(False))

    def own_along_z(self):
        p = self.place
        base = len(NAMES) * p.depth

        def start(up):
            pltpu.make_async_remote_copy(
                src_ref=self.own,
                dst_ref=self.ref(p.z, 0, 0, 0, None),
                send_sem=self.sends.at[base + (0 if up else p.depth) + p.z],
                recv_sem=self.recvs.at[base + p.z],
                device_id=p.to["up" if up else "down"],
                device_id_type=MESH,
            ).start()

        self.each_z(p.z, start)

    def take_z(self, zz):
        ref = self.ref(zz, 0, 0, 0, None)
        at = len(NAMES) * self.place.depth + zz
        pltpu.make_async_remote_copy(
            src_ref=ref,
            dst_ref=ref,
            send_sem=self.sends.at[at],
            recv_sem=self.recvs.at[at],
            device_id=self.place.to["c"],
            device_id_type=MESH,
        ).wait_recv()

    def along_z(self, zz):
        self.take_z(zz)
        self.each_z(zz, lambda up: self.z_copy(zz, up).start())

    def first(self, zz, mine=False):
        whole, part_a, part_b = None, None, None
        if mine:
            whole = self.own
            part_a, part_b = whole.at[pl.ds(0, self.half)], whole.at[pl.ds(self.half, self.half)]
        self.copy("x1", zz, part_a).start()
        self.copy("y1", zz, part_b).start()
        self.copy("x3", zz, part_b).start()
        self.copy("y3", zz, part_a).start()
        self.copy("c0", zz, whole).start()

    def second(self, zz):
        self.take("x1", zz)
        self.copy("y2", zz).start()
        self.take("y1", zz)
        self.copy("x2", zz).start()

    def third_y(self, zz):
        self.take("y3", zz)
        self.copy("cy", zz).start()

    def third_x(self, zz):
        self.take("x3", zz)
        self.copy("cx", zz).start()
        self.take("x2", zz)
        self.take("y2", zz)
        self.copy("cxy", zz).start()

    def arrived_y(self, zz):
        self.take("c0", zz)
        self.take("cy", zz)

    def arrived_x(self, zz):
        self.take("cx", zz)
        self.take("cxy", zz)

    def finish(self, zs, z_zs):
        for zz in zs:
            for site in NAMES:
                self.copy(site, zz).wait_send()
        for zz in z_zs:
            self.each_z(zz, lambda up, zz=zz: self.z_copy(zz, up).wait_send())


def plane_sems(depth):
    return [pltpu.SemaphoreType.DMA(((len(NAMES) + 2) * depth,))] * 2


def same_document(seg_row):
    row = seg_row[...]
    column = jnp.transpose(jnp.broadcast_to(row, (LANES, row.shape[1])))[:, 0:1]
    return column == row


def first_kernel(
    depth, wq, wk, wv, wo, inp, og, gain, seg_row,
    qkv_hbm, o_hbm, rows_hbm, act_hbm, proj_hbm, att_hbm, part_hbm, grad_all,
    weights, full_o, rows, act, proj, att, part, og_send, og_recv, send, recv, local,
):
    p = Place(depth)
    net = Net(p, send, recv, local)
    grads = Plane(p, grad_all, og, og_send, og_recv)
    w_rows, w_cols = wq.shape
    o_cols = wo.shape[1]
    count, width = inp.shape
    fsdp, heads = 2 * depth, w_cols // HEAD

    def column(f):
        return full_o.at[:, pl.ds(pl.multiple_of(f * o_cols, LANES), o_cols)]

    def columns(z):
        return full_o.at[:, pl.ds(pl.multiple_of(z * (2 * o_cols), LANES), 2 * o_cols)]

    def slab(i):
        return lambda z, x: weights.at[i, z * 2 + x]

    greet(p, ("x", "y", "c", "z"))
    mine = rows.at[p.t]
    net.put(inp, mine, "y", ("rows", "y"))
    net.put(inp, mine, "c", ("rows", "c0"))
    placed = net.local(wo, column(p.f))
    owns = [net.local(inp, mine)]
    owns += [net.local(w, weights.at[i, p.f]) for i, w in enumerate((wq, wk, wv))]
    kept = net.local(og, grads.ref(p.z, 0, 0, 0, None))
    flows = [spread_zx(net, f"w{i}", slab(i), w) for i, w in enumerate((wq, wk, wv))]
    o_begin, o_step = spread_xz(net, "o", lambda z, x: column(z * 2 + x), columns, wo, placed)
    steps = len(p.offs)

    def norm():
        other = rows.at[(1 - p.y) * 2 + p.c]
        net.got(other, ("rows", "y"))
        net.put(other, other, "c", ("rows", "c1"))
        net.got(rows.at[p.y * 2 + 1 - p.c], ("rows", "c0"))
        net.got(rows.at[(1 - p.y) * 2 + 1 - p.c], ("rows", "c1"))
        owns[0].wait()
        for t in range(rows.shape[0]):

            def body(i, carry):
                at = pl.ds(pl.multiple_of(i * 16, 16), 16)
                values = rows[t, at, :].astype(F32)
                inverse = lax.rsqrt(jnp.mean(values * values, axis=-1, keepdims=True) + EPSILON)
                to = pl.ds(pl.multiple_of(t * count + i * 16, 16), 16)
                act[to, :] = (values * inverse * gain[...]).astype(BF16)
                return carry

            lax.fori_loop(0, count // 16, body, 0)

    saves = []

    def rows_in():
        norm()
        saves.append(net.local(rows, rows_hbm))
        saves.append(net.local(act, act_hbm))

    def project_with(i):
        owns[1 + i].wait()
        flows[i][1]()
        saves.append(net.local(weights.at[i], qkv_hbm.at[i]))
        wide = 256

        def project(k, carry):
            at = pl.ds(pl.multiple_of(k * wide, wide), wide)
            to = pl.ds(pl.multiple_of(i * w_cols + k * wide, wide), wide)
            matrix = weights[i, :, :, at].reshape(width, wide)
            proj[:, to] = jnp.dot(act[...], matrix, preferred_element_type=F32).astype(BF16)
            return carry

        lax.fori_loop(0, w_cols // wide, project, 0)

    scale = 1.0 / math.sqrt(HEAD)

    def head(h):
        if h == 0:
            saves.append(net.local(proj, proj_hbm))
        same = same_document(seg_row)
        query, keys, values = [
            proj[:, i * w_cols + h * HEAD : i * w_cols + (h + 1) * HEAD] for i in range(3)
        ]
        scores = lax.dot_general(query, keys, CONTRACT_LAST, preferred_element_type=F32) * scale
        scores = jnp.where(same, scores, -1e30)
        expo = jnp.exp(scores - jnp.max(scores, axis=-1, keepdims=True))
        probs = (expo / jnp.sum(expo, axis=-1, keepdims=True)).astype(BF16)
        att[:, h * HEAD : (h + 1) * HEAD] = jnp.dot(
            probs, values, preferred_element_type=F32
        ).astype(BF16)

    def out_rows(k, carry):
        at = pl.ds(pl.multiple_of(k * 256, 256), 256)
        part[:, at] = jnp.dot(att[...], full_o[:, at], preferred_element_type=F32).astype(BF16)
        return carry

    def branch():
        saves.append(net.local(full_o, o_hbm))
        saves.append(net.local(att, att_hbm))
        lax.fori_loop(0, width // 256, out_rows, 0)
        saves.append(net.local(part, part_hbm))

    (q_step, _), (k_step, _), (v_step, _) = flows

    def g_first():
        grads.first(p.z, True)

    if depth == 4 and heads == 4:
        perform(
            (o_begin,), (v_step, 0), (q_step, 0), (k_step, 0), (q_step, 1), (q_step, 2),
            (q_step, 3), (v_step, 1), (k_step, 1), (k_step, 2), (q_step, 4), (k_step, 3),
            (v_step, 2), (q_step, 5), (rows_in,), (v_step, 3), (q_step, 6), (k_step, 4),
            (o_step, 0), (v_step, 4), (k_step, 5), (o_step, 1), (v_step, 5), (o_step, 2),
            (k_step, 6), (project_with, 0), (v_step, 6), (project_with, 1), (g_first,),
            (o_step, 3), (o_step, 4), (project_with, 2), (head, 0), (grads.second, p.z),
            (head, 1), (head, 2), (head, 3), (o_step, 5), (o_step, 6), (branch,),
            (grads.third_y, p.z), (grads.third_x, p.z),
            (grads.arrived_y, p.z), (grads.arrived_x, p.z),
        )
    else:
        perform((o_begin,), (g_first,), *every(steps, q_step, k_step, v_step, o_step), (rows_in,))
        perform((grads.second, p.z), (grads.third_y, p.z), (grads.third_x, p.z))
        perform(*every(3, project_with))
        perform(*every(heads, head), (branch,))
        perform((grads.arrived_y, p.z), (grads.arrived_x, p.z))
    kept.wait()
    for copy in saves:
        copy.wait()
    grads.finish([p.z], [])
    net.finish()


def first_gather(depth, w_query, w_key, w_value, w_output, inputs, out_grad, gain, segments, tp):
    fsdp = 2 * depth
    w_rows, w_cols = w_query.shape
    o_rows, o_cols = w_output.shape
    rows, width = inputs.shape
    seq = tp * rows
    shape = jax.ShapeDtypeStruct
    return pl.pallas_call(
        functools.partial(first_kernel, depth),
        out_shape=[
            shape((3, fsdp, w_rows, w_cols), BF16),
            shape((o_rows, fsdp * o_cols), BF16),
            shape((tp, rows, width), BF16),
            shape((seq, width), BF16),
            shape((seq, 3 * w_cols), BF16),
            shape((seq, w_cols), BF16),
            shape((seq, width), BF16),
            shape((fsdp * tp, rows, width), BF16),
        ],
        in_specs=[VMEM] * 8,
        out_specs=[ANY] * 8,
        scratch_shapes=[
            pltpu.VMEM((3, fsdp, w_rows, w_cols), BF16),
            pltpu.VMEM((o_rows, fsdp * o_cols), BF16),
            pltpu.VMEM((tp, rows, width), BF16),
            pltpu.VMEM((seq, width), BF16),
            pltpu.VMEM((seq, 3 * w_cols), BF16),
            pltpu.VMEM((seq, w_cols), BF16),
            pltpu.VMEM((seq, width), BF16),
        ]
        + plane_sems(depth)
        + sems(),
        compiler_params=comm_params(1, 60),
        name="first_gather",
    )(
        w_query, w_key, w_value, w_output, inputs, out_grad, gain[None, :], segments[None, :],
    )


def moe_kernel(
    depth, capacity, experts, blocks,
    part, inp, og, gain, router, mask, rank, gate_hbm, up_hbm, down_hbm, grad_in_hbm,
    resid, gates_out, act_all, grad_all, out_hbm, back_hbm, x_hbm, g_hbm, hid_hbm, gl_hbm, ul_hbm,
    acc, rc, ry, own, w_gate, w_up, w_down, act_in, grad_in, x_rows, g_rows, tails, hid, gl, ul,
    keep, out, back,
    act_send, act_recv, og_send, og_recv, send, recv, local, load_sems, save_sems,
):
    p = Place(depth)
    net = Net(p, send, recv, local)
    rows, width = inp.shape
    local_experts = w_gate.shape[0]
    weights = [
        net.local(src, dst)
        for src, dst in ((gate_hbm, w_gate), (up_hbm, w_up), (down_hbm, w_down))
    ]
    part_in = net.local(part.at[:, p.c], acc)
    acts = Plane(p, act_all, own, act_send, act_recv)
    grads = Plane(p, grad_all, og, og_send, og_recv)
    greet(p, ("x", "y", "c", "z"))

    net.put(part.at[:, 1 - p.c], rc, "c", ("rc",))
    far = 1 - p.y

    def along_y():
        part_in.wait()
        net.got(rc, ("rc",))
        add_rows(acc.at[far], rc.at[far], rows)
        net.put(acc.at[far], ry, "y", ("ry",))
        add_rows(acc.at[p.y], rc.at[p.y], rows)

    kept = []

    def norm():
        net.got(ry, ("ry",))

        def body(i, carry):
            at = pl.ds(pl.multiple_of(i * 16, 16), 16)
            branch = acc[p.y, at, :].astype(F32) + ry[at, :].astype(F32)
            values = inp[at, :].astype(F32) + branch
            resid[at, :] = values
            inverse = lax.rsqrt(jnp.mean(values * values, axis=-1, keepdims=True) + EPSILON)
            own[at, pl.ds(0, width)] = (values * inverse * gain[...]).astype(BF16)
            return carry

        lax.fori_loop(0, rows // 16, body, 0)
        twice = jnp.concatenate(
            [router[...]] * 2 + [jnp.zeros((LANES - 2 * experts, width), BF16)], axis=0
        )
        logits = lax.dot_general(
            own[:, pl.ds(0, width)], twice, CONTRACT_LAST, preferred_element_type=F32
        )
        chosen = mask[...] > 0.0
        peak = jnp.max(jnp.where(chosen, logits, -1e30), axis=1, keepdims=True)
        expo = jnp.where(chosen, jnp.exp(jnp.minimum(logits - peak, 0.0)), 0.0)
        lane = lax.broadcasted_iota(jnp.int32, expo.shape, 1)
        total = jnp.sum(jnp.where(lane < experts, expo, 0.0), axis=1, keepdims=True)
        gates = expo / total
        gates_out[...] = gates
        high = gates.astype(BF16).astype(F32)
        tail = jnp.where(
            lane < experts, high, jnp.where(lane < 2 * experts, gates - high, rank[...])
        )
        own[:, pl.ds(width, LANES)] = tail.astype(BF16)
        kept.append(net.local(own, acts.ref(p.z, 0, 0, 0, None)))

    first_expert = p.f * local_experts
    tp_lane = p.t * experts + first_expert
    pick_row = lax.broadcasted_iota(jnp.int32, (8, LANES), 0)
    pick_lane = lax.broadcasted_iota(jnp.int32, (8, LANES), 1)
    pick = (
        (pick_lane == 2 * experts + first_expert + pick_row) & (pick_row < local_experts)
    ).astype(BF16)
    places = lax.broadcasted_iota(jnp.int32, (capacity, rows), 0).astype(F32)
    slots = blocks * capacity

    def blocks_of(zz, j):
        return (zz * 2 + (1 - p.x if j else p.x)) * blocks

    def loads(zz, j):
        at = pl.ds(blocks_of(zz, j), blocks)
        return [
            pltpu.make_async_copy(act_all.at[at], act_in.at[j], load_sems.at[j, 0]),
            pltpu.make_async_copy(grad_all.at[at], grad_in.at[j], load_sems.at[j, 1]),
        ]

    def save(zz, j, k):
        if k < 5:
            where = pl.ds(pl.multiple_of(blocks_of(zz, j) * capacity, 16), slots)
            src = (x_rows, g_rows, hid, gl, ul)[k]
            dst = (x_hbm, g_hbm, hid_hbm, gl_hbm, ul_hbm)[k].at[:, where]
        else:
            src = (out, back)[k - 5]
            dst = (out_hbm, back_hbm)[k - 5].at[pl.ds(blocks_of(zz, j), blocks)]
        return pltpu.make_async_copy(src, dst, save_sems.at[k])

    def one_hot(j, b):
        tail = act_in[j, b, :, pl.ds(width, LANES)]
        ranks = lax.dot_general(pick, tail, CONTRACT_LAST, preferred_element_type=F32)
        return jnp.concatenate(
            [
                (jnp.broadcast_to(ranks[e : e + 1, :], (capacity, rows)) == places).astype(BF16)
                for e in range(local_experts)
            ],
            axis=0,
        )

    def work(zz, j, started, serve):
        for copy in loads(zz, j):
            copy.wait()

        def settle(ks):
            def body():
                for k in ks:
                    save(zz, j, k).wait()

            when(started, body)

        settle((0, 1))

        def gather(pair, carry):
            b = pair * 2
            blank = jnp.zeros((local_experts * capacity, rows), BF16)
            hot = jnp.concatenate(
                [
                    jnp.concatenate([one_hot(j, b), blank], axis=1),
                    jnp.concatenate([blank, one_hot(j, b + 1)], axis=1),
                ],
                axis=0,
            )
            acts_two = act_in[j, pl.ds(b, 2)].reshape(2 * rows, width + LANES)
            grads_two = grad_in[j, pl.ds(b, 2)].reshape(2 * rows, width)
            picked = jnp.dot(hot, acts_two, preferred_element_type=F32)
            pulled = jnp.dot(hot, grads_two, preferred_element_type=F32).astype(BF16)
            for k in range(2):
                at = pl.ds(pl.multiple_of((b + k) * capacity, 16), capacity)
                for e in range(local_experts):
                    first = (k * local_experts + e) * capacity
                    piece = picked[first : first + capacity]
                    x_rows[e, at, :] = piece[:, :width].astype(BF16)
                    tails[e, at, :] = piece[:, width:]
                    g_rows[e, at, :] = pulled[first : first + capacity]
            return carry

        lax.fori_loop(0, blocks // 2, gather, 0)
        for k in (0, 1):
            save(zz, j, k).start()
        serve(0)
        settle((2, 3, 4))
        for e in range(local_experts):
            tail_lane = lax.broadcasted_iota(jnp.int32, (slots, LANES), 1)
            mine = (tail_lane == first_expert + e) | (tail_lane == experts + first_expert + e)
            gates_of = jnp.sum(jnp.where(mine, tails[e], 0.0), axis=1, keepdims=True)
            pre = jnp.dot(x_rows[e], w_gate[e], preferred_element_type=F32)
            up = jnp.dot(x_rows[e], w_up[e], preferred_element_type=F32)
            raw = lax.dot_general(g_rows[e], w_down[e], CONTRACT_LAST, preferred_element_type=F32)
            sig = jax.nn.sigmoid(pre)
            silu = pre * sig
            hidden = silu * up
            gate_grad = jnp.sum(hidden * raw, axis=1, keepdims=True)
            scaled = raw * gates_of
            hid_low = (hidden * gates_of).astype(BF16)
            gate_low = (scaled * up * sig * (1.0 + pre * (1.0 - sig))).astype(BF16)
            up_low = (scaled * silu).astype(BF16)
            hid[e] = hid_low
            gl[e] = gate_low
            ul[e] = up_low
            o_rows = jnp.dot(hid_low, w_down[e], preferred_element_type=F32).astype(BF16)
            r_rows = (
                lax.dot_general(gate_low, w_gate[e], CONTRACT_LAST, preferred_element_type=F32)
                + lax.dot_general(up_low, w_up[e], CONTRACT_LAST, preferred_element_type=F32)
            ).astype(BF16)
            r_tail = jnp.where(tail_lane == tp_lane + e, gate_grad, 0.0).astype(BF16)
            for b in range(blocks):
                at = slice(b * capacity, (b + 1) * capacity)
                to = slice(e * capacity, (e + 1) * capacity)
                keep[b, to, pl.ds(0, width)] = o_rows[at]
                keep[b, to, pl.ds(width, width)] = r_rows[at]
                keep[b, to, pl.ds(2 * width, LANES)] = r_tail[at]
            serve(1 + e)
        for k in (2, 3, 4):
            save(zz, j, k).start()
        settle((5, 6))

        def combine(b, carry):
            hot = one_hot(j, b)
            found = lax.dot_general(hot, keep[b], CONTRACT_FIRST, preferred_element_type=F32)
            out[b] = found[:, :width].astype(BF16)
            back[b] = found[:, width:].astype(BF16)
            return carry

        lax.fori_loop(0, blocks, combine, 0)
        for k in (5, 6):
            save(zz, j, k).start()
        serve(5)

    def load(i, j):
        if i == j == 0:
            kept[0].wait()
            for copy in weights:
                copy.wait()
        for copy in loads(p.near[i], j):
            copy.start()

    near = p.near
    g1, g2, g3y, g3x = grads.first, grads.second, grads.third_y, grads.third_x
    a1, a2, a3y, a3x = acts.first, acts.second, acts.third_y, acts.third_x
    if depth == 4:
        perform(
            (grads.own_along_z,), (along_y,), (grads.along_z, near[1]), (g1, near[1]), (norm,),
            (acts.own_along_z,), (a1, p.z, True), (a2, p.z), (acts.along_z, near[1]), (a3y, p.z),
            (a1, near[1]), (acts.arrived_y, p.z), (load, 0, 0), (g2, near[1]),
            (grads.along_z, near[2]), (g1, near[2]),
        )
        service = {
            (0, 0, 1): [(a3x, p.z)],
            (0, 0, 3): [(acts.arrived_x, p.z), (load, 0, 1)],
            (0, 0, 4): [(acts.along_z, near[2])],
            (0, 0, 5): [(a2, near[1])],
            (0, 1, 0): [(a1, near[2]), (g3y, near[1])],
            (0, 1, 2): [(a3y, near[1])],
            (0, 1, 3): [
                (acts.arrived_y, near[1]), (grads.along_z, near[3]), (grads.arrived_y, near[1]),
                (load, 1, 0),
            ],
            (1, 0, 0): [(g2, near[2])],
            (1, 0, 1): [(g3x, near[1]), (g3y, near[2])],
            (1, 0, 2): [(g1, near[3])],
            (1, 0, 3): [(a3x, near[1])],
            (1, 0, 4): [
                (acts.along_z, near[3]), (a2, near[2]), (a3y, near[2]), (acts.arrived_x, near[1]),
                (grads.arrived_x, near[1]), (load, 1, 1),
            ],
            (1, 0, 5): [(g3x, near[2])],
            (1, 1, 3): [(grads.arrived_y, near[2]), (acts.arrived_y, near[2]), (load, 2, 0)],
            (1, 1, 4): [(a1, near[3])],
            (2, 0, 0): [(a3x, near[2])],
            (2, 0, 3): [(g2, near[3]), (grads.arrived_x, near[2])],
            (2, 0, 4): [(g3y, near[3]), (a2, near[3]), (acts.arrived_x, near[2]), (load, 2, 1)],
            (2, 0, 5): [(a3y, near[3])],
            (2, 1, 1): [(acts.arrived_y, near[3]), (grads.arrived_y, near[3]), (load, 3, 0)],
            (3, 0, 0): [(a3x, near[3])],
            (3, 0, 1): [(g3x, near[3])],
            (3, 0, 4): [(grads.arrived_x, near[3]), (acts.arrived_x, near[3]), (load, 3, 1)],
        }
    else:
        perform((along_y,), (norm,), (acts.own_along_z,), (grads.own_along_z,))
        for i, zz in enumerate(near):
            if i:
                perform((acts.along_z, zz), (grads.along_z, zz), (g1, zz), (g2, zz))
                perform((g3y, zz), (g3x, zz), (grads.arrived_y, zz), (grads.arrived_x, zz))
            perform((a1, zz, i == 0), (a2, zz), (a3y, zz), (a3x, zz))
            perform((acts.arrived_y, zz), (acts.arrived_x, zz))
        load(0, 0)
        service = {(g, 0, 0): [(load, g, 1)] for g in range(depth)}
        service.update({(g, 1, 4): [(load, g + 1, 0)] for g in range(depth - 1)})

    def group(g, carry):
        zz = p.nearest(g)

        def serve(j, k):
            for (at, half, place), steps in service.items():
                if (half, place) == (j, k):
                    pl.when(g == at)(functools.partial(perform, *steps))

        work(zz, 0, g > 0, functools.partial(serve, 0))
        work(zz, 1, None, functools.partial(serve, 1))
        return carry

    lax.fori_loop(0, depth, group, 0)
    for k in range(7):
        save(0, 1, k).wait()
    acts.finish(range(depth), range(depth))
    grads.finish(near[1:], near)
    net.finish()


def run_moe(
    depth, capacity, experts, part, inputs, out_grad, gain, router, mask, rank, w_gate, w_up, w_down,
    grad_all,
):
    tp, rows, width = part.shape
    wide = width + LANES
    count = 2 * depth * tp
    local_experts, _, hidden = w_gate.shape
    blocks = tp
    slots = blocks * capacity
    total = count * capacity
    shape = jax.ShapeDtypeStruct
    kept = [shape((local_experts, total, width), BF16)] * 2
    kept += [shape((local_experts, total, hidden), BF16)] * 3
    return pl.pallas_call(
        functools.partial(moe_kernel, depth, capacity, experts, blocks),
        out_shape=[
            shape((rows, width), F32),
            shape((rows, LANES), F32),
            shape((count, rows, wide), BF16),
            shape((count, rows, width), BF16),
            shape((count, rows, width), BF16),
            shape((count, rows, wide), BF16),
        ]
        + kept,
        in_specs=[ANY] + [VMEM] * 6 + [ANY] * 4,
        out_specs=[VMEM] * 2 + [ANY] * 9,
        input_output_aliases={10: 3},
        scratch_shapes=[
            pltpu.VMEM((2, rows, width), BF16),
            pltpu.VMEM((2, rows, width), BF16),
            pltpu.VMEM((rows, width), BF16),
            pltpu.VMEM((rows, wide), BF16),
            pltpu.VMEM(w_gate.shape, BF16),
            pltpu.VMEM(w_up.shape, BF16),
            pltpu.VMEM(w_down.shape, BF16),
            pltpu.VMEM((2, blocks, rows, wide), BF16),
            pltpu.VMEM((2, blocks, rows, width), BF16),
            pltpu.VMEM((local_experts, slots, width), BF16),
            pltpu.VMEM((local_experts, slots, width), BF16),
            pltpu.VMEM((local_experts, slots, LANES), F32),
            pltpu.VMEM((local_experts, slots, hidden), BF16),
            pltpu.VMEM((local_experts, slots, hidden), BF16),
            pltpu.VMEM((local_experts, slots, hidden), BF16),
            pltpu.VMEM((blocks, local_experts * capacity, width + wide), BF16),
            pltpu.VMEM((blocks, rows, width), BF16),
            pltpu.VMEM((blocks, rows, wide), BF16),
        ]
        + plane_sems(depth) * 2
        + sems()
        + [pltpu.SemaphoreType.DMA((2, 2)), pltpu.SemaphoreType.DMA((7,))],
        compiler_params=comm_params(2, 60),
        name="moe",
    )(
        part.reshape(tp // 2, 2, rows, width), inputs, out_grad, gain[None, :], router, mask, rank,
        w_gate, w_up, w_down, grad_all,
    )


def chain_z(net, name, zz, acc, inbox, rows, add=None):
    p = net.place
    extra = p.depth

    def take(slot):
        net.got(inbox.at[slot], (name, "at", extra + 1, slot))
        (add or add_rows)(acc, inbox.at[slot], rows)

    pl.when((zz >= p.z) & p.can_down)(lambda: take(jnp.where(zz == p.z, extra, zz)))
    pl.when((zz <= p.z) & p.can_up)(lambda: take(zz))
    slot = jnp.where(zz == p.z + 1, extra, zz)
    net.put(acc, inbox.at[slot], "up", (name, "at", extra + 1, slot), zz > p.z)
    net.put(acc, inbox.at[zz], "down", (name, "at", extra + 1, zz), zz < p.z)


class Reduce:
    def __init__(self, net, name, fill, acc, ya, xa, xb, yb, inbox, z_inbox, xc, yc):
        self.net, self.name, self.fill, self.acc = net, name, fill, acc
        self.ya, self.xa, self.xb, self.yb = ya, xa, xb, yb
        self.inbox, self.z_inbox, self.xc, self.yc = inbox, z_inbox, xc, yc
        self.rows_a, self.rows_b, self.rows_c = ya.shape[2], xb.shape[2], yc.shape[0]
        self.rows_ab = self.rows_a + self.rows_b
        self.a, self.b = pl.ds(0, self.rows_a), pl.ds(self.rows_a, self.rows_b)
        self.ab, self.c = pl.ds(0, self.rows_ab), pl.ds(self.rows_ab, self.rows_c)

    def key(self, what, zz):
        return (self.name + what, "at", self.net.place.depth, zz)

    def one(self, i):
        p, net, acc = self.net.place, self.net, self.acc
        zz = p.far[i]
        self.fill(i, zz)
        net.put(acc.at[zz, :, 1 - p.y, self.a], self.ya.at[zz], "y", self.key("ya", zz))
        net.put(acc.at[zz, 1 - p.x, :, self.b], self.xb.at[zz], "x", self.key("xb", zz))

    def two(self, i):
        p, net, acc = self.net.place, self.net, self.acc
        x, y, zz = p.x, p.y, p.far[i]
        net.got(self.xb.at[zz], self.key("xb", zz))
        add_rows(acc.at[zz, x, 1 - y, self.b], self.xb.at[zz, 1 - y], self.rows_b)
        net.put(acc.at[zz, x, 1 - y, self.b], self.yb.at[zz], "y", self.key("yb", zz))
        net.got(self.ya.at[zz], self.key("ya", zz))
        add_rows(acc.at[zz, 1 - x, y, self.a], self.ya.at[zz, 1 - x], self.rows_a)
        net.put(acc.at[zz, 1 - x, y, self.a], self.xa.at[zz], "x", self.key("xa", zz))
        add_rows(acc.at[zz, x, y, self.a], self.ya.at[zz, x], self.rows_a)
        add_rows(acc.at[zz, x, y, self.b], self.xb.at[zz, y], self.rows_b)

    def three(self, i):
        p, net, acc = self.net.place, self.net, self.acc
        x, y, zz = p.x, p.y, p.far[i]
        net.got(self.xa.at[zz], self.key("xa", zz))
        add_rows(acc.at[zz, x, y, self.a], self.xa.at[zz], self.rows_a)
        net.got(self.yb.at[zz], self.key("yb", zz))
        add_rows(acc.at[zz, x, y, self.b], self.yb.at[zz], self.rows_b)
        chain_z(net, self.name + "z", zz, acc.at[zz, x, y, self.ab], self.inbox, self.rows_ab)

    def along_z(self, i):
        p = self.net.place
        zz = p.far[i]

        def add(dst, src, rows):
            for xx in range(2):
                for yy in range(2):
                    add_rows(dst.at[xx, yy], src.at[xx, yy], rows)

        chain_z(
            self.net, self.name + "c", zz, self.acc.at[zz, :, :, self.c], self.z_inbox, self.rows_c, add
        )

    def then_x(self):
        p, net = self.net.place, self.net
        net.put(self.acc.at[p.z, 1 - p.x, :, self.c], self.xc, "x", (self.name + "xc",))

    def then_y(self):
        p, net, x, y = self.net.place, self.net, self.net.place.x, self.net.place.y
        net.got(self.xc, (self.name + "xc",))
        add_rows(self.acc.at[p.z, x, 1 - y, self.c], self.xc.at[1 - y], self.rows_c)
        net.put(self.acc.at[p.z, x, 1 - y, self.c], self.yc, "y", (self.name + "yc",))
        add_rows(self.acc.at[p.z, x, y, self.c], self.xc.at[y], self.rows_c)

    def end(self):
        p, net = self.net.place, self.net
        net.got(self.yc, (self.name + "yc",))
        add_rows(self.acc.at[p.z, p.x, p.y, self.c], self.yc, self.rows_c)


def reduce_scratch(depth, rows, wide, parts):
    a, b = parts
    c = rows - a - b
    return [
        pltpu.VMEM((depth, 2, 2, rows, wide), BF16),
        pltpu.VMEM((depth, 2, a, wide), BF16),
        pltpu.VMEM((depth, a, wide), BF16),
        pltpu.VMEM((depth, 2, b, wide), BF16),
        pltpu.VMEM((depth, b, wide), BF16),
        pltpu.VMEM((depth + 1, a + b, wide), BF16),
        pltpu.VMEM((depth + 1, 2, 2, c, wide), BF16),
        pltpu.VMEM((2, c, wide), BF16),
        pltpu.VMEM((c, wide), BF16),
    ]


def tile_rows(rows, share):
    return max(16, int(rows * share) // 16 * 16)


def perform(*steps):
    for function, *args in steps:
        function(*args)


def every(depth, *functions):
    return [(function, i) for function in functions for i in range(depth)]


def widen(dst, src, rows):
    def body(i, carry):
        at = pl.ds(pl.multiple_of(i * 16, 16), 16)
        dst[at, :] = src[at, :].astype(F32)
        return carry

    lax.fori_loop(0, rows // 16, body, 0)


def back_kernel(
    depth, part, out_part, x_rows, g_rows, hid, gate_low, up_low,
    total, out_other, w_gate_grad, w_up_grad, w_down_grad,
    acc, ya, xa, xb, yb, inbox, z_inbox, xc, yc, rc, big, left, right, found, found_down,
    send, recv, local, load_sems, save_sems,
):
    p = Place(depth)
    net = Net(p, send, recv, local)
    c = p.c
    rows, width = total.shape
    local_experts = x_rows.shape[0]

    def loads(u):
        e, slot = u // 2, u % 2
        if u % 2 == 0:
            pairs = ((x_rows, big.at[slot]), (gate_low, left.at[slot]), (up_low, right.at[slot]))
        else:
            pairs = ((g_rows, big.at[slot]), (hid, left.at[slot]))
        return [
            pltpu.make_async_copy(src.at[e], dst, load_sems.at[slot, j])
            for j, (src, dst) in enumerate(pairs)
        ]

    def saves(u):
        e = u // 2
        if u % 2 == 0:
            targets = (w_gate_grad, w_up_grad)
            return [
                pltpu.make_async_copy(found.at[j], ref.at[e], save_sems.at[j])
                for j, ref in enumerate(targets)
            ]
        return [pltpu.make_async_copy(found_down, w_down_grad.at[e], save_sems.at[2])]

    units = 2 * local_experts

    def unit(u):
        slot = u % 2
        for copy in loads(u):
            copy.wait()
        if u >= 2:
            for copy in saves(u - 2):
                copy.wait()
        if u % 2 == 0:
            wide = 256

            def body(i, carry):
                at = pl.ds(pl.multiple_of(i * wide, wide), wide)
                tile = big[slot, :, at]
                for j, ref in enumerate((left, right)):
                    found[j, at, :] = lax.dot_general(
                        tile, ref[slot], CONTRACT_FIRST, preferred_element_type=F32
                    ).astype(BF16)
                return carry

            lax.fori_loop(0, width // wide, body, 0)
        else:
            wide = 512

            def body(i, carry):
                at = pl.ds(pl.multiple_of(i * wide, wide), wide)
                found_down[:, at] = lax.dot_general(
                    left[slot], big[slot, :, at], CONTRACT_FIRST, preferred_element_type=F32
                ).astype(BF16)
                return carry

            lax.fori_loop(0, width // wide, body, 0)
        for copy in saves(u):
            copy.start()
        if u + 2 < units:
            for copy in loads(u + 2):
                copy.start()

    fills = []
    for i in range(depth):
        zz = p.far[i]
        fills.append(net.local(part.at[zz, :, :, c], acc.at[zz]))
    greet(p, ("x", "y", "c", "z"))
    for i in range(depth):
        zz = p.far[i]
        net.put(part.at[zz, :, :, 1 - c], rc.at[zz], "c", ("c", "at", depth, zz))

    def fill(i, zz):
        fills[i].wait()
        net.got(rc.at[zz], ("c", "at", depth, zz))
        for xx in range(2):
            for yy in range(2):
                add_rows(acc.at[zz, xx, yy], rc.at[zz, xx, yy], rows)

    flow = Reduce(net, "b", fill, acc, ya, xa, xb, yb, inbox, z_inbox, xc, yc)
    def begin():
        for v in range(2):
            for copy in loads(v):
                copy.start()
        for zz in range(depth):
            net.put(out_part.at[zz, :, :, 1 - c], out_other.at[zz], "c", ("oc", "at", depth, zz))

    one, two, three, along_z = flow.one, flow.two, flow.three, flow.along_z
    if depth == 4 and units == 8:
        perform(
            (one, 0), (along_z, 0), (one, 1), (begin,), (one, 2), (unit, 0), (along_z, 1),
            (along_z, 2), (two, 0), (one, 3), (unit, 1), (unit, 2), (two, 1), (unit, 3), (two, 2),
            (three, 0), (unit, 4), (along_z, 3), (flow.then_x,), (unit, 5), (three, 1),
            (three, 2), (two, 3), (unit, 6), (flow.then_y,), (unit, 7), (flow.end,), (three, 3),
        )
    else:
        perform(*every(depth, one), (begin,), *every(depth, two, three, along_z))
        perform((flow.then_x,), (flow.then_y,), (flow.end,), *every(units, unit))
    for k in (units - 2, units - 1):
        for copy in saves(k):
            copy.wait()

    def last(i, carry):
        at = pl.ds(pl.multiple_of(i * 16, 16), 16)
        total[at, :] = acc[p.z, p.x, p.y, at, :].astype(F32)
        return carry

    lax.fori_loop(0, rows // 16, last, 0)
    for zz in range(depth):
        net.got(out_other.at[zz], ("oc", "at", depth, zz))
    net.finish()


def reduce_back(depth, part, out_part, x_rows, g_rows, hid, gate_low, up_low):
    count, rows, wide = part.shape
    width = out_part.shape[2]
    local_experts, slots, hidden = hid.shape
    shape = jax.ShapeDtypeStruct
    return pl.pallas_call(
        functools.partial(back_kernel, depth),
        out_shape=[
            shape((rows, wide), F32),
            shape((depth, 2, 2, rows, width), BF16),
            shape((local_experts, width, hidden), BF16),
            shape((local_experts, width, hidden), BF16),
            shape((local_experts, hidden, width), BF16),
        ],
        in_specs=[ANY] * 7,
        out_specs=[VMEM] + [ANY] * 4,
        scratch_shapes=reduce_scratch(depth, rows, wide, [tile_rows(rows, 0.375)] * 2)
        + [
            pltpu.VMEM((depth, 2, 2, rows, wide), BF16),
            pltpu.VMEM((2, slots, width), BF16),
            pltpu.VMEM((2, slots, hidden), BF16),
            pltpu.VMEM((2, slots, hidden), BF16),
            pltpu.VMEM((2, width, hidden), BF16),
            pltpu.VMEM((hidden, width), BF16),
        ]
        + sems()
        + [pltpu.SemaphoreType.DMA((2, 3)), pltpu.SemaphoreType.DMA((3,))],
        compiler_params=comm_params(3, 60),
        name="reduce_back",
    )(
        part.reshape(depth, 2, 2, 2, rows, wide),
        out_part.reshape(depth, 2, 2, 2, rows, width),
        x_rows, g_rows, hid, gate_low, up_low,
    )


def attend_back_kernel(
    depth, mine, act_hbm, wqkv_hbm, wo_hbm, qkv_hbm, att_hbm, whole_hbm, seg_row, gain, resid, out_part, out_other,
    qkv_part, whole_part, gain_part, o_sum, o_rest, output,
    acc, ya, xa, xb, yb, inbox, z_inbox, xc, yc, other, bg, act, wqkv, wo, qkv, att, ag, low, o_acc, o_inbox, o_rx,
    whole, act_grad, send, recv, local, other_sems,
):
    p = Place(depth)
    net = Net(p, send, recv, local)
    x, y, c = p.x, p.y, p.c
    rows, width = output.shape
    seq = act.shape[0]
    cols = wo.shape[0]
    heads = cols // HEAD
    o_rows, o_cols = o_sum.shape

    def block(t):
        return bg.at[pl.ds(pl.multiple_of(t * rows, rows), rows)]

    own = net.local(mine, block(p.t))
    load_wo = net.local(wo_hbm, wo)
    load_att = net.local(att_hbm, att)
    load_qkv = net.local(qkv_hbm, qkv)
    load_act = net.local(act_hbm, act)
    load_w = net.local(wqkv_hbm, wqkv)
    load_whole = net.local(whole_hbm, whole)
    greet(p, ("x", "y", "c", "z"))
    own.wait()
    net.put(block(p.t), block(p.t), "y", ("bg", "y"))
    net.put(block(p.t), block(p.t), "c", ("bg", "c0"))

    def load_other(i):
        zz = p.far[i]
        return [
            pltpu.make_async_copy(out_part.at[zz, :, :, c], acc.at[zz], other_sems.at[0, i % 2]),
            pltpu.make_async_copy(out_other.at[zz], other.at[i % 2], other_sems.at[1, i % 2]),
        ]

    for i in range(2):
        for copy in load_other(i):
            copy.start()

    def fill(i, zz):
        for copy in load_other(i):
            copy.wait()
        for xx in range(2):
            for yy in range(2):
                add_rows(acc.at[zz, xx, yy], other.at[i % 2, xx, yy], rows)
        if i + 2 < depth:
            for copy in load_other(i + 2):
                copy.start()

    flow = Reduce(net, "out", fill, acc, ya, xa, xb, yb, inbox, z_inbox, xc, yc)

    def o_pair(z):
        return o_acc.at[:, pl.ds(pl.multiple_of(z * (2 * o_cols), LANES), 2 * o_cols)]

    def o_step(i):
        if i < depth:
            chain_z(net, "oz", p.far[i], o_pair(p.far[i]), o_inbox, o_rows)

    def o_along_x():
        theirs = pl.ds(pl.multiple_of((p.z * 2 + 1 - x) * o_cols, LANES), o_cols)
        net.put(o_acc.at[:, theirs], o_rx, "x", ("ox",))

    def rows_in():
        far = block((1 - y) * 2 + c)
        net.got(far, ("bg", "y"))
        net.put(far, far, "c", ("bg", "c1"))
        net.got(block(y * 2 + 1 - c), ("bg", "c0"))
        net.got(block((1 - y) * 2 + 1 - c), ("bg", "c1"))

    def attended_grad():
        load_wo.wait()
        ag[...] = lax.dot_general(
            bg[...], wo[...], CONTRACT_LAST, preferred_element_type=F32
        ).astype(BF16)

    wide = 512

    def o_body(i, carry):
        at = pl.ds(pl.multiple_of(i * wide, wide), wide)
        found = lax.dot_general(
            att[...], bg[:, at], CONTRACT_FIRST, preferred_element_type=F32
        ).astype(BF16)
        o_acc[:, at] = found[:o_rows]
        o_rest[:, at] = found[o_rows:]
        return carry

    def o_terms():
        load_att.wait()
        load_qkv.wait()
        lax.fori_loop(0, width // wide, o_body, 0)

    scale = 1.0 / math.sqrt(HEAD)
    same = same_document(seg_row)

    def head(h):
        at = slice(h * HEAD, (h + 1) * HEAD)
        query = qkv[:, h * HEAD : (h + 1) * HEAD]
        keys = qkv[:, cols + h * HEAD : cols + (h + 1) * HEAD]
        values = qkv[:, 2 * cols + h * HEAD : 2 * cols + (h + 1) * HEAD]
        grad = ag[:, at]
        scores = lax.dot_general(query, keys, CONTRACT_LAST, preferred_element_type=F32) * scale
        scores = jnp.where(same, scores, -1e30)
        expo = jnp.exp(scores - jnp.max(scores, axis=-1, keepdims=True))
        probs = expo / jnp.sum(expo, axis=-1, keepdims=True)
        prob_grad = lax.dot_general(grad, values, CONTRACT_LAST, preferred_element_type=F32)
        inner = jnp.sum(probs * prob_grad, axis=-1, keepdims=True)
        score_grad = (probs * (prob_grad - inner) * scale).astype(BF16)
        low[:, at] = jnp.dot(score_grad, keys, preferred_element_type=F32).astype(BF16)
        low[:, cols + h * HEAD : cols + (h + 1) * HEAD] = lax.dot_general(
            score_grad, query, CONTRACT_FIRST, preferred_element_type=F32
        ).astype(BF16)
        low[:, 2 * cols + h * HEAD : 2 * cols + (h + 1) * HEAD] = lax.dot_general(
            probs.astype(BF16), grad, CONTRACT_FIRST, preferred_element_type=F32
        ).astype(BF16)

    w_rows, w_cols = wqkv.shape[2:]

    def w_body(f, carry):
        at = pl.ds(pl.multiple_of(f * w_rows, w_rows), w_rows)
        qkv_part[f] = lax.dot_general(
            act[:, at], low[...], CONTRACT_FIRST, preferred_element_type=F32
        ).astype(BF16)
        act_grad[:, at] = sum(
            lax.dot_general(
                low[:, i * w_cols : (i + 1) * w_cols], wqkv[i, f], CONTRACT_LAST,
                preferred_element_type=F32,
            )
            for i in range(3)
        )
        return carry

    count = wqkv.shape[1]
    pieces = 4

    def w_piece(i):
        if i == 0:
            load_act.wait()
            load_w.wait()
        lax.fori_loop(i * count // pieces, (i + 1) * count // pieces, w_body, 0)

    def norm_piece(i):
        if i == 0:
            load_whole.wait()
            gain_part[...] = jnp.zeros_like(gain_part)
        span = seq // pieces // 16

        def body(k, total):
            at = pl.ds(pl.multiple_of((i * span + k) * 16, 16), 16)
            values, grad = whole[at, :].astype(F32), act_grad[at, :]
            inverse = lax.rsqrt(jnp.mean(values * values, axis=-1, keepdims=True) + EPSILON)
            scaled = gain[...] * grad
            pull = jnp.mean(values * scaled, axis=-1, keepdims=True)
            whole_part[at, :] = (
                inverse * scaled - values * (inverse * inverse * inverse) * pull
            ).astype(BF16)
            return total + jnp.sum(grad * values * inverse, axis=0, keepdims=True)

        total = lax.fori_loop(0, span, body, jnp.zeros(gain_part.shape, F32))
        gain_part[...] += total

    one, two, three, along_z = flow.one, flow.two, flow.three, flow.along_z
    if depth == 4 and heads == 4:
        perform(
            (one, 0), (along_z, 0), (one, 1), (along_z, 1), (rows_in,), (attended_grad,),
            (o_terms,), (o_step, 0), (two, 0), (one, 2), (along_z, 2), (head, 0), (head, 1),
            (o_step, 1), (o_step, 2), (two, 1), (head, 2), (head, 3), (one, 3), (along_z, 3),
            (three, 0), (w_piece, 0), (two, 2), (o_step, 3), (flow.then_x,), (w_piece, 1),
            (three, 1), (three, 2), (o_along_x,), (two, 3), (w_piece, 2), (flow.then_y,),
            (w_piece, 3), (norm_piece, 0), (norm_piece, 1), (norm_piece, 2), (three, 3),
            (norm_piece, 3), (flow.end,),
        )
    else:
        perform(*every(depth, one), (rows_in,), (attended_grad,), (o_terms,))
        perform(*every(heads, head), *every(pieces, w_piece, norm_piece))
        perform(*every(depth, two, three, along_z, o_step), (o_along_x,))
        perform((flow.then_x,), (flow.then_y,), (flow.end,))

    def add_resid(i, carry):
        at = pl.ds(pl.multiple_of(i * 16, 16), 16)
        output[at, :] = (resid[at, :] + acc[p.z, x, y, at, :].astype(F32)).astype(BF16)
        return carry

    lax.fori_loop(0, rows // 16, add_resid, 0)
    net.got(o_rx, ("ox",))
    at_o = pl.ds(pl.multiple_of((p.z * 2 + x) * o_cols, LANES), o_cols)

    def o_last(i, carry):
        at = pl.ds(pl.multiple_of(i * 16, 16), 16)
        o_sum[at, :] = o_acc[at, at_o].astype(F32) + o_rx[at, :].astype(F32)
        return carry

    lax.fori_loop(0, o_rows // 16, o_last, 0)
    net.finish()


def attend_back(
    depth, mine, act, wqkv, wo, qkv, att, whole, segments, gain, resid, out_part, out_other, o_cols
):
    rows, width = mine.shape
    seq, cols = att.shape
    _, fsdp, w_rows, w_cols = wqkv.shape
    w_wide = 3 * w_cols
    shape = jax.ShapeDtypeStruct
    return pl.pallas_call(
        functools.partial(attend_back_kernel, depth),
        out_shape=[
            shape((fsdp, w_rows, w_wide), BF16),
            shape((seq, width), BF16),
            shape((1, width), F32),
            shape((cols // 2, o_cols), F32),
            shape((cols // 2, width), BF16),
            shape((rows, width), BF16),
        ],
        in_specs=[ANY] * 7 + [VMEM] * 3 + [ANY] * 2,
        out_specs=[VMEM] * 6,
        scratch_shapes=reduce_scratch(
            depth, rows, width, [tile_rows(rows, 0.375), tile_rows(rows, 0.5)]
        )
        + [
            pltpu.VMEM((2, 2, 2, rows, width), BF16),
            pltpu.VMEM((seq, width), BF16),
            pltpu.VMEM((seq, width), BF16),
            pltpu.VMEM(wqkv.shape, BF16),
            pltpu.VMEM((cols, width), BF16),
            pltpu.VMEM((seq, w_wide), BF16),
            pltpu.VMEM((seq, cols), BF16),
            pltpu.VMEM((seq, cols), BF16),
            pltpu.VMEM((seq, w_wide), BF16),
            pltpu.VMEM((cols // 2, width), BF16),
            pltpu.VMEM((depth + 1, cols // 2, 2 * o_cols), BF16),
            pltpu.VMEM((cols // 2, o_cols), BF16),
            pltpu.VMEM((seq, width), BF16),
            pltpu.VMEM((seq, width), F32),
        ]
        + sems()
        + [pltpu.SemaphoreType.DMA((2, 2))],
        compiler_params=comm_params(4, 63),
        name="attend_back",
    )(
        mine, act, wqkv, wo, qkv, att, whole, segments[None, :], gain[None, :], resid,
        out_part.reshape(depth, 2, 2, 2, rows, width), out_other,
    )


def last_kernel(
    depth, tail, qkv_part, row_part, o_part, q_sum, k_sum, v_sum, row_sum, tail_sum, o_sum,
    q_acc, q_rx, q_inbox, t_acc, t_rc, t_ry, s_acc, s_rc, s_ry, s_rx, s_inbox,
    o_acc, o_inbox, o_rx, send, recv, local,
):
    p = Place(depth)
    net = Net(p, send, recv, local)
    x, y, c = p.x, p.y, p.c
    rows, width = row_sum.shape
    w_rows, w_cols = q_sum.shape
    o_rows, o_cols = o_sum.shape
    small = s_acc.shape[3]
    o_load = net.local(o_part, o_acc)
    t_load = net.local(row_part.at[:, c], t_acc)
    s_load = net.local(tail.at[:, :, :, c], s_acc)
    loads = [net.local(qkv_part.at[p.far[i], x], q_acc.at[p.far[i]]) for i in range(depth)]
    greet(p, ("x", "y", "c", "z"))

    def q_along_x(i):
        zz = p.far[i]
        net.put(qkv_part.at[zz, 1 - x], q_rx.at[zz], "x", ("qx", "at", depth, zz))

    def q_along_z(i):
        zz = p.far[i]
        loads[i].wait()
        net.got(q_rx.at[zz], ("qx", "at", depth, zz))
        add_rows(q_acc.at[zz], q_rx.at[zz], w_rows)
        chain_z(net, "qz", zz, q_acc.at[zz], q_inbox, w_rows)

    def o_along_z(i):
        if i == 0:
            o_load.wait()
        zz = p.far[i]
        pair = o_acc.at[:, pl.ds(pl.multiple_of(zz * (2 * o_cols), LANES), 2 * o_cols)]
        chain_z(net, "oz", zz, pair, o_inbox, o_rows)

    def o_along_x():
        theirs = pl.ds(pl.multiple_of((p.z * 2 + 1 - x) * o_cols, LANES), o_cols)
        net.put(o_acc.at[:, theirs], o_rx, "x", ("ox",))

    def cores():
        net.put(row_part.at[:, 1 - c], t_rc, "c", ("tc",))
        net.put(tail.at[:, :, :, 1 - c], s_rc, "c", ("sc",))

    def along_y():
        t_load.wait()
        net.got(t_rc, ("tc",))
        add_rows(t_acc.at[1 - y], t_rc.at[1 - y], rows)
        net.put(t_acc.at[1 - y], t_ry, "y", ("ty",))
        s_load.wait()
        net.got(s_rc, ("sc",))
        for zz in range(depth):
            for xx in range(2):
                add_rows(s_acc.at[zz, xx, 1 - y], s_rc.at[zz, xx, 1 - y], small)
        net.put(s_acc.at[:, :, 1 - y], s_ry, "y", ("sy",))
        for zz in range(depth):
            for xx in range(2):
                add_rows(s_acc.at[zz, xx, y], s_rc.at[zz, xx, y], small)

    def s_along_x():
        net.got(s_ry, ("sy",))
        for z in range(depth):
            for xx in range(2):
                add_rows(s_acc.at[z, xx, y], s_ry.at[z, xx], small)
        net.put(s_acc.at[:, 1 - x, y], s_rx, "x", ("sx",))

    def s_in():
        net.got(s_rx, ("sx",))
        for z in range(depth):
            add_rows(s_acc.at[z, x, y], s_rx.at[z], small)

    def s_along_z(i):
        chain_z(net, "sz", p.far[i], s_acc.at[p.far[i], x, y], s_inbox, small)

    def rows_in():
        net.got(t_ry, ("ty",))

        def body(i, carry):
            at = pl.ds(pl.multiple_of(i * 16, 16), 16)
            row_sum[at, :] = (
                t_acc[y, at, :].astype(F32) + t_rc[y, at, :].astype(F32) + t_ry[at, :].astype(F32)
            )
            return carry

        lax.fori_loop(0, rows // 16, body, 0)

    def o_in():
        net.got(o_rx, ("ox",))
        at_o = pl.ds(pl.multiple_of((p.z * 2 + x) * o_cols, LANES), o_cols)

        def body(i, carry):
            at = pl.ds(pl.multiple_of(i * 16, 16), 16)
            o_sum[at, :] = o_acc[at, at_o].astype(F32) + o_rx[at, :].astype(F32)
            return carry

        lax.fori_loop(0, o_rows // 16, body, 0)

    if depth == 4:
        perform(
            (q_along_x, 0), (cores,), (o_along_z, 0), (q_along_x, 1), (o_along_z, 1), (along_y,),
            (o_along_z, 2), (s_along_x,), (q_along_x, 2), (q_along_z, 0), (q_along_x, 3),
            (o_along_z, 3), (rows_in,), (s_in,), (o_along_x,), (s_along_z, 0), (q_along_z, 1),
            (q_along_z, 2), (s_along_z, 1), (o_in,), (s_along_z, 2), (q_along_z, 3),
            (s_along_z, 3),
        )
    else:
        perform(*every(depth, q_along_x), (cores,), (along_y,), (s_along_x,))
        perform(*every(depth, q_along_z, o_along_z), (s_in,), (o_along_x,))
        perform(*every(depth, s_along_z), (rows_in,), (o_in,))

    def q_last(i, carry):
        at = pl.ds(pl.multiple_of(i * 16, 16), 16)
        for j, ref in enumerate((q_sum, k_sum, v_sum)):
            ref[at, :] = q_acc[p.z, at, pl.ds(j * w_cols, w_cols)].astype(F32)
        return carry

    lax.fori_loop(0, w_rows // 16, q_last, 0)
    widen(tail_sum, s_acc.at[p.z, x, y], small)
    net.finish()


def last_reduce(depth, tail, qkv_part, row_part, o_part):
    count, small, lanes = tail.shape
    fsdp, w_rows, w_wide = qkv_part.shape
    tp, rows, width = row_part.shape
    w_cols = w_wide // 3
    o_rows, o_cols = o_part.shape[0], width // fsdp
    shape = jax.ShapeDtypeStruct
    return pl.pallas_call(
        functools.partial(last_kernel, depth),
        out_shape=[shape((w_rows, w_cols), F32)] * 3
        + [shape((rows, width), F32), shape((small, lanes), F32), shape((o_rows, o_cols), F32)],
        in_specs=[ANY] * 4,
        out_specs=[VMEM] * 6,
        scratch_shapes=[
            pltpu.VMEM((depth, w_rows, w_wide), BF16),
            pltpu.VMEM((depth, w_rows, w_wide), BF16),
            pltpu.VMEM((depth + 1, w_rows, w_wide), BF16),
            pltpu.VMEM((2, rows, width), BF16),
            pltpu.VMEM((2, rows, width), BF16),
            pltpu.VMEM((rows, width), BF16),
            pltpu.VMEM((depth, 2, 2, small, lanes), BF16),
            pltpu.VMEM((depth, 2, 2, small, lanes), BF16),
            pltpu.VMEM((depth, 2, small, lanes), BF16),
            pltpu.VMEM((depth, small, lanes), BF16),
            pltpu.VMEM((depth + 1, small, lanes), BF16),
            pltpu.VMEM((o_rows, width), BF16),
            pltpu.VMEM((depth + 1, o_rows, 2 * o_cols), BF16),
            pltpu.VMEM((o_rows, o_cols), BF16),
        ]
        + sems(),
        compiler_params=comm_params(5, 48),
        name="last_reduce",
    )(
        tail.reshape(depth, 2, 2, 2, small, lanes),
        qkv_part.reshape(depth, 2, w_rows, w_wide),
        row_part.reshape(2, 2, rows, width),
        o_part,
    )


def norm_rows(values, gain):
    inverse = lax.rsqrt(jnp.mean(values * values, axis=-1, keepdims=True) + EPSILON)
    return (values * inverse * gain, inverse)


def norm_back(values, inverse, gain, grad):
    scaled = gain * grad
    gain_grad = jnp.sum(grad * values * inverse, axis=0)
    cubed = inverse * inverse * inverse
    values_grad = inverse * scaled - values * cubed * jnp.mean(
        values * scaled, axis=-1, keepdims=True
    )
    return (values_grad, gain_grad)


def contract_last(left, right):
    return lax.dot_general(
        left, right, (((1,), (1,)), ((), ())), preferred_element_type=jnp.float32
    )


def contract_first(left, right):
    return lax.dot_general(
        left, right, (((0,), (0,)), ((), ())), preferred_element_type=jnp.float32
    )


def dense_layer(
    inputs, out_grad, segments, routes, attn_gain, w_query, w_key, w_value, w_output,
    moe_gain, router, w_gate, w_up, w_down,
):
    tp, fsdp = lax.axis_size("tp"), lax.axis_size("fsdp")
    depth = fsdp // 2
    rows, width = inputs.shape
    local_experts = w_gate.shape[0]
    experts = local_experts * fsdp
    top_k = routes.shape[1]
    capacity = 3 * rows * top_k // (2 * experts)
    w_rows, w_cols = w_query.shape
    heads = w_cols // HEAD
    seq = tp * rows

    named = jnp.any(
        routes[:, :, None] == jnp.arange(experts, dtype=jnp.int32)[None, None, :], axis=1
    )
    hits = named.astype(F32)
    before = (jnp.arange(rows)[:, None] > jnp.arange(rows)[None, :]).astype(F32)
    ranks = jnp.where(named, jnp.dot(before, hits, preferred_element_type=F32), -1.0)
    fill = jnp.zeros((rows, LANES - 3 * experts), F32)
    blank = jnp.zeros((rows, experts), F32)
    mask = jnp.concatenate([hits, hits, blank, fill], axis=1)
    rank = jnp.concatenate([blank, blank, ranks, fill], axis=1)
    qkv_full, full_output, whole, act_one, qkv, attended, partial, grad_all = first_gather(
        depth, w_query, w_key, w_value, w_output, inputs, out_grad, attn_gain, segments, tp
    )
    resid, gates_wide, _, _, out_part, back_part, x_rows, g_rows, hid_low, gate_low, up_low = run_moe(
        depth, capacity, experts, partial.reshape(tp, rows, width), inputs, out_grad, moe_gain,
        router.T, mask, rank, w_gate, w_up, w_down, grad_all,
    )
    back, out_other, w_gate_grad, w_up_grad, w_down_grad = reduce_back(
        depth, back_part, out_part, x_rows, g_rows, hid_low, gate_low, up_low
    )
    gates = gates_wide[:, :experts]
    act_two = (
        resid
        * (inverse_two := lax.rsqrt(jnp.mean(resid * resid, axis=-1, keepdims=True) + EPSILON))
        * moe_gain
    ).astype(BF16)
    gate_grad = jnp.sum(back[:, width : width + tp * experts].reshape(rows, tp, experts), axis=1)
    logit_grad = gates * (gate_grad - jnp.sum(gates * gate_grad, axis=1, keepdims=True))
    act_two_grad = back[:, :width] + lax.dot_general(
        logit_grad, router.astype(F32), (((1,), (1,)), ((), ())), precision=HIGHEST
    )
    router_part = lax.dot_general(
        act_two.astype(F32), logit_grad, (((0,), (0,)), ((), ())), precision=HIGHEST
    )
    resid_part, gain_two_part = norm_back(resid, inverse_two, moe_gain, act_two_grad)
    resid_grad = out_grad.astype(F32) + resid_part
    qkv_part, whole_part, gain_one_part, o_first, o_rest, output = attend_back(
        depth, resid_grad.astype(BF16), act_one, qkv_full, full_output, qkv, attended,
        whole.reshape(seq, width), segments, attn_gain, resid, out_part, out_other,
        w_output.shape[1],
    )
    count = fsdp * tp
    piece = width // count
    small = jnp.concatenate([router_part, gain_one_part.reshape(-1, 1), gain_two_part[:, None]], axis=1)
    small = small.astype(BF16).reshape(count, piece, experts + 2)
    tail = jnp.pad(small, ((0, 0), (0, -piece % 16), (0, LANES - experts - 2)))
    q_sum, k_sum, v_sum, row_sum, side, o_second = last_reduce(
        depth, tail, qkv_part, whole_part.reshape(tp, rows, width), o_rest
    )
    o_sum = jnp.concatenate([o_first, o_second], axis=0)
    input_grad = resid_grad + row_sum
    side = side[:piece]
    return (
        output,
        input_grad,
        side[:, experts],
        q_sum,
        k_sum,
        v_sum,
        o_sum,
        side[:, experts + 1],
        side[:, :experts],
        w_gate_grad.astype(F32),
        w_up_grad.astype(F32),
        w_down_grad.astype(F32),
    )


def send_rows(buffer):
    return lax.all_to_all(buffer, "fsdp", split_axis=1, concat_axis=1, tiled=True)


def per_device(
    inputs,
    out_grad,
    segments,
    routes,
    attn_gain,
    w_query,
    w_key,
    w_value,
    w_output,
    moe_gain,
    router,
    w_gate,
    w_up,
    w_down,
):
    tp_count = lax.axis_size("tp")
    fsdp_count = lax.axis_size("fsdp")
    rows_piece, width = inputs.shape
    head_size = HEAD
    full_query, full_key, full_value, full_output = (
        lax.all_gather(w_query, "fsdp", axis=0, tiled=True),
        lax.all_gather(w_key, "fsdp", axis=0, tiled=True),
        lax.all_gather(w_value, "fsdp", axis=0, tiled=True),
        lax.all_gather(w_output, "fsdp", axis=1, tiled=True),
    )
    whole_rows = lax.all_gather(inputs, "tp", axis=0, tiled=True)
    seq_len = whole_rows.shape[0]
    whole_float = whole_rows.astype(jnp.float32)
    normed_one, inverse_one = norm_rows(whole_float, attn_gain)
    act_one = normed_one.astype(jnp.bfloat16)
    local_heads = full_query.shape[1] // head_size
    query = (
        jnp.dot(act_one, full_query, preferred_element_type=jnp.float32)
        .astype(jnp.bfloat16)
        .reshape(seq_len, local_heads, head_size)
    )
    key_rows = (
        jnp.dot(act_one, full_key, preferred_element_type=jnp.float32)
        .astype(jnp.bfloat16)
        .reshape(seq_len, local_heads, head_size)
    )
    value_rows = (
        jnp.dot(act_one, full_value, preferred_element_type=jnp.float32)
        .astype(jnp.bfloat16)
        .reshape(seq_len, local_heads, head_size)
    )
    block_rows = min(512, seq_len)
    score_scale = 1.0 / math.sqrt(head_size)

    def block_scores(query_block):
        scores = (
            jnp.einsum("qhd,khd->hqk", query_block, key_rows, preferred_element_type=jnp.float32)
            * score_scale
        )
        same_doc = segments[:, None] == segments[None, :]
        return jnp.where(same_doc[None], scores, -1e30)

    scores = block_scores(query)
    peak = jnp.max(scores, axis=-1, keepdims=True)
    expo = jnp.exp(scores - peak)
    total = jnp.sum(expo, axis=-1, keepdims=True)
    softmax_rows = (expo / total).astype(jnp.bfloat16)
    block_outputs = jnp.einsum(
        "hqk,khd->qhd", softmax_rows, value_rows, preferred_element_type=jnp.float32
    )
    log_totals = [peak + jnp.log(total)]
    attended = block_outputs.reshape(seq_len, -1).astype(jnp.bfloat16)
    branch = lax.psum_scatter(
        jnp.dot(attended, full_output, preferred_element_type=jnp.float32).astype(jnp.bfloat16),
        "tp",
        scatter_dimension=0,
        tiled=True,
    ).astype(jnp.float32)
    resid = inputs.astype(jnp.float32) + branch
    normed_two, inverse_two = norm_rows(resid, moe_gain)
    act_two = normed_two.astype(jnp.bfloat16)
    local_experts = w_gate.shape[0]
    experts = local_experts * fsdp_count
    top_k = routes.shape[1]
    capacity = 3 * rows_piece * top_k // (2 * experts)
    logits = jnp.dot(act_two, router, preferred_element_type=jnp.float32)
    picks = (routes[:, :, None] == jnp.arange(experts, dtype=jnp.int32)[None, None, :]).astype(
        jnp.float32
    )
    chosen = jnp.einsum("tke,te->tk", picks, logits, precision=HIGHEST)
    gates = jax.nn.softmax(chosen, axis=-1)
    flat_routes = routes.reshape(-1)
    route_count = flat_routes.shape[0]
    hits = (flat_routes[:, None] == jnp.arange(experts, dtype=jnp.int32)[None, :]).astype(jnp.int32)
    ranks = jnp.sum((jnp.cumsum(hits, axis=0) - 1) * hits, axis=1)
    slots = flat_routes * capacity + ranks
    sources = (
        jnp.full((experts * capacity,), route_count, jnp.int32)
        .at[slots]
        .set(jnp.arange(route_count, dtype=jnp.int32))
    )
    padded_act = jnp.concatenate([act_two, jnp.zeros((1, width), jnp.bfloat16)], 0)
    send_buffer = padded_act[sources // top_k].reshape(
        1, fsdp_count, local_experts * capacity, width
    )
    gate_full, up_full, down_full = (
        lax.all_gather(w_gate, "tp", axis=2, tiled=True),
        lax.all_gather(w_up, "tp", axis=2, tiled=True),
        lax.all_gather(w_down, "tp", axis=1, tiled=True),
    )
    own_in = send_rows(send_buffer)
    own_rows = own_in.reshape(fsdp_count, local_experts, capacity, width)
    own_gate = jnp.einsum("secd,edf->secf", own_rows, gate_full, preferred_element_type=jnp.float32)
    own_up = jnp.einsum("secd,edf->secf", own_rows, up_full, preferred_element_type=jnp.float32)
    own_sigmoid = jax.nn.sigmoid(own_gate)
    own_silu = own_gate * own_sigmoid
    own_hidden = (own_silu * own_up).astype(jnp.bfloat16)
    own_out = jnp.einsum(
        "secf,efd->secd", own_hidden, down_full, preferred_element_type=jnp.float32
    )
    expert_out = own_out.reshape(1, fsdp_count, local_experts * capacity, width).astype(
        jnp.bfloat16
    )
    returned = lax.all_to_all(expert_out, "fsdp", split_axis=1, concat_axis=1, tiled=True).reshape(
        experts * capacity, width
    )
    routed = returned[slots].reshape(rows_piece, top_k, width).astype(jnp.float32)
    mixture = jnp.sum(gates[:, :, None] * routed, axis=1)
    output = (resid + mixture).astype(jnp.bfloat16)
    grad_float = out_grad.astype(jnp.float32)
    gate_grad = jnp.sum(routed * grad_float[:, None, :], axis=2)
    route_grad = (
        (gates[:, :, None] * grad_float[:, None, :])
        .astype(jnp.bfloat16)
        .reshape(route_count, width)
    )
    padded_grad = jnp.concatenate([route_grad, jnp.zeros((1, width), jnp.bfloat16)], 0)
    grad_buffer = padded_grad[sources].reshape(1, fsdp_count, local_experts * capacity, width)
    own_grads = send_rows(grad_buffer).reshape(fsdp_count, local_experts, capacity, width)
    own_hidden_grad = jnp.einsum(
        "secd,efd->secf", own_grads, down_full, preferred_element_type=jnp.float32
    )
    own_gate_low = (
        own_hidden_grad * own_up * own_sigmoid * (1.0 + own_gate * (1.0 - own_sigmoid))
    ).astype(jnp.bfloat16)
    own_up_low = (own_hidden_grad * own_silu).astype(jnp.bfloat16)
    down_term = jnp.einsum(
        "secf,secd->efd", own_hidden, own_grads, preferred_element_type=jnp.float32
    )
    gate_term = jnp.einsum(
        "secd,secf->edf", own_rows, own_gate_low, preferred_element_type=jnp.float32
    )
    up_term = jnp.einsum("secd,secf->edf", own_rows, own_up_low, preferred_element_type=jnp.float32)
    w_gate_grad, w_up_grad, w_down_grad = (
        lax.psum_scatter(
            gate_term.astype(jnp.bfloat16), "tp", scatter_dimension=2, tiled=True
        ).astype(jnp.float32),
        lax.psum_scatter(
            up_term.astype(jnp.bfloat16), "tp", scatter_dimension=2, tiled=True
        ).astype(jnp.float32),
        lax.psum_scatter(
            down_term.astype(jnp.bfloat16), "tp", scatter_dimension=1, tiled=True
        ).astype(jnp.float32),
    )
    own_back = jnp.einsum(
        "secf,edf->secd", own_gate_low, gate_full, preferred_element_type=jnp.float32
    )
    own_back = own_back + jnp.einsum(
        "secf,edf->secd", own_up_low, up_full, preferred_element_type=jnp.float32
    )
    expert_grad = own_back.reshape(1, fsdp_count, local_experts * capacity, width).astype(
        jnp.bfloat16
    )
    back_rows = lax.all_to_all(
        expert_grad, "fsdp", split_axis=1, concat_axis=1, tiled=True
    ).reshape(experts * capacity, width)
    act_two_grad = jnp.sum(
        back_rows[slots].reshape(rows_piece, top_k, width).astype(jnp.float32), axis=1
    )
    centered = gate_grad - jnp.sum(gates * gate_grad, axis=1, keepdims=True)
    chosen_grad = gates * centered
    logit_grad = jnp.einsum("tke,tk->te", picks, chosen_grad, precision=HIGHEST)
    router_float = router.astype(jnp.float32)
    act_two_grad = act_two_grad + lax.dot_general(
        logit_grad, router_float, (((1,), (1,)), ((), ())), precision=HIGHEST
    )
    router_part = lax.dot_general(
        act_two.astype(jnp.float32), logit_grad, (((0,), (0,)), ((), ())), precision=HIGHEST
    )
    resid_part, gain_two_part = norm_back(resid, inverse_two, moe_gain, act_two_grad)
    resid_grad = grad_float + resid_part
    branch_grad = lax.all_gather(resid_grad.astype(jnp.bfloat16), "tp", axis=0, tiled=True)
    attended_grad = (
        contract_last(branch_grad, full_output)
        .astype(jnp.bfloat16)
        .reshape(seq_len, local_heads, head_size)
    )
    w_output_part = contract_first(attended, branch_grad)
    query_parts = []
    key_grad = jnp.zeros((seq_len, local_heads, head_size), jnp.float32)
    value_grad = jnp.zeros((seq_len, local_heads, head_size), jnp.float32)
    for block_index, first_row in enumerate(range(0, seq_len, block_rows)):
        query_block = query
        scores = block_scores(query_block)
        softmax_rows = jnp.exp(scores - log_totals[block_index])
        prob_grad = jnp.einsum(
            "qhd,khd->hqk", attended_grad, value_rows, preferred_element_type=jnp.float32
        )
        inner = jnp.sum(softmax_rows * prob_grad, axis=-1, keepdims=True)
        score_grad = (softmax_rows * (prob_grad - inner) * score_scale).astype(jnp.bfloat16)
        query_parts.append(
            jnp.einsum("hqk,khd->qhd", score_grad, key_rows, preferred_element_type=jnp.float32)
        )
        key_grad = jnp.einsum(
            "hqk,qhd->khd", score_grad, query_block, preferred_element_type=jnp.float32
        )
        value_grad = jnp.einsum(
            "hqk,qhd->khd",
            softmax_rows.astype(jnp.bfloat16),
            attended_grad,
            preferred_element_type=jnp.float32,
        )
    query_low = query_parts[0].reshape(seq_len, -1).astype(jnp.bfloat16)
    key_low = key_grad.reshape(seq_len, -1).astype(jnp.bfloat16)
    value_low = value_grad.reshape(seq_len, -1).astype(jnp.bfloat16)
    w_query_part = contract_first(act_one, query_low)
    w_key_part = contract_first(act_one, key_low)
    w_value_part = contract_first(act_one, value_low)
    act_one_grad = (
        contract_last(query_low, full_query)
        + contract_last(key_low, full_key)
        + contract_last(value_low, full_value)
    )
    whole_part, gain_one_part = norm_back(whole_float, inverse_one, attn_gain, act_one_grad)

    def arrange(values):
        shaped = values.reshape((fsdp_count, tp_count, -1) + values.shape[1:])
        return jnp.swapaxes(shaped, 0, 1)

    input_part, gain_one_tp, gain_two_tp, router_tp = (
        lax.psum_scatter(
            whole_part.astype(jnp.bfloat16), "tp", scatter_dimension=0, tiled=True
        ).astype(jnp.float32),
        lax.psum_scatter(
            arrange(gain_one_part).astype(jnp.bfloat16), "tp", scatter_dimension=0, tiled=True
        ).astype(jnp.float32),
        lax.psum_scatter(
            arrange(gain_two_part).astype(jnp.bfloat16), "tp", scatter_dimension=0, tiled=True
        ).astype(jnp.float32),
        lax.psum_scatter(
            arrange(router_part).astype(jnp.bfloat16), "tp", scatter_dimension=0, tiled=True
        ).astype(jnp.float32),
    )
    input_grad = resid_grad + input_part
    query_sum, key_sum, value_sum, output_sum, gain_one_sum, gain_two_sum, router_sum = (
        lax.psum_scatter(
            w_query_part.astype(jnp.bfloat16), "fsdp", scatter_dimension=0, tiled=True
        ).astype(jnp.float32),
        lax.psum_scatter(
            w_key_part.astype(jnp.bfloat16), "fsdp", scatter_dimension=0, tiled=True
        ).astype(jnp.float32),
        lax.psum_scatter(
            w_value_part.astype(jnp.bfloat16), "fsdp", scatter_dimension=0, tiled=True
        ).astype(jnp.float32),
        lax.psum_scatter(
            w_output_part.astype(jnp.bfloat16), "fsdp", scatter_dimension=1, tiled=True
        ).astype(jnp.float32),
        lax.psum_scatter(
            gain_one_tp.astype(jnp.bfloat16), "fsdp", scatter_dimension=1, tiled=True
        ).astype(jnp.float32),
        lax.psum_scatter(
            gain_two_tp.astype(jnp.bfloat16), "fsdp", scatter_dimension=1, tiled=True
        ).astype(jnp.float32),
        lax.psum_scatter(
            router_tp.astype(jnp.bfloat16), "fsdp", scatter_dimension=1, tiled=True
        ).astype(jnp.float32),
    )
    return (
        output,
        input_grad,
        gain_one_sum.reshape(-1),
        query_sum,
        key_sum,
        value_sum,
        output_sum,
        gain_two_sum.reshape(-1),
        router_sum.reshape(-1, experts),
        w_gate_grad,
        w_up_grad,
        w_down_grad,
    )


def layer(*args):
    tokens = args[0].shape[0] * lax.axis_size("fsdp") * lax.axis_size("tp")
    held = 6 * tokens * (args[0].shape[1] + LANES) * 2
    even = lax.axis_size("tp") == 4 and lax.axis_size("fsdp") % 2 == 0
    experts = args[11].shape[0] * lax.axis_size("fsdp")
    narrow = lax.axis_size("tp") * experts <= LANES and args[1].shape[1] // (lax.axis_size("tp") * lax.axis_size("fsdp")) <= args[0].shape[0]
    if held <= HBM_BUDGET and even and narrow:
        return dense_layer(*args)
    return per_device(*args)


def solution(mesh):
    return jax.shard_map(
        layer,
        mesh=mesh,
        in_specs=(
            P(("fsdp", "tp"), None),
            P(("fsdp", "tp"), None),
            P("fsdp"),
            P(("fsdp", "tp"), None),
            P(),
            P("fsdp", "tp"),
            P("fsdp", "tp"),
            P("fsdp", "tp"),
            P("tp", "fsdp"),
            P(),
            P(),
            P("fsdp", None, "tp"),
            P("fsdp", None, "tp"),
            P("fsdp", "tp", None),
        ),
        out_specs=(
            P(("fsdp", "tp"), None),
            P(("fsdp", "tp"), None),
            P(("fsdp", "tp")),
            P("fsdp", "tp"),
            P("fsdp", "tp"),
            P("fsdp", "tp"),
            P("tp", "fsdp"),
            P(("fsdp", "tp")),
            P(("fsdp", "tp"), None),
            P("fsdp", None, "tp"),
            P("fsdp", None, "tp"),
            P("fsdp", "tp", None),
        ),
        check_vma=False,
    )
```

```python
import functools
import math

import jax
import jax.numpy as jnp
from jax import lax
from jax.experimental import pallas as pl
from jax.experimental.pallas import tpu as pltpu
from jax.sharding import PartitionSpec as P

HEAD = 128
LANES = 128
EPSILON = 1e-05
HIGHEST = lax.Precision.HIGHEST
MESH = pl.DeviceIdType.MESH
ANY = pl.BlockSpec(memory_space=pl.ANY)
VMEM = pl.BlockSpec(memory_space=pltpu.VMEM)
MIB = 1 << 20
HBM_BUDGET = 300 * MIB
BF16 = jnp.bfloat16
F32 = jnp.float32
CONTRACT_FIRST = (((0,), (0,)), ((), ()))
CONTRACT_LAST = (((1,), (1,)), ((), ()))


class Place:
    def __init__(self, depth):
        self.depth = depth
        f, t = lax.axis_index("fsdp"), lax.axis_index("tp")
        self.f, self.t = f, t
        self.z, self.x = lax.div(f, 2), lax.rem(f, 2)
        self.y, self.c = lax.div(t, 2), lax.rem(t, 2)
        self.to = {
            "x": (self.z * 2 + 1 - self.x, t),
            "y": (f, (1 - self.y) * 2 + self.c),
            "c": (f, self.y * 2 + 1 - self.c),
            "up": (f + 2, t),
            "down": (f - 2, t),
        }
        self.can_up = self.z < depth - 1
        self.can_down = self.z > 0
        offs = [0]
        for step in range(1, depth):
            offs += [-step, step]
        self.offs = offs
        tables = [sorted(range(depth), key=lambda zz: (abs(zz - z), zz)) for z in range(depth)]
        self.near = [
            sum(jnp.where(self.z == z, tables[z][i], 0) for z in range(depth)) for i in range(depth)
        ]
        self.far = self.near[::-1]
        self.tables = tables

    def nearest(self, i):
        pairs = [(z, k) for z in range(self.depth) for k in range(self.depth)]
        return sum(
            jnp.where((self.z == z) & (i == k), self.tables[z][k], 0) for z, k in pairs
        )

    def valid(self, off):
        if off == 0:
            return None
        return self.z + off >= 0 if off < 0 else self.z + off < self.depth


def when(cond, body):
    if cond is None:
        body()
    else:
        pl.when(cond)(body)


def both(first, second):
    if first is None:
        return second
    if second is None:
        return first
    return jnp.logical_and(first, second)


class Net:
    def __init__(self, place, send_sems, recv_sems, local_sems):
        self.place = place
        self.send_sems, self.recv_sems, self.local_sems = send_sems, recv_sems, local_sems
        self.keys, self.used, self.sent, self.locals_used = {}, 0, [], 0

    def slot(self, key):
        if len(key) == 4 and key[1] == "at":
            base = self.keys.setdefault(key[0], self.used)
            if base == self.used:
                self.used += key[2]
            return base + key[3]
        base = self.keys.setdefault(key, self.used)
        if base == self.used:
            self.used += 1
        return base

    def put(self, src, dst, to, key, cond=None, guard=None):
        copy = pltpu.make_async_remote_copy(
            src_ref=src,
            dst_ref=dst,
            send_sem=self.send_sems.at[len(self.sent)],
            recv_sem=self.recv_sems.at[self.slot(key)],
            device_id=self.place.to[to],
            device_id_type=MESH,
        )
        self.sent.append((both(cond, guard), copy))
        when(cond, copy.start)

    def got(self, dst, key):
        pltpu.make_async_remote_copy(
            src_ref=dst,
            dst_ref=dst,
            send_sem=self.send_sems.at[0],
            recv_sem=self.recv_sems.at[self.slot(key)],
            device_id=self.place.to["c"],
            device_id_type=MESH,
        ).wait_recv()

    def local(self, src, dst):
        copy = pltpu.make_async_copy(src, dst, self.local_sems.at[self.locals_used])
        self.locals_used += 1
        copy.start()
        return copy

    def finish(self):
        for cond, copy in self.sent:
            when(cond, copy.wait_send)


def greet(place, links):
    barrier = pltpu.get_barrier_semaphore()
    count = 0
    for link in links:
        if link == "z":
            for name, cond in (("up", place.can_up), ("down", place.can_down)):
                target = place.to[name]
                pl.when(cond)(
                    lambda target=target: pl.semaphore_signal(
                        barrier, inc=1, device_id=target, device_id_type=MESH
                    )
                )
                count = count + cond.astype(jnp.int32)
        else:
            pl.semaphore_signal(barrier, inc=1, device_id=place.to[link], device_id_type=MESH)
            count = count + 1
    pl.semaphore_wait(barrier, count)


SENDS, RECVS, LOCALS = 160, 160, 24


def sems():
    return [
        pltpu.SemaphoreType.DMA((SENDS,)),
        pltpu.SemaphoreType.DMA((RECVS,)),
        pltpu.SemaphoreType.DMA((LOCALS,)),
    ]


def add_rows(dst, src, rows, step=16):
    def body(i, carry):
        at = pl.ds(pl.multiple_of(i * step, step), step)
        dst[at, :] = (dst[at, :].astype(F32) + src[at, :].astype(F32)).astype(dst.dtype)
        return carry

    lax.fori_loop(0, rows // step, body, 0)


def comm_params(ident, mib=None):
    limit = None if mib is None else mib * MIB
    return pltpu.CompilerParams(collective_id=ident, has_side_effects=True, vmem_limit_bytes=limit)


def spread_zx(net, name, block, own):
    p = net.place
    offs = p.offs

    def step(i):
        if i >= len(offs):
            return
        off = offs[i]
        zz = p.z + off
        valid = p.valid(off)
        ref = block(zz, p.x)

        def body():
            if off:
                net.got(ref, (name, "z", off))

        when(valid, body)
        src = ref if off else own
        if off <= 0:
            net.put(src, ref, "up", (name, "z", off - 1), both(valid, p.can_up))
        if off >= 0:
            net.put(src, ref, "down", (name, "z", off + 1), both(valid, p.can_down))
        net.put(src, ref, "x", (name, "x", off), valid)

    def finish():
        for off in offs:
            ref = block(p.z + off, 1 - p.x)
            when(p.valid(off), lambda: net.got(ref, (name, "x", off)))

    return step, finish


def spread_xz(net, name, block, pair, own, placed):
    p = net.place
    offs = p.offs

    def begin():
        net.put(own, block(p.z, p.x), "x", (name, "x"))

    def step(i):
        off = offs[i]
        if off == 0:
            placed.wait()
            net.got(block(p.z, 1 - p.x), (name, "x"))
        valid = p.valid(off)
        ref = pair(p.z + off)
        if off:
            when(valid, lambda: net.got(ref, (name, "z", off)))
        if off <= 0:
            net.put(ref, ref, "up", (name, "z", off - 1), both(valid, p.can_up))
        if off >= 0:
            net.put(ref, ref, "down", (name, "z", off + 1), both(valid, p.can_down))

    return begin, step


SITES = {
    "x1": ("x", 0, 0, 0),
    "y1": ("y", 0, 0, 1),
    "x3": ("x", 0, 0, 1),
    "y3": ("y", 0, 0, 0),
    "y2": ("y", 1, 0, 0),
    "x2": ("x", 0, 1, 1),
    "c0": ("c", 0, 0, None),
    "cx": ("c", 1, 0, None),
    "cy": ("c", 0, 1, None),
    "cxy": ("c", 1, 1, None),
}
NAMES = list(SITES)


class Plane:
    def __init__(self, place, everyone, own, sends, recvs):
        self.place, self.everyone, self.own = place, everyone, own
        self.sends, self.recvs = sends, recvs
        self.half = own.shape[0] // 2

    def ref(self, zz, dx, dy, dc, part):
        p = self.place
        x, y, c = p.x + dx - 2 * p.x * dx, p.y + dy - 2 * p.y * dy, p.c + dc - 2 * p.c * dc
        ref = self.everyone.at[((zz * 2 + x) * 2 + y) * 2 + c]
        return ref if part is None else ref.at[pl.ds(part * self.half, self.half)]

    def copy(self, site, zz, src=None):
        link, dx, dy, part = SITES[site]
        dst = self.ref(zz, dx, dy, 0, part)
        at = NAMES.index(site) * self.place.depth + zz
        return pltpu.make_async_remote_copy(
            src_ref=dst if src is None else src,
            dst_ref=dst,
            send_sem=self.sends.at[at],
            recv_sem=self.recvs.at[at],
            device_id=self.place.to[link],
            device_id_type=MESH,
        )

    def take(self, site, zz):
        link, dx, dy, part = SITES[site]
        dx, dy = dx ^ (link == "x"), dy ^ (link == "y")
        ref = self.ref(zz, dx, dy, int(link == "c"), part)
        at = NAMES.index(site) * self.place.depth + zz
        pltpu.make_async_remote_copy(
            src_ref=ref,
            dst_ref=ref,
            send_sem=self.sends.at[at],
            recv_sem=self.recvs.at[at],
            device_id=self.place.to[link],
            device_id_type=MESH,
        ).wait_recv()

    def z_copy(self, zz, up):
        p = self.place
        ref = self.ref(zz, 0, 0, 0, None)
        base = len(NAMES) * p.depth
        return pltpu.make_async_remote_copy(
            src_ref=ref,
            dst_ref=ref,
            send_sem=self.sends.at[base + (0 if up else p.depth) + zz],
            recv_sem=self.recvs.at[base + zz],
            device_id=p.to["up" if up else "down"],
            device_id_type=MESH,
        )

    def each_z(self, zz, act):
        p = self.place
        pl.when((zz <= p.z) & p.can_up)(lambda: act(True))
        pl.when((zz >= p.z) & p.can_down)(lambda: act(False))

    def own_along_z(self):
        p = self.place
        base = len(NAMES) * p.depth

        def start(up):
            pltpu.make_async_remote_copy(
                src_ref=self.own,
                dst_ref=self.ref(p.z, 0, 0, 0, None),
                send_sem=self.sends.at[base + (0 if up else p.depth) + p.z],
                recv_sem=self.recvs.at[base + p.z],
                device_id=p.to["up" if up else "down"],
                device_id_type=MESH,
            ).start()

        self.each_z(p.z, start)

    def take_z(self, zz):
        ref = self.ref(zz, 0, 0, 0, None)
        at = len(NAMES) * self.place.depth + zz
        pltpu.make_async_remote_copy(
            src_ref=ref,
            dst_ref=ref,
            send_sem=self.sends.at[at],
            recv_sem=self.recvs.at[at],
            device_id=self.place.to["c"],
            device_id_type=MESH,
        ).wait_recv()

    def along_z(self, zz):
        self.take_z(zz)
        self.each_z(zz, lambda up: self.z_copy(zz, up).start())

    def first(self, zz, mine=False):
        whole, part_a, part_b = None, None, None
        if mine:
            whole = self.own
            part_a, part_b = whole.at[pl.ds(0, self.half)], whole.at[pl.ds(self.half, self.half)]
        self.copy("x1", zz, part_a).start()
        self.copy("y1", zz, part_b).start()
        self.copy("x3", zz, part_b).start()
        self.copy("y3", zz, part_a).start()
        self.copy("c0", zz, whole).start()

    def first_of_own(self, part):
        zz, rows = self.place.z, self.own.at[pl.ds(part * self.half, self.half)]
        self.copy("y1" if part else "x1", zz, rows).start()
        self.copy("x3" if part else "y3", zz, rows).start()
        if part:
            self.copy("c0", zz, self.own).start()

    def second(self, zz):
        self.take("x1", zz)
        self.copy("y2", zz).start()
        self.take("y1", zz)
        self.copy("x2", zz).start()

    def third_y(self, zz):
        self.take("y3", zz)
        self.copy("cy", zz).start()

    def third_x(self, zz):
        self.take("x3", zz)
        self.copy("cx", zz).start()
        self.take("x2", zz)
        self.take("y2", zz)
        self.copy("cxy", zz).start()

    def arrived_y(self, zz):
        self.take("c0", zz)
        self.take("cy", zz)

    def arrived_x(self, zz):
        self.take("cx", zz)
        self.take("cxy", zz)

    def finish(self, zs, z_zs):
        for zz in zs:
            for site in NAMES:
                self.copy(site, zz).wait_send()
        for zz in z_zs:
            self.each_z(zz, lambda up, zz=zz: self.z_copy(zz, up).wait_send())


def plane_sems(depth):
    return [pltpu.SemaphoreType.DMA(((len(NAMES) + 2) * depth,))] * 2


def same_document(seg_row):
    row = seg_row[...]
    column = jnp.transpose(jnp.broadcast_to(row, (LANES, row.shape[1])))[:, 0:1]
    return column == row


def first_kernel(
    depth, wq, wk, wv, wo, inp, og, gain, seg_row,
    qkv_hbm, o_hbm, rows_hbm, act_hbm, proj_hbm, att_hbm, part_hbm, grad_all,
    weights, full_o, rows, act, proj, att, part, og_send, og_recv, send, recv, local,
):
    p = Place(depth)
    net = Net(p, send, recv, local)
    grads = Plane(p, grad_all, og, og_send, og_recv)
    w_rows, w_cols = wq.shape
    o_cols = wo.shape[1]
    count, width = inp.shape
    fsdp, heads = 2 * depth, w_cols // HEAD

    def column(f):
        return full_o.at[:, pl.ds(pl.multiple_of(f * o_cols, LANES), o_cols)]

    def columns(z):
        return full_o.at[:, pl.ds(pl.multiple_of(z * (2 * o_cols), LANES), 2 * o_cols)]

    def slab(i):
        return lambda z, x: weights.at[i, z * 2 + x]

    greet(p, ("x", "y", "c", "z"))
    mine = rows.at[p.t]
    net.put(inp, mine, "y", ("rows", "y"))
    net.put(inp, mine, "c", ("rows", "c0"))
    placed = net.local(wo, column(p.f))
    owns = [net.local(inp, mine)]
    owns += [net.local(w, weights.at[i, p.f]) for i, w in enumerate((wq, wk, wv))]
    kept = net.local(og, grads.ref(p.z, 0, 0, 0, None))
    flows = [spread_zx(net, f"w{i}", slab(i), w) for i, w in enumerate((wq, wk, wv))]
    o_begin, o_step = spread_xz(net, "o", lambda z, x: column(z * 2 + x), columns, wo, placed)
    steps = len(p.offs)

    def norm():
        other = rows.at[(1 - p.y) * 2 + p.c]
        net.got(other, ("rows", "y"))
        net.put(other, other, "c", ("rows", "c1"))
        net.got(rows.at[p.y * 2 + 1 - p.c], ("rows", "c0"))
        net.got(rows.at[(1 - p.y) * 2 + 1 - p.c], ("rows", "c1"))
        owns[0].wait()
        for t in range(rows.shape[0]):

            def body(i, carry):
                at = pl.ds(pl.multiple_of(i * 16, 16), 16)
                values = rows[t, at, :].astype(F32)
                inverse = lax.rsqrt(jnp.mean(values * values, axis=-1, keepdims=True) + EPSILON)
                to = pl.ds(pl.multiple_of(t * count + i * 16, 16), 16)
                act[to, :] = (values * inverse * gain[...]).astype(BF16)
                return carry

            lax.fori_loop(0, count // 16, body, 0)

    saves = []

    def rows_in():
        norm()
        saves.append(net.local(rows, rows_hbm))
        saves.append(net.local(act, act_hbm))

    def project_with(i):
        owns[1 + i].wait()
        flows[i][1]()
        saves.append(net.local(weights.at[i], qkv_hbm.at[i]))
        wide = 256

        def project(k, carry):
            at = pl.ds(pl.multiple_of(k * wide, wide), wide)
            to = pl.ds(pl.multiple_of(i * w_cols + k * wide, wide), wide)
            matrix = weights[i, :, :, at].reshape(width, wide)
            proj[:, to] = jnp.dot(act[...], matrix, preferred_element_type=F32).astype(BF16)
            return carry

        lax.fori_loop(0, w_cols // wide, project, 0)

    scale = 1.0 / math.sqrt(HEAD)

    def head(h):
        if h == 0:
            saves.append(net.local(proj, proj_hbm))
        same = same_document(seg_row)
        query, keys, values = [
            proj[:, i * w_cols + h * HEAD : i * w_cols + (h + 1) * HEAD] for i in range(3)
        ]
        scores = lax.dot_general(query, keys, CONTRACT_LAST, preferred_element_type=F32) * scale
        scores = jnp.where(same, scores, -1e30)
        expo = jnp.exp(scores - jnp.max(scores, axis=-1, keepdims=True))
        probs = (expo / jnp.sum(expo, axis=-1, keepdims=True)).astype(BF16)
        att[:, h * HEAD : (h + 1) * HEAD] = jnp.dot(
            probs, values, preferred_element_type=F32
        ).astype(BF16)

    def out_rows(k, carry):
        at = pl.ds(pl.multiple_of(k * 256, 256), 256)
        part[:, at] = jnp.dot(att[...], full_o[:, at], preferred_element_type=F32).astype(BF16)
        return carry

    def branch():
        saves.append(net.local(full_o, o_hbm))
        saves.append(net.local(att, att_hbm))
        lax.fori_loop(0, width // 256, out_rows, 0)
        saves.append(net.local(part, part_hbm))

    (q_step, _), (k_step, _), (v_step, _) = flows

    def g_first():
        grads.first(p.z, True)

    if depth == 4 and heads == 4:
        perform(
            (o_begin,), (v_step, 0), (q_step, 0), (k_step, 0), (q_step, 1), (q_step, 2),
            (q_step, 3), (v_step, 1), (k_step, 1), (k_step, 2), (q_step, 4), (k_step, 3),
            (v_step, 2), (q_step, 5), (rows_in,), (v_step, 3), (q_step, 6), (k_step, 4),
            (o_step, 0), (v_step, 4), (k_step, 5), (o_step, 1), (v_step, 5), (o_step, 2),
            (k_step, 6), (project_with, 0), (v_step, 6), (project_with, 1), (g_first,),
            (o_step, 3), (o_step, 4), (project_with, 2), (head, 0), (grads.second, p.z),
            (head, 1), (head, 2), (head, 3), (o_step, 5), (o_step, 6), (branch,),
            (grads.third_y, p.z), (grads.third_x, p.z),
            (grads.arrived_y, p.z), (grads.arrived_x, p.z),
        )
    else:
        perform((o_begin,), (g_first,), *every(steps, q_step, k_step, v_step, o_step), (rows_in,))
        perform((grads.second, p.z), (grads.third_y, p.z), (grads.third_x, p.z))
        perform(*every(3, project_with))
        perform(*every(heads, head), (branch,))
        perform((grads.arrived_y, p.z), (grads.arrived_x, p.z))
    kept.wait()
    for copy in saves:
        copy.wait()
    grads.finish([p.z], [])
    net.finish()


def first_gather(depth, w_query, w_key, w_value, w_output, inputs, out_grad, gain, segments, tp):
    fsdp = 2 * depth
    w_rows, w_cols = w_query.shape
    o_rows, o_cols = w_output.shape
    rows, width = inputs.shape
    seq = tp * rows
    shape = jax.ShapeDtypeStruct
    return pl.pallas_call(
        functools.partial(first_kernel, depth),
        out_shape=[
            shape((3, fsdp, w_rows, w_cols), BF16),
            shape((o_rows, fsdp * o_cols), BF16),
            shape((tp, rows, width), BF16),
            shape((seq, width), BF16),
            shape((seq, 3 * w_cols), BF16),
            shape((seq, w_cols), BF16),
            shape((seq, width), BF16),
            shape((fsdp * tp, rows, width), BF16),
        ],
        in_specs=[VMEM] * 8,
        out_specs=[ANY] * 8,
        scratch_shapes=[
            pltpu.VMEM((3, fsdp, w_rows, w_cols), BF16),
            pltpu.VMEM((o_rows, fsdp * o_cols), BF16),
            pltpu.VMEM((tp, rows, width), BF16),
            pltpu.VMEM((seq, width), BF16),
            pltpu.VMEM((seq, 3 * w_cols), BF16),
            pltpu.VMEM((seq, w_cols), BF16),
            pltpu.VMEM((seq, width), BF16),
        ]
        + plane_sems(depth)
        + sems(),
        compiler_params=comm_params(1, 60),
        name="first_gather",
    )(
        w_query, w_key, w_value, w_output, inputs, out_grad, gain[None, :], segments[None, :],
    )


def moe_kernel(
    depth, capacity, experts, blocks,
    part, inp, og, gain, router, mask, rank, gate_hbm, up_hbm, down_hbm, grad_in_hbm,
    resid, gates_out, act_all, grad_all, out_hbm, back_hbm, x_hbm, g_hbm, hid_hbm, gl_hbm, ul_hbm,
    acc, rc, ry, own, w_gate, w_up, w_down, act_in, grad_in, x_rows, g_rows, tails, hid, gl, ul,
    keep, out, back,
    act_send, act_recv, og_send, og_recv, send, recv, local, load_sems, save_sems,
):
    p = Place(depth)
    net = Net(p, send, recv, local)
    rows, width = inp.shape
    local_experts = w_gate.shape[0]
    weights = [
        net.local(src, dst)
        for src, dst in ((gate_hbm, w_gate), (up_hbm, w_up), (down_hbm, w_down))
    ]
    part_in = net.local(part.at[:, p.c], acc)
    acts = Plane(p, act_all, own, act_send, act_recv)
    grads = Plane(p, grad_all, og, og_send, og_recv)
    greet(p, ("x", "y", "c", "z"))

    net.put(part.at[:, 1 - p.c], rc, "c", ("rc",))
    far = 1 - p.y

    half = rows // 2

    def along_y():
        part_in.wait()
        net.got(rc, ("rc",))
        for i in range(2):
            at = pl.ds(i * half, half)
            add_rows(acc.at[far, at], rc.at[far, at], half)
            net.put(acc.at[far, at], ry.at[at], "y", ("ry", i))
        add_rows(acc.at[p.y], rc.at[p.y], rows)

    kept = []

    def norm(part_of):
        here = pl.ds(part_of * half, half)
        net.got(ry.at[here], ("ry", part_of))

        def body(i, carry):
            at = pl.ds(pl.multiple_of(part_of * half + i * 16, 16), 16)
            branch = acc[p.y, at, :].astype(F32) + ry[at, :].astype(F32)
            values = inp[at, :].astype(F32) + branch
            resid[at, :] = values
            inverse = lax.rsqrt(jnp.mean(values * values, axis=-1, keepdims=True) + EPSILON)
            own[at, pl.ds(0, width)] = (values * inverse * gain[...]).astype(BF16)
            return carry

        lax.fori_loop(0, half // 16, body, 0)
        twice = jnp.concatenate(
            [router[...]] * 2 + [jnp.zeros((LANES - 2 * experts, width), BF16)], axis=0
        )
        logits = lax.dot_general(
            own[here, pl.ds(0, width)], twice, CONTRACT_LAST, preferred_element_type=F32
        )
        chosen = mask[here, :] > 0.0
        peak = jnp.max(jnp.where(chosen, logits, -1e30), axis=1, keepdims=True)
        expo = jnp.where(chosen, jnp.exp(jnp.minimum(logits - peak, 0.0)), 0.0)
        lane = lax.broadcasted_iota(jnp.int32, expo.shape, 1)
        total = jnp.sum(jnp.where(lane < experts, expo, 0.0), axis=1, keepdims=True)
        gates = expo / total
        gates_out[here, :] = gates
        high = gates.astype(BF16).astype(F32)
        tail = jnp.where(
            lane < experts, high, jnp.where(lane < 2 * experts, gates - high, rank[here, :])
        )
        own[here, pl.ds(width, LANES)] = tail.astype(BF16)
        if part_of == 1:
            kept.append(net.local(own, acts.ref(p.z, 0, 0, 0, None)))

    first_expert = p.f * local_experts
    tp_lane = p.t * experts + first_expert
    pick_row = lax.broadcasted_iota(jnp.int32, (8, LANES), 0)
    pick_lane = lax.broadcasted_iota(jnp.int32, (8, LANES), 1)
    pick = (
        (pick_lane == 2 * experts + first_expert + pick_row) & (pick_row < local_experts)
    ).astype(BF16)
    places = lax.broadcasted_iota(jnp.int32, (capacity, rows), 0).astype(F32)
    slots = blocks * capacity

    def blocks_of(zz, j):
        return (zz * 2 + (1 - p.x if j else p.x)) * blocks

    def loads(zz, j):
        at = pl.ds(blocks_of(zz, j), blocks)
        return [
            pltpu.make_async_copy(act_all.at[at], act_in.at[j], load_sems.at[j, 0]),
            pltpu.make_async_copy(grad_all.at[at], grad_in.at[j], load_sems.at[j, 1]),
        ]

    def save(zz, j, k):
        if k < 5:
            where = pl.ds(pl.multiple_of(blocks_of(zz, j) * capacity, 16), slots)
            src = (x_rows, g_rows, hid, gl, ul)[k]
            dst = (x_hbm, g_hbm, hid_hbm, gl_hbm, ul_hbm)[k].at[:, where]
        else:
            src = (out, back)[k - 5]
            dst = (out_hbm, back_hbm)[k - 5].at[pl.ds(blocks_of(zz, j), blocks)]
        return pltpu.make_async_copy(src, dst, save_sems.at[k])

    def one_hot(j, b):
        tail = act_in[j, b, :, pl.ds(width, LANES)]
        ranks = lax.dot_general(pick, tail, CONTRACT_LAST, preferred_element_type=F32)
        return jnp.concatenate(
            [
                (jnp.broadcast_to(ranks[e : e + 1, :], (capacity, rows)) == places).astype(BF16)
                for e in range(local_experts)
            ],
            axis=0,
        )

    def work(zz, j, started, serve):
        for copy in loads(zz, j):
            copy.wait()

        def settle(ks):
            def body():
                for k in ks:
                    save(zz, j, k).wait()

            when(started, body)

        settle((0, 1))

        def gather(pair, carry):
            b = pair * 2
            blank = jnp.zeros((local_experts * capacity, rows), BF16)
            hot = jnp.concatenate(
                [
                    jnp.concatenate([one_hot(j, b), blank], axis=1),
                    jnp.concatenate([blank, one_hot(j, b + 1)], axis=1),
                ],
                axis=0,
            )
            acts_two = act_in[j, pl.ds(b, 2)].reshape(2 * rows, width + LANES)
            grads_two = grad_in[j, pl.ds(b, 2)].reshape(2 * rows, width)
            picked = jnp.dot(hot, acts_two, preferred_element_type=F32)
            pulled = jnp.dot(hot, grads_two, preferred_element_type=F32).astype(BF16)
            for k in range(2):
                at = pl.ds(pl.multiple_of((b + k) * capacity, 16), capacity)
                for e in range(local_experts):
                    first = (k * local_experts + e) * capacity
                    piece = picked[first : first + capacity]
                    x_rows[e, at, :] = piece[:, :width].astype(BF16)
                    tails[e, at, :] = piece[:, width:]
                    g_rows[e, at, :] = pulled[first : first + capacity]
            return carry

        lax.fori_loop(0, blocks // 2, gather, 0)
        for k in (0, 1):
            save(zz, j, k).start()
        serve(0)
        settle((2, 3, 4))
        for e in range(local_experts):
            tail_lane = lax.broadcasted_iota(jnp.int32, (slots, LANES), 1)
            mine = (tail_lane == first_expert + e) | (tail_lane == experts + first_expert + e)
            gates_of = jnp.sum(jnp.where(mine, tails[e], 0.0), axis=1, keepdims=True)
            pre = jnp.dot(x_rows[e], w_gate[e], preferred_element_type=F32)
            up = jnp.dot(x_rows[e], w_up[e], preferred_element_type=F32)
            raw = lax.dot_general(g_rows[e], w_down[e], CONTRACT_LAST, preferred_element_type=F32)
            sig = jax.nn.sigmoid(pre)
            silu = pre * sig
            hidden = silu * up
            gate_grad = jnp.sum(hidden * raw, axis=1, keepdims=True)
            scaled = raw * gates_of
            hid_low = (hidden * gates_of).astype(BF16)
            gate_low = (scaled * up * sig * (1.0 + pre * (1.0 - sig))).astype(BF16)
            up_low = (scaled * silu).astype(BF16)
            hid[e] = hid_low
            gl[e] = gate_low
            ul[e] = up_low
            o_rows = jnp.dot(hid_low, w_down[e], preferred_element_type=F32).astype(BF16)
            r_rows = (
                lax.dot_general(gate_low, w_gate[e], CONTRACT_LAST, preferred_element_type=F32)
                + lax.dot_general(up_low, w_up[e], CONTRACT_LAST, preferred_element_type=F32)
            ).astype(BF16)
            r_tail = jnp.where(tail_lane == tp_lane + e, gate_grad, 0.0).astype(BF16)
            for b in range(blocks):
                at = slice(b * capacity, (b + 1) * capacity)
                to = slice(e * capacity, (e + 1) * capacity)
                keep[b, to, pl.ds(0, width)] = o_rows[at]
                keep[b, to, pl.ds(width, width)] = r_rows[at]
                keep[b, to, pl.ds(2 * width, LANES)] = r_tail[at]
            serve(1 + e)
        for k in (2, 3, 4):
            save(zz, j, k).start()
        settle((5, 6))

        def combine(b, carry):
            hot = one_hot(j, b)
            found = lax.dot_general(hot, keep[b], CONTRACT_FIRST, preferred_element_type=F32)
            out[b] = found[:, :width].astype(BF16)
            back[b] = found[:, width:].astype(BF16)
            return carry

        lax.fori_loop(0, blocks, combine, 0)
        for k in (5, 6):
            save(zz, j, k).start()
        serve(5)

    def load(i, j):
        if i == j == 0:
            kept[0].wait()
            for copy in weights:
                copy.wait()
        for copy in loads(p.near[i], j):
            copy.start()

    near = p.near
    g1, g2, g3y, g3x = grads.first, grads.second, grads.third_y, grads.third_x
    a1, a2, a3y, a3x = acts.first, acts.second, acts.third_y, acts.third_x
    if depth == 4:
        perform(
            (along_y,), (grads.own_along_z,), (norm, 0), (acts.first_of_own, 0), (norm, 1),
            (acts.own_along_z,), (acts.first_of_own, 1), (grads.along_z, near[1]), (g1, near[1]),
            (a2, p.z), (a3y, p.z), (grads.along_z, near[2]), (acts.arrived_y, p.z), (load, 0, 0),
            (acts.along_z, near[1]), (a1, near[1]), (g2, near[1]),
        )
        service = {
            (0, 0, 0): [(g1, near[2])],
            (0, 0, 3): [(acts.along_z, near[2])],
            (0, 0, 4): [(a3x, p.z), (acts.arrived_x, p.z), (load, 0, 1)],
            (0, 1, 1): [(grads.along_z, near[3])],
            (0, 1, 2): [(a2, near[1])],
            (0, 1, 3): [(a3y, near[1]), (g3y, near[1]), (a1, near[2])],
            (0, 1, 4): [(grads.arrived_y, near[1]), (acts.arrived_y, near[1]), (load, 1, 0)],
            (1, 0, 0): [(g1, near[3]), (g3x, near[1])],
            (1, 0, 2): [(acts.along_z, near[3])],
            (1, 0, 3): [(g2, near[2]), (a3x, near[1]), (grads.arrived_x, near[1])],
            (1, 0, 4): [(a2, near[2]), (acts.arrived_x, near[1]), (load, 1, 1)],
            (1, 1, 0): [(a3y, near[2])],
            (1, 1, 2): [(g3y, near[2])],
            (1, 1, 3): [(acts.arrived_y, near[2])],
            (1, 1, 4): [(grads.arrived_y, near[2]), (load, 2, 0)],
            (2, 0, 1): [(a1, near[3]), (g3x, near[2]), (g2, near[3])],
            (2, 0, 2): [(g3y, near[3])],
            (2, 0, 3): [(a3x, near[2]), (grads.arrived_x, near[2])],
            (2, 0, 4): [(acts.arrived_x, near[2]), (load, 2, 1)],
            (2, 1, 2): [(a2, near[3])],
            (2, 1, 3): [(a3y, near[3])],
            (2, 1, 4): [(acts.arrived_y, near[3]), (grads.arrived_y, near[3]), (load, 3, 0)],
            (3, 0, 0): [(g3x, near[3])],
            (3, 0, 2): [(grads.arrived_x, near[3]), (a3x, near[3])],
            (3, 0, 4): [(acts.arrived_x, near[3]), (load, 3, 1)],
        }
    else:
        perform((along_y,), (norm, 0), (norm, 1), (acts.own_along_z,), (grads.own_along_z,))
        for i, zz in enumerate(near):
            if i:
                perform((acts.along_z, zz), (grads.along_z, zz), (g1, zz), (g2, zz))
                perform((g3y, zz), (g3x, zz), (grads.arrived_y, zz), (grads.arrived_x, zz))
            perform((a1, zz, i == 0), (a2, zz), (a3y, zz), (a3x, zz))
            perform((acts.arrived_y, zz), (acts.arrived_x, zz))
        load(0, 0)
        service = {(g, 0, 0): [(load, g, 1)] for g in range(depth)}
        service.update({(g, 1, 4): [(load, g + 1, 0)] for g in range(depth - 1)})

    def group(g, carry):
        zz = p.nearest(g)

        def serve(j, k):
            for (at, half, place), steps in service.items():
                if (half, place) == (j, k):
                    pl.when(g == at)(functools.partial(perform, *steps))

        work(zz, 0, g > 0, functools.partial(serve, 0))
        work(zz, 1, None, functools.partial(serve, 1))
        return carry

    lax.fori_loop(0, depth, group, 0)
    for k in range(7):
        save(0, 1, k).wait()
    acts.finish(range(depth), range(depth))
    grads.finish(near[1:], near)
    net.finish()


def run_moe(
    depth, capacity, experts, part, inputs, out_grad, gain, router, mask, rank, w_gate, w_up, w_down,
    grad_all,
):
    tp, rows, width = part.shape
    wide = width + LANES
    count = 2 * depth * tp
    local_experts, _, hidden = w_gate.shape
    blocks = tp
    slots = blocks * capacity
    total = count * capacity
    shape = jax.ShapeDtypeStruct
    kept = [shape((local_experts, total, width), BF16)] * 2
    kept += [shape((local_experts, total, hidden), BF16)] * 3
    return pl.pallas_call(
        functools.partial(moe_kernel, depth, capacity, experts, blocks),
        out_shape=[
            shape((rows, width), F32),
            shape((rows, LANES), F32),
            shape((count, rows, wide), BF16),
            shape((count, rows, width), BF16),
            shape((count, rows, width), BF16),
            shape((count, rows, wide), BF16),
        ]
        + kept,
        in_specs=[ANY] + [VMEM] * 6 + [ANY] * 4,
        out_specs=[VMEM] * 2 + [ANY] * 9,
        input_output_aliases={10: 3},
        scratch_shapes=[
            pltpu.VMEM((2, rows, width), BF16),
            pltpu.VMEM((2, rows, width), BF16),
            pltpu.VMEM((rows, width), BF16),
            pltpu.VMEM((rows, wide), BF16),
            pltpu.VMEM(w_gate.shape, BF16),
            pltpu.VMEM(w_up.shape, BF16),
            pltpu.VMEM(w_down.shape, BF16),
            pltpu.VMEM((2, blocks, rows, wide), BF16),
            pltpu.VMEM((2, blocks, rows, width), BF16),
            pltpu.VMEM((local_experts, slots, width), BF16),
            pltpu.VMEM((local_experts, slots, width), BF16),
            pltpu.VMEM((local_experts, slots, LANES), F32),
            pltpu.VMEM((local_experts, slots, hidden), BF16),
            pltpu.VMEM((local_experts, slots, hidden), BF16),
            pltpu.VMEM((local_experts, slots, hidden), BF16),
            pltpu.VMEM((blocks, local_experts * capacity, width + wide), BF16),
            pltpu.VMEM((blocks, rows, width), BF16),
            pltpu.VMEM((blocks, rows, wide), BF16),
        ]
        + plane_sems(depth) * 2
        + sems()
        + [pltpu.SemaphoreType.DMA((2, 2)), pltpu.SemaphoreType.DMA((7,))],
        compiler_params=comm_params(2, 60),
        name="moe",
    )(
        part.reshape(tp // 2, 2, rows, width), inputs, out_grad, gain[None, :], router, mask, rank,
        w_gate, w_up, w_down, grad_all,
    )


def chain_z(net, name, zz, acc, inbox, rows, add=None):
    p = net.place
    extra = p.depth

    def take(slot):
        net.got(inbox.at[slot], (name, "at", extra + 1, slot))
        (add or add_rows)(acc, inbox.at[slot], rows)

    pl.when((zz >= p.z) & p.can_down)(lambda: take(jnp.where(zz == p.z, extra, zz)))
    pl.when((zz <= p.z) & p.can_up)(lambda: take(zz))
    slot = jnp.where(zz == p.z + 1, extra, zz)
    net.put(acc, inbox.at[slot], "up", (name, "at", extra + 1, slot), zz > p.z)
    net.put(acc, inbox.at[zz], "down", (name, "at", extra + 1, zz), zz < p.z)


class Reduce:
    def __init__(self, net, name, fill, acc, ya, xa, xb, yb, inbox, z_inbox, xc, yc):
        self.net, self.name, self.fill, self.acc = net, name, fill, acc
        self.ya, self.xa, self.xb, self.yb = ya, xa, xb, yb
        self.inbox, self.z_inbox, self.xc, self.yc = inbox, z_inbox, xc, yc
        self.rows_a, self.rows_b, self.rows_c = ya.shape[2], xb.shape[2], yc.shape[0]
        self.rows_ab = self.rows_a + self.rows_b
        self.a, self.b = pl.ds(0, self.rows_a), pl.ds(self.rows_a, self.rows_b)
        self.ab, self.c = pl.ds(0, self.rows_ab), pl.ds(self.rows_ab, self.rows_c)

    def key(self, what, zz):
        return (self.name + what, "at", self.net.place.depth, zz)

    def one(self, i):
        p, net, acc = self.net.place, self.net, self.acc
        zz = p.far[i]
        self.fill(i, zz)
        net.put(acc.at[zz, :, 1 - p.y, self.a], self.ya.at[zz], "y", self.key("ya", zz))
        net.put(acc.at[zz, 1 - p.x, :, self.b], self.xb.at[zz], "x", self.key("xb", zz))

    def two(self, i):
        p, net, acc = self.net.place, self.net, self.acc
        x, y, zz = p.x, p.y, p.far[i]
        net.got(self.xb.at[zz], self.key("xb", zz))
        add_rows(acc.at[zz, x, 1 - y, self.b], self.xb.at[zz, 1 - y], self.rows_b)
        net.put(acc.at[zz, x, 1 - y, self.b], self.yb.at[zz], "y", self.key("yb", zz))
        net.got(self.ya.at[zz], self.key("ya", zz))
        add_rows(acc.at[zz, 1 - x, y, self.a], self.ya.at[zz, 1 - x], self.rows_a)
        net.put(acc.at[zz, 1 - x, y, self.a], self.xa.at[zz], "x", self.key("xa", zz))
        add_rows(acc.at[zz, x, y, self.a], self.ya.at[zz, x], self.rows_a)
        add_rows(acc.at[zz, x, y, self.b], self.xb.at[zz, y], self.rows_b)

    def three(self, i):
        p, net, acc = self.net.place, self.net, self.acc
        x, y, zz = p.x, p.y, p.far[i]
        net.got(self.xa.at[zz], self.key("xa", zz))
        add_rows(acc.at[zz, x, y, self.a], self.xa.at[zz], self.rows_a)
        net.got(self.yb.at[zz], self.key("yb", zz))
        add_rows(acc.at[zz, x, y, self.b], self.yb.at[zz], self.rows_b)
        chain_z(net, self.name + "z", zz, acc.at[zz, x, y, self.ab], self.inbox, self.rows_ab)

    def along_z(self, i):
        p = self.net.place
        zz = p.far[i]

        def add(dst, src, rows):
            for xx in range(2):
                for yy in range(2):
                    add_rows(dst.at[xx, yy], src.at[xx, yy], rows)

        chain_z(
            self.net, self.name + "c", zz, self.acc.at[zz, :, :, self.c], self.z_inbox, self.rows_c, add
        )

    def then_x(self):
        p, net = self.net.place, self.net
        net.put(self.acc.at[p.z, 1 - p.x, :, self.c], self.xc, "x", (self.name + "xc",))

    def then_y(self):
        p, net, x, y = self.net.place, self.net, self.net.place.x, self.net.place.y
        net.got(self.xc, (self.name + "xc",))
        add_rows(self.acc.at[p.z, x, 1 - y, self.c], self.xc.at[1 - y], self.rows_c)
        net.put(self.acc.at[p.z, x, 1 - y, self.c], self.yc, "y", (self.name + "yc",))
        add_rows(self.acc.at[p.z, x, y, self.c], self.xc.at[y], self.rows_c)

    def end(self):
        p, net = self.net.place, self.net
        net.got(self.yc, (self.name + "yc",))
        add_rows(self.acc.at[p.z, p.x, p.y, self.c], self.yc, self.rows_c)


def reduce_scratch(depth, rows, wide, parts):
    a, b = parts
    c = rows - a - b
    return [
        pltpu.VMEM((depth, 2, 2, rows, wide), BF16),
        pltpu.VMEM((depth, 2, a, wide), BF16),
        pltpu.VMEM((depth, a, wide), BF16),
        pltpu.VMEM((depth, 2, b, wide), BF16),
        pltpu.VMEM((depth, b, wide), BF16),
        pltpu.VMEM((depth + 1, a + b, wide), BF16),
        pltpu.VMEM((depth + 1, 2, 2, c, wide), BF16),
        pltpu.VMEM((2, c, wide), BF16),
        pltpu.VMEM((c, wide), BF16),
    ]


def tile_rows(rows, share):
    return max(16, int(rows * share) // 16 * 16)


def perform(*steps):
    for function, *args in steps:
        function(*args)


def every(depth, *functions):
    return [(function, i) for function in functions for i in range(depth)]


def widen(dst, src, rows):
    def body(i, carry):
        at = pl.ds(pl.multiple_of(i * 16, 16), 16)
        dst[at, :] = src[at, :].astype(F32)
        return carry

    lax.fori_loop(0, rows // 16, body, 0)


def back_kernel(
    depth, part, out_part, x_rows, g_rows, hid, gate_low, up_low,
    total, out_other, w_gate_grad, w_up_grad, w_down_grad,
    acc, ya, xa, xb, yb, inbox, z_inbox, xc, yc, rc, big, left, right, found, found_down,
    send, recv, local, load_sems, save_sems,
):
    p = Place(depth)
    net = Net(p, send, recv, local)
    c = p.c
    rows, width = total.shape
    local_experts = x_rows.shape[0]

    def loads(u):
        e, slot = u // 2, u % 2
        if u % 2 == 0:
            pairs = ((x_rows, big.at[slot]), (gate_low, left.at[slot]), (up_low, right.at[slot]))
        else:
            pairs = ((g_rows, big.at[slot]), (hid, left.at[slot]))
        return [
            pltpu.make_async_copy(src.at[e], dst, load_sems.at[slot, j])
            for j, (src, dst) in enumerate(pairs)
        ]

    def saves(u):
        e = u // 2
        if u % 2 == 0:
            targets = (w_gate_grad, w_up_grad)
            return [
                pltpu.make_async_copy(found.at[j], ref.at[e], save_sems.at[j])
                for j, ref in enumerate(targets)
            ]
        return [pltpu.make_async_copy(found_down, w_down_grad.at[e], save_sems.at[2])]

    units = 2 * local_experts

    def unit(u):
        slot = u % 2
        for copy in loads(u):
            copy.wait()
        if u >= 2:
            for copy in saves(u - 2):
                copy.wait()
        if u % 2 == 0:
            wide = 256

            def body(i, carry):
                at = pl.ds(pl.multiple_of(i * wide, wide), wide)
                tile = big[slot, :, at]
                for j, ref in enumerate((left, right)):
                    found[j, at, :] = lax.dot_general(
                        tile, ref[slot], CONTRACT_FIRST, preferred_element_type=F32
                    ).astype(BF16)
                return carry

            lax.fori_loop(0, width // wide, body, 0)
        else:
            wide = 512

            def body(i, carry):
                at = pl.ds(pl.multiple_of(i * wide, wide), wide)
                found_down[:, at] = lax.dot_general(
                    left[slot], big[slot, :, at], CONTRACT_FIRST, preferred_element_type=F32
                ).astype(BF16)
                return carry

            lax.fori_loop(0, width // wide, body, 0)
        for copy in saves(u):
            copy.start()
        if u + 2 < units:
            for copy in loads(u + 2):
                copy.start()

    fills = []
    for i in range(depth):
        zz = p.far[i]
        fills.append(net.local(part.at[zz, :, :, c], acc.at[zz]))
    greet(p, ("x", "y", "c", "z"))
    for i in range(depth):
        zz = p.far[i]
        net.put(part.at[zz, :, :, 1 - c], rc.at[zz], "c", ("c", "at", depth, zz))

    def fill(i, zz):
        fills[i].wait()
        net.got(rc.at[zz], ("c", "at", depth, zz))
        for xx in range(2):
            for yy in range(2):
                add_rows(acc.at[zz, xx, yy], rc.at[zz, xx, yy], rows)

    flow = Reduce(net, "b", fill, acc, ya, xa, xb, yb, inbox, z_inbox, xc, yc)
    def begin():
        for v in range(2):
            for copy in loads(v):
                copy.start()
        for zz in range(depth):
            net.put(out_part.at[zz, :, :, 1 - c], out_other.at[zz], "c", ("oc", "at", depth, zz))

    one, two, three, along_z = flow.one, flow.two, flow.three, flow.along_z
    if depth == 4 and units == 8:
        perform(
            (one, 0), (along_z, 0), (one, 1), (begin,), (one, 2), (unit, 0), (along_z, 1),
            (along_z, 2), (two, 0), (one, 3), (unit, 1), (unit, 2), (two, 1), (unit, 3), (two, 2),
            (three, 0), (unit, 4), (along_z, 3), (flow.then_x,), (unit, 5), (three, 1),
            (three, 2), (two, 3), (unit, 6), (flow.then_y,), (unit, 7), (flow.end,), (three, 3),
        )
    else:
        perform(*every(depth, one), (begin,), *every(depth, two, three, along_z))
        perform((flow.then_x,), (flow.then_y,), (flow.end,), *every(units, unit))
    for k in (units - 2, units - 1):
        for copy in saves(k):
            copy.wait()

    def last(i, carry):
        at = pl.ds(pl.multiple_of(i * 16, 16), 16)
        total[at, :] = acc[p.z, p.x, p.y, at, :].astype(F32)
        return carry

    lax.fori_loop(0, rows // 16, last, 0)
    for zz in range(depth):
        net.got(out_other.at[zz], ("oc", "at", depth, zz))
    net.finish()


def reduce_back(depth, part, out_part, x_rows, g_rows, hid, gate_low, up_low):
    count, rows, wide = part.shape
    width = out_part.shape[2]
    local_experts, slots, hidden = hid.shape
    shape = jax.ShapeDtypeStruct
    return pl.pallas_call(
        functools.partial(back_kernel, depth),
        out_shape=[
            shape((rows, wide), F32),
            shape((depth, 2, 2, rows, width), BF16),
            shape((local_experts, width, hidden), BF16),
            shape((local_experts, width, hidden), BF16),
            shape((local_experts, hidden, width), BF16),
        ],
        in_specs=[ANY] * 7,
        out_specs=[VMEM] + [ANY] * 4,
        scratch_shapes=reduce_scratch(depth, rows, wide, [tile_rows(rows, 0.375)] * 2)
        + [
            pltpu.VMEM((depth, 2, 2, rows, wide), BF16),
            pltpu.VMEM((2, slots, width), BF16),
            pltpu.VMEM((2, slots, hidden), BF16),
            pltpu.VMEM((2, slots, hidden), BF16),
            pltpu.VMEM((2, width, hidden), BF16),
            pltpu.VMEM((hidden, width), BF16),
        ]
        + sems()
        + [pltpu.SemaphoreType.DMA((2, 3)), pltpu.SemaphoreType.DMA((3,))],
        compiler_params=comm_params(3, 60),
        name="reduce_back",
    )(
        part.reshape(depth, 2, 2, 2, rows, wide),
        out_part.reshape(depth, 2, 2, 2, rows, width),
        x_rows, g_rows, hid, gate_low, up_low,
    )


def attend_back_kernel(
    depth, mine, act_hbm, wqkv_hbm, wo_hbm, qkv_hbm, att_hbm, whole_hbm, seg_row, gain, resid, out_part, out_other,
    qkv_part, whole_part, gain_part, o_sum, o_rest, output,
    acc, ya, xa, xb, yb, inbox, z_inbox, xc, yc, other, bg, act, wqkv, wo, qkv, att, ag, low, o_acc, o_inbox, o_rx,
    whole, act_grad, send, recv, local, other_sems,
):
    p = Place(depth)
    net = Net(p, send, recv, local)
    x, y, c = p.x, p.y, p.c
    rows, width = output.shape
    seq = act.shape[0]
    cols = wo.shape[0]
    heads = cols // HEAD
    o_rows, o_cols = o_sum.shape

    def block(t):
        return bg.at[pl.ds(pl.multiple_of(t * rows, rows), rows)]

    own = net.local(mine, block(p.t))
    load_wo = net.local(wo_hbm, wo)
    load_att = net.local(att_hbm, att)
    load_qkv = net.local(qkv_hbm, qkv)
    load_act = net.local(act_hbm, act)
    load_w = net.local(wqkv_hbm, wqkv)
    load_whole = net.local(whole_hbm, whole)
    greet(p, ("x", "y", "c", "z"))
    own.wait()
    net.put(block(p.t), block(p.t), "y", ("bg", "y"))
    net.put(block(p.t), block(p.t), "c", ("bg", "c0"))

    def load_other(i):
        zz = p.far[i]
        return [
            pltpu.make_async_copy(out_part.at[zz, :, :, c], acc.at[zz], other_sems.at[0, i % 2]),
            pltpu.make_async_copy(out_other.at[zz], other.at[i % 2], other_sems.at[1, i % 2]),
        ]

    for i in range(2):
        for copy in load_other(i):
            copy.start()

    def fill(i, zz):
        for copy in load_other(i):
            copy.wait()
        for xx in range(2):
            for yy in range(2):
                add_rows(acc.at[zz, xx, yy], other.at[i % 2, xx, yy], rows)
        if i + 2 < depth:
            for copy in load_other(i + 2):
                copy.start()

    flow = Reduce(net, "out", fill, acc, ya, xa, xb, yb, inbox, z_inbox, xc, yc)

    def o_pair(z):
        return o_acc.at[:, pl.ds(pl.multiple_of(z * (2 * o_cols), LANES), 2 * o_cols)]

    def o_step(i):
        if i < depth:
            chain_z(net, "oz", p.far[i], o_pair(p.far[i]), o_inbox, o_rows)

    def o_along_x():
        theirs = pl.ds(pl.multiple_of((p.z * 2 + 1 - x) * o_cols, LANES), o_cols)
        net.put(o_acc.at[:, theirs], o_rx, "x", ("ox",))

    def rows_in():
        far = block((1 - y) * 2 + c)
        net.got(far, ("bg", "y"))
        net.put(far, far, "c", ("bg", "c1"))
        net.got(block(y * 2 + 1 - c), ("bg", "c0"))
        net.got(block((1 - y) * 2 + 1 - c), ("bg", "c1"))

    def attended_grad():
        load_wo.wait()
        ag[...] = lax.dot_general(
            bg[...], wo[...], CONTRACT_LAST, preferred_element_type=F32
        ).astype(BF16)

    wide = 512

    def o_body(i, carry):
        at = pl.ds(pl.multiple_of(i * wide, wide), wide)
        found = lax.dot_general(
            att[...], bg[:, at], CONTRACT_FIRST, preferred_element_type=F32
        ).astype(BF16)
        o_acc[:, at] = found[:o_rows]
        o_rest[:, at] = found[o_rows:]
        return carry

    def o_terms():
        load_att.wait()
        load_qkv.wait()
        lax.fori_loop(0, width // wide, o_body, 0)

    scale = 1.0 / math.sqrt(HEAD)
    same = same_document(seg_row)

    def head(h):
        at = slice(h * HEAD, (h + 1) * HEAD)
        query = qkv[:, h * HEAD : (h + 1) * HEAD]
        keys = qkv[:, cols + h * HEAD : cols + (h + 1) * HEAD]
        values = qkv[:, 2 * cols + h * HEAD : 2 * cols + (h + 1) * HEAD]
        grad = ag[:, at]
        scores = lax.dot_general(query, keys, CONTRACT_LAST, preferred_element_type=F32) * scale
        scores = jnp.where(same, scores, -1e30)
        expo = jnp.exp(scores - jnp.max(scores, axis=-1, keepdims=True))
        probs = expo / jnp.sum(expo, axis=-1, keepdims=True)
        prob_grad = lax.dot_general(grad, values, CONTRACT_LAST, preferred_element_type=F32)
        inner = jnp.sum(probs * prob_grad, axis=-1, keepdims=True)
        score_grad = (probs * (prob_grad - inner) * scale).astype(BF16)
        low[:, at] = jnp.dot(score_grad, keys, preferred_element_type=F32).astype(BF16)
        low[:, cols + h * HEAD : cols + (h + 1) * HEAD] = lax.dot_general(
            score_grad, query, CONTRACT_FIRST, preferred_element_type=F32
        ).astype(BF16)
        low[:, 2 * cols + h * HEAD : 2 * cols + (h + 1) * HEAD] = lax.dot_general(
            probs.astype(BF16), grad, CONTRACT_FIRST, preferred_element_type=F32
        ).astype(BF16)

    w_rows, w_cols = wqkv.shape[2:]

    def w_body(f, carry):
        at = pl.ds(pl.multiple_of(f * w_rows, w_rows), w_rows)
        qkv_part[f] = lax.dot_general(
            act[:, at], low[...], CONTRACT_FIRST, preferred_element_type=F32
        ).astype(BF16)
        act_grad[:, at] = sum(
            lax.dot_general(
                low[:, i * w_cols : (i + 1) * w_cols], wqkv[i, f], CONTRACT_LAST,
                preferred_element_type=F32,
            )
            for i in range(3)
        )
        return carry

    count = wqkv.shape[1]
    pieces = 4

    def w_piece(i):
        if i == 0:
            load_act.wait()
            load_w.wait()
        lax.fori_loop(i * count // pieces, (i + 1) * count // pieces, w_body, 0)

    def norm_piece(i):
        if i == 0:
            load_whole.wait()
            gain_part[...] = jnp.zeros_like(gain_part)
        span = seq // pieces // 16

        def body(k, total):
            at = pl.ds(pl.multiple_of((i * span + k) * 16, 16), 16)
            values, grad = whole[at, :].astype(F32), act_grad[at, :]
            inverse = lax.rsqrt(jnp.mean(values * values, axis=-1, keepdims=True) + EPSILON)
            scaled = gain[...] * grad
            pull = jnp.mean(values * scaled, axis=-1, keepdims=True)
            whole_part[at, :] = (
                inverse * scaled - values * (inverse * inverse * inverse) * pull
            ).astype(BF16)
            return total + jnp.sum(grad * values * inverse, axis=0, keepdims=True)

        total = lax.fori_loop(0, span, body, jnp.zeros(gain_part.shape, F32))
        gain_part[...] += total

    one, two, three, along_z = flow.one, flow.two, flow.three, flow.along_z
    if depth == 4 and heads == 4:
        perform(
            (one, 0), (along_z, 0), (one, 1), (along_z, 1), (rows_in,), (attended_grad,),
            (o_terms,), (o_step, 0), (two, 0), (one, 2), (along_z, 2), (head, 0), (head, 1),
            (o_step, 1), (o_step, 2), (two, 1), (head, 2), (head, 3), (one, 3), (along_z, 3),
            (three, 0), (w_piece, 0), (two, 2), (o_step, 3), (flow.then_x,), (w_piece, 1),
            (three, 1), (three, 2), (o_along_x,), (two, 3), (w_piece, 2), (flow.then_y,),
            (w_piece, 3), (norm_piece, 0), (norm_piece, 1), (norm_piece, 2), (three, 3),
            (norm_piece, 3), (flow.end,),
        )
    else:
        perform(*every(depth, one), (rows_in,), (attended_grad,), (o_terms,))
        perform(*every(heads, head), *every(pieces, w_piece, norm_piece))
        perform(*every(depth, two, three, along_z, o_step), (o_along_x,))
        perform((flow.then_x,), (flow.then_y,), (flow.end,))

    def add_resid(i, carry):
        at = pl.ds(pl.multiple_of(i * 16, 16), 16)
        output[at, :] = (resid[at, :] + acc[p.z, x, y, at, :].astype(F32)).astype(BF16)
        return carry

    lax.fori_loop(0, rows // 16, add_resid, 0)
    net.got(o_rx, ("ox",))
    at_o = pl.ds(pl.multiple_of((p.z * 2 + x) * o_cols, LANES), o_cols)

    def o_last(i, carry):
        at = pl.ds(pl.multiple_of(i * 16, 16), 16)
        o_sum[at, :] = o_acc[at, at_o].astype(F32) + o_rx[at, :].astype(F32)
        return carry

    lax.fori_loop(0, o_rows // 16, o_last, 0)
    net.finish()


def attend_back(
    depth, mine, act, wqkv, wo, qkv, att, whole, segments, gain, resid, out_part, out_other, o_cols
):
    rows, width = mine.shape
    seq, cols = att.shape
    _, fsdp, w_rows, w_cols = wqkv.shape
    w_wide = 3 * w_cols
    shape = jax.ShapeDtypeStruct
    return pl.pallas_call(
        functools.partial(attend_back_kernel, depth),
        out_shape=[
            shape((fsdp, w_rows, w_wide), BF16),
            shape((seq, width), BF16),
            shape((1, width), F32),
            shape((cols // 2, o_cols), F32),
            shape((cols // 2, width), BF16),
            shape((rows, width), BF16),
        ],
        in_specs=[ANY] * 7 + [VMEM] * 3 + [ANY] * 2,
        out_specs=[VMEM] * 6,
        scratch_shapes=reduce_scratch(
            depth, rows, width, [tile_rows(rows, 0.375), tile_rows(rows, 0.5)]
        )
        + [
            pltpu.VMEM((2, 2, 2, rows, width), BF16),
            pltpu.VMEM((seq, width), BF16),
            pltpu.VMEM((seq, width), BF16),
            pltpu.VMEM(wqkv.shape, BF16),
            pltpu.VMEM((cols, width), BF16),
            pltpu.VMEM((seq, w_wide), BF16),
            pltpu.VMEM((seq, cols), BF16),
            pltpu.VMEM((seq, cols), BF16),
            pltpu.VMEM((seq, w_wide), BF16),
            pltpu.VMEM((cols // 2, width), BF16),
            pltpu.VMEM((depth + 1, cols // 2, 2 * o_cols), BF16),
            pltpu.VMEM((cols // 2, o_cols), BF16),
            pltpu.VMEM((seq, width), BF16),
            pltpu.VMEM((seq, width), F32),
        ]
        + sems()
        + [pltpu.SemaphoreType.DMA((2, 2))],
        compiler_params=comm_params(4, 63),
        name="attend_back",
    )(
        mine, act, wqkv, wo, qkv, att, whole, segments[None, :], gain[None, :], resid,
        out_part.reshape(depth, 2, 2, 2, rows, width), out_other,
    )


def last_kernel(
    depth, tail, qkv_part, row_part, o_part, q_sum, k_sum, v_sum, row_sum, tail_sum, o_sum,
    q_acc, q_rx, q_inbox, t_acc, t_rc, t_ry, s_acc, s_rc, s_ry, s_rx, s_inbox,
    o_acc, o_inbox, o_rx, send, recv, local,
):
    p = Place(depth)
    net = Net(p, send, recv, local)
    x, y, c = p.x, p.y, p.c
    rows, width = row_sum.shape
    w_rows, w_cols = q_sum.shape
    o_rows, o_cols = o_sum.shape
    small = s_acc.shape[3]
    o_load = net.local(o_part, o_acc)
    t_load = net.local(row_part.at[:, c], t_acc)
    s_load = net.local(tail.at[:, :, :, c], s_acc)
    loads = [net.local(qkv_part.at[p.far[i], x], q_acc.at[p.far[i]]) for i in range(depth)]
    greet(p, ("x", "y", "c", "z"))

    def q_along_x(i):
        zz = p.far[i]
        net.put(qkv_part.at[zz, 1 - x], q_rx.at[zz], "x", ("qx", "at", depth, zz))

    def q_along_z(i):
        zz = p.far[i]
        loads[i].wait()
        net.got(q_rx.at[zz], ("qx", "at", depth, zz))
        add_rows(q_acc.at[zz], q_rx.at[zz], w_rows)
        chain_z(net, "qz", zz, q_acc.at[zz], q_inbox, w_rows)

    def o_along_z(i):
        if i == 0:
            o_load.wait()
        zz = p.far[i]
        pair = o_acc.at[:, pl.ds(pl.multiple_of(zz * (2 * o_cols), LANES), 2 * o_cols)]
        chain_z(net, "oz", zz, pair, o_inbox, o_rows)

    def o_along_x():
        theirs = pl.ds(pl.multiple_of((p.z * 2 + 1 - x) * o_cols, LANES), o_cols)
        net.put(o_acc.at[:, theirs], o_rx, "x", ("ox",))

    def cores():
        net.put(row_part.at[:, 1 - c], t_rc, "c", ("tc",))
        net.put(tail.at[:, :, :, 1 - c], s_rc, "c", ("sc",))

    def along_y():
        t_load.wait()
        net.got(t_rc, ("tc",))
        add_rows(t_acc.at[1 - y], t_rc.at[1 - y], rows)
        net.put(t_acc.at[1 - y], t_ry, "y", ("ty",))
        s_load.wait()
        net.got(s_rc, ("sc",))
        for zz in range(depth):
            for xx in range(2):
                add_rows(s_acc.at[zz, xx, 1 - y], s_rc.at[zz, xx, 1 - y], small)
        net.put(s_acc.at[:, :, 1 - y], s_ry, "y", ("sy",))
        for zz in range(depth):
            for xx in range(2):
                add_rows(s_acc.at[zz, xx, y], s_rc.at[zz, xx, y], small)

    def s_along_x():
        net.got(s_ry, ("sy",))
        for z in range(depth):
            for xx in range(2):
                add_rows(s_acc.at[z, xx, y], s_ry.at[z, xx], small)
        net.put(s_acc.at[:, 1 - x, y], s_rx, "x", ("sx",))

    def s_in():
        net.got(s_rx, ("sx",))
        for z in range(depth):
            add_rows(s_acc.at[z, x, y], s_rx.at[z], small)

    def s_along_z(i):
        chain_z(net, "sz", p.far[i], s_acc.at[p.far[i], x, y], s_inbox, small)

    def rows_in():
        net.got(t_ry, ("ty",))

        def body(i, carry):
            at = pl.ds(pl.multiple_of(i * 16, 16), 16)
            row_sum[at, :] = (
                t_acc[y, at, :].astype(F32) + t_rc[y, at, :].astype(F32) + t_ry[at, :].astype(F32)
            )
            return carry

        lax.fori_loop(0, rows // 16, body, 0)

    def o_in():
        net.got(o_rx, ("ox",))
        at_o = pl.ds(pl.multiple_of((p.z * 2 + x) * o_cols, LANES), o_cols)

        def body(i, carry):
            at = pl.ds(pl.multiple_of(i * 16, 16), 16)
            o_sum[at, :] = o_acc[at, at_o].astype(F32) + o_rx[at, :].astype(F32)
            return carry

        lax.fori_loop(0, o_rows // 16, body, 0)

    if depth == 4:
        perform(
            (q_along_x, 0), (cores,), (o_along_z, 0), (q_along_x, 1), (o_along_z, 1), (along_y,),
            (o_along_z, 2), (s_along_x,), (q_along_x, 2), (q_along_z, 0), (q_along_x, 3),
            (o_along_z, 3), (rows_in,), (s_in,), (o_along_x,), (s_along_z, 0), (q_along_z, 1),
            (q_along_z, 2), (s_along_z, 1), (o_in,), (s_along_z, 2), (q_along_z, 3),
            (s_along_z, 3),
        )
    else:
        perform(*every(depth, q_along_x), (cores,), (along_y,), (s_along_x,))
        perform(*every(depth, q_along_z, o_along_z), (s_in,), (o_along_x,))
        perform(*every(depth, s_along_z), (rows_in,), (o_in,))

    def q_last(i, carry):
        at = pl.ds(pl.multiple_of(i * 16, 16), 16)
        for j, ref in enumerate((q_sum, k_sum, v_sum)):
            ref[at, :] = q_acc[p.z, at, pl.ds(j * w_cols, w_cols)].astype(F32)
        return carry

    lax.fori_loop(0, w_rows // 16, q_last, 0)
    widen(tail_sum, s_acc.at[p.z, x, y], small)
    net.finish()


def last_reduce(depth, tail, qkv_part, row_part, o_part):
    count, small, lanes = tail.shape
    fsdp, w_rows, w_wide = qkv_part.shape
    tp, rows, width = row_part.shape
    w_cols = w_wide // 3
    o_rows, o_cols = o_part.shape[0], width // fsdp
    shape = jax.ShapeDtypeStruct
    return pl.pallas_call(
        functools.partial(last_kernel, depth),
        out_shape=[shape((w_rows, w_cols), F32)] * 3
        + [shape((rows, width), F32), shape((small, lanes), F32), shape((o_rows, o_cols), F32)],
        in_specs=[ANY] * 4,
        out_specs=[VMEM] * 6,
        scratch_shapes=[
            pltpu.VMEM((depth, w_rows, w_wide), BF16),
            pltpu.VMEM((depth, w_rows, w_wide), BF16),
            pltpu.VMEM((depth + 1, w_rows, w_wide), BF16),
            pltpu.VMEM((2, rows, width), BF16),
            pltpu.VMEM((2, rows, width), BF16),
            pltpu.VMEM((rows, width), BF16),
            pltpu.VMEM((depth, 2, 2, small, lanes), BF16),
            pltpu.VMEM((depth, 2, 2, small, lanes), BF16),
            pltpu.VMEM((depth, 2, small, lanes), BF16),
            pltpu.VMEM((depth, small, lanes), BF16),
            pltpu.VMEM((depth + 1, small, lanes), BF16),
            pltpu.VMEM((o_rows, width), BF16),
            pltpu.VMEM((depth + 1, o_rows, 2 * o_cols), BF16),
            pltpu.VMEM((o_rows, o_cols), BF16),
        ]
        + sems(),
        compiler_params=comm_params(5, 48),
        name="last_reduce",
    )(
        tail.reshape(depth, 2, 2, 2, small, lanes),
        qkv_part.reshape(depth, 2, w_rows, w_wide),
        row_part.reshape(2, 2, rows, width),
        o_part,
    )


def norm_rows(values, gain):
    inverse = lax.rsqrt(jnp.mean(values * values, axis=-1, keepdims=True) + EPSILON)
    return (values * inverse * gain, inverse)


def norm_back(values, inverse, gain, grad):
    scaled = gain * grad
    gain_grad = jnp.sum(grad * values * inverse, axis=0)
    cubed = inverse * inverse * inverse
    values_grad = inverse * scaled - values * cubed * jnp.mean(
        values * scaled, axis=-1, keepdims=True
    )
    return (values_grad, gain_grad)


def contract_last(left, right):
    return lax.dot_general(
        left, right, (((1,), (1,)), ((), ())), preferred_element_type=jnp.float32
    )


def contract_first(left, right):
    return lax.dot_general(
        left, right, (((0,), (0,)), ((), ())), preferred_element_type=jnp.float32
    )


def dense_layer(
    inputs, out_grad, segments, routes, attn_gain, w_query, w_key, w_value, w_output,
    moe_gain, router, w_gate, w_up, w_down,
):
    tp, fsdp = lax.axis_size("tp"), lax.axis_size("fsdp")
    depth = fsdp // 2
    rows, width = inputs.shape
    local_experts = w_gate.shape[0]
    experts = local_experts * fsdp
    top_k = routes.shape[1]
    capacity = 3 * rows * top_k // (2 * experts)
    w_rows, w_cols = w_query.shape
    heads = w_cols // HEAD
    seq = tp * rows

    named = jnp.any(
        routes[:, :, None] == jnp.arange(experts, dtype=jnp.int32)[None, None, :], axis=1
    )
    hits = named.astype(F32)
    before = (jnp.arange(rows)[:, None] > jnp.arange(rows)[None, :]).astype(F32)
    ranks = jnp.where(named, jnp.dot(before, hits, preferred_element_type=F32), -1.0)
    fill = jnp.zeros((rows, LANES - 3 * experts), F32)
    blank = jnp.zeros((rows, experts), F32)
    mask = jnp.concatenate([hits, hits, blank, fill], axis=1)
    rank = jnp.concatenate([blank, blank, ranks, fill], axis=1)
    qkv_full, full_output, whole, act_one, qkv, attended, partial, grad_all = first_gather(
        depth, w_query, w_key, w_value, w_output, inputs, out_grad, attn_gain, segments, tp
    )
    resid, gates_wide, _, _, out_part, back_part, x_rows, g_rows, hid_low, gate_low, up_low = run_moe(
        depth, capacity, experts, partial.reshape(tp, rows, width), inputs, out_grad, moe_gain,
        router.T, mask, rank, w_gate, w_up, w_down, grad_all,
    )
    back, out_other, w_gate_grad, w_up_grad, w_down_grad = reduce_back(
        depth, back_part, out_part, x_rows, g_rows, hid_low, gate_low, up_low
    )
    gates = gates_wide[:, :experts]
    act_two = (
        resid
        * (inverse_two := lax.rsqrt(jnp.mean(resid * resid, axis=-1, keepdims=True) + EPSILON))
        * moe_gain
    ).astype(BF16)
    gate_grad = jnp.sum(back[:, width : width + tp * experts].reshape(rows, tp, experts), axis=1)
    logit_grad = gates * (gate_grad - jnp.sum(gates * gate_grad, axis=1, keepdims=True))
    act_two_grad = back[:, :width] + lax.dot_general(
        logit_grad, router.astype(F32), (((1,), (1,)), ((), ())), precision=HIGHEST
    )
    router_part = lax.dot_general(
        act_two.astype(F32), logit_grad, (((0,), (0,)), ((), ())), precision=HIGHEST
    )
    resid_part, gain_two_part = norm_back(resid, inverse_two, moe_gain, act_two_grad)
    resid_grad = out_grad.astype(F32) + resid_part
    qkv_part, whole_part, gain_one_part, o_first, o_rest, output = attend_back(
        depth, resid_grad.astype(BF16), act_one, qkv_full, full_output, qkv, attended,
        whole.reshape(seq, width), segments, attn_gain, resid, out_part, out_other,
        w_output.shape[1],
    )
    count = fsdp * tp
    piece = width // count
    small = jnp.concatenate([router_part, gain_one_part.reshape(-1, 1), gain_two_part[:, None]], axis=1)
    small = small.astype(BF16).reshape(count, piece, experts + 2)
    tail = jnp.pad(small, ((0, 0), (0, -piece % 16), (0, LANES - experts - 2)))
    q_sum, k_sum, v_sum, row_sum, side, o_second = last_reduce(
        depth, tail, qkv_part, whole_part.reshape(tp, rows, width), o_rest
    )
    o_sum = jnp.concatenate([o_first, o_second], axis=0)
    input_grad = resid_grad + row_sum
    side = side[:piece]
    return (
        output,
        input_grad,
        side[:, experts],
        q_sum,
        k_sum,
        v_sum,
        o_sum,
        side[:, experts + 1],
        side[:, :experts],
        w_gate_grad.astype(F32),
        w_up_grad.astype(F32),
        w_down_grad.astype(F32),
    )


def send_rows(buffer):
    return lax.all_to_all(buffer, "fsdp", split_axis=1, concat_axis=1, tiled=True)


def per_device(
    inputs,
    out_grad,
    segments,
    routes,
    attn_gain,
    w_query,
    w_key,
    w_value,
    w_output,
    moe_gain,
    router,
    w_gate,
    w_up,
    w_down,
):
    tp_count = lax.axis_size("tp")
    fsdp_count = lax.axis_size("fsdp")
    rows_piece, width = inputs.shape
    head_size = HEAD
    full_query, full_key, full_value, full_output = (
        lax.all_gather(w_query, "fsdp", axis=0, tiled=True),
        lax.all_gather(w_key, "fsdp", axis=0, tiled=True),
        lax.all_gather(w_value, "fsdp", axis=0, tiled=True),
        lax.all_gather(w_output, "fsdp", axis=1, tiled=True),
    )
    whole_rows = lax.all_gather(inputs, "tp", axis=0, tiled=True)
    seq_len = whole_rows.shape[0]
    whole_float = whole_rows.astype(jnp.float32)
    normed_one, inverse_one = norm_rows(whole_float, attn_gain)
    act_one = normed_one.astype(jnp.bfloat16)
    local_heads = full_query.shape[1] // head_size
    query = (
        jnp.dot(act_one, full_query, preferred_element_type=jnp.float32)
        .astype(jnp.bfloat16)
        .reshape(seq_len, local_heads, head_size)
    )
    key_rows = (
        jnp.dot(act_one, full_key, preferred_element_type=jnp.float32)
        .astype(jnp.bfloat16)
        .reshape(seq_len, local_heads, head_size)
    )
    value_rows = (
        jnp.dot(act_one, full_value, preferred_element_type=jnp.float32)
        .astype(jnp.bfloat16)
        .reshape(seq_len, local_heads, head_size)
    )
    block_rows = min(512, seq_len)
    score_scale = 1.0 / math.sqrt(head_size)

    def block_scores(query_block):
        scores = (
            jnp.einsum("qhd,khd->hqk", query_block, key_rows, preferred_element_type=jnp.float32)
            * score_scale
        )
        same_doc = segments[:, None] == segments[None, :]
        return jnp.where(same_doc[None], scores, -1e30)

    scores = block_scores(query)
    peak = jnp.max(scores, axis=-1, keepdims=True)
    expo = jnp.exp(scores - peak)
    total = jnp.sum(expo, axis=-1, keepdims=True)
    softmax_rows = (expo / total).astype(jnp.bfloat16)
    block_outputs = jnp.einsum(
        "hqk,khd->qhd", softmax_rows, value_rows, preferred_element_type=jnp.float32
    )
    log_totals = [peak + jnp.log(total)]
    attended = block_outputs.reshape(seq_len, -1).astype(jnp.bfloat16)
    branch = lax.psum_scatter(
        jnp.dot(attended, full_output, preferred_element_type=jnp.float32).astype(jnp.bfloat16),
        "tp",
        scatter_dimension=0,
        tiled=True,
    ).astype(jnp.float32)
    resid = inputs.astype(jnp.float32) + branch
    normed_two, inverse_two = norm_rows(resid, moe_gain)
    act_two = normed_two.astype(jnp.bfloat16)
    local_experts = w_gate.shape[0]
    experts = local_experts * fsdp_count
    top_k = routes.shape[1]
    capacity = 3 * rows_piece * top_k // (2 * experts)
    logits = jnp.dot(act_two, router, preferred_element_type=jnp.float32)
    picks = (routes[:, :, None] == jnp.arange(experts, dtype=jnp.int32)[None, None, :]).astype(
        jnp.float32
    )
    chosen = jnp.einsum("tke,te->tk", picks, logits, precision=HIGHEST)
    gates = jax.nn.softmax(chosen, axis=-1)
    flat_routes = routes.reshape(-1)
    route_count = flat_routes.shape[0]
    hits = (flat_routes[:, None] == jnp.arange(experts, dtype=jnp.int32)[None, :]).astype(jnp.int32)
    ranks = jnp.sum((jnp.cumsum(hits, axis=0) - 1) * hits, axis=1)
    slots = flat_routes * capacity + ranks
    sources = (
        jnp.full((experts * capacity,), route_count, jnp.int32)
        .at[slots]
        .set(jnp.arange(route_count, dtype=jnp.int32))
    )
    padded_act = jnp.concatenate([act_two, jnp.zeros((1, width), jnp.bfloat16)], 0)
    send_buffer = padded_act[sources // top_k].reshape(
        1, fsdp_count, local_experts * capacity, width
    )
    gate_full, up_full, down_full = (
        lax.all_gather(w_gate, "tp", axis=2, tiled=True),
        lax.all_gather(w_up, "tp", axis=2, tiled=True),
        lax.all_gather(w_down, "tp", axis=1, tiled=True),
    )
    own_in = send_rows(send_buffer)
    own_rows = own_in.reshape(fsdp_count, local_experts, capacity, width)
    own_gate = jnp.einsum("secd,edf->secf", own_rows, gate_full, preferred_element_type=jnp.float32)
    own_up = jnp.einsum("secd,edf->secf", own_rows, up_full, preferred_element_type=jnp.float32)
    own_sigmoid = jax.nn.sigmoid(own_gate)
    own_silu = own_gate * own_sigmoid
    own_hidden = (own_silu * own_up).astype(jnp.bfloat16)
    own_out = jnp.einsum(
        "secf,efd->secd", own_hidden, down_full, preferred_element_type=jnp.float32
    )
    expert_out = own_out.reshape(1, fsdp_count, local_experts * capacity, width).astype(
        jnp.bfloat16
    )
    returned = lax.all_to_all(expert_out, "fsdp", split_axis=1, concat_axis=1, tiled=True).reshape(
        experts * capacity, width
    )
    routed = returned[slots].reshape(rows_piece, top_k, width).astype(jnp.float32)
    mixture = jnp.sum(gates[:, :, None] * routed, axis=1)
    output = (resid + mixture).astype(jnp.bfloat16)
    grad_float = out_grad.astype(jnp.float32)
    gate_grad = jnp.sum(routed * grad_float[:, None, :], axis=2)
    route_grad = (
        (gates[:, :, None] * grad_float[:, None, :])
        .astype(jnp.bfloat16)
        .reshape(route_count, width)
    )
    padded_grad = jnp.concatenate([route_grad, jnp.zeros((1, width), jnp.bfloat16)], 0)
    grad_buffer = padded_grad[sources].reshape(1, fsdp_count, local_experts * capacity, width)
    own_grads = send_rows(grad_buffer).reshape(fsdp_count, local_experts, capacity, width)
    own_hidden_grad = jnp.einsum(
        "secd,efd->secf", own_grads, down_full, preferred_element_type=jnp.float32
    )
    own_gate_low = (
        own_hidden_grad * own_up * own_sigmoid * (1.0 + own_gate * (1.0 - own_sigmoid))
    ).astype(jnp.bfloat16)
    own_up_low = (own_hidden_grad * own_silu).astype(jnp.bfloat16)
    down_term = jnp.einsum(
        "secf,secd->efd", own_hidden, own_grads, preferred_element_type=jnp.float32
    )
    gate_term = jnp.einsum(
        "secd,secf->edf", own_rows, own_gate_low, preferred_element_type=jnp.float32
    )
    up_term = jnp.einsum("secd,secf->edf", own_rows, own_up_low, preferred_element_type=jnp.float32)
    w_gate_grad, w_up_grad, w_down_grad = (
        lax.psum_scatter(
            gate_term.astype(jnp.bfloat16), "tp", scatter_dimension=2, tiled=True
        ).astype(jnp.float32),
        lax.psum_scatter(
            up_term.astype(jnp.bfloat16), "tp", scatter_dimension=2, tiled=True
        ).astype(jnp.float32),
        lax.psum_scatter(
            down_term.astype(jnp.bfloat16), "tp", scatter_dimension=1, tiled=True
        ).astype(jnp.float32),
    )
    own_back = jnp.einsum(
        "secf,edf->secd", own_gate_low, gate_full, preferred_element_type=jnp.float32
    )
    own_back = own_back + jnp.einsum(
        "secf,edf->secd", own_up_low, up_full, preferred_element_type=jnp.float32
    )
    expert_grad = own_back.reshape(1, fsdp_count, local_experts * capacity, width).astype(
        jnp.bfloat16
    )
    back_rows = lax.all_to_all(
        expert_grad, "fsdp", split_axis=1, concat_axis=1, tiled=True
    ).reshape(experts * capacity, width)
    act_two_grad = jnp.sum(
        back_rows[slots].reshape(rows_piece, top_k, width).astype(jnp.float32), axis=1
    )
    centered = gate_grad - jnp.sum(gates * gate_grad, axis=1, keepdims=True)
    chosen_grad = gates * centered
    logit_grad = jnp.einsum("tke,tk->te", picks, chosen_grad, precision=HIGHEST)
    router_float = router.astype(jnp.float32)
    act_two_grad = act_two_grad + lax.dot_general(
        logit_grad, router_float, (((1,), (1,)), ((), ())), precision=HIGHEST
    )
    router_part = lax.dot_general(
        act_two.astype(jnp.float32), logit_grad, (((0,), (0,)), ((), ())), precision=HIGHEST
    )
    resid_part, gain_two_part = norm_back(resid, inverse_two, moe_gain, act_two_grad)
    resid_grad = grad_float + resid_part
    branch_grad = lax.all_gather(resid_grad.astype(jnp.bfloat16), "tp", axis=0, tiled=True)
    attended_grad = (
        contract_last(branch_grad, full_output)
        .astype(jnp.bfloat16)
        .reshape(seq_len, local_heads, head_size)
    )
    w_output_part = contract_first(attended, branch_grad)
    query_parts = []
    key_grad = jnp.zeros((seq_len, local_heads, head_size), jnp.float32)
    value_grad = jnp.zeros((seq_len, local_heads, head_size), jnp.float32)
    for block_index, first_row in enumerate(range(0, seq_len, block_rows)):
        query_block = query
        scores = block_scores(query_block)
        softmax_rows = jnp.exp(scores - log_totals[block_index])
        prob_grad = jnp.einsum(
            "qhd,khd->hqk", attended_grad, value_rows, preferred_element_type=jnp.float32
        )
        inner = jnp.sum(softmax_rows * prob_grad, axis=-1, keepdims=True)
        score_grad = (softmax_rows * (prob_grad - inner) * score_scale).astype(jnp.bfloat16)
        query_parts.append(
            jnp.einsum("hqk,khd->qhd", score_grad, key_rows, preferred_element_type=jnp.float32)
        )
        key_grad = jnp.einsum(
            "hqk,qhd->khd", score_grad, query_block, preferred_element_type=jnp.float32
        )
        value_grad = jnp.einsum(
            "hqk,qhd->khd",
            softmax_rows.astype(jnp.bfloat16),
            attended_grad,
            preferred_element_type=jnp.float32,
        )
    query_low = query_parts[0].reshape(seq_len, -1).astype(jnp.bfloat16)
    key_low = key_grad.reshape(seq_len, -1).astype(jnp.bfloat16)
    value_low = value_grad.reshape(seq_len, -1).astype(jnp.bfloat16)
    w_query_part = contract_first(act_one, query_low)
    w_key_part = contract_first(act_one, key_low)
    w_value_part = contract_first(act_one, value_low)
    act_one_grad = (
        contract_last(query_low, full_query)
        + contract_last(key_low, full_key)
        + contract_last(value_low, full_value)
    )
    whole_part, gain_one_part = norm_back(whole_float, inverse_one, attn_gain, act_one_grad)

    def arrange(values):
        shaped = values.reshape((fsdp_count, tp_count, -1) + values.shape[1:])
        return jnp.swapaxes(shaped, 0, 1)

    input_part, gain_one_tp, gain_two_tp, router_tp = (
        lax.psum_scatter(
            whole_part.astype(jnp.bfloat16), "tp", scatter_dimension=0, tiled=True
        ).astype(jnp.float32),
        lax.psum_scatter(
            arrange(gain_one_part).astype(jnp.bfloat16), "tp", scatter_dimension=0, tiled=True
        ).astype(jnp.float32),
        lax.psum_scatter(
            arrange(gain_two_part).astype(jnp.bfloat16), "tp", scatter_dimension=0, tiled=True
        ).astype(jnp.float32),
        lax.psum_scatter(
            arrange(router_part).astype(jnp.bfloat16), "tp", scatter_dimension=0, tiled=True
        ).astype(jnp.float32),
    )
    input_grad = resid_grad + input_part
    query_sum, key_sum, value_sum, output_sum, gain_one_sum, gain_two_sum, router_sum = (
        lax.psum_scatter(
            w_query_part.astype(jnp.bfloat16), "fsdp", scatter_dimension=0, tiled=True
        ).astype(jnp.float32),
        lax.psum_scatter(
            w_key_part.astype(jnp.bfloat16), "fsdp", scatter_dimension=0, tiled=True
        ).astype(jnp.float32),
        lax.psum_scatter(
            w_value_part.astype(jnp.bfloat16), "fsdp", scatter_dimension=0, tiled=True
        ).astype(jnp.float32),
        lax.psum_scatter(
            w_output_part.astype(jnp.bfloat16), "fsdp", scatter_dimension=1, tiled=True
        ).astype(jnp.float32),
        lax.psum_scatter(
            gain_one_tp.astype(jnp.bfloat16), "fsdp", scatter_dimension=1, tiled=True
        ).astype(jnp.float32),
        lax.psum_scatter(
            gain_two_tp.astype(jnp.bfloat16), "fsdp", scatter_dimension=1, tiled=True
        ).astype(jnp.float32),
        lax.psum_scatter(
            router_tp.astype(jnp.bfloat16), "fsdp", scatter_dimension=1, tiled=True
        ).astype(jnp.float32),
    )
    return (
        output,
        input_grad,
        gain_one_sum.reshape(-1),
        query_sum,
        key_sum,
        value_sum,
        output_sum,
        gain_two_sum.reshape(-1),
        router_sum.reshape(-1, experts),
        w_gate_grad,
        w_up_grad,
        w_down_grad,
    )


def layer(*args):
    tokens = args[0].shape[0] * lax.axis_size("fsdp") * lax.axis_size("tp")
    held = 6 * tokens * (args[0].shape[1] + LANES) * 2
    even = lax.axis_size("tp") == 4 and lax.axis_size("fsdp") % 2 == 0
    experts = args[11].shape[0] * lax.axis_size("fsdp")
    narrow = lax.axis_size("tp") * experts <= LANES and args[1].shape[1] // (lax.axis_size("tp") * lax.axis_size("fsdp")) <= args[0].shape[0]
    if held <= HBM_BUDGET and even and narrow:
        return dense_layer(*args)
    return per_device(*args)


def solution(mesh):
    return jax.shard_map(
        layer,
        mesh=mesh,
        in_specs=(
            P(("fsdp", "tp"), None),
            P(("fsdp", "tp"), None),
            P("fsdp"),
            P(("fsdp", "tp"), None),
            P(),
            P("fsdp", "tp"),
            P("fsdp", "tp"),
            P("fsdp", "tp"),
            P("tp", "fsdp"),
            P(),
            P(),
            P("fsdp", None, "tp"),
            P("fsdp", None, "tp"),
            P("fsdp", "tp", None),
        ),
        out_specs=(
            P(("fsdp", "tp"), None),
            P(("fsdp", "tp"), None),
            P(("fsdp", "tp")),
            P("fsdp", "tp"),
            P("fsdp", "tp"),
            P("fsdp", "tp"),
            P("tp", "fsdp"),
            P(("fsdp", "tp")),
            P(("fsdp", "tp"), None),
            P("fsdp", None, "tp"),
            P("fsdp", None, "tp"),
            P("fsdp", "tp", None),
        ),
        check_vma=False,
    )
```
